32 devices in a mesh: gz: 4 (over y, core), xy: 8 (over z, x).
Axes of the slice: x: 2, y: 2, z: 4, core: 2. Of those that a mesh axis runs over, the one named last changes fastest.
Arguments:
- density: float32 [128, 256, 1024], P('gz', 'xy')
- uptake: float32 [128, 256, 1024], P('gz', 'xy'), may hold values from 0.5 to 50
- brick_values: bfloat16 [2304, 4096], P(('gz', 'xy'))
- brick_ids: int32 [2304], P(('gz', 'xy')), may hold values from 0 to 8191, as said below
- slot_counts: int32 [32, 9], P(('gz', 'xy')), may hold values from 0 to 8, as said below
Outputs:
- supply: float32 [128, 256, 1024], P('gz', 'xy')
- concentration: float32 [128, 256, 1024], P('gz', 'xy')
The draws below stay inside these ranges and needn't reach their ends.
Inputs may be any that keep to these rules, and one draw needn't show every extreme that they name: `brick_ids`: the slots 8 j to 8 j + 7 of each device (j = 0 to 8) name bricks of the device whose gz index differs by j // 3 - 1 and whose xy index differs by j % 3 - 1, or of the device itself where no such device exists; the first and the last brick of the grid are both named. `slot_counts`: entry j of a device counts the live slots at the start of its block j; it is 0 where block j's device does not exist, and 8 for j = 4.
All inputs are finite; a program needn't handle non-finite values.
Results may differ from the reference program's by a relative error of at most 0.0014.
Values may be sent and summed in bfloat16 or wider, within the bound.
No kernel may reach another device: no remote copies, remote signals or barrier semaphores. Data moves between devices by JAX's collectives and lax.ppermute only.
A program may use at most 576 MiB of HBM per device.

```python
import math
import jax
import jax.numpy as jnp

CZ = 32
CX = 32
NY = 1024
EDGE = 16
CAP = 8
LEVELS = 4
NU = 2
NC = 4
BRICK = 4096
SLOTS = 72
NZ = 128
NX = 256
BZD = 2
BXD = 2
NBY = 64
NBX = 16
NBZ = 8
BPD = 256
NBRICKS = 8192
DEVICES = 32


def draw_density(key, part):
    base = jax.random.normal(key, (NZ, NX, NY), jnp.float32)
    zpos = jnp.arange(NZ, dtype=jnp.float32)[:, None, None] / NZ
    xpos = jnp.arange(NX, dtype=jnp.float32)[None, :, None] / NX
    ypos = jnp.arange(NY, dtype=jnp.float32)[None, None, :] / NY
    smooth = 0.6 * jnp.sin(2.0 * math.pi * xpos + 1.0) * jnp.cos(math.pi * zpos) + 0.3 * jnp.sin(2.0 * math.pi * ypos)
    return base + smooth


def draw_brick_values(key, part):
    noise_key = jax.random.fold_in(key, 11)
    level_key = jax.random.fold_in(key, 12)
    offsets = jax.random.uniform(level_key, (DEVICES * SLOTS, 1), jnp.float32, 0.0, 2.0)
    noise = jax.random.normal(noise_key, (DEVICES * SLOTS, BRICK), jnp.float32)
    return (noise + offsets).astype(jnp.bfloat16)


def draw_brick_ids(key, part):
    tiles = NX // CX
    slabs = NZ // CZ
    slot_index = jnp.arange(DEVICES * SLOTS, dtype=jnp.int32)
    device = slot_index // SLOTS
    direction = slot_index % SLOTS // CAP
    slab_at = device // tiles + direction // 3 - 1
    tile_at = device % tiles + direction % 3 - 1
    inside = (slab_at >= 0) & (slab_at < slabs) & (tile_at >= 0) & (tile_at < tiles)
    slab_at = jnp.where(inside, slab_at, device // tiles)
    tile_at = jnp.where(inside, tile_at, device % tiles)
    local_brick = jax.random.randint(jax.random.fold_in(key, 21), (DEVICES * SLOTS,), 0, BPD).astype(jnp.int32)
    local_brick = jnp.where(slot_index == 4 * CAP, 0, local_brick)
    local_brick = jnp.where(slot_index == (DEVICES - 1) * SLOTS + 4 * CAP, BPD - 1, local_brick)
    brick_z = local_brick // (BXD * NBY)
    brick_x = local_brick // NBY % BXD
    brick_y = local_brick % NBY
    global_id = ((slab_at * BZD + brick_z) * NBX + tile_at * BXD + brick_x) * NBY + brick_y
    return global_id.astype(jnp.int32)


def draw_slot_counts(key, part):
    tiles = NX // CX
    slabs = NZ // CZ
    counts = jax.random.randint(jax.random.fold_in(key, 31), (DEVICES, 9), 0, CAP + 1).astype(jnp.int32)
    device = jnp.arange(DEVICES, dtype=jnp.int32)[:, None]
    direction = jnp.arange(9, dtype=jnp.int32)[None, :]
    slab_at = device // tiles + direction // 3 - 1
    tile_at = device % tiles + direction % 3 - 1
    inside = (slab_at >= 0) & (slab_at < slabs) & (tile_at >= 0) & (tile_at < tiles)
    counts = jnp.where(direction == 4, CAP, counts)
    return jnp.where(inside, counts, 0).astype(jnp.int32)


def shard_levels(stream_key, shape, pieces, least, largest):
    def one(axis_at, blocks):
        heights = jax.random.uniform(jax.random.fold_in(jax.random.fold_in(stream_key, 6), axis_at), (blocks,), jnp.float32, least / len(pieces), largest / len(pieces))
        return jnp.repeat(jnp.exp(heights), shape[axis_at] // blocks).reshape((-1,) + (1,) * (len(shape) - axis_at - 1))

    level = one(*pieces[0])
    for cut in pieces[1:]:
        level = level * one(*cut)
    return level


def setup_inputs(seed: int = 0) -> dict:
    keys = jax.random.split(jax.random.key(seed), 6)
    return {
        "density": draw_density(jax.random.fold_in(keys[5], 71), 0),
        "uptake": jnp.clip(jnp.exp(math.log(50.0) - 4.6051702 * jax.random.uniform(keys[1], (NZ, NX, NY), jnp.float32) ** shard_levels(keys[1], (NZ, NX, NY), ((0, 4), (1, 8)), -0.2, 0.2)), 0.5, 50.0),
        "brick_values": draw_brick_values(jax.random.fold_in(keys[5], 71), 0),
        "brick_ids": draw_brick_ids(jax.random.fold_in(keys[5], 71), 0),
        "slot_counts": draw_slot_counts(jax.random.fold_in(keys[5], 71), 0),
    }


KAPPA = 32.0
OMEGA = 0.8


def neighbours(padded, values):
    y_padded = jnp.pad(values, ((0, 0), (0, 0), (1, 1)))
    summed = padded[2:, 1:-1] + padded[:-2, 1:-1]
    summed = summed + padded[1:-1, 2:] + padded[1:-1, :-2]
    summed = summed + y_padded[:, :, 2:] + y_padded[:, :, :-2]
    return summed


def operate(values, diagonal, spread):
    padded = jnp.pad(values, ((1, 1), (1, 1), (0, 0)))
    return diagonal * values - spread * neighbours(padded, values)


def smooth_once(values, source, diagonal, spread):
    return values + OMEGA * (source - operate(values, diagonal, spread)) / diagonal


def shrink(values):
    zsize, xsize, ysize = values.shape
    return values.reshape(zsize // 2, 2, xsize // 2, 2, ysize // 2, 2).mean(axis=(1, 3, 5))


def expand(values):
    return jnp.repeat(jnp.repeat(jnp.repeat(values, 2, 0), 2, 1), 2, 2)


def descend(level_index, source, start, rates):
    spread = KAPPA / 4.0 ** level_index
    diagonal = 1.0 + rates + 6.0 * spread
    estimate = start
    if level_index == LEVELS - 1:
        for repeat in range(NC):
            estimate = smooth_once(estimate, source, diagonal, spread)
        return estimate
    for repeat in range(NU):
        estimate = smooth_once(estimate, source, diagonal, spread)
    remainder = source - operate(estimate, diagonal, spread)
    coarser = shrink(remainder)
    update = descend(level_index + 1, coarser, jnp.zeros_like(coarser), shrink(rates))
    estimate = estimate + expand(update)
    for repeat in range(NU):
        estimate = smooth_once(estimate, source, diagonal, spread)
    return estimate


def reference(density, uptake, brick_values, brick_ids, slot_counts):
    values = brick_values.astype(jnp.float32)
    slot_index = jnp.arange(DEVICES * SLOTS, dtype=jnp.int32)
    owners = slot_index // SLOTS
    within = slot_index % SLOTS
    is_live = (within % CAP) < slot_counts[owners, within // CAP]
    values = jnp.where(is_live[:, None], values, 0.0)
    bricks = jnp.zeros((NBRICKS, BRICK), jnp.float32).at[brick_ids].add(values)
    secretion = bricks.reshape(NBZ, NBX, NBY, EDGE, EDGE, EDGE).transpose(0, 3, 1, 4, 2, 5).reshape(NZ, NX, NY)
    supply = density + secretion
    concentration = descend(0, supply, density, uptake)
    return supply, concentration
```

```python
import jax
import jax.numpy as jnp
from jax import lax
from jax.experimental import pallas as pl
from jax.experimental.pallas import tpu as pltpu
from jax.sharding import PartitionSpec as P

EDGE = 16
CAP = 8
BRICK = 4096
SLOTS = 72
KAPPA = 32.0
OMEGA = 0.8
KEEP = 1.0 - OMEGA

C = 32
NT = 8
F32 = jnp.float32
BF16 = jnp.bfloat16


def spread(level):
    return KAPPA / 4.0**level


def shifted(values, distance, axis):
    return pltpu.roll(values, distance % values.shape[axis], axis)


def iota(shape, dim):
    return lax.broadcasted_iota(jnp.int32, shape, dim)


def lanes(t):
    return slice(t * 128, (t + 1) * 128)


def along_y(tiles):
    lane = iota(tiles[0].shape, 1)
    ahead = [shifted(a, 1, 1) for a in tiles]
    behind = [shifted(a, -1, 1) for a in tiles]
    sums = []
    for t in range(len(tiles)):
        low = ahead[t - 1] if t else 0.0
        high = behind[t + 1] if t + 1 < len(tiles) else 0.0
        sums.append(jnp.where(lane == 0, low, ahead[t]) + jnp.where(lane == 127, high, behind[t]))
    return sums


def plane(ref, p):
    count = ref.shape[2] // 128
    here = [ref[p, :, lanes(t)] for t in range(count)]
    sums = along_y(here)
    for t in range(count):
        near = ref[p - 1, :, lanes(t)] + ref[p + 1, :, lanes(t)]
        near = near + (shifted(here[t], 1, 0) + shifted(here[t], -1, 0))
        sums[t] = sums[t] + near
    return here, sums


def loop(start, stop, body):
    def step(i, carry):
        body(i)
        return carry

    lax.fori_loop(start, stop, step, 0)


def split_dot(a, b):
    high = a.astype(BF16)
    low = (a - high.astype(F32)).astype(BF16)
    return jnp.dot(high, b, preferred_element_type=F32) + jnp.dot(low, b, preferred_element_type=F32)


def pooling():
    return jnp.where(iota((256, 128), 0) // 2 == iota((256, 128), 1), 0.125, 0.0).astype(BF16)


def doubling():
    return jnp.where(iota((128, 256), 1) // 2 == iota((128, 256), 0), 1.0, 0.0).astype(BF16)


def halve_rows(values, rs, t):
    rows = values.shape[0]
    rs[t, 0:rows, :] = values
    return rs[t, pl.ds(0, rows // 2, stride=2), :] + rs[t, pl.ds(1, rows // 2, stride=2), :]


def halve_lanes(xp, planes, rows):
    matrix = pooling()
    tiles = []
    for t in range(0, xp.shape[0], 2):
        pair = jnp.concatenate([xp[t].reshape(planes * rows, 128), xp[t + 1].reshape(planes * rows, 128)], axis=1)
        tiles.append(split_dot(pair, matrix).reshape(planes, rows, 128))
    return tiles


def inside(shape, dim, first, wrap, index, size, count):
    place = iota(shape, dim) + first
    if wrap is not None:
        place = jnp.where(place < wrap, place, place - shape[dim])
    place = place + index * size
    return (place >= 0) & (place < count * size)


def brick_kernel(bricks_x, ids, counts, bricks, out, xs):
    xs[...] = bricks[...].astype(F32)
    row = iota((1, 8, 128), 1)
    group = iota((1, 8, 128), 2) // 16
    group16 = iota((16, 128), 1) // 16
    per_y = 64

    def block(j):
        start = pl.multiple_of(j * 8, 8)
        x = jnp.stack([xs[pl.ds(start, 8), lanes(k)] for k in range(32)])
        for s in (4, 2, 1):
            up = shifted(shifted(x, -s, 1), 16 * s, 2)
            down = shifted(shifted(x, s, 1), -16 * s, 2)
            row_bit = (row // s) % 2
            group_bit = (group // s) % 2
            x = jnp.where(row_bit == group_bit, x, jnp.where(row_bit == 0, up, down))
        x = jnp.where(group < counts[0, j], x, 0.0)
        out[j, 0:256, :] = x.reshape(256, 128).astype(BF16)
        names = jnp.zeros((16, 128), jnp.int32)
        for e in range(CAP):
            number = ids[j * 8 + e]
            by = lax.rem(number, per_y)
            rest = lax.div(number, per_y)
            bx = lax.rem(rest, 2)
            bz = lax.rem(lax.div(rest, bricks_x), 2)
            names = jnp.where(group16 == e, (bz * 2 + bx) * per_y + by, names)
        out[j, 256:272, :] = names.astype(F32).astype(BF16)

    loop(0, 9, block)


def rates_kernel(uptake, r1, r2, rs, xp, rs1, xp1):
    def pair(m):
        for t in range(NT):
            both = uptake[2 * m, :, lanes(t)] + uptake[2 * m + 1, :, lanes(t)]
            xp[t, m] = halve_rows(both, rs, t)

    loop(0, 16, pair)
    for t, tile in enumerate(halve_lanes(xp, 16, 16)):
        r1[:, :, lanes(t)] = tile

    def pair1(m):
        for t in range(4):
            both = r1[2 * m, :, lanes(t)] + r1[2 * m + 1, :, lanes(t)]
            xp1[t, m] = halve_rows(both, rs1, t)

    loop(0, 8, pair1)
    for t, tile in enumerate(halve_lanes(xp1, 8, 8)):
        r2[:, lanes(t)] = tile.reshape(64, 128)


def pre_kernel(
    nz, nx, info, density, uptake, uzl, uzh, uxl, uxr, own, zl, zh, xl, xr, r1,
    supply, c1, mzl, mzh, vzl, vzh, pxl, pxh, v_out, g_out,
    va, vb, dd, gg, hot, rs, xp, sems,
):
    iz, ix = info[0], info[1]
    k = spread(0)
    base = 1.0 + 6.0 * k
    O = 5
    Q = 2

    for p in (0, 1, 2, 3, 4, 37, 38, 39, 40, 41):
        va[p] = jnp.zeros((40, 1024), F32)
    for p in (2, 3, 38, 39):
        vb[p] = jnp.zeros((40, 1024), F32)

    sub8 = iota((8, 1024), 0)

    def set_plane(q, rates, valid_z):
        gz = jnp.where(valid_z, OMEGA, 0.0)
        d = rates + base
        dd[q, 0:32, :] = d
        gg[q, 0:32, :] = gz / d
        high = jnp.concatenate([uxr[q], jnp.zeros((6, 1024), F32)], axis=0)
        low = jnp.concatenate([jnp.zeros((6, 1024), F32), uxl[q]], axis=0)
        d = high + low + base
        dd[q, 32:40, :] = d
        omega = jnp.where(sub8 < 2, jnp.where(ix < nx - 1, gz, 0.0), jnp.where(sub8 >= 6, jnp.where(ix > 0, gz, 0.0), 0.0))
        gg[q, 32:40, :] = omega / d

    def own_plane(z):
        va[z + O, 0:32, :] = density[z]
        va[z + O, 32:40, :] = jnp.zeros((8, 1024), F32)
        set_plane(z + Q, uptake[z], True)

    loop(0, C, own_plane)
    for i in range(2):
        set_plane(i, uzl[i].astype(F32), iz > 0)
        set_plane(34 + i, uzh[i].astype(F32), iz < nz - 1)

    blocks = [own.at[4], zl.at[1], zh.at[1]] + [xl.at[i] for i in range(3)] + [xr.at[i] for i in range(3)]
    lane = iota((1, 128), 1)
    at_y = iota((1024, 128), 0)
    tiles = []
    for i, ref in enumerate(blocks):
        name = ref[256:272, :].astype(F32).astype(jnp.int32)[0:1]
        tiles.append(lax.shift_right_logical(name, 6))
        y = (name & 63) * 16 + (lane & 15)
        hot[:, lanes(i)] = jnp.where(at_y == y, 1.0, 0.0).astype(BF16)
    for tile in range(4):
        bz, bx = tile // 2, tile % 2
        left = jnp.concatenate(
            [jnp.where(tiles[i] == tile, ref[0:256, :].astype(F32), 0.0).astype(BF16) for i, ref in enumerate(blocks)],
            axis=1,
        )
        for n in range(4):
            cols = slice(n * 256, (n + 1) * 256)
            part = lax.dot_general(left, hot[cols, :], (((1,), (1,)), ((), ())), preferred_element_type=F32)
            zs, xs = slice(16 * bz, 16 * bz + 16), slice(16 * bx, 16 * bx + 16)
            supply[zs, xs, cols] = density[zs, xs, cols] + part.reshape(16, 16, 256)

    def sweep(src, dst, z, sourced):
        here, sums = plane(src, z + O)
        for t in range(NT):
            inner = k * sums[t]
            g = gg[z + Q, :, lanes(t)]
            if sourced:
                body = inner[0:32] + supply[z, :, lanes(t)]
                dst[z + O, 0:32, lanes(t)] = KEEP * here[t][0:32] + g[0:32] * body
                dst[z + O, 32:40, lanes(t)] = KEEP * here[t][32:40] + g[32:40] * inner[32:40]
            else:
                dst[z + O, :, lanes(t)] = KEEP * here[t] + g * inner

    def halo_planes(src, dst, width):
        def step(i):
            sweep(src, dst, jnp.where(i < width, i - width, i - width + C), False)

        loop(0, 2 * width, step)

    loop(0, C, lambda z: sweep(va, vb, z, True))
    halo_planes(va, vb, 1)
    loop(0, C, lambda z: sweep(vb, va, z, True))
    halo_planes(vb, va, 2)

    v_copy = pltpu.make_async_copy(va.at[3:39], v_out, sems.at[0])
    g_copy = pltpu.make_async_copy(gg, g_out, sems.at[1])
    v_copy.start()
    g_copy.start()

    def residual(z, sourced, edge):
        here, sums = plane(va, z + O)
        out = []
        for t in range(NT):
            r = k * sums[t]
            if not edge:
                r = r - dd[z + Q, :, lanes(t)] * here[t]
            if sourced:
                r = jnp.concatenate([r[0:32] + supply[z, :, lanes(t)], r[32:40]], axis=0)
            out.append(r)
        return out

    def coarse(m, sourced):
        first = residual(2 * m - 4, sourced, False)
        second = residual(2 * m - 3, sourced, False)
        for t in range(NT):
            xp[t, m, 0:20, :] = halve_rows(first[t] + second[t], rs, t)

    loop(2, 18, lambda m: coarse(m, True))
    loop(0, 2, lambda i: coarse(1 + 17 * i, False))

    def outer(i):
        r = residual(jnp.where(i == 0, -3, 34), False, True)
        for t in range(NT):
            xp[t, 19 * i, 0:20, :] = halve_rows(r[t], rs, t)

    loop(0, 2, outer)

    sub = iota((20, 8, 128), 1)
    for t, tile in enumerate(halve_lanes(xp, 20, 24)):
        last = tile[:, 16:24]
        last = jnp.where(sub < 2, last, jnp.where(sub >= 6, shifted(last, 4, 1), 0.0))
        c1[:, 0:16, lanes(t)] = tile[:, 0:16]
        c1[:, 16:24, lanes(t)] = last

    blank = jnp.zeros((4, 8, 512), F32)
    low = jnp.concatenate([c1[0:6], jnp.concatenate([r1[0:4], blank], axis=1)], axis=0)
    mzl[...] = low.reshape(240, 512).astype(BF16)
    high = jnp.concatenate([c1[14:20], jnp.concatenate([r1[12:16], blank], axis=1)], axis=0)
    mzh[...] = high.reshape(240, 512).astype(BF16)

    empty = jnp.zeros((1, 8, 1024), F32)
    low = jnp.concatenate([va[3:7], jnp.concatenate([supply[0:1], empty], axis=1)], axis=0)
    vzl[...] = low.reshape(200, 1024).astype(BF16)
    high = jnp.concatenate([va[35:39], jnp.concatenate([supply[31:32], empty], axis=1)], axis=0)
    vzh[...] = high.reshape(200, 1024).astype(BF16)

    def sides(i):
        lows, highs = [], []
        for j in range(2):
            p = 2 * i + j
            z = p - 2
            held = jnp.where((z >= 0) & (z < C), 1.0, 0.0)
            zc = jnp.clip(z, 0, C - 1)
            f_low = shifted(supply[zc, 0:8, :], 4, 0) * held
            f_high = shifted(supply[zc, 24:32, :], 5, 0) * held
            first, last, halo = va[p + 3, 0:8, :], va[p + 3, 24:32, :], va[p + 3, 32:40, :]
            lows.append(pack_low(sub8, first, halo, f_low))
            highs.append(pack_high(sub8, last, halo, f_high))
        rows = pl.ds(pl.multiple_of(16 * i, 16), 16)
        pxl[rows, :] = jnp.concatenate(lows, axis=0).astype(BF16)
        pxh[rows, :] = jnp.concatenate(highs, axis=0).astype(BF16)

    loop(0, 18, sides)
    v_copy.wait()
    g_copy.wait()


def pack_low(sub, first, halo, f):
    return jnp.where(sub < 2, first, jnp.where(sub >= 6, halo, jnp.where(sub == 4, f, 0.0)))


def pack_high(sub, last, halo, f):
    return jnp.where(sub >= 6, last, jnp.where(sub < 2, halo, jnp.where(sub == 4, f, 0.0)))


def sides_kernel(pxl, pxh, vzl, vzh, out_l, out_h):
    sub = iota((8, 1024), 0)
    for ref, out, low_side in ((pxl, out_l, True), (pxh, out_h, False)):
        out[...] = ref[...]
        for message, start, f_plane in ((vzl, 0, 1), (vzh, 32, 2)):
            planes = message[...].astype(F32).reshape(5, 40, 1024)
            for pair in range(2):
                added = []
                for i in (2 * pair, 2 * pair + 1):
                    v, f = planes[i], planes[4]
                    f_low = shifted(f[0:8], 4, 0) if i == f_plane else 0.0
                    f_high = shifted(f[24:32], 5, 0) if i == f_plane else 0.0
                    if low_side:
                        added.append(pack_low(sub, v[0:8], v[32:40], f_low))
                    else:
                        added.append(pack_high(sub, v[24:32], v[32:40], f_high))
                rows = slice((start + 2 * pair) * 8, (start + 2 * pair) * 8 + 16)
                total = ref[rows, :].astype(F32) + jnp.concatenate(added, axis=0)
                out[rows, :] = total.astype(BF16)


def merge_kernel(c1, r1, mzl, mzh, f1, q1, mxl, mxh):
    zeros = jnp.zeros((24, 512), F32)
    for p in (0, 1, 22, 23):
        f1[p] = zeros
    f1[2:22] = c1[...]
    low = mzl[...].astype(F32).reshape(10, 24, 512)
    high = mzh[...].astype(F32).reshape(10, 24, 512)
    f1[0:6] = f1[0:6] + low[0:6]
    f1[18:24] = f1[18:24] + high[0:6]
    q1[0:4] = low[6:10]
    q1[20:24] = high[6:10]
    q1[4:20, 0:16, :] = r1[...]
    q1[4:20, 16:24, :] = jnp.zeros((16, 8, 512), F32)
    sub = iota((24, 8, 512), 1)
    first, last, halo = f1[:, 0:8], f1[:, 8:16], f1[:, 16:24]
    to_high = jnp.where(sub >= 4, last, jnp.where(sub < 2, halo, 0.0))
    to_low = jnp.where(sub >= 6, halo, jnp.where(sub < 4, first, 0.0))
    mxh[0:192, :] = to_high.reshape(192, 512).astype(BF16)
    mxh[192:384, :] = q1[:, 8:16].reshape(192, 512).astype(BF16)
    mxl[0:192, :] = to_low.reshape(192, 512).astype(BF16)
    mxl[192:384, :] = q1[:, 0:8].reshape(192, 512).astype(BF16)


def middle_kernel(nz, nx, info, f0, q0, mxl, mxh, f1, g1, v1, g2, va, rs, xp):
    iz, ix = info[0], info[1]
    k = spread(1)
    base = 1.0 + 6.0 * k
    low = mxl[...].astype(F32).reshape(48, 8, 512)
    high = mxh[...].astype(F32).reshape(48, 8, 512)
    sub = iota((24, 8, 512), 1)
    f1[:, 0:8] = f0[:, 0:8] + jnp.where(sub < 2, low[0:24], 0.0)
    f1[:, 8:16] = f0[:, 8:16] + jnp.where(sub >= 6, high[0:24], 0.0)
    f1[:, 16:24] = f0[:, 16:24] + jnp.where(sub >= 4, low[0:24], high[0:24])
    q0[:, 16:24] = jnp.where(sub >= 4, low[24:48], high[24:48])
    shape = (24, 24, 128)
    valid = inside(shape, 0, -4, None, iz, 16, nz) & inside(shape, 1, 0, 20, ix, 16, nx)
    for t in range(4):
        g = jnp.where(valid, OMEGA, 0.0) / (q0[:, :, lanes(t)] + base)
        g1[:, :, lanes(t)] = g
        va[:, :, lanes(t)] = g * f1[:, :, lanes(t)]
    v1[0] = va[0]
    v1[23] = va[23]

    def sweep(p):
        here, sums = plane(va, p)
        for t in range(4):
            v1[p, :, lanes(t)] = KEEP * here[t] + g1[p, :, lanes(t)] * (f1[p, :, lanes(t)] + k * sums[t])

    loop(1, 23, sweep)

    def coarse(m):
        total = None
        for j in range(2):
            p = 2 * m + 4 + j
            here, sums = plane(v1, p)
            r = [
                f1[p, :, lanes(t)] + k * sums[t] - (q0[p, :, lanes(t)] + base) * here[t]
                for t in range(4)
            ]
            total = r if total is None else [a + b for a, b in zip(total, r)]
        for t in range(4):
            xp[t, m] = halve_rows(total[t][0:16], rs, t)

    loop(0, 8, coarse)
    for t, tile in enumerate(halve_lanes(xp, 8, 8)):
        g2[:, lanes(t)] = tile.reshape(64, 128)


def back_kernel(
    nz, nx, info, f1, g1, v1, vzl, vzh, vxl, vxh, g2, r2, v_in, g_in, s_in,
    out,
    f2, q2, h2, a2, b2, rs, xp, xpr, wa, w1, zsl, zsh, vb, ws,
    g2s, r2s, v2, gg, supply, sems, sems2,
):
    iz, ix = info[0], info[1]
    matrix = doubling()

    x_first = jnp.clip(ix - 2, 0, nx - 5)
    near = []
    for dz in range(5):
        at = pl.ds(jnp.clip(iz + dz - 2, 0, nz - 1) * nx + x_first, 5)
        near.append(pltpu.make_async_copy(g2.at[at], g2s.at[dz], sems2.at[0, dz]))
        near.append(pltpu.make_async_copy(r2.at[at], r2s.at[dz], sems2.at[1, dz]))
    level0 = [
        pltpu.make_async_copy(src, dst, sems.at[i])
        for i, (src, dst) in enumerate(((v_in, v2), (g_in, gg), (s_in, supply)))
    ]
    for copy in near + level0:
        copy.start()
    for copy in near:
        copy.wait()

    sub4 = iota((8, 8, 256), 1)
    for dz in range(-2, 3):
        lo = 4 if dz == -2 else 0
        hi = 4 if dz == 2 else 8
        planes = slice(12 + 8 * dz + lo, 12 + 8 * dz + hi)
        for src, ref in ((g2s, f2), (r2s, q2)):
            parts = {}
            for dx in range(-2, 3):
                at = jnp.clip(ix + dx, 0, nx - 1) - x_first
                parts[dx] = src[dz + 2, at].reshape(8, 8, 256)
            far = jnp.where(sub4 < 4, parts[2], parts[-2])
            for n, tile in enumerate((parts[0], parts[1], far, parts[-1])):
                ref[planes, 8 * n : 8 * n + 8, :] = tile[lo:hi]

    k = spread(2)
    base = 1.0 + 6.0 * k
    shape = (32, 32, 128)
    valid = inside(shape, 0, -12, None, iz, 8, nz) & inside(shape, 1, 0, 20, ix, 8, nx)
    for t in range(2):
        g = jnp.where(valid, OMEGA, 0.0) / (q2[:, :, lanes(t)] + base)
        h2[:, :, lanes(t)] = g
        a2[:, :, lanes(t)] = g * f2[:, :, lanes(t)]
    b2[0] = a2[0]
    b2[31] = a2[31]

    def sweep2(src, dst):
        def body(p):
            here, sums = plane(src, p)
            for t in range(2):
                dst[p, :, lanes(t)] = KEEP * here[t] + h2[p, :, lanes(t)] * (f2[p, :, lanes(t)] + k * sums[t])

        return body

    loop(1, 31, sweep2(a2, b2))

    def coarse(m):
        total, rates = [0.0, 0.0], [0.0, 0.0]
        for j in range(2):
            p = 2 * m + j
            here, sums = plane(b2, p)
            for t in range(2):
                r = f2[p, :, lanes(t)] + k * sums[t] - (q2[p, :, lanes(t)] + base) * here[t]
                total[t] = total[t] + r
                rates[t] = rates[t] + q2[p, :, lanes(t)]
        for t in range(2):
            xp[t, m] = halve_rows(total[t], rs, t)
            xpr[t, m] = halve_rows(rates[t], rs, t + 2)

    for t in range(2):
        for m in (0, 15):
            xp[t, m] = jnp.zeros((16, 128), F32)
            xpr[t, m] = jnp.zeros((16, 128), F32)
    loop(1, 15, coarse)

    shape = (16, 16, 128)
    valid = inside(shape, 0, -6, None, iz, 4, nz) & inside(shape, 1, 0, 10, ix, 4, nx)
    k3 = spread(3)
    (source,) = halve_lanes(xp, 16, 16)
    (rates,) = halve_lanes(xpr, 16, 16)
    g = jnp.where(valid, OMEGA, 0.0) / (rates + (1.0 + 6.0 * k3))
    v = g * source
    lane = iota(shape, 2)
    for repeat in range(3):
        edge = jnp.zeros((1, 16, 128), F32)
        sums = jnp.concatenate([v[1:], edge], axis=0) + jnp.concatenate([edge, v[:-1]], axis=0)
        sums = sums + shifted(v, 1, 1) + shifted(v, -1, 1)
        sums = sums + jnp.where(lane == 0, 0.0, shifted(v, 1, 2)) + jnp.where(lane == 127, 0.0, shifted(v, -1, 2))
        v = KEEP * v + g * (source + k3 * sums)

    wide = split_dot(v[4:12].reshape(128, 128), matrix).reshape(8, 16, 256)
    for m in range(8):
        for t in range(2):
            part = wide[m, :, lanes(t)]
            rs[t, pl.ds(0, 16, stride=2), :] = part
            rs[t, pl.ds(1, 16, stride=2), :] = part
            for j in range(2):
                p = 8 + 2 * m + j
                b2[p, :, lanes(t)] = b2[p, :, lanes(t)] + rs[t, 0:32, :]
    loop(9, 23, sweep2(b2, a2))
    loop(10, 22, sweep2(a2, b2))

    w = b2[10:22]
    near, far = w[:, 8:16], w[:, 24:32]
    near = jnp.where(iota((12, 8, 256), 1) < 2, near, shifted(far, 4, 1))
    w = jnp.concatenate([w[:, 0:8], near], axis=1).reshape(192, 256)
    wide = [split_dot(w[:, lanes(t)], matrix) for t in range(2)]
    wide = jnp.concatenate(wide, axis=1).reshape(12, 16, 512)
    for m in range(12):
        for t in range(4):
            part = wide[m, :, lanes(t)]
            rs[t, pl.ds(0, 16, stride=2), :] = part
            rs[t, pl.ds(1, 16, stride=2), :] = part
            for j in range(2):
                p = 2 * m + j
                wa[p, :, lanes(t)] = v1[p, :, lanes(t)] + rs[t, 0:24, :]
    k1 = spread(1)

    def sweep1(src, dst):
        def body(p):
            here, sums = plane(src, p)
            for t in range(4):
                dst[p, :, lanes(t)] = KEEP * here[t] + g1[p, :, lanes(t)] * (f1[p, :, lanes(t)] + k1 * sums[t])

        return body

    loop(2, 22, sweep1(wa, w1))
    loop(3, 21, sweep1(w1, wa))

    sub = iota((18, 8, 128), 1)
    for t in range(4):
        halo = wa[3:21, 16:24, lanes(t)]
        halo = jnp.where(sub < 2, halo, shifted(halo, 4, 1))
        w = jnp.concatenate([wa[3:21, 0:16, lanes(t)], halo], axis=1)
        ws[:, :, t * 256 : t * 256 + 256] = split_dot(w.reshape(432, 128), matrix).reshape(18, 24, 256)

    for copy in level0:
        copy.wait()
    zsl[...] = vzl[...].astype(F32)
    zsh[...] = vzh[...].astype(F32)
    for i in range(4):
        v2[i] = v2[i] + zsl[40 * i : 40 * i + 40, :]
        v2[32 + i] = v2[32 + i] + zsh[40 * i : 40 * i + 40, :]

    s8 = iota((8, 128), 0)

    def correct(m):
        rows = pl.ds(pl.multiple_of(16 * m, 16), 16)
        for t in range(NT):
            part = ws[m, :, lanes(t)]
            rs[t, pl.ds(0, 24, stride=2), :] = part
            rs[t, pl.ds(1, 24, stride=2), :] = part
            low = vxl[rows, lanes(t)].astype(F32)
            high = vxh[rows, lanes(t)].astype(F32)
            for j in range(2):
                p = 2 * m + j
                lo, hi = low[8 * j : 8 * j + 8], high[8 * j : 8 * j + 8]
                v2[p, 0:8, lanes(t)] = v2[p, 0:8, lanes(t)] + rs[t, 0:8, :] + jnp.where(s8 < 2, lo, 0.0)
                v2[p, 8:24, lanes(t)] = v2[p, 8:24, lanes(t)] + rs[t, 8:24, :]
                v2[p, 24:32, lanes(t)] = v2[p, 24:32, lanes(t)] + rs[t, 24:32, :] + jnp.where(s8 >= 6, hi, 0.0)
                extra = jnp.where(s8 >= 6, lo, jnp.where(s8 < 2, hi, 0.0))
                v2[p, 32:40, lanes(t)] = v2[p, 32:40, lanes(t)] + rs[t, 32:40, :] + extra

    loop(0, 18, correct)
    k0 = spread(0)

    def first(i):
        rows = pl.ds(pl.multiple_of(16 * i + 16, 16), 16)
        for j in range(2):
            z = 2 * i + j
            here, sums = plane(v2, z + 2)
            for t in range(NT):
                lo = vxl[rows, lanes(t)].astype(F32)[8 * j : 8 * j + 8]
                hi = vxh[rows, lanes(t)].astype(F32)[8 * j : 8 * j + 8]
                f = jnp.where(s8 == 7, shifted(lo, 3, 0), jnp.where(s8 == 0, shifted(hi, 4, 0), 0.0))
                g = gg[z + 2, :, lanes(t)]
                inner = k0 * sums[t]
                vb[z + 1, 0:32, lanes(t)] = KEEP * here[t][0:32] + g[0:32] * (supply[z, :, lanes(t)] + inner[0:32])
                vb[z + 1, 32:40, lanes(t)] = KEEP * here[t][32:40] + g[32:40] * (f + inner[32:40])

    loop(0, 16, first)
    for p, ref in ((1, zsl), (34, zsh)):
        here, sums = plane(v2, p)
        for t in range(NT):
            g = gg[p, :, lanes(t)]
            vb[p - 1, :, lanes(t)] = KEEP * here[t] + g * (ref[160:200, lanes(t)] + k0 * sums[t])

    def second(z):
        here, sums = plane(vb, z + 1)
        for t in range(NT):
            g = gg[z + 2, 0:32, lanes(t)]
            out[z, :, lanes(t)] = KEEP * here[t][0:32] + g * (supply[z, :, lanes(t)] + k0 * sums[t][0:32])

    loop(0, C, second)


VMEM = pl.BlockSpec(memory_space=pltpu.VMEM)
SMEM = pl.BlockSpec(memory_space=pltpu.SMEM)
ANY = pl.BlockSpec(memory_space=pl.ANY)


def call(kernel, outs, scratch, smem, args, out_specs=None, in_hbm=0):
    moved = sum(a.size * a.dtype.itemsize for a in list(args) + list(outs))
    return pl.pallas_call(
        kernel,
        out_shape=tuple(outs),
        in_specs=[SMEM] * smem + [VMEM] * (len(args) - smem - in_hbm) + [ANY] * in_hbm,
        out_specs=tuple(out_specs or [VMEM] * len(outs)),
        scratch_shapes=scratch,
        compiler_params=pltpu.CompilerParams(vmem_limit_bytes=58 * 2**20),
        cost_estimate=pl.CostEstimate(flops=20 * moved, bytes_accessed=moved, transcendentals=0),
    )(*args)


def shaped(shape, dtype=F32):
    return jax.ShapeDtypeStruct(shape, dtype)


def both_ways(to_low, to_high, axis):
    count = lax.axis_size(axis)
    up = [(i, i + 1) for i in range(count - 1)]
    down = [(j, i) for i, j in up]
    return lax.ppermute(to_high, axis, up), lax.ppermute(to_low, axis, down)


def shards(density, uptake, brick_values, brick_ids, slot_counts):
    nz, nx = lax.axis_size("gz"), lax.axis_size("xy")
    info = jnp.stack([lax.axis_index("gz"), lax.axis_index("xy")]).astype(jnp.int32)
    scratch = pltpu.VMEM

    (blocks,) = call(
        lambda *refs: brick_kernel(2 * nx, *refs),
        [shaped((9, 272, 128), BF16)],
        [scratch((SLOTS, BRICK), F32)],
        2,
        (brick_ids, slot_counts, brick_values),
    )
    uzl, uzh = both_ways(uptake[0:2].astype(BF16), uptake[30:32].astype(BF16), "gz")
    zl, zh = both_ways(blocks[0:3], blocks[6:9], "gz")
    r1, r2 = call(
        rates_kernel,
        [shaped((16, 16, 512)), shaped((64, 256))],
        [scratch((8, 32, 128), F32), scratch((8, 16, 16, 128), F32), scratch((4, 16, 128), F32), scratch((4, 8, 8, 128), F32)],
        0,
        (uptake,),
    )
    r2_all = lax.all_gather(r2, ("gz", "xy"))
    column = lambda s: jnp.concatenate([uzl[:, s].astype(F32), uptake[:, s], uzh[:, s].astype(F32)], axis=0)
    uxl, uxr = both_ways(column(slice(0, 2)), column(slice(30, 32)), "xy")
    hop = lambda d: jnp.stack([blocks[3 + d], zl[d], zh[d]])
    xl, xr = both_ways(hop(0), hop(2), "xy")

    supply, c1, mzl, mzh, vzl, vzh, pxl, pxh, v2, gg = call(
        lambda *refs: pre_kernel(nz, nx, *refs),
        [
            shaped((C, C, 1024)),
            shaped((20, 24, 512)),
            shaped((240, 512), BF16),
            shaped((240, 512), BF16),
            shaped((200, 1024), BF16),
            shaped((200, 1024), BF16),
            shaped((288, 1024), BF16),
            shaped((288, 1024), BF16),
            shaped((36, 40, 1024)),
            shaped((36, 40, 1024)),
        ],
        [
            scratch((42, 40, 1024), F32),
            scratch((42, 40, 1024), F32),
            scratch((36, 40, 1024), F32),
            scratch((36, 40, 1024), F32),
            scratch((1024, 1152), BF16),
            scratch((8, 40, 128), F32),
            scratch((8, 20, 24, 128), F32),
            pltpu.SemaphoreType.DMA((2,)),
        ],
        1,
        (info, density, uptake, uzl, uzh, uxl, uxr, blocks, zl, zh, xl, xr, r1),
        [VMEM] * 8 + [ANY] * 2,
    )
    mzl, mzh = both_ways(mzl, mzh, "gz")
    vzl, vzh = both_ways(vzl, vzh, "gz")
    f1, q1, mxl, mxh = call(
        merge_kernel,
        [shaped((24, 24, 512)), shaped((24, 24, 512)), shaped((384, 512), BF16), shaped((384, 512), BF16)],
        [],
        0,
        (c1, r1, mzl, mzh),
    )
    mxl, mxh = both_ways(mxl, mxh, "xy")
    pxl, pxh = call(
        sides_kernel,
        [shaped((288, 1024), BF16), shaped((288, 1024), BF16)],
        [],
        0,
        (pxl, pxh, vzl, vzh),
    )
    f1, g1, v1, g2 = call(
        lambda *refs: middle_kernel(nz, nx, *refs),
        [shaped((24, 24, 512)), shaped((24, 24, 512)), shaped((24, 24, 512)), shaped((64, 256))],
        [scratch((24, 24, 512), F32), scratch((4, 16, 128), F32), scratch((4, 8, 8, 128), F32)],
        1,
        (info, f1, q1, mxl, mxh),
    )
    g2_all = lax.all_gather(g2, ("gz", "xy"))
    vxl, vxh = both_ways(pxl, pxh, "xy")
    window2 = scratch((32, 32, 256), F32)
    window1 = scratch((24, 24, 512), F32)
    (concentration,) = call(
        lambda *refs: back_kernel(nz, nx, *refs),
        [shaped((C, C, 1024))],
        [
            window2, window2, window2, window2, window2,
            scratch((8, 48, 128), F32),
            scratch((2, 16, 16, 128), F32),
            scratch((2, 16, 16, 128), F32),
            window1, window1,
            scratch((200, 1024), F32),
            scratch((200, 1024), F32),
            scratch((34, 40, 1024), F32),
            scratch((18, 24, 1024), F32),
            scratch((5, 5, 64, 256), F32),
            scratch((5, 5, 64, 256), F32),
            scratch((36, 40, 1024), F32),
            scratch((36, 40, 1024), F32),
            scratch((C, C, 1024), F32),
            pltpu.SemaphoreType.DMA((3,)),
            pltpu.SemaphoreType.DMA((2, 5)),
        ],
        1,
        (info, f1, g1, v1, vzl, vzh, vxl, vxh, g2_all, r2_all, v2, gg, supply),
        in_hbm=5,
    )
    return supply, concentration


def solution(mesh):
    return jax.shard_map(
        shards,
        mesh=mesh,
        in_specs=(
            P("gz", "xy", None),
            P("gz", "xy", None),
            P(("gz", "xy"), None),
            P(("gz", "xy")),
            P(("gz", "xy"), None),
        ),
        out_specs=(P("gz", "xy", None), P("gz", "xy", None)),
        check_vma=False,
    )
```

```python
import jax
import jax.numpy as jnp
from jax import lax
from jax.experimental import pallas as pl
from jax.experimental.pallas import tpu as pltpu
from jax.sharding import PartitionSpec as P

EDGE = 16
CAP = 8
BRICK = 4096
SLOTS = 72
KAPPA = 32.0
OMEGA = 0.8
KEEP = 1.0 - OMEGA

C = 32
NT = 8
F32 = jnp.float32
BF16 = jnp.bfloat16


def spread(level):
    return KAPPA / 4.0**level


def shifted(values, distance, axis):
    return pltpu.roll(values, distance % values.shape[axis], axis)


def iota(shape, dim):
    return lax.broadcasted_iota(jnp.int32, shape, dim)


def lanes(t):
    return slice(t * 128, (t + 1) * 128)


def along_y(tiles):
    lane = iota(tiles[0].shape, 1)
    ahead = [shifted(a, 1, 1) for a in tiles]
    behind = [shifted(a, -1, 1) for a in tiles]
    sums = []
    for t in range(len(tiles)):
        low = ahead[t - 1] if t else 0.0
        high = behind[t + 1] if t + 1 < len(tiles) else 0.0
        sums.append(jnp.where(lane == 0, low, ahead[t]) + jnp.where(lane == 127, high, behind[t]))
    return sums


def plane(ref, p):
    count = ref.shape[2] // 128
    here = [ref[p, :, lanes(t)] for t in range(count)]
    sums = along_y(here)
    for t in range(count):
        near = ref[p - 1, :, lanes(t)] + ref[p + 1, :, lanes(t)]
        near = near + (shifted(here[t], 1, 0) + shifted(here[t], -1, 0))
        sums[t] = sums[t] + near
    return here, sums


def loop(start, stop, body):
    def step(i, carry):
        body(i)
        return carry

    lax.fori_loop(start, stop, step, 0)


def split_dot(a, b):
    high = a.astype(BF16)
    low = (a - high.astype(F32)).astype(BF16)
    return jnp.dot(high, b, preferred_element_type=F32) + jnp.dot(low, b, preferred_element_type=F32)


def pooling():
    return jnp.where(iota((256, 128), 0) // 2 == iota((256, 128), 1), 0.125, 0.0).astype(BF16)


def doubling():
    return jnp.where(iota((128, 256), 1) // 2 == iota((128, 256), 0), 1.0, 0.0).astype(BF16)


def halve_rows(values, rs, t):
    rows = values.shape[0]
    rs[t, 0:rows, :] = values
    return rs[t, pl.ds(0, rows // 2, stride=2), :] + rs[t, pl.ds(1, rows // 2, stride=2), :]


def halve_lanes(xp, planes, rows):
    matrix = pooling()
    tiles = []
    for t in range(0, xp.shape[0], 2):
        pair = jnp.concatenate([xp[t].reshape(planes * rows, 128), xp[t + 1].reshape(planes * rows, 128)], axis=1)
        tiles.append(split_dot(pair, matrix).reshape(planes, rows, 128))
    return tiles


def inside(shape, dim, first, wrap, index, size, count):
    place = iota(shape, dim) + first
    if wrap is not None:
        place = jnp.where(place < wrap, place, place - shape[dim])
    place = place + index * size
    return (place >= 0) & (place < count * size)


def brick_kernel(bricks_x, ids, counts, bricks, out, xs):
    xs[...] = bricks[...].astype(F32)
    row = iota((1, 8, 128), 1)
    group = iota((1, 8, 128), 2) // 16
    group16 = iota((16, 128), 1) // 16
    per_y = 64

    def block(j):
        start = pl.multiple_of(j * 8, 8)
        x = jnp.stack([xs[pl.ds(start, 8), lanes(k)] for k in range(32)])
        for s in (4, 2, 1):
            up = shifted(shifted(x, -s, 1), 16 * s, 2)
            down = shifted(shifted(x, s, 1), -16 * s, 2)
            row_bit = (row // s) % 2
            group_bit = (group // s) % 2
            x = jnp.where(row_bit == group_bit, x, jnp.where(row_bit == 0, up, down))
        x = jnp.where(group < counts[0, j], x, 0.0)
        out[j, 0:256, :] = x.reshape(256, 128).astype(BF16)
        names = jnp.zeros((16, 128), jnp.int32)
        for e in range(CAP):
            number = ids[j * 8 + e]
            by = lax.rem(number, per_y)
            rest = lax.div(number, per_y)
            bx = lax.rem(rest, 2)
            bz = lax.rem(lax.div(rest, bricks_x), 2)
            names = jnp.where(group16 == e, (bz * 2 + bx) * per_y + by, names)
        out[j, 256:272, :] = names.astype(F32).astype(BF16)

    loop(0, 9, block)


def rates_kernel(uptake, r1, r2, zl, zh, z2l, z2h, xl, xh, rs, xp, rs1, xp1):
    def pair(m):
        for t in range(NT):
            both = uptake[2 * m, :, lanes(t)] + uptake[2 * m + 1, :, lanes(t)]
            xp[t, m] = halve_rows(both, rs, t)

    loop(0, 16, pair)
    for t, tile in enumerate(halve_lanes(xp, 16, 16)):
        r1[:, :, lanes(t)] = tile

    def pair1(m):
        for t in range(4):
            both = r1[2 * m, :, lanes(t)] + r1[2 * m + 1, :, lanes(t)]
            xp1[t, m] = halve_rows(both, rs1, t)

    loop(0, 8, pair1)
    coarse = []
    for t, tile in enumerate(halve_lanes(xp1, 8, 8)):
        r2[:, lanes(t)] = tile.reshape(64, 128)
        coarse.append(tile.reshape(64, 128).astype(BF16))
    z2l[...] = r2[0:32, :].astype(BF16)
    z2h[...] = r2[32:64, :].astype(BF16)
    for ref, u, r in ((zl, slice(0, 2), slice(0, 4)), (zh, slice(30, 32), slice(12, 16))):
        ref[0:64, :] = uptake[u].reshape(64, 1024).astype(BF16)
        ref[64:128, 0:512] = r1[r].reshape(64, 512).astype(BF16)
        for t in range(2):
            ref[64:128, lanes(4 + t)] = coarse[t]
        ref[64:128, 768:1024] = jnp.zeros((64, 256), BF16)

    sub = iota((8, 1024), 0)

    def columns(i):
        lows, highs = [], []
        for j in range(2):
            low, high = jnp.zeros((8, 1024), F32), jnp.zeros((8, 1024), F32)
            for n in range(4):
                z = 8 * i + 4 * j + n
                low = jnp.where(sub // 2 == n, shifted(uptake[z, 0:8, :], 2 * n, 0), low)
                high = jnp.where(sub // 2 == n, shifted(uptake[z, 24:32, :], 2 * n + 2, 0), high)
            lows.append(low)
            highs.append(high)
        rows = pl.ds(pl.multiple_of(16 * i, 16), 16)
        xl[rows, :] = jnp.concatenate(lows, axis=0).astype(BF16)
        xh[rows, :] = jnp.concatenate(highs, axis=0).astype(BF16)

    loop(0, 4, columns)


def halves(sub, first, second):
    return jnp.where(sub < 4, first, shifted(second, 4, 1))


def uppers(sub, first, second):
    return jnp.where(sub < 4, shifted(first, 4, 1), second)


def far_messages(window):
    planes, _, width = window.shape
    pairs = window.reshape(planes // 2, 2, 8, width)
    sub = iota((planes // 2, 8, width), 1)
    size = (planes * 4, width)
    return halves(sub, pairs[:, 0], pairs[:, 1]).reshape(size), uppers(sub, pairs[:, 0], pairs[:, 1]).reshape(size)


def far_tile(from_low, from_high):
    width = from_low.shape[-1]
    low, high = from_low.reshape(-1, 8, width), from_high.reshape(-1, 8, width)
    sub = iota(low.shape, 1)
    even = jnp.where(sub < 4, high, shifted(low, 4, 1))
    odd = jnp.where(sub < 4, shifted(high, 4, 1), low)
    return jnp.stack([even, odd], axis=1).reshape(-1, 8, width)


def rates_window_kernel(r1, r2, xl, xh, zl, zh, z2l, z2h, q1, q2, ul, uh, cl, ch, fl, fh):
    low, high = zl[...].astype(F32), zh[...].astype(F32)
    sub = iota((8, 1024), 0)
    ul[0:64, :] = xl[...]
    uh[0:64, :] = xh[...]
    planes = [low[0:32], low[32:64], high[0:32], high[32:64]]
    to_low, to_high = jnp.zeros((8, 1024), F32), jnp.zeros((8, 1024), F32)
    for n, p in enumerate(planes):
        to_low = jnp.where(sub // 2 == n, shifted(p[0:8], 2 * n, 0), to_low)
        to_high = jnp.where(sub // 2 == n, shifted(p[24:32], 2 * n + 2, 0), to_high)
    blank = jnp.zeros((8, 1024), F32)
    ul[64:80, :] = jnp.concatenate([to_low, blank], axis=0).astype(BF16)
    uh[64:80, :] = jnp.concatenate([to_high, blank], axis=0).astype(BF16)

    q1[0:4, 0:16, :] = low[64:128, 0:512].reshape(4, 16, 512)
    q1[4:20, 0:16, :] = r1[...]
    q1[20:24, 0:16, :] = high[64:128, 0:512].reshape(4, 16, 512)
    q1[:, 16:24, :] = jnp.zeros((24, 8, 512), F32)
    sub1 = iota((12, 8, 512), 1)
    first = q1[:, 0:8, :].reshape(12, 2, 8, 512)
    last = q1[:, 8:16, :].reshape(12, 2, 8, 512)
    cl[0:96, :] = halves(sub1, first[:, 0], first[:, 1]).reshape(96, 512).astype(BF16)
    ch[0:96, :] = uppers(sub1, last[:, 0], last[:, 1]).reshape(96, 512).astype(BF16)

    window = window_planes(r2[...], low[64:128, 512:768], high[64:128, 512:768], z2l[...].astype(F32), z2h[...].astype(F32))
    q2[...] = window
    for ref in (cl, ch):
        ref[96:224, 0:256] = window[0:16].reshape(128, 256).astype(BF16)
        ref[96:224, 256:512] = window[16:32].reshape(128, 256).astype(BF16)
    to_low, to_high = far_messages(window)
    fl[...] = to_low.astype(BF16)
    fh[...] = to_high.astype(BF16)


def window_planes(own, low, high, low2, high2):
    parts = (low2, low, own, high, high2)
    return jnp.concatenate([a.reshape(-1, 8, 256) for a in parts], axis=0)


def source_window_kernel(own, low, high, low2, high2, window, near, fl, fh):
    planes = window_planes(own[...], low[...], high[...], low2[...], high2[...])
    window[...] = planes
    near[...] = planes.reshape(256, 256).astype(BF16)
    to_low, to_high = far_messages(planes)
    fl[...] = to_low.astype(BF16)
    fh[...] = to_high.astype(BF16)


def pre_kernel(
    nz, nx, info, density, uptake, uz_low, uz_high, ux_low, ux_high, own, zl, zh, xl, xr,
    supply, c1, mzl, mzh, vzl, vzh, pxl, pxh, v_out, g_out,
    va, vb, dd, gg, hot, rs, xp, usl, ush, sems,
):
    iz, ix = info[0], info[1]
    k = spread(0)
    base = 1.0 + 6.0 * k
    O = 5
    Q = 2

    for p in (0, 1, 2, 3, 4, 37, 38, 39, 40, 41):
        va[p] = jnp.zeros((40, 1024), F32)
    for p in (2, 3, 38, 39):
        vb[p] = jnp.zeros((40, 1024), F32)

    sub8 = iota((8, 1024), 0)

    usl[...] = ux_low[...].astype(F32)
    ush[...] = ux_high[...].astype(F32)

    def set_plane(q, rates, low, high, valid_z):
        gz = jnp.where(valid_z, OMEGA, 0.0)
        d = rates + base
        dd[q, 0:32, :] = d
        gg[q, 0:32, :] = gz / d
        d = jnp.where(sub8 < 2, high, jnp.where(sub8 >= 6, low, 0.0)) + base
        dd[q, 32:40, :] = d
        omega = jnp.where(sub8 < 2, jnp.where(ix < nx - 1, gz, 0.0), jnp.where(sub8 >= 6, jnp.where(ix > 0, gz, 0.0), 0.0))
        gg[q, 32:40, :] = omega / d

    def own_planes(i):
        rows = pl.ds(pl.multiple_of(8 * i, 8), 8)
        low, high = usl[rows, :], ush[rows, :]
        for n in range(4):
            z = 4 * i + n
            va[z + O, 0:32, :] = density[z]
            va[z + O, 32:40, :] = jnp.zeros((8, 1024), F32)
            set_plane(z + Q, uptake[z], shifted(low, 6 - 2 * n, 0), shifted(high, -2 * n, 0), True)

    loop(0, C // 4, own_planes)
    low, high = usl[64:72, :], ush[64:72, :]
    for n in range(4):
        rates = (uz_low if n < 2 else uz_high)[0:64, :].astype(F32)[32 * (n % 2) : 32 * (n % 2) + 32]
        exists = iz > 0 if n < 2 else iz < nz - 1
        set_plane(n if n < 2 else 32 + n, rates, shifted(low, 6 - 2 * n, 0), shifted(high, -2 * n, 0), exists)

    blocks = [own.at[4], zl.at[1], zh.at[1]] + [xl.at[i] for i in range(3)] + [xr.at[i] for i in range(3)]
    lane = iota((1, 128), 1)
    at_y = iota((1024, 128), 0)
    tiles = []
    for i, ref in enumerate(blocks):
        name = ref[256:272, :].astype(F32).astype(jnp.int32)[0:1]
        tiles.append(lax.shift_right_logical(name, 6))
        y = (name & 63) * 16 + (lane & 15)
        hot[:, lanes(i)] = jnp.where(at_y == y, 1.0, 0.0).astype(BF16)
    for tile in range(4):
        bz, bx = tile // 2, tile % 2
        left = jnp.concatenate(
            [jnp.where(tiles[i] == tile, ref[0:256, :].astype(F32), 0.0).astype(BF16) for i, ref in enumerate(blocks)],
            axis=1,
        )
        for n in range(4):
            cols = slice(n * 256, (n + 1) * 256)
            part = lax.dot_general(left, hot[cols, :], (((1,), (1,)), ((), ())), preferred_element_type=F32)
            zs, xs = slice(16 * bz, 16 * bz + 16), slice(16 * bx, 16 * bx + 16)
            supply[zs, xs, cols] = density[zs, xs, cols] + part.reshape(16, 16, 256)

    def sweep(src, dst, z, sourced):
        here, sums = plane(src, z + O)
        for t in range(NT):
            inner = k * sums[t]
            g = gg[z + Q, :, lanes(t)]
            if sourced:
                body = inner[0:32] + supply[z, :, lanes(t)]
                dst[z + O, 0:32, lanes(t)] = KEEP * here[t][0:32] + g[0:32] * body
                dst[z + O, 32:40, lanes(t)] = KEEP * here[t][32:40] + g[32:40] * inner[32:40]
            else:
                dst[z + O, :, lanes(t)] = KEEP * here[t] + g * inner

    def halo_planes(src, dst, width):
        def step(i):
            sweep(src, dst, jnp.where(i < width, i - width, i - width + C), False)

        loop(0, 2 * width, step)

    loop(0, C, lambda z: sweep(va, vb, z, True))
    halo_planes(va, vb, 1)
    loop(0, C, lambda z: sweep(vb, va, z, True))
    halo_planes(vb, va, 2)

    v_copy = pltpu.make_async_copy(va.at[3:39], v_out, sems.at[0])
    g_copy = pltpu.make_async_copy(gg, g_out, sems.at[1])
    v_copy.start()
    g_copy.start()

    def residual(z, sourced, edge):
        here, sums = plane(va, z + O)
        out = []
        for t in range(NT):
            r = k * sums[t]
            if not edge:
                r = r - dd[z + Q, :, lanes(t)] * here[t]
            if sourced:
                r = jnp.concatenate([r[0:32] + supply[z, :, lanes(t)], r[32:40]], axis=0)
            out.append(r)
        return out

    def coarse(m, sourced):
        first = residual(2 * m - 4, sourced, False)
        second = residual(2 * m - 3, sourced, False)
        for t in range(NT):
            xp[t, m, 0:20, :] = halve_rows(first[t] + second[t], rs, t)

    loop(2, 18, lambda m: coarse(m, True))
    loop(0, 2, lambda i: coarse(1 + 17 * i, False))

    def outer(i):
        r = residual(jnp.where(i == 0, -3, 34), False, True)
        for t in range(NT):
            xp[t, 19 * i, 0:20, :] = halve_rows(r[t], rs, t)

    loop(0, 2, outer)

    sub = iota((20, 8, 128), 1)
    for t, tile in enumerate(halve_lanes(xp, 20, 24)):
        last = tile[:, 16:24]
        last = jnp.where(sub < 2, last, jnp.where(sub >= 6, shifted(last, 4, 1), 0.0))
        c1[:, 0:16, lanes(t)] = tile[:, 0:16]
        c1[:, 16:24, lanes(t)] = last

    mzl[...] = c1[0:6].reshape(144, 512).astype(BF16)
    mzh[...] = c1[14:20].reshape(144, 512).astype(BF16)

    empty = jnp.zeros((1, 8, 1024), F32)
    low = jnp.concatenate([va[3:7], jnp.concatenate([supply[0:1], empty], axis=1)], axis=0)
    vzl[...] = low.reshape(200, 1024).astype(BF16)
    high = jnp.concatenate([va[35:39], jnp.concatenate([supply[31:32], empty], axis=1)], axis=0)
    vzh[...] = high.reshape(200, 1024).astype(BF16)

    def sides(i):
        lows, highs = [], []
        for j in range(2):
            p = 4 * i + 2 * j + 3
            lows.append(pack_low(va[p], va[p + 1]))
            highs.append(pack_high(va[p], va[p + 1]))
        rows = pl.ds(pl.multiple_of(16 * i, 16), 16)
        pxl[rows, :] = jnp.concatenate(lows, axis=0).astype(BF16)
        pxh[rows, :] = jnp.concatenate(highs, axis=0).astype(BF16)

    loop(0, 9, sides)

    def sources(i):
        lows, highs = [], []
        for j in range(2):
            low, high = jnp.zeros((8, 1024), F32), jnp.zeros((8, 1024), F32)
            for n in range(8):
                z = 16 * i + 8 * j + n
                low = jnp.where(sub8 == n, shifted(supply[z, 0:8, :], n, 0), low)
                high = jnp.where(sub8 == n, shifted(supply[z, 24:32, :], n + 1, 0), high)
            lows.append(low)
            highs.append(high)
        rows = pl.ds(pl.multiple_of(16 * i + 144, 16), 16)
        pxl[rows, :] = jnp.concatenate(lows, axis=0).astype(BF16)
        pxh[rows, :] = jnp.concatenate(highs, axis=0).astype(BF16)

    loop(0, 2, sources)
    v_copy.wait()
    g_copy.wait()


def outer_rows(sub):
    return (sub < 2) | (sub >= 6)


def pack_pair(sub, a, b):
    return jnp.where(outer_rows(sub), a, shifted(b, 4, 0))


def pack_low(first, second):
    sub = iota((8, 1024), 0)
    a, b = [jnp.where(sub < 4, v[0:8], v[32:40]) for v in (first, second)]
    return pack_pair(sub, a, b)


def pack_high(first, second):
    sub = iota((8, 1024), 0)
    a, b = [jnp.where(sub >= 4, v[24:32], v[32:40]) for v in (first, second)]
    return pack_pair(sub, a, b)


def sides_kernel(pxl, pxh, vzl, vzh, out_l, out_h):
    out_l[...] = pxl[...]
    out_h[...] = pxh[...]
    for message, start in ((vzl, 0), (vzh, 128)):
        planes = message[...].astype(F32).reshape(5, 40, 1024)
        rows = slice(start, start + 16)
        for ref, out, pack in ((pxl, out_l, pack_low), (pxh, out_h, pack_high)):
            added = [pack(planes[2 * i], planes[2 * i + 1]) for i in range(2)]
            out[rows, :] = (ref[rows, :].astype(F32) + jnp.concatenate(added, axis=0)).astype(BF16)


def in_three(sub, tiles, free, turns):
    spare = (sub == free) | (sub == free + 1)
    last = tiles[:, 3]
    parts = [jnp.where(spare, shifted(last, turn, 1), tiles[:, i]) for i, turn in enumerate(turns)]
    return jnp.stack(parts, axis=1)


def out_of_three(sub, parts, free, turns):
    last = None
    for i, turn in enumerate(turns):
        back = shifted(parts[:, i], -turn, 1)
        home = (free - turn) % 8
        here = (sub == home) | (sub == home + 1)
        last = jnp.where(here, back, 0.0 if last is None else last)
    return jnp.stack([parts[:, 0], parts[:, 1], parts[:, 2], last], axis=1)


HIGH_PACK = (2, (-2, 4, 2))
LOW_PACK = (4, (-2, 4, 2))


def merge_kernel(c1, mzl, mzh, f1, mxl, mxh):
    zeros = jnp.zeros((24, 512), F32)
    for p in (0, 1, 22, 23):
        f1[p] = zeros
    f1[2:22] = c1[...]
    f1[0:6] = f1[0:6] + mzl[...].astype(F32).reshape(6, 24, 512)
    f1[18:24] = f1[18:24] + mzh[...].astype(F32).reshape(6, 24, 512)
    sub = iota((6, 8, 512), 1)
    first, last, halo = [f1[:, 8 * n : 8 * n + 8].reshape(6, 4, 8, 512) for n in range(3)]
    sub4 = iota((6, 4, 8, 512), 2)
    to_high = in_three(sub, jnp.where(sub4 >= 4, last, halo), *HIGH_PACK)
    to_low = in_three(sub, jnp.where(sub4 >= 4, halo, first), *LOW_PACK)
    mxh[...] = to_high.reshape(144, 512).astype(BF16)
    mxl[...] = to_low.reshape(144, 512).astype(BF16)


def middle_kernel(nz, nx, info, f0, q_in, cl, ch, mxl, mxh, f1, g1, v1, g2, g2l, g2h, q0, va, rs, xp):
    iz, ix = info[0], info[1]
    k = spread(1)
    base = 1.0 + 6.0 * k
    sub6 = iota((6, 8, 512), 1)
    low = out_of_three(sub6, mxl[...].astype(F32).reshape(6, 3, 8, 512), *HIGH_PACK).reshape(24, 8, 512)
    high = out_of_three(sub6, mxh[...].astype(F32).reshape(6, 3, 8, 512), *LOW_PACK).reshape(24, 8, 512)
    sub = iota((24, 8, 512), 1)
    f1[:, 0:8] = f0[:, 0:8] + jnp.where(sub < 2, low, 0.0)
    f1[:, 8:16] = f0[:, 8:16] + jnp.where(sub >= 6, high, 0.0)
    f1[:, 16:24] = f0[:, 16:24] + jnp.where(sub >= 4, low, high)
    low = cl[0:96, :].astype(F32).reshape(12, 8, 512)
    high = ch[0:96, :].astype(F32).reshape(12, 8, 512)
    sub12 = iota((12, 8, 512), 1)
    even = jnp.where(sub12 >= 4, shifted(low, 4, 1), high)
    odd = jnp.where(sub12 >= 4, low, shifted(high, 4, 1))
    q0[:, 0:16] = q_in[:, 0:16]
    q0[:, 16:24] = jnp.stack([even, odd], axis=1).reshape(24, 8, 512)
    shape = (24, 24, 128)
    valid = inside(shape, 0, -4, None, iz, 16, nz) & inside(shape, 1, 0, 20, ix, 16, nx)
    for t in range(4):
        g = jnp.where(valid, OMEGA, 0.0) / (q0[:, :, lanes(t)] + base)
        g1[:, :, lanes(t)] = g
        va[:, :, lanes(t)] = g * f1[:, :, lanes(t)]
    v1[0] = va[0]
    v1[23] = va[23]

    def sweep(p):
        here, sums = plane(va, p)
        for t in range(4):
            v1[p, :, lanes(t)] = KEEP * here[t] + g1[p, :, lanes(t)] * (f1[p, :, lanes(t)] + k * sums[t])

    loop(1, 23, sweep)

    def coarse(m):
        total = None
        for j in range(2):
            p = 2 * m + 4 + j
            here, sums = plane(v1, p)
            r = [
                f1[p, :, lanes(t)] + k * sums[t] - (q0[p, :, lanes(t)] + base) * here[t]
                for t in range(4)
            ]
            total = r if total is None else [a + b for a, b in zip(total, r)]
        for t in range(4):
            xp[t, m] = halve_rows(total[t][0:16], rs, t)

    loop(0, 8, coarse)
    for t, tile in enumerate(halve_lanes(xp, 8, 8)):
        g2[:, lanes(t)] = tile.reshape(64, 128)
        g2l[:, lanes(t)] = tile[0:4].reshape(32, 128)
        g2h[:, lanes(t)] = tile[4:8].reshape(32, 128)


def back_kernel(
    nz, nx, info, f1, g1, v1, vzl, vzh, vxl, vxh, own2, n2l, n2h, m2l, m2h, q_own, cl, ch, w2l, w2h, v_in, g_in, s_in,
    out,
    f2, q2, h2, a2, b2, rs, xp, xpr, wa, w1, zsl, zsh, vb, ws,
    v2, gg, supply, fsl, fsh, sems,
):
    iz, ix = info[0], info[1]
    matrix = doubling()
    level0 = [
        pltpu.make_async_copy(src, dst, sems.at[i])
        for i, (src, dst) in enumerate(((v_in, v2), (g_in, gg), (s_in, supply)))
    ]
    for copy in level0:
        copy.start()

    f2[:, 0:8, :] = own2[...]
    f2[:, 8:16, :] = n2h[...].astype(F32).reshape(32, 8, 256)
    f2[:, 16:24, :] = far_tile(m2l[...].astype(F32), m2h[...].astype(F32))
    f2[:, 24:32, :] = n2l[...].astype(F32).reshape(32, 8, 256)
    q2[:, 0:8, :] = q_own[...]
    q2[:, 16:24, :] = far_tile(w2l[...].astype(F32), w2h[...].astype(F32))
    for ref, rows in ((ch, slice(8, 16)), (cl, slice(24, 32))):
        q2[0:16, rows, :] = ref[96:224, 0:256].astype(F32).reshape(16, 8, 256)
        q2[16:32, rows, :] = ref[96:224, 256:512].astype(F32).reshape(16, 8, 256)

    k = spread(2)
    base = 1.0 + 6.0 * k
    shape = (32, 32, 128)
    valid = inside(shape, 0, -12, None, iz, 8, nz) & inside(shape, 1, 0, 20, ix, 8, nx)
    for t in range(2):
        g = jnp.where(valid, OMEGA, 0.0) / (q2[:, :, lanes(t)] + base)
        h2[:, :, lanes(t)] = g
        a2[:, :, lanes(t)] = g * f2[:, :, lanes(t)]
    b2[0] = a2[0]
    b2[31] = a2[31]

    def sweep2(src, dst):
        def body(p):
            here, sums = plane(src, p)
            for t in range(2):
                dst[p, :, lanes(t)] = KEEP * here[t] + h2[p, :, lanes(t)] * (f2[p, :, lanes(t)] + k * sums[t])

        return body

    loop(1, 31, sweep2(a2, b2))

    def coarse(m):
        total, rates = [0.0, 0.0], [0.0, 0.0]
        for j in range(2):
            p = 2 * m + j
            here, sums = plane(b2, p)
            for t in range(2):
                r = f2[p, :, lanes(t)] + k * sums[t] - (q2[p, :, lanes(t)] + base) * here[t]
                total[t] = total[t] + r
                rates[t] = rates[t] + q2[p, :, lanes(t)]
        for t in range(2):
            xp[t, m] = halve_rows(total[t], rs, t)
            xpr[t, m] = halve_rows(rates[t], rs, t + 2)

    for t in range(2):
        for m in (0, 15):
            xp[t, m] = jnp.zeros((16, 128), F32)
            xpr[t, m] = jnp.zeros((16, 128), F32)
    loop(1, 15, coarse)

    shape = (16, 16, 128)
    valid = inside(shape, 0, -6, None, iz, 4, nz) & inside(shape, 1, 0, 10, ix, 4, nx)
    k3 = spread(3)
    (source,) = halve_lanes(xp, 16, 16)
    (rates,) = halve_lanes(xpr, 16, 16)
    g = jnp.where(valid, OMEGA, 0.0) / (rates + (1.0 + 6.0 * k3))
    v = g * source
    lane = iota(shape, 2)
    for repeat in range(3):
        edge = jnp.zeros((1, 16, 128), F32)
        sums = jnp.concatenate([v[1:], edge], axis=0) + jnp.concatenate([edge, v[:-1]], axis=0)
        sums = sums + shifted(v, 1, 1) + shifted(v, -1, 1)
        sums = sums + jnp.where(lane == 0, 0.0, shifted(v, 1, 2)) + jnp.where(lane == 127, 0.0, shifted(v, -1, 2))
        v = KEEP * v + g * (source + k3 * sums)

    wide = split_dot(v[4:12].reshape(128, 128), matrix).reshape(8, 16, 256)
    for m in range(8):
        for t in range(2):
            part = wide[m, :, lanes(t)]
            rs[t, pl.ds(0, 16, stride=2), :] = part
            rs[t, pl.ds(1, 16, stride=2), :] = part
            for j in range(2):
                p = 8 + 2 * m + j
                b2[p, :, lanes(t)] = b2[p, :, lanes(t)] + rs[t, 0:32, :]
    loop(9, 23, sweep2(b2, a2))
    loop(10, 22, sweep2(a2, b2))

    w = b2[10:22]
    near, far = w[:, 8:16], w[:, 24:32]
    near = jnp.where(iota((12, 8, 256), 1) < 2, near, shifted(far, 4, 1))
    w = jnp.concatenate([w[:, 0:8], near], axis=1).reshape(192, 256)
    wide = [split_dot(w[:, lanes(t)], matrix) for t in range(2)]
    wide = jnp.concatenate(wide, axis=1).reshape(12, 16, 512)
    for m in range(12):
        for t in range(4):
            part = wide[m, :, lanes(t)]
            rs[t, pl.ds(0, 16, stride=2), :] = part
            rs[t, pl.ds(1, 16, stride=2), :] = part
            for j in range(2):
                p = 2 * m + j
                wa[p, :, lanes(t)] = v1[p, :, lanes(t)] + rs[t, 0:24, :]
    k1 = spread(1)

    def sweep1(src, dst):
        def body(p):
            here, sums = plane(src, p)
            for t in range(4):
                dst[p, :, lanes(t)] = KEEP * here[t] + g1[p, :, lanes(t)] * (f1[p, :, lanes(t)] + k1 * sums[t])

        return body

    loop(2, 22, sweep1(wa, w1))
    loop(3, 21, sweep1(w1, wa))

    sub = iota((18, 8, 128), 1)
    for t in range(4):
        halo = wa[3:21, 16:24, lanes(t)]
        halo = jnp.where(sub < 2, halo, shifted(halo, 4, 1))
        w = jnp.concatenate([wa[3:21, 0:16, lanes(t)], halo], axis=1)
        ws[:, :, t * 256 : t * 256 + 256] = split_dot(w.reshape(432, 128), matrix).reshape(18, 24, 256)

    for copy in level0:
        copy.wait()
    zsl[...] = vzl[...].astype(F32)
    zsh[...] = vzh[...].astype(F32)
    for i in range(4):
        v2[i] = v2[i] + zsl[40 * i : 40 * i + 40, :]
        v2[32 + i] = v2[32 + i] + zsh[40 * i : 40 * i + 40, :]

    s8 = iota((8, 128), 0)

    outer = outer_rows(s8)

    def correct(i):
        rows = pl.ds(pl.multiple_of(16 * i, 16), 16)
        for t in range(NT):
            low = vxl[rows, lanes(t)].astype(F32)
            high = vxh[rows, lanes(t)].astype(F32)
            for n in range(2):
                part = ws[2 * i + n, :, lanes(t)]
                rs[t, pl.ds(0, 24, stride=2), :] = part
                rs[t, pl.ds(1, 24, stride=2), :] = part
                for j in range(2):
                    p = 4 * i + 2 * n + j
                    lo, hi = low[8 * n : 8 * n + 8], high[8 * n : 8 * n + 8]
                    if j:
                        lo, hi = shifted(lo, 4, 0), shifted(hi, 4, 0)
                    v2[p, 0:8, lanes(t)] = v2[p, 0:8, lanes(t)] + rs[t, 0:8, :] + jnp.where(s8 < 2, lo, 0.0)
                    v2[p, 8:24, lanes(t)] = v2[p, 8:24, lanes(t)] + rs[t, 8:24, :]
                    v2[p, 24:32, lanes(t)] = v2[p, 24:32, lanes(t)] + rs[t, 24:32, :] + jnp.where(s8 >= 6, hi, 0.0)
                    extra = jnp.where(outer, jnp.where(s8 >= 4, lo, hi), 0.0)
                    v2[p, 32:40, lanes(t)] = v2[p, 32:40, lanes(t)] + rs[t, 32:40, :] + extra

    loop(0, 9, correct)
    k0 = spread(0)

    def first(i):
        rows = pl.ds(pl.multiple_of(16 * i + 144, 16), 16)
        for t in range(NT):
            fsl[:, lanes(t)] = vxl[rows, lanes(t)].astype(F32)
            fsh[:, lanes(t)] = vxh[rows, lanes(t)].astype(F32)

        def step(j):
            z = 16 * i + j
            start = pl.multiple_of((j // 8) * 8, 8)
            turn = lax.rem(j, 8)
            here, sums = plane(v2, z + 2)
            for t in range(NT):
                lo = pltpu.roll(fsl[pl.ds(start, 8), lanes(t)], 7 - turn, 0)
                hi = pltpu.roll(fsh[pl.ds(start, 8), lanes(t)], lax.rem(8 - turn, 8), 0)
                f = jnp.where(s8 == 7, lo, jnp.where(s8 == 0, hi, 0.0))
                g = gg[z + 2, :, lanes(t)]
                inner = k0 * sums[t]
                vb[z + 1, 0:32, lanes(t)] = KEEP * here[t][0:32] + g[0:32] * (supply[z, :, lanes(t)] + inner[0:32])
                vb[z + 1, 32:40, lanes(t)] = KEEP * here[t][32:40] + g[32:40] * (f + inner[32:40])

        loop(0, 16, step)

    loop(0, 2, first)
    for p, ref in ((1, zsl), (34, zsh)):
        here, sums = plane(v2, p)
        for t in range(NT):
            g = gg[p, :, lanes(t)]
            vb[p - 1, :, lanes(t)] = KEEP * here[t] + g * (ref[160:200, lanes(t)] + k0 * sums[t])

    def second(z):
        here, sums = plane(vb, z + 1)
        for t in range(NT):
            g = gg[z + 2, 0:32, lanes(t)]
            out[z, :, lanes(t)] = KEEP * here[t][0:32] + g * (supply[z, :, lanes(t)] + k0 * sums[t][0:32])

    loop(0, C, second)


VMEM = pl.BlockSpec(memory_space=pltpu.VMEM)
SMEM = pl.BlockSpec(memory_space=pltpu.SMEM)
ANY = pl.BlockSpec(memory_space=pl.ANY)


def call(kernel, outs, scratch, smem, args, out_specs=None, in_hbm=0):
    moved = sum(a.size * a.dtype.itemsize for a in list(args) + list(outs))
    return pl.pallas_call(
        kernel,
        out_shape=tuple(outs),
        in_specs=[SMEM] * smem + [VMEM] * (len(args) - smem - in_hbm) + [ANY] * in_hbm,
        out_specs=tuple(out_specs or [VMEM] * len(outs)),
        scratch_shapes=scratch,
        compiler_params=pltpu.CompilerParams(vmem_limit_bytes=58 * 2**20),
        cost_estimate=pl.CostEstimate(flops=20 * moved, bytes_accessed=moved, transcendentals=0),
    )(*args)


def shaped(shape, dtype=F32):
    return jax.ShapeDtypeStruct(shape, dtype)


def both_ways(to_low, to_high, axis, distance=1):
    count = lax.axis_size(axis)
    up = [(i, i + distance) for i in range(count - distance)]
    down = [(j, i) for i, j in up]
    return lax.ppermute(to_high, axis, up), lax.ppermute(to_low, axis, down)


def shards(density, uptake, brick_values, brick_ids, slot_counts):
    nz, nx = lax.axis_size("gz"), lax.axis_size("xy")
    info = jnp.stack([lax.axis_index("gz"), lax.axis_index("xy")]).astype(jnp.int32)
    scratch = pltpu.VMEM
    half = lambda *shape: shaped(shape, BF16)
    full = lambda *shape: shaped(shape, F32)

    (blocks,) = call(
        lambda *refs: brick_kernel(2 * nx, *refs),
        [half(9, 272, 128)],
        [scratch((SLOTS, BRICK), F32)],
        2,
        (brick_ids, slot_counts, brick_values),
    )
    zl, zh = both_ways(blocks[0:3], blocks[6:9], "gz")
    r1, r2, rzl, rzh, rz2l, rz2h, uxl, uxh = call(
        rates_kernel,
        [full(16, 16, 512), full(64, 256), half(128, 1024), half(128, 1024), half(32, 256), half(32, 256), half(64, 1024), half(64, 1024)],
        [scratch((8, 32, 128), F32), scratch((8, 16, 16, 128), F32), scratch((4, 16, 128), F32), scratch((4, 8, 8, 128), F32)],
        0,
        (uptake,),
    )
    rzl, rzh = both_ways(rzl, rzh, "gz")
    rz2l, rz2h = both_ways(rz2l, rz2h, "gz", 2)
    hop = lambda d: jnp.stack([blocks[3 + d], zl[d], zh[d]])
    xl, xr = both_ways(hop(0), hop(2), "xy")
    q1, q2, ul, uh, cl, ch, wl, wh = call(
        rates_window_kernel,
        [full(24, 24, 512), full(32, 8, 256), half(80, 1024), half(80, 1024), half(224, 512), half(224, 512), half(128, 256), half(128, 256)],
        [],
        0,
        (r1, r2, uxl, uxh, rzl, rzh, rz2l, rz2h),
    )
    ul, uh = both_ways(ul, uh, "xy")
    cl, ch = both_ways(cl, ch, "xy")
    wl, wh = both_ways(wl, wh, "xy", 2)

    supply, c1, mzl, mzh, vzl, vzh, pxl, pxh, v2, gg = call(
        lambda *refs: pre_kernel(nz, nx, *refs),
        [
            full(C, C, 1024),
            full(20, 24, 512),
            half(144, 512),
            half(144, 512),
            half(200, 1024),
            half(200, 1024),
            half(176, 1024),
            half(176, 1024),
            full(36, 40, 1024),
            full(36, 40, 1024),
        ],
        [
            scratch((42, 40, 1024), F32),
            scratch((42, 40, 1024), F32),
            scratch((36, 40, 1024), F32),
            scratch((36, 40, 1024), F32),
            scratch((1024, 1152), BF16),
            scratch((8, 40, 128), F32),
            scratch((8, 20, 24, 128), F32),
            scratch((80, 1024), F32),
            scratch((80, 1024), F32),
            pltpu.SemaphoreType.DMA((2,)),
        ],
        1,
        (info, density, uptake, rzl, rzh, ul, uh, blocks, zl, zh, xl, xr),
        [VMEM] * 8 + [ANY] * 2,
    )
    mzl, mzh = both_ways(mzl, mzh, "gz")
    vzl, vzh = both_ways(vzl, vzh, "gz")
    f1, mxl, mxh = call(
        merge_kernel,
        [full(24, 24, 512), half(144, 512), half(144, 512)],
        [],
        0,
        (c1, mzl, mzh),
    )
    mxl, mxh = both_ways(mxl, mxh, "xy")
    pxl, pxh = call(
        sides_kernel,
        [half(176, 1024), half(176, 1024)],
        [],
        0,
        (pxl, pxh, vzl, vzh),
    )
    vxl, vxh = both_ways(pxl, pxh, "xy")
    f1, pxl, pxh = lax.optimization_barrier((f1, pxl, pxh))
    f1, g1, v1, g2, g2l, g2h = call(
        lambda *refs: middle_kernel(nz, nx, *refs),
        [full(24, 24, 512), full(24, 24, 512), full(24, 24, 512), full(64, 256), full(32, 256), full(32, 256)],
        [scratch((24, 24, 512), F32), scratch((24, 24, 512), F32), scratch((4, 16, 128), F32), scratch((4, 8, 8, 128), F32)],
        1,
        (info, f1, q1, cl, ch, mxl, mxh),
    )
    low, high = both_ways(g2, g2, "gz")
    low2, high2 = both_ways(g2l, g2h, "gz", 2)
    own2, near, fl, fh = call(
        source_window_kernel,
        [full(32, 8, 256), half(256, 256), half(128, 256), half(128, 256)],
        [],
        0,
        (g2, low, high, low2, high2),
    )
    nl, nh = both_ways(near, near, "xy")
    fl, fh = both_ways(fl, fh, "xy", 2)
    window2 = scratch((32, 32, 256), F32)
    window1 = scratch((24, 24, 512), F32)
    (concentration,) = call(
        lambda *refs: back_kernel(nz, nx, *refs),
        [full(C, C, 1024)],
        [
            window2, window2, window2, window2, window2,
            scratch((8, 48, 128), F32),
            scratch((2, 16, 16, 128), F32),
            scratch((2, 16, 16, 128), F32),
            window1, window1,
            scratch((200, 1024), F32),
            scratch((200, 1024), F32),
            scratch((34, 40, 1024), F32),
            scratch((18, 24, 1024), F32),
            scratch((36, 40, 1024), F32),
            scratch((36, 40, 1024), F32),
            scratch((C, C, 1024), F32),
            scratch((16, 1024), F32),
            scratch((16, 1024), F32),
            pltpu.SemaphoreType.DMA((3,)),
        ],
        1,
        (info, f1, g1, v1, vzl, vzh, vxl, vxh, own2, nl, nh, fl, fh, q2, cl, ch, wl, wh, v2, gg, supply),
        in_hbm=3,
    )
    return supply, concentration


def solution(mesh):
    return jax.shard_map(
        shards,
        mesh=mesh,
        in_specs=(
            P("gz", "xy", None),
            P("gz", "xy", None),
            P(("gz", "xy"), None),
            P(("gz", "xy")),
            P(("gz", "xy"), None),
        ),
        out_specs=(P("gz", "xy", None), P("gz", "xy", None)),
        check_vma=False,
    )
```

```python
import jax
import jax.numpy as jnp
from jax import lax
from jax.experimental import pallas as pl
from jax.experimental.pallas import tpu as pltpu
from jax.sharding import PartitionSpec as P

EDGE = 16
CAP = 8
BRICK = 4096
SLOTS = 72
KAPPA = 32.0
OMEGA = 0.8
KEEP = 1.0 - OMEGA

C = 32
NT = 8
F32 = jnp.float32
BF16 = jnp.bfloat16


def spread(level):
    return KAPPA / 4.0**level


def shifted(values, distance, axis):
    return pltpu.roll(values, distance % values.shape[axis], axis)


def iota(shape, dim):
    return lax.broadcasted_iota(jnp.int32, shape, dim)


def lanes(t):
    return slice(t * 128, (t + 1) * 128)


def along_y(tiles):
    lane = iota(tiles[0].shape, 1)
    ahead = [shifted(a, 1, 1) for a in tiles]
    behind = [shifted(a, -1, 1) for a in tiles]
    sums = []
    for t in range(len(tiles)):
        low = ahead[t - 1] if t else 0.0
        high = behind[t + 1] if t + 1 < len(tiles) else 0.0
        sums.append(jnp.where(lane == 0, low, ahead[t]) + jnp.where(lane == 127, high, behind[t]))
    return sums


def plane(ref, p):
    count = ref.shape[2] // 128
    here = [ref[p, :, lanes(t)] for t in range(count)]
    sums = along_y(here)
    for t in range(count):
        near = ref[p - 1, :, lanes(t)] + ref[p + 1, :, lanes(t)]
        near = near + (shifted(here[t], 1, 0) + shifted(here[t], -1, 0))
        sums[t] = sums[t] + near
    return here, sums


def loop(start, stop, body):
    def step(i, carry):
        body(i)
        return carry

    lax.fori_loop(start, stop, step, 0)


def split_dot(a, b):
    high = a.astype(BF16)
    low = (a - high.astype(F32)).astype(BF16)
    return jnp.dot(high, b, preferred_element_type=F32) + jnp.dot(low, b, preferred_element_type=F32)


def pooling():
    return jnp.where(iota((256, 128), 0) // 2 == iota((256, 128), 1), 0.125, 0.0).astype(BF16)


def doubling():
    return jnp.where(iota((128, 256), 1) // 2 == iota((128, 256), 0), 1.0, 0.0).astype(BF16)


def halve_rows(values, rs, t):
    rows = values.shape[0]
    rs[t, 0:rows, :] = values
    return rs[t, pl.ds(0, rows // 2, stride=2), :] + rs[t, pl.ds(1, rows // 2, stride=2), :]


def halve_lanes(xp, planes, rows):
    matrix = pooling()
    tiles = []
    for t in range(0, xp.shape[0], 2):
        pair = jnp.concatenate([xp[t].reshape(planes * rows, 128), xp[t + 1].reshape(planes * rows, 128)], axis=1)
        tiles.append(split_dot(pair, matrix).reshape(planes, rows, 128))
    return tiles


def inside(shape, dim, first, wrap, index, size, count):
    place = iota(shape, dim) + first
    if wrap is not None:
        place = jnp.where(place < wrap, place, place - shape[dim])
    place = place + index * size
    return (place >= 0) & (place < count * size)


BLOCK = 272
Z_ROWS = BLOCK + 5 * 64
X_ROWS = BLOCK + 3 * 80 + 128


def z_part(t):
    return slice(BLOCK + 64 * (t // 3), BLOCK + 64 * (t // 3) + 64), lanes(t % 3)


def x_part(t):
    return slice(BLOCK + 80 * (t // 3), BLOCK + 80 * (t // 3) + 80), lanes(t % 3)


def transposed_bricks(bricks_x, ids, counts, bricks, xs, targets):
    xs[...] = bricks[...].astype(F32)
    row = iota((1, 8, 128), 1)
    group = iota((1, 8, 128), 2) // 16
    group16 = iota((16, 128), 1) // 16
    per_y = 64

    def block(j, out, part):
        start = pl.multiple_of(j * 8, 8)
        x = jnp.stack([xs[pl.ds(start, 8), lanes(k)] for k in range(32)])
        for s in (4, 2, 1):
            up = shifted(shifted(x, -s, 1), 16 * s, 2)
            down = shifted(shifted(x, s, 1), -16 * s, 2)
            row_bit = (row // s) % 2
            group_bit = (group // s) % 2
            x = jnp.where(row_bit == group_bit, x, jnp.where(row_bit == 0, up, down))
        x = jnp.where(group < counts[0, j], x, 0.0)
        out[0:256, part] = x.reshape(256, 128).astype(BF16)
        names = jnp.zeros((16, 128), jnp.int32)
        for e in range(CAP):
            number = ids[j * 8 + e]
            by = lax.rem(number, per_y)
            rest = lax.div(number, per_y)
            bx = lax.rem(rest, 2)
            bz = lax.rem(lax.div(rest, bricks_x), 2)
            names = jnp.where(group16 == e, (bz * 2 + bx) * per_y + by, names)
        out[256:272, part] = names.astype(F32).astype(BF16)

    for i, out in enumerate(targets):
        for d in range(3):
            block(3 * i + d, out, lanes(d))


def first_kernel(bricks_x, nz, info, ids, counts, bricks, uptake, own, r1, r2, zl, zh, z2l, z2h, xl, xh, rs, xp, rs1, xp1, xs):
    transposed_bricks(bricks_x, ids, counts, bricks, xs, (zl, own, zh))

    def pair(m):
        for t in range(NT):
            both = uptake[2 * m, :, lanes(t)] + uptake[2 * m + 1, :, lanes(t)]
            xp[t, m] = halve_rows(both, rs, t)

    loop(0, 16, pair)
    for t, tile in enumerate(halve_lanes(xp, 16, 16)):
        r1[:, :, lanes(t)] = tile

    def pair1(m):
        for t in range(4):
            both = r1[2 * m, :, lanes(t)] + r1[2 * m + 1, :, lanes(t)]
            xp1[t, m] = halve_rows(both, rs1, t)

    loop(0, 8, pair1)
    coarse = []
    for t, tile in enumerate(halve_lanes(xp1, 8, 8)):
        r2[:, lanes(t)] = tile.reshape(64, 128)
        coarse.append(tile.reshape(64, 128).astype(BF16))
    low, high = far_along_z(nz, info[0], r2[0:32, :], r2[32:64, :])
    z2l[...] = low.astype(BF16)
    z2h[...] = high.astype(BF16)
    for ref, u, r in ((zl, slice(0, 2), slice(0, 4)), (zh, slice(30, 32), slice(12, 16))):
        for t in range(8):
            ref[z_part(t)] = uptake[u, :, lanes(t)].reshape(64, 128).astype(BF16)
        for t in range(4):
            ref[z_part(8 + t)] = r1[r, :, lanes(t)].reshape(64, 128).astype(BF16)
        for t in range(2):
            ref[z_part(12 + t)] = coarse[t]
        ref[z_part(14)] = jnp.zeros((64, 128), BF16)

    sub = iota((8, 1024), 0)

    def columns(i):
        lows, highs = [], []
        for j in range(2):
            low, high = jnp.zeros((8, 1024), F32), jnp.zeros((8, 1024), F32)
            for n in range(4):
                z = 8 * i + 4 * j + n
                low = jnp.where(sub // 2 == n, shifted(uptake[z, 0:8, :], 2 * n, 0), low)
                high = jnp.where(sub // 2 == n, shifted(uptake[z, 24:32, :], 2 * n + 2, 0), high)
            lows.append(low)
            highs.append(high)
        rows = pl.ds(pl.multiple_of(16 * i, 16), 16)
        xl[rows, :] = jnp.concatenate(lows, axis=0).astype(BF16)
        xh[rows, :] = jnp.concatenate(highs, axis=0).astype(BF16)

    loop(0, 4, columns)


def far_along_z(nz, iz, to_low, to_high):
    if nz != 4:
        return to_low, to_high
    one = jnp.where(iz < 2, to_high, to_low)
    return one, one


def halves(sub, first, second):
    return jnp.where(sub < 4, first, shifted(second, 4, 1))


def uppers(sub, first, second):
    return jnp.where(sub < 4, shifted(first, 4, 1), second)


def far_messages(window):
    planes, _, width = window.shape
    pairs = window.reshape(planes // 2, 2, 8, width)
    sub = iota((planes // 2, 8, width), 1)
    size = (planes * 4, width)
    return halves(sub, pairs[:, 0], pairs[:, 1]).reshape(size), uppers(sub, pairs[:, 0], pairs[:, 1]).reshape(size)


def far_tile(from_low, from_high):
    width = from_low.shape[-1]
    low, high = from_low.reshape(-1, 8, width), from_high.reshape(-1, 8, width)
    sub = iota(low.shape, 1)
    even = jnp.where(sub < 4, high, shifted(low, 4, 1))
    odd = jnp.where(sub < 4, shifted(high, 4, 1), low)
    return jnp.stack([even, odd], axis=1).reshape(-1, 8, width)


def rates_window_kernel(own, r1, r2, uxl, uxh, zl, zh, z2l, z2h, q1, q2, xl, xh):
    for ref, d in ((xl, 0), (xh, 2)):
        for n, src in enumerate((own, zl, zh)):
            ref[0:BLOCK, lanes(n)] = src[0:BLOCK, lanes(d)]
    sub = iota((16, 128), 0)
    for t in range(8):
        rows, part = x_part(t)
        rows = rows.start
        xl[rows : rows + 64, part] = uxl[:, lanes(t)]
        xh[rows : rows + 64, part] = uxh[:, lanes(t)]
        both = [ref[z_part(t)].astype(F32) for ref in (zl, zh)]
        planes = [both[0][0:32], both[0][32:64], both[1][0:32], both[1][32:64]]
        to_low, to_high = jnp.zeros((16, 128), F32), jnp.zeros((16, 128), F32)
        for n, p in enumerate(planes):
            here = sub // 2 == n
            to_low = jnp.where(here, shifted(p[0:16], 2 * n, 0), to_low)
            to_high = jnp.where(here, shifted(p[16:32], 2 * n + 2, 0), to_high)
        xl[rows + 64 : rows + 80, part] = to_low.astype(BF16)
        xh[rows + 64 : rows + 80, part] = to_high.astype(BF16)
    rows, part = x_part(8)
    for ref in (xl, xh):
        ref[rows, part] = jnp.zeros((80, 128), BF16)

    low = jnp.concatenate([zl[z_part(8 + t)].astype(F32) for t in range(6)], axis=1)
    high = jnp.concatenate([zh[z_part(8 + t)].astype(F32) for t in range(6)], axis=1)
    q1[0:4, 0:16, :] = low[:, 0:512].reshape(4, 16, 512)
    q1[4:20, 0:16, :] = r1[...]
    q1[20:24, 0:16, :] = high[:, 0:512].reshape(4, 16, 512)
    q1[:, 16:24, :] = jnp.zeros((24, 8, 512), F32)
    sub1 = iota((12, 8, 512), 1)
    first = q1[:, 0:8, :].reshape(12, 2, 8, 512)
    last = q1[:, 8:16, :].reshape(12, 2, 8, 512)
    to_low = halves(sub1, first[:, 0], first[:, 1]).reshape(96, 512).astype(BF16)
    to_high = uppers(sub1, last[:, 0], last[:, 1]).reshape(96, 512).astype(BF16)
    start = X_ROWS - 128
    for ref, message in ((xl, to_low), (xh, to_high)):
        for t in range(3):
            ref[start : start + 96, lanes(t)] = message[:, lanes(t)]
            ref[start + 96 : start + 128, lanes(t)] = message[32 * t : 32 * t + 32, lanes(3)]
    q2[...] = window_planes(r2[...], low[:, 512:768], high[:, 512:768], z2l[...].astype(F32), z2h[...].astype(F32))


def rates_from_x(ref):
    start = X_ROWS - 128
    last = jnp.concatenate([ref[start + 96 : start + 128, lanes(t)] for t in range(3)], axis=0)
    tiles = [ref[start : start + 96, lanes(t)] for t in range(3)] + [last]
    return jnp.concatenate([a.astype(F32) for a in tiles], axis=1).reshape(12, 8, 512)


def window_planes(own, low, high, low2, high2):
    parts = (low2, low, own, high, high2)
    return jnp.concatenate([a.reshape(-1, 8, 256) for a in parts], axis=0)


def source_window_kernel(own, low, high, low2, high2, q2, window, near, fl, fh):
    planes = window_planes(own[...], low[...], high[...], low2[...], high2[...])
    window[...] = planes
    near[...] = planes.reshape(256, 256).astype(BF16)
    for i, values in enumerate((planes, q2[...])):
        to_low, to_high = far_messages(values)
        fl[128 * i : 128 * i + 128, :] = to_low.astype(BF16)
        fh[128 * i : 128 * i + 128, :] = to_high.astype(BF16)


def pre_kernel(
    nz, nx, info, density, uptake, own, zl, zh, xl, xh,
    supply, c1, mzl, mzh, pxl, pxh, v_out, g_out,
    va, vb, dd, gg, hot, rs, xp, usl, ush, sems,
):
    iz, ix = info[0], info[1]
    k = spread(0)
    base = 1.0 + 6.0 * k
    O = 5
    Q = 2

    for p in (0, 1, 2, 3, 4, 37, 38, 39, 40, 41):
        va[p] = jnp.zeros((40, 1024), F32)
    for p in (2, 3, 38, 39):
        vb[p] = jnp.zeros((40, 1024), F32)

    sub8 = iota((8, 1024), 0)

    for t in range(NT):
        usl[:, lanes(t)] = xl[x_part(t)].astype(F32)
        ush[:, lanes(t)] = xh[x_part(t)].astype(F32)

    def set_plane(q, rates, low, high, valid_z):
        gz = jnp.where(valid_z, OMEGA, 0.0)
        d = rates + base
        dd[q, 0:32, :] = d
        gg[q, 0:32, :] = gz / d
        d = jnp.where(sub8 < 2, high, jnp.where(sub8 >= 6, low, 0.0)) + base
        dd[q, 32:40, :] = d
        omega = jnp.where(sub8 < 2, jnp.where(ix < nx - 1, gz, 0.0), jnp.where(sub8 >= 6, jnp.where(ix > 0, gz, 0.0), 0.0))
        gg[q, 32:40, :] = omega / d

    def own_planes(i):
        rows = pl.ds(pl.multiple_of(8 * i, 8), 8)
        low, high = usl[rows, :], ush[rows, :]
        for n in range(4):
            z = 4 * i + n
            va[z + O, 0:32, :] = density[z]
            va[z + O, 32:40, :] = jnp.zeros((8, 1024), F32)
            set_plane(z + Q, uptake[z], shifted(low, 6 - 2 * n, 0), shifted(high, -2 * n, 0), True)

    loop(0, C // 4, own_planes)
    low, high = usl[64:72, :], ush[64:72, :]
    for n in range(4):
        ref = zl if n < 2 else zh
        rates = [ref[z_part(t)].astype(F32)[32 * (n % 2) : 32 * (n % 2) + 32] for t in range(NT)]
        rates = jnp.concatenate(rates, axis=1)
        exists = iz > 0 if n < 2 else iz < nz - 1
        set_plane(n if n < 2 else 32 + n, rates, shifted(low, 6 - 2 * n, 0), shifted(high, -2 * n, 0), exists)

    blocks = [(ref, lanes(1)) for ref in (own, zl, zh)] + [(ref, lanes(n)) for ref in (xl, xh) for n in range(3)]
    lane = iota((1, 128), 1)
    at_y = iota((1024, 128), 0)
    tiles = []
    for i, (ref, part) in enumerate(blocks):
        name = ref[256:272, part].astype(F32).astype(jnp.int32)[0:1]
        tiles.append(lax.shift_right_logical(name, 6))
        y = (name & 63) * 16 + (lane & 15)
        hot[:, lanes(i)] = jnp.where(at_y == y, 1.0, 0.0).astype(BF16)
    for tile in range(4):
        bz, bx = tile // 2, tile % 2
        left = jnp.concatenate(
            [jnp.where(tiles[i] == tile, ref[0:256, part].astype(F32), 0.0).astype(BF16) for i, (ref, part) in enumerate(blocks)],
            axis=1,
        )
        for n in range(4):
            cols = slice(n * 256, (n + 1) * 256)
            part = lax.dot_general(left, hot[cols, :], (((1,), (1,)), ((), ())), preferred_element_type=F32)
            zs, xs = slice(16 * bz, 16 * bz + 16), slice(16 * bx, 16 * bx + 16)
            supply[zs, xs, cols] = density[zs, xs, cols] + part.reshape(16, 16, 256)

    def sweep(src, dst, z, sourced):
        here, sums = plane(src, z + O)
        for t in range(NT):
            inner = k * sums[t]
            g = gg[z + Q, :, lanes(t)]
            if sourced:
                body = inner[0:32] + supply[z, :, lanes(t)]
                dst[z + O, 0:32, lanes(t)] = KEEP * here[t][0:32] + g[0:32] * body
                dst[z + O, 32:40, lanes(t)] = KEEP * here[t][32:40] + g[32:40] * inner[32:40]
            else:
                dst[z + O, :, lanes(t)] = KEEP * here[t] + g * inner

    def halo_planes(src, dst, width):
        def step(i):
            sweep(src, dst, jnp.where(i < width, i - width, i - width + C), False)

        loop(0, 2 * width, step)

    loop(0, C, lambda z: sweep(va, vb, z, True))
    halo_planes(va, vb, 1)
    loop(0, C, lambda z: sweep(vb, va, z, True))
    halo_planes(vb, va, 2)

    v_copy = pltpu.make_async_copy(va.at[3:39], v_out, sems.at[0])
    g_copy = pltpu.make_async_copy(gg, g_out, sems.at[1])
    v_copy.start()
    g_copy.start()

    def residual(z, sourced, edge):
        here, sums = plane(va, z + O)
        out = []
        for t in range(NT):
            r = k * sums[t]
            if not edge:
                r = r - dd[z + Q, :, lanes(t)] * here[t]
            if sourced:
                r = jnp.concatenate([r[0:32] + supply[z, :, lanes(t)], r[32:40]], axis=0)
            out.append(r)
        return out

    def coarse(m, sourced):
        first = residual(2 * m - 4, sourced, False)
        second = residual(2 * m - 3, sourced, False)
        for t in range(NT):
            xp[t, m, 0:20, :] = halve_rows(first[t] + second[t], rs, t)

    loop(2, 18, lambda m: coarse(m, True))
    loop(0, 2, lambda i: coarse(1 + 17 * i, False))

    def outer(i):
        r = residual(jnp.where(i == 0, -3, 34), False, True)
        for t in range(NT):
            xp[t, 19 * i, 0:20, :] = halve_rows(r[t], rs, t)

    loop(0, 2, outer)

    sub = iota((20, 8, 128), 1)
    for t, tile in enumerate(halve_lanes(xp, 20, 24)):
        last = tile[:, 16:24]
        last = jnp.where(sub < 2, last, jnp.where(sub >= 6, shifted(last, 4, 1), 0.0))
        c1[:, 0:16, lanes(t)] = tile[:, 0:16]
        c1[:, 16:24, lanes(t)] = last

    empty = jnp.zeros((1, 8, 1024), F32)
    blank = jnp.zeros((8, 1024), F32)
    for ref, planes, values, z in ((mzl, slice(0, 6), va[3:7], 0), (mzh, slice(14, 20), va[35:39], 31)):
        source = c1[planes].reshape(144, 512)
        ref[0:80, 0:512] = source[0:80].astype(BF16)
        ref[0:64, 512:1024] = source[80:144].astype(BF16)
        ref[64:80, 512:1024] = jnp.zeros((16, 512), BF16)
        level0 = jnp.concatenate([values, jnp.concatenate([supply[z : z + 1], empty], axis=1)], axis=0)
        ref[80:288, :] = jnp.concatenate([level0.reshape(200, 1024), blank], axis=0).astype(BF16)

    def sides(i):
        lows, highs = [], []
        for j in range(2):
            p = 4 * i + 2 * j + 3
            lows.append(pack_low(va[p], va[p + 1]))
            highs.append(pack_high(va[p], va[p + 1]))
        rows = pl.ds(pl.multiple_of(16 * i, 16), 16)
        pxl[rows, :] = jnp.concatenate(lows, axis=0).astype(BF16)
        pxh[rows, :] = jnp.concatenate(highs, axis=0).astype(BF16)

    loop(0, 9, sides)

    def sources(i):
        lows, highs = [], []
        for j in range(2):
            low, high = jnp.zeros((8, 1024), F32), jnp.zeros((8, 1024), F32)
            for n in range(8):
                z = 16 * i + 8 * j + n
                low = jnp.where(sub8 == n, shifted(supply[z, 0:8, :], n, 0), low)
                high = jnp.where(sub8 == n, shifted(supply[z, 24:32, :], n + 1, 0), high)
            lows.append(low)
            highs.append(high)
        rows = pl.ds(pl.multiple_of(16 * i + 144, 16), 16)
        pxl[rows, :] = jnp.concatenate(lows, axis=0).astype(BF16)
        pxh[rows, :] = jnp.concatenate(highs, axis=0).astype(BF16)

    loop(0, 2, sources)
    v_copy.wait()
    g_copy.wait()


def outer_rows(sub):
    return (sub < 2) | (sub >= 6)


def pack_pair(sub, a, b):
    return jnp.where(outer_rows(sub), a, shifted(b, 4, 0))


def pack_low(first, second):
    sub = iota((8, 1024), 0)
    a, b = [jnp.where(sub < 4, v[0:8], v[32:40]) for v in (first, second)]
    return pack_pair(sub, a, b)


def pack_high(first, second):
    sub = iota((8, 1024), 0)
    a, b = [jnp.where(sub >= 4, v[24:32], v[32:40]) for v in (first, second)]
    return pack_pair(sub, a, b)


def sides_kernel(pxl, pxh, mzl, mzh, q2, out_l, out_h):
    for ref, out in ((pxl, out_l), (pxh, out_h)):
        out[0:176, :] = ref[...]
        for n in range(4):
            out[176:240, n * 256 : n * 256 + 256] = q2[8 * n : 8 * n + 8].reshape(64, 256).astype(BF16)
    for message, start in ((mzl, 0), (mzh, 128)):
        planes = message[80:240, :].astype(F32).reshape(4, 40, 1024)
        rows = slice(start, start + 16)
        for ref, out, pack in ((pxl, out_l, pack_low), (pxh, out_h, pack_high)):
            added = [pack(planes[2 * i], planes[2 * i + 1]) for i in range(2)]
            out[rows, :] = (ref[rows, :].astype(F32) + jnp.concatenate(added, axis=0)).astype(BF16)


def in_three(sub, tiles, free, turns):
    spare = (sub == free) | (sub == free + 1)
    last = tiles[:, 3]
    parts = [jnp.where(spare, shifted(last, turn, 1), tiles[:, i]) for i, turn in enumerate(turns)]
    return jnp.stack(parts, axis=1)


def out_of_three(sub, parts, free, turns):
    last = None
    for i, turn in enumerate(turns):
        back = shifted(parts[:, i], -turn, 1)
        home = (free - turn) % 8
        here = (sub == home) | (sub == home + 1)
        last = jnp.where(here, back, 0.0 if last is None else last)
    return jnp.stack([parts[:, 0], parts[:, 1], parts[:, 2], last], axis=1)


HIGH_PACK = (2, (-2, 4, 2))
LOW_PACK = (4, (-2, 4, 2))


def merge_kernel(c1, mzl, mzh, f1, mxl, mxh):
    zeros = jnp.zeros((24, 512), F32)
    for p in (0, 1, 22, 23):
        f1[p] = zeros
    f1[2:22] = c1[...]
    for ref, planes in ((mzl, slice(0, 6)), (mzh, slice(18, 24))):
        parts = [ref[0:80, 0:512].astype(F32), ref[0:64, 512:1024].astype(F32)]
        f1[planes] = f1[planes] + jnp.concatenate(parts, axis=0).reshape(6, 24, 512)
    sub = iota((6, 8, 512), 1)
    first, last, halo = [f1[:, 8 * n : 8 * n + 8].reshape(6, 4, 8, 512) for n in range(3)]
    sub4 = iota((6, 4, 8, 512), 2)
    to_high = in_three(sub, jnp.where(sub4 >= 4, last, halo), *HIGH_PACK)
    to_low = in_three(sub, jnp.where(sub4 >= 4, halo, first), *LOW_PACK)
    mxh[...] = to_high.reshape(144, 512).astype(BF16)
    mxl[...] = to_low.reshape(144, 512).astype(BF16)


def middle_kernel(nz, nx, info, f0, q_in, xl, xh, mxl, mxh, f1, g1, v1, g2, g2l, g2h, q0, va, rs, xp):
    iz, ix = info[0], info[1]
    k = spread(1)
    base = 1.0 + 6.0 * k
    sub6 = iota((6, 8, 512), 1)
    low = out_of_three(sub6, mxl[...].astype(F32).reshape(6, 3, 8, 512), *HIGH_PACK).reshape(24, 8, 512)
    high = out_of_three(sub6, mxh[...].astype(F32).reshape(6, 3, 8, 512), *LOW_PACK).reshape(24, 8, 512)
    sub = iota((24, 8, 512), 1)
    f1[:, 0:8] = f0[:, 0:8] + jnp.where(sub < 2, low, 0.0)
    f1[:, 8:16] = f0[:, 8:16] + jnp.where(sub >= 6, high, 0.0)
    f1[:, 16:24] = f0[:, 16:24] + jnp.where(sub >= 4, low, high)
    low, high = rates_from_x(xl), rates_from_x(xh)
    sub12 = iota((12, 8, 512), 1)
    even = jnp.where(sub12 >= 4, shifted(low, 4, 1), high)
    odd = jnp.where(sub12 >= 4, low, shifted(high, 4, 1))
    q0[:, 0:16] = q_in[:, 0:16]
    q0[:, 16:24] = jnp.stack([even, odd], axis=1).reshape(24, 8, 512)
    shape = (24, 24, 128)
    valid = inside(shape, 0, -4, None, iz, 16, nz) & inside(shape, 1, 0, 20, ix, 16, nx)
    for t in range(4):
        g = jnp.where(valid, OMEGA, 0.0) / (q0[:, :, lanes(t)] + base)
        g1[:, :, lanes(t)] = g
        va[:, :, lanes(t)] = g * f1[:, :, lanes(t)]
    v1[0] = va[0]
    v1[23] = va[23]

    def sweep(p):
        here, sums = plane(va, p)
        for t in range(4):
            v1[p, :, lanes(t)] = KEEP * here[t] + g1[p, :, lanes(t)] * (f1[p, :, lanes(t)] + k * sums[t])

    loop(1, 23, sweep)

    def coarse(m):
        total = None
        for j in range(2):
            p = 2 * m + 4 + j
            here, sums = plane(v1, p)
            r = [
                f1[p, :, lanes(t)] + k * sums[t] - (q0[p, :, lanes(t)] + base) * here[t]
                for t in range(4)
            ]
            total = r if total is None else [a + b for a, b in zip(total, r)]
        for t in range(4):
            xp[t, m] = halve_rows(total[t][0:16], rs, t)

    loop(0, 8, coarse)
    for t, tile in enumerate(halve_lanes(xp, 8, 8)):
        g2[:, lanes(t)] = tile.reshape(64, 128)
        low, high = far_along_z(nz, iz, tile[0:4].reshape(32, 128), tile[4:8].reshape(32, 128))
        g2l[:, lanes(t)] = low
        g2h[:, lanes(t)] = high


def back_kernel(
    nz, nx, info, f1, g1, v1, vzl, vzh, vxl, vxh, own2, n2l, n2h, m2l, m2h, q_own, v_in, g_in, s_in,
    out,
    f2, q2, h2, a2, b2, rs, xp, xpr, wa, w1, zsl, zsh, vb, ws,
    v2, gg, supply, fsl, fsh, sems,
):
    iz, ix = info[0], info[1]
    matrix = doubling()
    level0 = [
        pltpu.make_async_copy(src, dst, sems.at[i])
        for i, (src, dst) in enumerate(((v_in, v2), (g_in, gg), (s_in, supply)))
    ]
    for copy in level0:
        copy.start()

    f2[:, 0:8, :] = own2[...]
    f2[:, 8:16, :] = n2h[...].astype(F32).reshape(32, 8, 256)
    f2[:, 16:24, :] = far_tile(m2l[0:128, :].astype(F32), m2h[0:128, :].astype(F32))
    f2[:, 24:32, :] = n2l[...].astype(F32).reshape(32, 8, 256)
    q2[:, 0:8, :] = q_own[...]
    q2[:, 16:24, :] = far_tile(m2l[128:256, :].astype(F32), m2h[128:256, :].astype(F32))
    for ref, rows in ((vxh, slice(8, 16)), (vxl, slice(24, 32))):
        for n in range(4):
            q2[8 * n : 8 * n + 8, rows, :] = ref[176:240, n * 256 : n * 256 + 256].astype(F32).reshape(8, 8, 256)

    k = spread(2)
    base = 1.0 + 6.0 * k
    shape = (32, 32, 128)
    valid = inside(shape, 0, -12, None, iz, 8, nz) & inside(shape, 1, 0, 20, ix, 8, nx)
    for t in range(2):
        g = jnp.where(valid, OMEGA, 0.0) / (q2[:, :, lanes(t)] + base)
        h2[:, :, lanes(t)] = g
        a2[:, :, lanes(t)] = g * f2[:, :, lanes(t)]
    b2[0] = a2[0]
    b2[31] = a2[31]

    def sweep2(src, dst):
        def body(p):
            here, sums = plane(src, p)
            for t in range(2):
                dst[p, :, lanes(t)] = KEEP * here[t] + h2[p, :, lanes(t)] * (f2[p, :, lanes(t)] + k * sums[t])

        return body

    loop(1, 31, sweep2(a2, b2))

    def coarse(m):
        total, rates = [0.0, 0.0], [0.0, 0.0]
        for j in range(2):
            p = 2 * m + j
            here, sums = plane(b2, p)
            for t in range(2):
                r = f2[p, :, lanes(t)] + k * sums[t] - (q2[p, :, lanes(t)] + base) * here[t]
                total[t] = total[t] + r
                rates[t] = rates[t] + q2[p, :, lanes(t)]
        for t in range(2):
            xp[t, m] = halve_rows(total[t], rs, t)
            xpr[t, m] = halve_rows(rates[t], rs, t + 2)

    for t in range(2):
        for m in (0, 15):
            xp[t, m] = jnp.zeros((16, 128), F32)
            xpr[t, m] = jnp.zeros((16, 128), F32)
    loop(1, 15, coarse)

    shape = (16, 16, 128)
    valid = inside(shape, 0, -6, None, iz, 4, nz) & inside(shape, 1, 0, 10, ix, 4, nx)
    k3 = spread(3)
    (source,) = halve_lanes(xp, 16, 16)
    (rates,) = halve_lanes(xpr, 16, 16)
    g = jnp.where(valid, OMEGA, 0.0) / (rates + (1.0 + 6.0 * k3))
    v = g * source
    lane = iota(shape, 2)
    for repeat in range(3):
        edge = jnp.zeros((1, 16, 128), F32)
        sums = jnp.concatenate([v[1:], edge], axis=0) + jnp.concatenate([edge, v[:-1]], axis=0)
        sums = sums + shifted(v, 1, 1) + shifted(v, -1, 1)
        sums = sums + jnp.where(lane == 0, 0.0, shifted(v, 1, 2)) + jnp.where(lane == 127, 0.0, shifted(v, -1, 2))
        v = KEEP * v + g * (source + k3 * sums)

    wide = split_dot(v[4:12].reshape(128, 128), matrix).reshape(8, 16, 256)
    for m in range(8):
        for t in range(2):
            part = wide[m, :, lanes(t)]
            rs[t, pl.ds(0, 16, stride=2), :] = part
            rs[t, pl.ds(1, 16, stride=2), :] = part
            for j in range(2):
                p = 8 + 2 * m + j
                b2[p, :, lanes(t)] = b2[p, :, lanes(t)] + rs[t, 0:32, :]
    loop(9, 23, sweep2(b2, a2))
    loop(10, 22, sweep2(a2, b2))

    w = b2[10:22]
    near, far = w[:, 8:16], w[:, 24:32]
    near = jnp.where(iota((12, 8, 256), 1) < 2, near, shifted(far, 4, 1))
    w = jnp.concatenate([w[:, 0:8], near], axis=1).reshape(192, 256)
    wide = [split_dot(w[:, lanes(t)], matrix) for t in range(2)]
    wide = jnp.concatenate(wide, axis=1).reshape(12, 16, 512)
    for m in range(12):
        for t in range(4):
            part = wide[m, :, lanes(t)]
            rs[t, pl.ds(0, 16, stride=2), :] = part
            rs[t, pl.ds(1, 16, stride=2), :] = part
            for j in range(2):
                p = 2 * m + j
                wa[p, :, lanes(t)] = v1[p, :, lanes(t)] + rs[t, 0:24, :]
    k1 = spread(1)

    def sweep1(src, dst):
        def body(p):
            here, sums = plane(src, p)
            for t in range(4):
                dst[p, :, lanes(t)] = KEEP * here[t] + g1[p, :, lanes(t)] * (f1[p, :, lanes(t)] + k1 * sums[t])

        return body

    loop(2, 22, sweep1(wa, w1))
    loop(3, 21, sweep1(w1, wa))

    sub = iota((18, 8, 128), 1)
    for t in range(4):
        halo = wa[3:21, 16:24, lanes(t)]
        halo = jnp.where(sub < 2, halo, shifted(halo, 4, 1))
        w = jnp.concatenate([wa[3:21, 0:16, lanes(t)], halo], axis=1)
        ws[:, :, t * 256 : t * 256 + 256] = split_dot(w.reshape(432, 128), matrix).reshape(18, 24, 256)

    for copy in level0:
        copy.wait()
    zsl[...] = vzl[80:288, :].astype(F32)
    zsh[...] = vzh[80:288, :].astype(F32)
    for i in range(4):
        v2[i] = v2[i] + zsl[40 * i : 40 * i + 40, :]
        v2[32 + i] = v2[32 + i] + zsh[40 * i : 40 * i + 40, :]

    s8 = iota((8, 128), 0)

    outer = outer_rows(s8)

    def correct(i):
        rows = pl.ds(pl.multiple_of(16 * i, 16), 16)
        for t in range(NT):
            low = vxl[rows, lanes(t)].astype(F32)
            high = vxh[rows, lanes(t)].astype(F32)
            for n in range(2):
                part = ws[2 * i + n, :, lanes(t)]
                rs[t, pl.ds(0, 24, stride=2), :] = part
                rs[t, pl.ds(1, 24, stride=2), :] = part
                for j in range(2):
                    p = 4 * i + 2 * n + j
                    lo, hi = low[8 * n : 8 * n + 8], high[8 * n : 8 * n + 8]
                    if j:
                        lo, hi = shifted(lo, 4, 0), shifted(hi, 4, 0)
                    v2[p, 0:8, lanes(t)] = v2[p, 0:8, lanes(t)] + rs[t, 0:8, :] + jnp.where(s8 < 2, lo, 0.0)
                    v2[p, 8:24, lanes(t)] = v2[p, 8:24, lanes(t)] + rs[t, 8:24, :]
                    v2[p, 24:32, lanes(t)] = v2[p, 24:32, lanes(t)] + rs[t, 24:32, :] + jnp.where(s8 >= 6, hi, 0.0)
                    extra = jnp.where(outer, jnp.where(s8 >= 4, lo, hi), 0.0)
                    v2[p, 32:40, lanes(t)] = v2[p, 32:40, lanes(t)] + rs[t, 32:40, :] + extra

    loop(0, 9, correct)
    k0 = spread(0)

    def first(i):
        rows = pl.ds(pl.multiple_of(16 * i + 144, 16), 16)
        for t in range(NT):
            fsl[:, lanes(t)] = vxl[rows, lanes(t)].astype(F32)
            fsh[:, lanes(t)] = vxh[rows, lanes(t)].astype(F32)

        def step(j):
            z = 16 * i + j
            start = pl.multiple_of((j // 8) * 8, 8)
            turn = lax.rem(j, 8)
            here, sums = plane(v2, z + 2)
            for t in range(NT):
                lo = pltpu.roll(fsl[pl.ds(start, 8), lanes(t)], 7 - turn, 0)
                hi = pltpu.roll(fsh[pl.ds(start, 8), lanes(t)], lax.rem(8 - turn, 8), 0)
                f = jnp.where(s8 == 7, lo, jnp.where(s8 == 0, hi, 0.0))
                g = gg[z + 2, :, lanes(t)]
                inner = k0 * sums[t]
                vb[z + 1, 0:32, lanes(t)] = KEEP * here[t][0:32] + g[0:32] * (supply[z, :, lanes(t)] + inner[0:32])
                vb[z + 1, 32:40, lanes(t)] = KEEP * here[t][32:40] + g[32:40] * (f + inner[32:40])

        loop(0, 16, step)

    loop(0, 2, first)
    for p, ref in ((1, zsl), (34, zsh)):
        here, sums = plane(v2, p)
        for t in range(NT):
            g = gg[p, :, lanes(t)]
            vb[p - 1, :, lanes(t)] = KEEP * here[t] + g * (ref[160:200, lanes(t)] + k0 * sums[t])

    def second(z):
        here, sums = plane(vb, z + 1)
        for t in range(NT):
            g = gg[z + 2, 0:32, lanes(t)]
            out[z, :, lanes(t)] = KEEP * here[t][0:32] + g * (supply[z, :, lanes(t)] + k0 * sums[t][0:32])

    loop(0, C, second)


VMEM = pl.BlockSpec(memory_space=pltpu.VMEM)
SMEM = pl.BlockSpec(memory_space=pltpu.SMEM)
ANY = pl.BlockSpec(memory_space=pl.ANY)


def call(kernel, outs, scratch, smem, args, out_specs=None, in_hbm=0):
    moved = sum(a.size * a.dtype.itemsize for a in list(args) + list(outs))
    return pl.pallas_call(
        kernel,
        out_shape=tuple(outs),
        in_specs=[SMEM] * smem + [VMEM] * (len(args) - smem - in_hbm) + [ANY] * in_hbm,
        out_specs=tuple(out_specs or [VMEM] * len(outs)),
        scratch_shapes=scratch,
        compiler_params=pltpu.CompilerParams(vmem_limit_bytes=58 * 2**20),
        cost_estimate=pl.CostEstimate(flops=20 * moved, bytes_accessed=moved, transcendentals=0),
    )(*args)


def shaped(shape, dtype=F32):
    return jax.ShapeDtypeStruct(shape, dtype)


def both_ways(to_low, to_high, axis, distance=1):
    count = lax.axis_size(axis)
    up = [(i, i + distance) for i in range(count - distance)]
    down = [(j, i) for i, j in up]
    return lax.ppermute(to_high, axis, up), lax.ppermute(to_low, axis, down)


def two_away(to_low, to_high):
    count = lax.axis_size("gz")
    if count != 4:
        return both_ways(to_low, to_high, "gz", 2)
    came = lax.ppermute(to_low, "gz", [(i, (i + 2) % 4) for i in range(4)])
    return came, came


def shards(density, uptake, brick_values, brick_ids, slot_counts):
    nz, nx = lax.axis_size("gz"), lax.axis_size("xy")
    info = jnp.stack([lax.axis_index("gz"), lax.axis_index("xy")]).astype(jnp.int32)
    scratch = pltpu.VMEM
    half = lambda *shape: shaped(shape, BF16)
    full = lambda *shape: shaped(shape, F32)

    own, r1, r2, zl, zh, z2l, z2h, uxl, uxh = call(
        lambda *refs: first_kernel(2 * nx, nz, *refs),
        [
            half(BLOCK, 384), full(16, 16, 512), full(64, 256), half(Z_ROWS, 384), half(Z_ROWS, 384),
            half(32, 256), half(32, 256), half(64, 1024), half(64, 1024),
        ],
        [
            scratch((8, 32, 128), F32), scratch((8, 16, 16, 128), F32), scratch((4, 16, 128), F32),
            scratch((4, 8, 8, 128), F32), scratch((SLOTS, BRICK), F32),
        ],
        3,
        (info, brick_ids, slot_counts, brick_values, uptake),
    )
    zl, zh = both_ways(zl, zh, "gz")
    z2l, z2h = two_away(z2l, z2h)
    q1, q2, xl, xh = call(
        rates_window_kernel,
        [full(24, 24, 512), full(32, 8, 256), half(X_ROWS, 384), half(X_ROWS, 384)],
        [],
        0,
        (own, r1, r2, uxl, uxh, zl, zh, z2l, z2h),
    )
    xl, xh = both_ways(xl, xh, "xy")

    supply, c1, mzl, mzh, pxl, pxh, v2, gg = call(
        lambda *refs: pre_kernel(nz, nx, *refs),
        [
            full(C, C, 1024),
            full(20, 24, 512),
            half(288, 1024),
            half(288, 1024),
            half(176, 1024),
            half(176, 1024),
            full(36, 40, 1024),
            full(36, 40, 1024),
        ],
        [
            scratch((42, 40, 1024), F32),
            scratch((42, 40, 1024), F32),
            scratch((36, 40, 1024), F32),
            scratch((36, 40, 1024), F32),
            scratch((1024, 1152), BF16),
            scratch((8, 40, 128), F32),
            scratch((8, 20, 24, 128), F32),
            scratch((80, 1024), F32),
            scratch((80, 1024), F32),
            pltpu.SemaphoreType.DMA((2,)),
        ],
        1,
        (info, density, uptake, own, zl, zh, xl, xh),
        [VMEM] * 6 + [ANY] * 2,
    )
    mzl, mzh = both_ways(mzl, mzh, "gz")
    f1, mxl, mxh = call(
        merge_kernel,
        [full(24, 24, 512), half(144, 512), half(144, 512)],
        [],
        0,
        (c1, mzl, mzh),
    )
    mxl, mxh = both_ways(mxl, mxh, "xy")
    pxl, pxh = call(
        sides_kernel,
        [half(240, 1024), half(240, 1024)],
        [],
        0,
        (pxl, pxh, mzl, mzh, q2),
    )
    vxl, vxh = both_ways(pxl, pxh, "xy")
    f1, pxl, pxh = lax.optimization_barrier((f1, pxl, pxh))
    f1, g1, v1, g2, g2l, g2h = call(
        lambda *refs: middle_kernel(nz, nx, *refs),
        [full(24, 24, 512), full(24, 24, 512), full(24, 24, 512), full(64, 256), full(32, 256), full(32, 256)],
        [scratch((24, 24, 512), F32), scratch((24, 24, 512), F32), scratch((4, 16, 128), F32), scratch((4, 8, 8, 128), F32)],
        1,
        (info, f1, q1, xl, xh, mxl, mxh),
    )
    low, high = both_ways(g2, g2, "gz")
    low2, high2 = two_away(g2l, g2h)
    own2, near, fl, fh = call(
        source_window_kernel,
        [full(32, 8, 256), half(256, 256), half(256, 256), half(256, 256)],
        [],
        0,
        (g2, low, high, low2, high2, q2),
    )
    nl, nh = both_ways(near, near, "xy")
    fl, fh = both_ways(fl, fh, "xy", 2)
    window2 = scratch((32, 32, 256), F32)
    window1 = scratch((24, 24, 512), F32)
    (concentration,) = call(
        lambda *refs: back_kernel(nz, nx, *refs),
        [full(C, C, 1024)],
        [
            window2, window2, window2, window2, window2,
            scratch((8, 48, 128), F32),
            scratch((2, 16, 16, 128), F32),
            scratch((2, 16, 16, 128), F32),
            window1, window1,
            scratch((208, 1024), F32),
            scratch((208, 1024), F32),
            scratch((34, 40, 1024), F32),
            scratch((18, 24, 1024), F32),
            scratch((36, 40, 1024), F32),
            scratch((36, 40, 1024), F32),
            scratch((C, C, 1024), F32),
            scratch((16, 1024), F32),
            scratch((16, 1024), F32),
            pltpu.SemaphoreType.DMA((3,)),
        ],
        1,
        (info, f1, g1, v1, mzl, mzh, vxl, vxh, own2, nl, nh, fl, fh, q2, v2, gg, supply),
        in_hbm=3,
    )
    return supply, concentration


def solution(mesh):
    return jax.shard_map(
        shards,
        mesh=mesh,
        in_specs=(
            P("gz", "xy", None),
            P("gz", "xy", None),
            P(("gz", "xy"), None),
            P(("gz", "xy")),
            P(("gz", "xy"), None),
        ),
        out_specs=(P("gz", "xy", None), P("gz", "xy", None)),
        check_vma=False,
    )
```

```python
import jax
import jax.numpy as jnp
from jax import lax
from jax.experimental import pallas as pl
from jax.experimental.pallas import tpu as pltpu
from jax.sharding import PartitionSpec as P

EDGE = 16
CAP = 8
BRICK = 4096
SLOTS = 72
KAPPA = 32.0
OMEGA = 0.8
KEEP = 1.0 - OMEGA

C = 32
NT = 8
F32 = jnp.float32
BF16 = jnp.bfloat16


def spread(level):
    return KAPPA / 4.0**level


def shifted(values, distance, axis):
    return pltpu.roll(values, distance % values.shape[axis], axis)


def iota(shape, dim):
    return lax.broadcasted_iota(jnp.int32, shape, dim)


def lanes(t):
    return slice(t * 128, (t + 1) * 128)


def plane(ref, p):
    count = ref.shape[2] // 128
    rows = ref.shape[1]
    lane = iota((rows, 128), 1)
    before, here = None, ref[p, :, lanes(0)]
    for t in range(count):
        after = ref[p, :, lanes(t + 1)] if t + 1 < count else None
        low = jnp.where(lane == 127, 0.0 if before is None else before, here)
        high = jnp.where(lane == 0, 0.0 if after is None else after, here)
        sums = shifted(low, 1, 1) + shifted(high, -1, 1)
        sums = sums + (shifted(here, 1, 0) + shifted(here, -1, 0))
        sums = sums + (ref[p - 1, :, lanes(t)] + ref[p + 1, :, lanes(t)])
        yield t, here, sums
        before, here = here, after


def loop(start, stop, body, unroll=1):
    def step(i, carry):
        body(i)
        return carry

    lax.fori_loop(start, stop, step, 0, unroll=unroll)


def split_dot(a, b):
    high = a.astype(BF16)
    low = (a - high.astype(F32)).astype(BF16)
    return jnp.dot(high, b, preferred_element_type=F32) + jnp.dot(low, b, preferred_element_type=F32)


def pooling():
    return jnp.where(iota((256, 128), 0) // 2 == iota((256, 128), 1), 0.125, 0.0).astype(BF16)


def doubling():
    return jnp.where(iota((128, 256), 1) // 2 == iota((128, 256), 0), 1.0, 0.0).astype(BF16)


def halve_rows(values, rs, t):
    rows = values.shape[0]
    rs[t, 0:rows, :] = values
    return rs[t, pl.ds(0, rows // 2, stride=2), :] + rs[t, pl.ds(1, rows // 2, stride=2), :]


def halve_lanes(xp, planes, rows):
    matrix = pooling()
    tiles = []
    for t in range(0, xp.shape[0], 2):
        pair = jnp.concatenate([xp[t].reshape(planes * rows, 128), xp[t + 1].reshape(planes * rows, 128)], axis=1)
        tiles.append(split_dot(pair, matrix).reshape(planes, rows, 128))
    return tiles


def inside(shape, dim, first, wrap, index, size, count):
    place = iota(shape, dim) + first
    if wrap is not None:
        place = jnp.where(place < wrap, place, place - shape[dim])
    place = place + index * size
    return (place >= 0) & (place < count * size)


BLOCK = 272
Z_ROWS = BLOCK + 5 * 64
X_ROWS = BLOCK + 3 * 80 + 128


def z_part(t):
    return slice(BLOCK + 64 * (t // 3), BLOCK + 64 * (t // 3) + 64), lanes(t % 3)


def x_part(t):
    return slice(BLOCK + 80 * (t // 3), BLOCK + 80 * (t // 3) + 80), lanes(t % 3)


def transposed_bricks(bricks_x, ids, counts, bricks, xs, targets):
    xs[...] = bricks[...].astype(F32)
    row = iota((1, 8, 128), 1)
    group = iota((1, 8, 128), 2) // 16
    group16 = iota((16, 128), 1) // 16
    per_y = 64

    def block(j, out, part):
        start = pl.multiple_of(j * 8, 8)
        x = jnp.stack([xs[pl.ds(start, 8), lanes(k)] for k in range(32)])
        for s in (4, 2, 1):
            up = shifted(shifted(x, -s, 1), 16 * s, 2)
            down = shifted(shifted(x, s, 1), -16 * s, 2)
            row_bit = (row // s) % 2
            group_bit = (group // s) % 2
            x = jnp.where(row_bit == group_bit, x, jnp.where(row_bit == 0, up, down))
        x = jnp.where(group < counts[0, j], x, 0.0)
        out[0:256, part] = x.reshape(256, 128).astype(BF16)
        names = jnp.zeros((16, 128), jnp.int32)
        for e in range(CAP):
            number = ids[j * 8 + e]
            by = lax.rem(number, per_y)
            rest = lax.div(number, per_y)
            bx = lax.rem(rest, 2)
            bz = lax.rem(lax.div(rest, bricks_x), 2)
            names = jnp.where(group16 == e, (bz * 2 + bx) * per_y + by, names)
        out[256:272, part] = names.astype(F32).astype(BF16)

    for i, out in enumerate(targets):
        for d in range(3):
            block(3 * i + d, out, lanes(d))


def first_kernel(bricks_x, nz, info, ids, counts, bricks, uptake, own, r1, r2, zl, zh, z2l, z2h, xl, xh, rs, xp, rs1, xp1, xs):
    transposed_bricks(bricks_x, ids, counts, bricks, xs, (zl, own, zh))

    def pair(m):
        for t in range(NT):
            both = uptake[2 * m, :, lanes(t)] + uptake[2 * m + 1, :, lanes(t)]
            xp[t, m] = halve_rows(both, rs, t)

    loop(0, 16, pair)
    for t, tile in enumerate(halve_lanes(xp, 16, 16)):
        r1[:, :, lanes(t)] = tile

    def pair1(m):
        for t in range(4):
            both = r1[2 * m, :, lanes(t)] + r1[2 * m + 1, :, lanes(t)]
            xp1[t, m] = halve_rows(both, rs1, t)

    loop(0, 8, pair1)
    coarse = []
    for t, tile in enumerate(halve_lanes(xp1, 8, 8)):
        r2[:, lanes(t)] = tile.reshape(64, 128)
        coarse.append(tile.reshape(64, 128).astype(BF16))
    low, high = far_along_z(nz, info[0], r2[0:32, :], r2[32:64, :])
    z2l[...] = low.astype(BF16)
    z2h[...] = high.astype(BF16)
    for ref, u, r in ((zl, slice(0, 2), slice(0, 4)), (zh, slice(30, 32), slice(12, 16))):
        for t in range(8):
            ref[z_part(t)] = uptake[u, :, lanes(t)].reshape(64, 128).astype(BF16)
        for t in range(4):
            ref[z_part(8 + t)] = r1[r, :, lanes(t)].reshape(64, 128).astype(BF16)
        for t in range(2):
            ref[z_part(12 + t)] = coarse[t]
        ref[z_part(14)] = jnp.zeros((64, 128), BF16)

    sub = iota((8, 1024), 0)

    def columns(i):
        lows, highs = [], []
        for j in range(2):
            low, high = jnp.zeros((8, 1024), F32), jnp.zeros((8, 1024), F32)
            for n in range(4):
                z = 8 * i + 4 * j + n
                low = jnp.where(sub // 2 == n, shifted(uptake[z, 0:8, :], 2 * n, 0), low)
                high = jnp.where(sub // 2 == n, shifted(uptake[z, 24:32, :], 2 * n + 2, 0), high)
            lows.append(low)
            highs.append(high)
        rows = pl.ds(pl.multiple_of(16 * i, 16), 16)
        xl[rows, :] = jnp.concatenate(lows, axis=0).astype(BF16)
        xh[rows, :] = jnp.concatenate(highs, axis=0).astype(BF16)

    loop(0, 4, columns)


def far_along_z(nz, iz, to_low, to_high):
    if nz != 4:
        return to_low, to_high
    one = jnp.where(iz < 2, to_high, to_low)
    return one, one


def halves(sub, first, second):
    return jnp.where(sub < 4, first, shifted(second, 4, 1))


def uppers(sub, first, second):
    return jnp.where(sub < 4, shifted(first, 4, 1), second)


def far_messages(window):
    planes, _, width = window.shape
    pairs = window.reshape(planes // 2, 2, 8, width)
    sub = iota((planes // 2, 8, width), 1)
    size = (planes * 4, width)
    return halves(sub, pairs[:, 0], pairs[:, 1]).reshape(size), uppers(sub, pairs[:, 0], pairs[:, 1]).reshape(size)


def far_tile(from_low, from_high):
    width = from_low.shape[-1]
    low, high = from_low.reshape(-1, 8, width), from_high.reshape(-1, 8, width)
    sub = iota(low.shape, 1)
    even = jnp.where(sub < 4, high, shifted(low, 4, 1))
    odd = jnp.where(sub < 4, shifted(high, 4, 1), low)
    return jnp.stack([even, odd], axis=1).reshape(-1, 8, width)


def rates_window_kernel(own, r1, r2, uxl, uxh, zl, zh, z2l, z2h, q1, q2, xl, xh):
    for ref, d in ((xl, 0), (xh, 2)):
        for n, src in enumerate((own, zl, zh)):
            ref[0:BLOCK, lanes(n)] = src[0:BLOCK, lanes(d)]
    sub = iota((16, 128), 0)
    for t in range(8):
        rows, part = x_part(t)
        rows = rows.start
        xl[rows : rows + 64, part] = uxl[:, lanes(t)]
        xh[rows : rows + 64, part] = uxh[:, lanes(t)]
        both = [ref[z_part(t)].astype(F32) for ref in (zl, zh)]
        planes = [both[0][0:32], both[0][32:64], both[1][0:32], both[1][32:64]]
        to_low, to_high = jnp.zeros((16, 128), F32), jnp.zeros((16, 128), F32)
        for n, p in enumerate(planes):
            here = sub // 2 == n
            to_low = jnp.where(here, shifted(p[0:16], 2 * n, 0), to_low)
            to_high = jnp.where(here, shifted(p[16:32], 2 * n + 2, 0), to_high)
        xl[rows + 64 : rows + 80, part] = to_low.astype(BF16)
        xh[rows + 64 : rows + 80, part] = to_high.astype(BF16)
    rows, part = x_part(8)
    for ref in (xl, xh):
        ref[rows, part] = jnp.zeros((80, 128), BF16)

    low = jnp.concatenate([zl[z_part(8 + t)].astype(F32) for t in range(6)], axis=1)
    high = jnp.concatenate([zh[z_part(8 + t)].astype(F32) for t in range(6)], axis=1)
    q1[0:4, 0:16, :] = low[:, 0:512].reshape(4, 16, 512)
    q1[4:20, 0:16, :] = r1[...]
    q1[20:24, 0:16, :] = high[:, 0:512].reshape(4, 16, 512)
    q1[:, 16:24, :] = jnp.zeros((24, 8, 512), F32)
    sub1 = iota((12, 8, 512), 1)
    first = q1[:, 0:8, :].reshape(12, 2, 8, 512)
    last = q1[:, 8:16, :].reshape(12, 2, 8, 512)
    to_low = halves(sub1, first[:, 0], first[:, 1]).reshape(96, 512).astype(BF16)
    to_high = uppers(sub1, last[:, 0], last[:, 1]).reshape(96, 512).astype(BF16)
    start = X_ROWS - 128
    for ref, message in ((xl, to_low), (xh, to_high)):
        for t in range(3):
            ref[start : start + 96, lanes(t)] = message[:, lanes(t)]
            ref[start + 96 : start + 128, lanes(t)] = message[32 * t : 32 * t + 32, lanes(3)]
    q2[...] = window_planes(r2[...], low[:, 512:768], high[:, 512:768], z2l[...].astype(F32), z2h[...].astype(F32))


def rates_from_x(ref):
    start = X_ROWS - 128
    last = jnp.concatenate([ref[start + 96 : start + 128, lanes(t)] for t in range(3)], axis=0)
    tiles = [ref[start : start + 96, lanes(t)] for t in range(3)] + [last]
    return jnp.concatenate([a.astype(F32) for a in tiles], axis=1).reshape(12, 8, 512)


def window_planes(own, low, high, low2, high2):
    parts = (low2, low, own, high, high2)
    return jnp.concatenate([a.reshape(-1, 8, 256) for a in parts], axis=0)


def source_window_kernel(own, low, high, low2, high2, q2, window, near, fl, fh):
    planes = window_planes(own[...], low[...], high[...], low2[...], high2[...])
    window[...] = planes
    near[...] = planes.reshape(256, 256).astype(BF16)
    for i, values in enumerate((planes, q2[...])):
        to_low, to_high = far_messages(values)
        fl[128 * i : 128 * i + 128, :] = to_low.astype(BF16)
        fh[128 * i : 128 * i + 128, :] = to_high.astype(BF16)


def pre_kernel(
    nz, nx, info, density, uptake, own, zl, zh, xl, xh,
    supply, c1, mzl, mzh, pxl, pxh, v_out, g_out,
    va, vb, dd, gg, hot, rs, xp, usl, ush, sems,
):
    iz, ix = info[0], info[1]
    k = spread(0)
    base = 1.0 + 6.0 * k
    O = 5
    Q = 2

    for p in (0, 1, 2, 3, 4, 37, 38, 39, 40, 41):
        va[p] = jnp.zeros((40, 1024), F32)
    for p in (2, 3, 38, 39):
        vb[p] = jnp.zeros((40, 1024), F32)

    sub8 = iota((8, 1024), 0)

    for t in range(NT):
        usl[:, lanes(t)] = xl[x_part(t)].astype(F32)
        ush[:, lanes(t)] = xh[x_part(t)].astype(F32)

    def set_plane(q, rates, low, high, valid_z):
        gz = jnp.where(valid_z, OMEGA, 0.0)
        d = rates + base
        dd[q, 0:32, :] = d
        gg[q, 0:32, :] = gz / d
        d = jnp.where(sub8 < 2, high, jnp.where(sub8 >= 6, low, 0.0)) + base
        dd[q, 32:40, :] = d
        omega = jnp.where(sub8 < 2, jnp.where(ix < nx - 1, gz, 0.0), jnp.where(sub8 >= 6, jnp.where(ix > 0, gz, 0.0), 0.0))
        gg[q, 32:40, :] = omega / d

    def own_planes(i):
        rows = pl.ds(pl.multiple_of(8 * i, 8), 8)
        low, high = usl[rows, :], ush[rows, :]
        for n in range(4):
            z = 4 * i + n
            va[z + O, 0:32, :] = density[z]
            va[z + O, 32:40, :] = jnp.zeros((8, 1024), F32)
            set_plane(z + Q, uptake[z], shifted(low, 6 - 2 * n, 0), shifted(high, -2 * n, 0), True)

    loop(0, C // 4, own_planes)
    low, high = usl[64:72, :], ush[64:72, :]
    for n in range(4):
        ref = zl if n < 2 else zh
        rates = [ref[z_part(t)].astype(F32)[32 * (n % 2) : 32 * (n % 2) + 32] for t in range(NT)]
        rates = jnp.concatenate(rates, axis=1)
        exists = iz > 0 if n < 2 else iz < nz - 1
        set_plane(n if n < 2 else 32 + n, rates, shifted(low, 6 - 2 * n, 0), shifted(high, -2 * n, 0), exists)

    blocks = [(ref, lanes(1)) for ref in (own, zl, zh)] + [(ref, lanes(n)) for ref in (xl, xh) for n in range(3)]
    lane = iota((1, 128), 1)
    at_y = iota((1024, 128), 0)
    tiles = []
    for i, (ref, part) in enumerate(blocks):
        name = ref[256:272, part].astype(F32).astype(jnp.int32)[0:1]
        tiles.append(lax.shift_right_logical(name, 6))
        y = (name & 63) * 16 + (lane & 15)
        hot[:, lanes(i)] = jnp.where(at_y == y, 1.0, 0.0).astype(BF16)
    for tile in range(4):
        bz, bx = tile // 2, tile % 2
        left = jnp.concatenate(
            [jnp.where(tiles[i] == tile, ref[0:256, part].astype(F32), 0.0).astype(BF16) for i, (ref, part) in enumerate(blocks)],
            axis=1,
        )
        for n in range(4):
            cols = slice(n * 256, (n + 1) * 256)
            part = lax.dot_general(left, hot[cols, :], (((1,), (1,)), ((), ())), preferred_element_type=F32)
            zs, xs = slice(16 * bz, 16 * bz + 16), slice(16 * bx, 16 * bx + 16)
            supply[zs, xs, cols] = density[zs, xs, cols] + part.reshape(16, 16, 256)

    def sweep(src, dst, z, sourced):
        for t, here, sums in plane(src, z + O):
            inner = k * sums
            g = gg[z + Q, :, lanes(t)]
            if sourced:
                body = inner[0:32] + supply[z, :, lanes(t)]
                dst[z + O, 0:32, lanes(t)] = KEEP * here[0:32] + g[0:32] * body
                dst[z + O, 32:40, lanes(t)] = KEEP * here[32:40] + g[32:40] * inner[32:40]
            else:
                dst[z + O, :, lanes(t)] = KEEP * here + g * inner

    def halo_planes(src, dst, width):
        def step(i):
            sweep(src, dst, jnp.where(i < width, i - width, i - width + C), False)

        loop(0, 2 * width, step)

    loop(0, C, lambda z: sweep(va, vb, z, True), 2)
    halo_planes(va, vb, 1)
    loop(0, C, lambda z: sweep(vb, va, z, True), 2)
    halo_planes(vb, va, 2)

    v_copy = pltpu.make_async_copy(va.at[3:39], v_out, sems.at[0])
    g_copy = pltpu.make_async_copy(gg, g_out, sems.at[1])
    v_copy.start()
    g_copy.start()

    def residual(z, sourced, edge):
        for t, here, sums in plane(va, z + O):
            r = k * sums
            if not edge:
                r = r - dd[z + Q, :, lanes(t)] * here
            if sourced:
                r = jnp.concatenate([r[0:32] + supply[z, :, lanes(t)], r[32:40]], axis=0)
            yield t, r

    def coarse(m, sourced):
        both = zip(residual(2 * m - 4, sourced, False), residual(2 * m - 3, sourced, False))
        for (t, first), (_, second) in both:
            xp[t, m, 0:20, :] = halve_rows(first + second, rs, t)

    loop(2, 18, lambda m: coarse(m, True))
    loop(0, 2, lambda i: coarse(1 + 17 * i, False))

    def outer(i):
        for t, r in residual(jnp.where(i == 0, -3, 34), False, True):
            xp[t, 19 * i, 0:20, :] = halve_rows(r, rs, t)

    loop(0, 2, outer)

    sub = iota((20, 8, 128), 1)
    for t, tile in enumerate(halve_lanes(xp, 20, 24)):
        last = tile[:, 16:24]
        last = jnp.where(sub < 2, last, jnp.where(sub >= 6, shifted(last, 4, 1), 0.0))
        c1[:, 0:16, lanes(t)] = tile[:, 0:16]
        c1[:, 16:24, lanes(t)] = last

    empty = jnp.zeros((1, 8, 1024), F32)
    blank = jnp.zeros((8, 1024), F32)
    for ref, planes, values, z in ((mzl, slice(0, 6), va[3:7], 0), (mzh, slice(14, 20), va[35:39], 31)):
        source = c1[planes].reshape(144, 512)
        ref[0:80, 0:512] = source[0:80].astype(BF16)
        ref[0:64, 512:1024] = source[80:144].astype(BF16)
        ref[64:80, 512:1024] = jnp.zeros((16, 512), BF16)
        level0 = jnp.concatenate([values, jnp.concatenate([supply[z : z + 1], empty], axis=1)], axis=0)
        ref[80:288, :] = jnp.concatenate([level0.reshape(200, 1024), blank], axis=0).astype(BF16)

    def sides(i):
        lows, highs = [], []
        for j in range(2):
            p = 4 * i + 2 * j + 3
            lows.append(pack_low(va[p], va[p + 1]))
            highs.append(pack_high(va[p], va[p + 1]))
        rows = pl.ds(pl.multiple_of(16 * i, 16), 16)
        pxl[rows, :] = jnp.concatenate(lows, axis=0).astype(BF16)
        pxh[rows, :] = jnp.concatenate(highs, axis=0).astype(BF16)

    loop(0, 9, sides)

    def sources(i):
        lows, highs = [], []
        for j in range(2):
            low, high = jnp.zeros((8, 1024), F32), jnp.zeros((8, 1024), F32)
            for n in range(8):
                z = 16 * i + 8 * j + n
                low = jnp.where(sub8 == n, shifted(supply[z, 0:8, :], n, 0), low)
                high = jnp.where(sub8 == n, shifted(supply[z, 24:32, :], n + 1, 0), high)
            lows.append(low)
            highs.append(high)
        rows = pl.ds(pl.multiple_of(16 * i + 144, 16), 16)
        pxl[rows, :] = jnp.concatenate(lows, axis=0).astype(BF16)
        pxh[rows, :] = jnp.concatenate(highs, axis=0).astype(BF16)

    loop(0, 2, sources)
    v_copy.wait()
    g_copy.wait()


def outer_rows(sub):
    return (sub < 2) | (sub >= 6)


def pack_pair(sub, a, b):
    return jnp.where(outer_rows(sub), a, shifted(b, 4, 0))


def pack_low(first, second):
    sub = iota((8, 1024), 0)
    a, b = [jnp.where(sub < 4, v[0:8], v[32:40]) for v in (first, second)]
    return pack_pair(sub, a, b)


def pack_high(first, second):
    sub = iota((8, 1024), 0)
    a, b = [jnp.where(sub >= 4, v[24:32], v[32:40]) for v in (first, second)]
    return pack_pair(sub, a, b)


def sides_kernel(pxl, pxh, mzl, mzh, q2, out_l, out_h):
    for ref, out in ((pxl, out_l), (pxh, out_h)):
        out[0:176, :] = ref[...]
        for n in range(4):
            out[176:240, n * 256 : n * 256 + 256] = q2[8 * n : 8 * n + 8].reshape(64, 256).astype(BF16)
    for message, start in ((mzl, 0), (mzh, 128)):
        planes = message[80:240, :].astype(F32).reshape(4, 40, 1024)
        rows = slice(start, start + 16)
        for ref, out, pack in ((pxl, out_l, pack_low), (pxh, out_h, pack_high)):
            added = [pack(planes[2 * i], planes[2 * i + 1]) for i in range(2)]
            out[rows, :] = (ref[rows, :].astype(F32) + jnp.concatenate(added, axis=0)).astype(BF16)


def in_three(sub, tiles, free, turns):
    spare = (sub == free) | (sub == free + 1)
    last = tiles[:, 3]
    parts = [jnp.where(spare, shifted(last, turn, 1), tiles[:, i]) for i, turn in enumerate(turns)]
    return jnp.stack(parts, axis=1)


def out_of_three(sub, parts, free, turns):
    last = None
    for i, turn in enumerate(turns):
        back = shifted(parts[:, i], -turn, 1)
        home = (free - turn) % 8
        here = (sub == home) | (sub == home + 1)
        last = jnp.where(here, back, 0.0 if last is None else last)
    return jnp.stack([parts[:, 0], parts[:, 1], parts[:, 2], last], axis=1)


HIGH_PACK = (2, (-2, 4, 2))
LOW_PACK = (4, (-2, 4, 2))


def merge_kernel(c1, mzl, mzh, f1, mxl, mxh):
    zeros = jnp.zeros((24, 512), F32)
    for p in (0, 1, 22, 23):
        f1[p] = zeros
    f1[2:22] = c1[...]
    for ref, planes in ((mzl, slice(0, 6)), (mzh, slice(18, 24))):
        parts = [ref[0:80, 0:512].astype(F32), ref[0:64, 512:1024].astype(F32)]
        f1[planes] = f1[planes] + jnp.concatenate(parts, axis=0).reshape(6, 24, 512)
    sub = iota((6, 8, 512), 1)
    first, last, halo = [f1[:, 8 * n : 8 * n + 8].reshape(6, 4, 8, 512) for n in range(3)]
    sub4 = iota((6, 4, 8, 512), 2)
    to_high = in_three(sub, jnp.where(sub4 >= 4, last, halo), *HIGH_PACK)
    to_low = in_three(sub, jnp.where(sub4 >= 4, halo, first), *LOW_PACK)
    mxh[...] = to_high.reshape(144, 512).astype(BF16)
    mxl[...] = to_low.reshape(144, 512).astype(BF16)


def middle_kernel(nz, nx, info, f0, q_in, xl, xh, mxl, mxh, f1, g1, v1, g2, g2l, g2h, q0, va, rs, xp):
    iz, ix = info[0], info[1]
    k = spread(1)
    base = 1.0 + 6.0 * k
    sub6 = iota((6, 8, 512), 1)
    low = out_of_three(sub6, mxl[...].astype(F32).reshape(6, 3, 8, 512), *HIGH_PACK).reshape(24, 8, 512)
    high = out_of_three(sub6, mxh[...].astype(F32).reshape(6, 3, 8, 512), *LOW_PACK).reshape(24, 8, 512)
    sub = iota((24, 8, 512), 1)
    f1[:, 0:8] = f0[:, 0:8] + jnp.where(sub < 2, low, 0.0)
    f1[:, 8:16] = f0[:, 8:16] + jnp.where(sub >= 6, high, 0.0)
    f1[:, 16:24] = f0[:, 16:24] + jnp.where(sub >= 4, low, high)
    low, high = rates_from_x(xl), rates_from_x(xh)
    sub12 = iota((12, 8, 512), 1)
    even = jnp.where(sub12 >= 4, shifted(low, 4, 1), high)
    odd = jnp.where(sub12 >= 4, low, shifted(high, 4, 1))
    q0[:, 0:16] = q_in[:, 0:16]
    q0[:, 16:24] = jnp.stack([even, odd], axis=1).reshape(24, 8, 512)
    shape = (24, 24, 128)
    valid = inside(shape, 0, -4, None, iz, 16, nz) & inside(shape, 1, 0, 20, ix, 16, nx)
    for t in range(4):
        g = jnp.where(valid, OMEGA, 0.0) / (q0[:, :, lanes(t)] + base)
        g1[:, :, lanes(t)] = g
        va[:, :, lanes(t)] = g * f1[:, :, lanes(t)]
    v1[0] = va[0]
    v1[23] = va[23]

    def sweep(p):
        for t, here, sums in plane(va, p):
            v1[p, :, lanes(t)] = KEEP * here + g1[p, :, lanes(t)] * (f1[p, :, lanes(t)] + k * sums)

    loop(1, 23, sweep, 2)

    def residual(p):
        for t, here, sums in plane(v1, p):
            yield t, f1[p, :, lanes(t)] + k * sums - (q0[p, :, lanes(t)] + base) * here

    def coarse(m):
        for (t, first), (_, second) in zip(residual(2 * m + 4), residual(2 * m + 5)):
            xp[t, m] = halve_rows((first + second)[0:16], rs, t)

    loop(0, 8, coarse)
    for t, tile in enumerate(halve_lanes(xp, 8, 8)):
        g2[:, lanes(t)] = tile.reshape(64, 128)
        low, high = far_along_z(nz, iz, tile[0:4].reshape(32, 128), tile[4:8].reshape(32, 128))
        g2l[:, lanes(t)] = low
        g2h[:, lanes(t)] = high


def back_kernel(
    nz, nx, info, f1, g1, v1, vzl, vzh, vxl, vxh, own2, n2l, n2h, m2l, m2h, q_own, v_in, g_in, s_in,
    out,
    f2, q2, h2, a2, b2, rs, xp, xpr, wa, w1, zsl, zsh, vb, ws,
    v2, gg, supply, fsl, fsh, sems,
):
    iz, ix = info[0], info[1]
    matrix = doubling()
    level0 = [
        pltpu.make_async_copy(src, dst, sems.at[i])
        for i, (src, dst) in enumerate(((v_in, v2), (g_in, gg), (s_in, supply)))
    ]
    for copy in level0:
        copy.start()

    f2[:, 0:8, :] = own2[...]
    f2[:, 8:16, :] = n2h[...].astype(F32).reshape(32, 8, 256)
    f2[:, 16:24, :] = far_tile(m2l[0:128, :].astype(F32), m2h[0:128, :].astype(F32))
    f2[:, 24:32, :] = n2l[...].astype(F32).reshape(32, 8, 256)
    q2[:, 0:8, :] = q_own[...]
    q2[:, 16:24, :] = far_tile(m2l[128:256, :].astype(F32), m2h[128:256, :].astype(F32))
    for ref, rows in ((vxh, slice(8, 16)), (vxl, slice(24, 32))):
        for n in range(4):
            q2[8 * n : 8 * n + 8, rows, :] = ref[176:240, n * 256 : n * 256 + 256].astype(F32).reshape(8, 8, 256)

    k = spread(2)
    base = 1.0 + 6.0 * k
    shape = (32, 32, 128)
    valid = inside(shape, 0, -12, None, iz, 8, nz) & inside(shape, 1, 0, 20, ix, 8, nx)
    for t in range(2):
        g = jnp.where(valid, OMEGA, 0.0) / (q2[:, :, lanes(t)] + base)
        h2[:, :, lanes(t)] = g
        a2[:, :, lanes(t)] = g * f2[:, :, lanes(t)]
    b2[0] = a2[0]
    b2[31] = a2[31]

    def sweep2(src, dst):
        def body(p):
            for t, here, sums in plane(src, p):
                dst[p, :, lanes(t)] = KEEP * here + h2[p, :, lanes(t)] * (f2[p, :, lanes(t)] + k * sums)

        return body

    loop(1, 31, sweep2(a2, b2), 2)

    def coarse(m):
        total, rates = [0.0, 0.0], [0.0, 0.0]
        for j in range(2):
            p = 2 * m + j
            for t, here, sums in plane(b2, p):
                r = f2[p, :, lanes(t)] + k * sums - (q2[p, :, lanes(t)] + base) * here
                total[t] = total[t] + r
                rates[t] = rates[t] + q2[p, :, lanes(t)]
        for t in range(2):
            xp[t, m] = halve_rows(total[t], rs, t)
            xpr[t, m] = halve_rows(rates[t], rs, t + 2)

    for t in range(2):
        for m in (0, 15):
            xp[t, m] = jnp.zeros((16, 128), F32)
            xpr[t, m] = jnp.zeros((16, 128), F32)
    loop(1, 15, coarse)

    shape = (16, 16, 128)
    valid = inside(shape, 0, -6, None, iz, 4, nz) & inside(shape, 1, 0, 10, ix, 4, nx)
    k3 = spread(3)
    (source,) = halve_lanes(xp, 16, 16)
    (rates,) = halve_lanes(xpr, 16, 16)
    g = jnp.where(valid, OMEGA, 0.0) / (rates + (1.0 + 6.0 * k3))
    v = g * source
    lane = iota(shape, 2)
    for repeat in range(3):
        edge = jnp.zeros((1, 16, 128), F32)
        sums = jnp.concatenate([v[1:], edge], axis=0) + jnp.concatenate([edge, v[:-1]], axis=0)
        sums = sums + shifted(v, 1, 1) + shifted(v, -1, 1)
        sums = sums + jnp.where(lane == 0, 0.0, shifted(v, 1, 2)) + jnp.where(lane == 127, 0.0, shifted(v, -1, 2))
        v = KEEP * v + g * (source + k3 * sums)

    wide = split_dot(v[4:12].reshape(128, 128), matrix).reshape(8, 16, 256)
    for m in range(8):
        for t in range(2):
            part = wide[m, :, lanes(t)]
            rs[t, pl.ds(0, 16, stride=2), :] = part
            rs[t, pl.ds(1, 16, stride=2), :] = part
            for j in range(2):
                p = 8 + 2 * m + j
                b2[p, :, lanes(t)] = b2[p, :, lanes(t)] + rs[t, 0:32, :]
    loop(9, 23, sweep2(b2, a2), 2)
    loop(10, 22, sweep2(a2, b2), 2)

    w = b2[10:22]
    near, far = w[:, 8:16], w[:, 24:32]
    near = jnp.where(iota((12, 8, 256), 1) < 2, near, shifted(far, 4, 1))
    w = jnp.concatenate([w[:, 0:8], near], axis=1).reshape(192, 256)
    wide = [split_dot(w[:, lanes(t)], matrix) for t in range(2)]
    wide = jnp.concatenate(wide, axis=1).reshape(12, 16, 512)
    for m in range(12):
        for t in range(4):
            part = wide[m, :, lanes(t)]
            rs[t, pl.ds(0, 16, stride=2), :] = part
            rs[t, pl.ds(1, 16, stride=2), :] = part
            for j in range(2):
                p = 2 * m + j
                wa[p, :, lanes(t)] = v1[p, :, lanes(t)] + rs[t, 0:24, :]
    k1 = spread(1)

    def sweep1(src, dst):
        def body(p):
            for t, here, sums in plane(src, p):
                dst[p, :, lanes(t)] = KEEP * here + g1[p, :, lanes(t)] * (f1[p, :, lanes(t)] + k1 * sums)

        return body

    loop(2, 22, sweep1(wa, w1), 2)
    loop(3, 21, sweep1(w1, wa), 2)

    sub = iota((18, 8, 128), 1)
    for t in range(4):
        halo = wa[3:21, 16:24, lanes(t)]
        halo = jnp.where(sub < 2, halo, shifted(halo, 4, 1))
        w = jnp.concatenate([wa[3:21, 0:16, lanes(t)], halo], axis=1)
        ws[:, :, t * 256 : t * 256 + 256] = split_dot(w.reshape(432, 128), matrix).reshape(18, 24, 256)

    for copy in level0:
        copy.wait()
    zsl[...] = vzl[80:288, :].astype(F32)
    zsh[...] = vzh[80:288, :].astype(F32)
    for i in range(4):
        v2[i] = v2[i] + zsl[40 * i : 40 * i + 40, :]
        v2[32 + i] = v2[32 + i] + zsh[40 * i : 40 * i + 40, :]

    s8 = iota((8, 128), 0)

    outer = outer_rows(s8)

    def correct(i):
        rows = pl.ds(pl.multiple_of(16 * i, 16), 16)
        for t in range(NT):
            low = vxl[rows, lanes(t)].astype(F32)
            high = vxh[rows, lanes(t)].astype(F32)
            for n in range(2):
                part = ws[2 * i + n, :, lanes(t)]
                rs[t, pl.ds(0, 24, stride=2), :] = part
                rs[t, pl.ds(1, 24, stride=2), :] = part
                for j in range(2):
                    p = 4 * i + 2 * n + j
                    lo, hi = low[8 * n : 8 * n + 8], high[8 * n : 8 * n + 8]
                    if j:
                        lo, hi = shifted(lo, 4, 0), shifted(hi, 4, 0)
                    v2[p, 0:8, lanes(t)] = v2[p, 0:8, lanes(t)] + rs[t, 0:8, :] + jnp.where(s8 < 2, lo, 0.0)
                    v2[p, 8:24, lanes(t)] = v2[p, 8:24, lanes(t)] + rs[t, 8:24, :]
                    v2[p, 24:32, lanes(t)] = v2[p, 24:32, lanes(t)] + rs[t, 24:32, :] + jnp.where(s8 >= 6, hi, 0.0)
                    extra = jnp.where(outer, jnp.where(s8 >= 4, lo, hi), 0.0)
                    v2[p, 32:40, lanes(t)] = v2[p, 32:40, lanes(t)] + rs[t, 32:40, :] + extra

    loop(0, 9, correct)
    k0 = spread(0)

    def first(i):
        rows = pl.ds(pl.multiple_of(16 * i + 144, 16), 16)
        for t in range(NT):
            fsl[:, lanes(t)] = vxl[rows, lanes(t)].astype(F32)
            fsh[:, lanes(t)] = vxh[rows, lanes(t)].astype(F32)

        def step(j):
            z = 16 * i + j
            start = pl.multiple_of((j // 8) * 8, 8)
            turn = lax.rem(j, 8)
            for t, here, sums in plane(v2, z + 2):
                lo = pltpu.roll(fsl[pl.ds(start, 8), lanes(t)], 7 - turn, 0)
                hi = pltpu.roll(fsh[pl.ds(start, 8), lanes(t)], lax.rem(8 - turn, 8), 0)
                f = jnp.where(s8 == 7, lo, jnp.where(s8 == 0, hi, 0.0))
                g = gg[z + 2, :, lanes(t)]
                inner = k0 * sums
                vb[z + 1, 0:32, lanes(t)] = KEEP * here[0:32] + g[0:32] * (supply[z, :, lanes(t)] + inner[0:32])
                vb[z + 1, 32:40, lanes(t)] = KEEP * here[32:40] + g[32:40] * (f + inner[32:40])

        loop(0, 16, step, 2)

    loop(0, 2, first)
    for p, ref in ((1, zsl), (34, zsh)):
        for t, here, sums in plane(v2, p):
            g = gg[p, :, lanes(t)]
            vb[p - 1, :, lanes(t)] = KEEP * here + g * (ref[160:200, lanes(t)] + k0 * sums)

    def second(z):
        for t, here, sums in plane(vb, z + 1):
            g = gg[z + 2, 0:32, lanes(t)]
            out[z, :, lanes(t)] = KEEP * here[0:32] + g * (supply[z, :, lanes(t)] + k0 * sums[0:32])

    loop(0, C, second, 2)


VMEM = pl.BlockSpec(memory_space=pltpu.VMEM)
SMEM = pl.BlockSpec(memory_space=pltpu.SMEM)
ANY = pl.BlockSpec(memory_space=pl.ANY)


def call(kernel, outs, scratch, smem, args, out_specs=None, in_hbm=0):
    moved = sum(a.size * a.dtype.itemsize for a in list(args) + list(outs))
    return pl.pallas_call(
        kernel,
        out_shape=tuple(outs),
        in_specs=[SMEM] * smem + [VMEM] * (len(args) - smem - in_hbm) + [ANY] * in_hbm,
        out_specs=tuple(out_specs or [VMEM] * len(outs)),
        scratch_shapes=scratch,
        compiler_params=pltpu.CompilerParams(vmem_limit_bytes=58 * 2**20),
        cost_estimate=pl.CostEstimate(flops=20 * moved, bytes_accessed=moved, transcendentals=0),
    )(*args)


def shaped(shape, dtype=F32):
    return jax.ShapeDtypeStruct(shape, dtype)


def both_ways(to_low, to_high, axis, distance=1):
    count = lax.axis_size(axis)
    up = [(i, i + distance) for i in range(count - distance)]
    down = [(j, i) for i, j in up]
    return lax.ppermute(to_high, axis, up), lax.ppermute(to_low, axis, down)


def two_away(to_low, to_high):
    count = lax.axis_size("gz")
    if count != 4:
        return both_ways(to_low, to_high, "gz", 2)
    came = lax.ppermute(to_low, "gz", [(i, (i + 2) % 4) for i in range(4)])
    return came, came


def shards(density, uptake, brick_values, brick_ids, slot_counts):
    nz, nx = lax.axis_size("gz"), lax.axis_size("xy")
    info = jnp.stack([lax.axis_index("gz"), lax.axis_index("xy")]).astype(jnp.int32)
    scratch = pltpu.VMEM
    half = lambda *shape: shaped(shape, BF16)
    full = lambda *shape: shaped(shape, F32)

    own, r1, r2, zl, zh, z2l, z2h, uxl, uxh = call(
        lambda *refs: first_kernel(2 * nx, nz, *refs),
        [
            half(BLOCK, 384), full(16, 16, 512), full(64, 256), half(Z_ROWS, 384), half(Z_ROWS, 384),
            half(32, 256), half(32, 256), half(64, 1024), half(64, 1024),
        ],
        [
            scratch((8, 32, 128), F32), scratch((8, 16, 16, 128), F32), scratch((4, 16, 128), F32),
            scratch((4, 8, 8, 128), F32), scratch((SLOTS, BRICK), F32),
        ],
        3,
        (info, brick_ids, slot_counts, brick_values, uptake),
    )
    zl, zh = both_ways(zl, zh, "gz")
    z2l, z2h = two_away(z2l, z2h)
    q1, q2, xl, xh = call(
        rates_window_kernel,
        [full(24, 24, 512), full(32, 8, 256), half(X_ROWS, 384), half(X_ROWS, 384)],
        [],
        0,
        (own, r1, r2, uxl, uxh, zl, zh, z2l, z2h),
    )
    xl, xh = both_ways(xl, xh, "xy")

    supply, c1, mzl, mzh, pxl, pxh, v2, gg = call(
        lambda *refs: pre_kernel(nz, nx, *refs),
        [
            full(C, C, 1024),
            full(20, 24, 512),
            half(288, 1024),
            half(288, 1024),
            half(176, 1024),
            half(176, 1024),
            full(36, 40, 1024),
            full(36, 40, 1024),
        ],
        [
            scratch((42, 40, 1024), F32),
            scratch((42, 40, 1024), F32),
            scratch((36, 40, 1024), F32),
            scratch((36, 40, 1024), F32),
            scratch((1024, 1152), BF16),
            scratch((8, 40, 128), F32),
            scratch((8, 20, 24, 128), F32),
            scratch((80, 1024), F32),
            scratch((80, 1024), F32),
            pltpu.SemaphoreType.DMA((2,)),
        ],
        1,
        (info, density, uptake, own, zl, zh, xl, xh),
        [VMEM] * 6 + [ANY] * 2,
    )
    mzl, mzh = both_ways(mzl, mzh, "gz")
    f1, mxl, mxh = call(
        merge_kernel,
        [full(24, 24, 512), half(144, 512), half(144, 512)],
        [],
        0,
        (c1, mzl, mzh),
    )
    mxl, mxh = both_ways(mxl, mxh, "xy")
    pxl, pxh = call(
        sides_kernel,
        [half(240, 1024), half(240, 1024)],
        [],
        0,
        (pxl, pxh, mzl, mzh, q2),
    )
    vxl, vxh = both_ways(pxl, pxh, "xy")
    f1, pxl, pxh = lax.optimization_barrier((f1, pxl, pxh))
    f1, g1, v1, g2, g2l, g2h = call(
        lambda *refs: middle_kernel(nz, nx, *refs),
        [full(24, 24, 512), full(24, 24, 512), full(24, 24, 512), full(64, 256), full(32, 256), full(32, 256)],
        [scratch((24, 24, 512), F32), scratch((24, 24, 512), F32), scratch((4, 16, 128), F32), scratch((4, 8, 8, 128), F32)],
        1,
        (info, f1, q1, xl, xh, mxl, mxh),
    )
    low, high = both_ways(g2, g2, "gz")
    low2, high2 = two_away(g2l, g2h)
    own2, near, fl, fh = call(
        source_window_kernel,
        [full(32, 8, 256), half(256, 256), half(256, 256), half(256, 256)],
        [],
        0,
        (g2, low, high, low2, high2, q2),
    )
    nl, nh = both_ways(near, near, "xy")
    fl, fh = both_ways(fl, fh, "xy", 2)
    window2 = scratch((32, 32, 256), F32)
    window1 = scratch((24, 24, 512), F32)
    (concentration,) = call(
        lambda *refs: back_kernel(nz, nx, *refs),
        [full(C, C, 1024)],
        [
            window2, window2, window2, window2, window2,
            scratch((8, 48, 128), F32),
            scratch((2, 16, 16, 128), F32),
            scratch((2, 16, 16, 128), F32),
            window1, window1,
            scratch((208, 1024), F32),
            scratch((208, 1024), F32),
            scratch((34, 40, 1024), F32),
            scratch((18, 24, 1024), F32),
            scratch((36, 40, 1024), F32),
            scratch((36, 40, 1024), F32),
            scratch((C, C, 1024), F32),
            scratch((16, 1024), F32),
            scratch((16, 1024), F32),
            pltpu.SemaphoreType.DMA((3,)),
        ],
        1,
        (info, f1, g1, v1, mzl, mzh, vxl, vxh, own2, nl, nh, fl, fh, q2, v2, gg, supply),
        in_hbm=3,
    )
    return supply, concentration


def solution(mesh):
    return jax.shard_map(
        shards,
        mesh=mesh,
        in_specs=(
            P("gz", "xy", None),
            P("gz", "xy", None),
            P(("gz", "xy"), None),
            P(("gz", "xy")),
            P(("gz", "xy"), None),
        ),
        out_specs=(P("gz", "xy", None), P("gz", "xy", None)),
        check_vma=False,
    )
```

```python
import jax
import jax.numpy as jnp
from jax import lax
from jax.experimental import pallas as pl
from jax.experimental.pallas import tpu as pltpu
from jax.sharding import PartitionSpec as P

EDGE = 16
CAP = 8
BRICK = 4096
SLOTS = 72
KAPPA = 32.0
OMEGA = 0.8
KEEP = 1.0 - OMEGA

C = 32
NT = 8
F32 = jnp.float32
BF16 = jnp.bfloat16


def spread(level):
    return KAPPA / 4.0**level


def shifted(values, distance, axis):
    return pltpu.roll(values, distance % values.shape[axis], axis)


def iota(shape, dim):
    return lax.broadcasted_iota(jnp.int32, shape, dim)


def lanes(t):
    return slice(t * 128, (t + 1) * 128)


def plane(ref, p):
    count = ref.shape[2] // 128
    rows = ref.shape[1]
    lane = iota((rows, 128), 1)
    before, here = None, ref[p, :, lanes(0)]
    for t in range(count):
        after = ref[p, :, lanes(t + 1)] if t + 1 < count else None
        low = jnp.where(lane == 127, 0.0 if before is None else before, here)
        high = jnp.where(lane == 0, 0.0 if after is None else after, here)
        sums = shifted(low, 1, 1) + shifted(high, -1, 1)
        sums = sums + (shifted(here, 1, 0) + shifted(here, -1, 0))
        sums = sums + (ref[p - 1, :, lanes(t)] + ref[p + 1, :, lanes(t)])
        yield t, here, sums
        before, here = here, after


def loop(start, stop, body, unroll=1):
    def step(i, carry):
        body(i)
        return carry

    lax.fori_loop(start, stop, step, 0, unroll=unroll)


def split_dot(a, b):
    high = a.astype(BF16)
    low = (a - high.astype(F32)).astype(BF16)
    return jnp.dot(high, b, preferred_element_type=F32) + jnp.dot(low, b, preferred_element_type=F32)


def pooling():
    return jnp.where(iota((256, 128), 0) // 2 == iota((256, 128), 1), 0.125, 0.0).astype(BF16)


def doubling():
    return jnp.where(iota((128, 256), 1) // 2 == iota((128, 256), 0), 1.0, 0.0).astype(BF16)


def halve_rows(values, rs, t):
    rows = values.shape[0]
    rs[t, 0:rows, :] = values
    return rs[t, pl.ds(0, rows // 2, stride=2), :] + rs[t, pl.ds(1, rows // 2, stride=2), :]


def halve_lanes(xp, planes, rows):
    matrix = pooling()
    tiles = []
    for t in range(0, xp.shape[0], 2):
        pair = jnp.concatenate([xp[t].reshape(planes * rows, 128), xp[t + 1].reshape(planes * rows, 128)], axis=1)
        tiles.append(split_dot(pair, matrix).reshape(planes, rows, 128))
    return tiles


def inside(shape, dim, first, wrap, index, size, count):
    place = iota(shape, dim) + first
    if wrap is not None:
        place = jnp.where(place < wrap, place, place - shape[dim])
    place = place + index * size
    return (place >= 0) & (place < count * size)


BLOCK = 272
FIRST_ROWS = BLOCK + 3 * 64


def uptake_part(t):
    return slice(BLOCK + 64 * (t // 3), BLOCK + 64 * (t // 3) + 64), lanes(t % 3)


def transposed_bricks(bricks_x, ids, counts, bricks, xs, targets):
    xs[...] = bricks[...].astype(F32)
    row = iota((1, 8, 128), 1)
    group = iota((1, 8, 128), 2) // 16
    group16 = iota((16, 128), 1) // 16
    per_y = 64

    def block(j, out, part):
        start = pl.multiple_of(j * 8, 8)
        x = jnp.stack([xs[pl.ds(start, 8), lanes(k)] for k in range(32)])
        for s in (4, 2, 1):
            up = shifted(shifted(x, -s, 1), 16 * s, 2)
            down = shifted(shifted(x, s, 1), -16 * s, 2)
            row_bit = (row // s) % 2
            group_bit = (group // s) % 2
            x = jnp.where(row_bit == group_bit, x, jnp.where(row_bit == 0, up, down))
        x = jnp.where(group < counts[0, j], x, 0.0)
        out[0:256, part] = x.reshape(256, 128).astype(BF16)
        names = jnp.zeros((16, 128), jnp.int32)
        for e in range(CAP):
            number = ids[j * 8 + e]
            by = lax.rem(number, per_y)
            rest = lax.div(number, per_y)
            bx = lax.rem(rest, 2)
            bz = lax.rem(lax.div(rest, bricks_x), 2)
            names = jnp.where(group16 == e, (bz * 2 + bx) * per_y + by, names)
        out[256:272, part] = names.astype(F32).astype(BF16)

    for i, out in enumerate(targets):
        for d in range(3):
            block(3 * i + d, out, lanes(d))


def first_kernel(bricks_x, ids, counts, bricks, uptake, own, zl, zh, xs, edges, sems):
    copies = [pltpu.make_async_copy(uptake.at[pl.ds(30 * i, 2)], edges.at[i], sems.at[i]) for i in range(2)]
    for copy in copies:
        copy.start()
    transposed_bricks(bricks_x, ids, counts, bricks, xs, (zl, own, zh))
    for i, ref in enumerate((zl, zh)):
        copies[i].wait()
        for t in range(8):
            ref[uptake_part(t)] = edges[i, :, :, lanes(t)].reshape(64, 128).astype(BF16)
        ref[uptake_part(8)] = jnp.zeros((64, 128), BF16)


def rates_kernel(uptake, r1, r2, xl, xh, rs, xp, rs1, xp1):
    def pair(m):
        for t in range(NT):
            both = uptake[2 * m, :, lanes(t)] + uptake[2 * m + 1, :, lanes(t)]
            xp[t, m] = halve_rows(both, rs, t)

    loop(0, 16, pair)
    for t, tile in enumerate(halve_lanes(xp, 16, 16)):
        r1[:, :, lanes(t)] = tile

    def pair1(m):
        for t in range(4):
            both = r1[2 * m, :, lanes(t)] + r1[2 * m + 1, :, lanes(t)]
            xp1[t, m] = halve_rows(both, rs1, t)

    loop(0, 8, pair1)
    for t, tile in enumerate(halve_lanes(xp1, 8, 8)):
        r2[:, lanes(t)] = tile.reshape(64, 128)

    sub = iota((8, 1024), 0)

    def columns(i):
        lows, highs = [], []
        for j in range(2):
            low, high = jnp.zeros((8, 1024), F32), jnp.zeros((8, 1024), F32)
            for n in range(4):
                z = 8 * i + 4 * j + n
                low = jnp.where(sub // 2 == n, shifted(uptake[z, 0:8, :], 2 * n, 0), low)
                high = jnp.where(sub // 2 == n, shifted(uptake[z, 24:32, :], 2 * n + 2, 0), high)
            lows.append(low)
            highs.append(high)
        rows = pl.ds(pl.multiple_of(16 * i, 16), 16)
        xl[rows, :] = jnp.concatenate(lows, axis=0).astype(BF16)
        xh[rows, :] = jnp.concatenate(highs, axis=0).astype(BF16)

    loop(0, 4, columns)


def far_along_z(nz, iz, to_low, to_high):
    if nz != 4:
        return to_low, to_high
    one = jnp.where(iz < 2, to_high, to_low)
    return one, one


def halves(sub, first, second):
    return jnp.where(sub < 4, first, shifted(second, 4, 1))


def uppers(sub, first, second):
    return jnp.where(sub < 4, shifted(first, 4, 1), second)


def far_messages(window):
    planes, _, width = window.shape
    pairs = window.reshape(planes // 2, 2, 8, width)
    sub = iota((planes // 2, 8, width), 1)
    size = (planes * 4, width)
    return halves(sub, pairs[:, 0], pairs[:, 1]).reshape(size), uppers(sub, pairs[:, 0], pairs[:, 1]).reshape(size)


def far_tile(from_low, from_high):
    width = from_low.shape[-1]
    low, high = from_low.reshape(-1, 8, width), from_high.reshape(-1, 8, width)
    sub = iota(low.shape, 1)
    even = jnp.where(sub < 4, high, shifted(low, 4, 1))
    odd = jnp.where(sub < 4, shifted(high, 4, 1), low)
    return jnp.stack([even, odd], axis=1).reshape(-1, 8, width)


def first_x_kernel(own, uxl, uxh, zl, zh, xl, xh):
    for ref, d in ((xl, 0), (xh, 2)):
        for n, src in enumerate((own, zl, zh)):
            ref[0:BLOCK, lanes(n)] = src[0:BLOCK, lanes(d)]
    sub = iota((8, 128), 0)
    lows, highs = [], []
    for t in range(8):
        xl[uptake_part(t)] = uxl[:, lanes(t)]
        xh[uptake_part(t)] = uxh[:, lanes(t)]
        both = [ref[uptake_part(t)].astype(F32) for ref in (zl, zh)]
        planes = [both[0][0:32], both[0][32:64], both[1][0:32], both[1][32:64]]
        to_low, to_high = jnp.zeros((8, 128), F32), jnp.zeros((8, 128), F32)
        for n, p in enumerate(planes):
            here = sub // 2 == n
            to_low = jnp.where(here, shifted(p[0:8], 2 * n, 0), to_low)
            to_high = jnp.where(here, shifted(p[24:32], 2 * n + 2, 0), to_high)
        lows.append(to_low)
        highs.append(to_high)
    xl[uptake_part(8)] = jnp.concatenate(lows, axis=0).astype(BF16)
    xh[uptake_part(8)] = jnp.concatenate(highs, axis=0).astype(BF16)


def window_planes(own, low, high, low2, high2):
    parts = (low2, low, own, high, high2)
    return jnp.concatenate([a.reshape(-1, 8, 256) for a in parts], axis=0)


def source_window_kernel(own, low, high, low2, high2, r2, zl, zh, f2, q2, near, fl, fh):
    planes = window_planes(own[...], low[...], high[...], low2[0:32, :], high2[0:32, :])
    f2[...] = planes
    below, above = [ref[80:144, 512:768].astype(F32) for ref in (zl, zh)]
    rates = window_planes(r2[...], below, above, low2[32:64, :], high2[32:64, :])
    q2[...] = rates
    near[0:256, :] = planes.reshape(256, 256).astype(BF16)
    near[256:320, :] = jnp.concatenate([low2[32:64, :], high2[32:64, :]], axis=0).astype(BF16)
    for i, values in enumerate((planes, rates)):
        to_low, to_high = far_messages(values)
        fl[128 * i : 128 * i + 128, :] = to_low.astype(BF16)
        fh[128 * i : 128 * i + 128, :] = to_high.astype(BF16)


O = 5
Q = 2
BASE = 1.0 + 6.0 * KAPPA


def spots(blocks, hot):
    lane = iota((1, 128), 1)
    at_y = iota((1024, 128), 0)
    tiles = []
    for i, (ref, part) in enumerate(blocks):
        name = ref[256:272, part].astype(F32).astype(jnp.int32)[0:1]
        tiles.append(lax.shift_right_logical(name, 6))
        y = (name & 63) * 16 + (lane & 15)
        hot[:, lanes(i)] = jnp.where(at_y == y, 1.0, 0.0).astype(BF16)
    return tiles


def scatter(blocks, hot):
    tiles = spots(blocks, hot)
    for tile in range(4):
        bz, bx = tile // 2, tile % 2
        left = [
            jnp.where(tiles[i] == tile, ref[0:256, part].astype(F32), 0.0).astype(BF16)
            for i, (ref, part) in enumerate(blocks)
        ]
        left = jnp.concatenate(left, axis=1)
        for n in range(4):
            cols = slice(n * 256, (n + 1) * 256)
            sums = lax.dot_general(left, hot[cols, :], (((1,), (1,)), ((), ())), preferred_element_type=F32)
            yield 16 * bz, slice(16 * bx, 16 * bx + 16), cols, sums.reshape(16, 16, 256)


def sweep(src, dst, source, gg, z, sourced):
    for t, here, sums in plane(src, z + O):
        inner = KAPPA * sums
        g = gg[z + Q, :, lanes(t)]
        if sourced:
            body = inner[0:32] + source[z, :, lanes(t)]
            dst[z + O, 0:32, lanes(t)] = KEEP * here[0:32] + g[0:32] * body
            dst[z + O, 32:40, lanes(t)] = KEEP * here[32:40] + g[32:40] * inner[32:40]
        else:
            dst[z + O, :, lanes(t)] = KEEP * here + g * inner


def own_kernel(nz, info, density, uptake, own, zl, zh, s0, g0, d0, v1, edge, va, hot):
    iz = info[0]
    for p in (3, 4, 37, 38):
        va[p] = jnp.zeros((40, 1024), F32)

    def own_plane(z):
        va[z + O, 0:32, :] = density[z]
        va[z + O, 32:40, :] = jnp.zeros((8, 1024), F32)
        d = uptake[z] + BASE
        d0[z + Q] = d
        g0[z + Q] = OMEGA / d

    loop(0, C, own_plane)
    for n in range(4):
        ref, valid = (zl, iz > 0) if n < 2 else (zh, iz < nz - 1)
        q = n if n < 2 else 32 + n
        rows = slice(32 * (n % 2), 32 * (n % 2) + 32)
        for t in range(NT):
            d = ref[uptake_part(t)].astype(F32)[rows] + BASE
            d0[q, :, lanes(t)] = d
            g0[q, :, lanes(t)] = jnp.where(valid, OMEGA, 0.0) / d

    blocks = [(ref, lanes(1)) for ref in (own, zl, zh)]
    for z, rows, cols, sums in scatter(blocks, hot):
        planes = slice(z, z + 16)
        s0[planes, rows, cols] = density[planes, rows, cols] + sums

    def first(z):
        for t, here, sums in plane(va, z + O):
            inner = KAPPA * sums
            body = inner[0:32] + s0[z, :, lanes(t)]
            v1[z + 1, :, lanes(t)] = KEEP * here[0:32] + g0[z + Q, :, lanes(t)] * body
            edge[z, :, lanes(t)] = inner[32:40]

    loop(0, C, first, 2)
    for z in (-1, C):
        for t in range(NT):
            near = va[z + O + (1 if z < 0 else -1), 0:32, lanes(t)]
            v1[z + 1, :, lanes(t)] = g0[z + Q, :, lanes(t)] * (KAPPA * near)


def pre_kernel(
    nz, nx, info, xl, xh, r1, r2, s0, g0, d0, v1, edge_in,
    supply, c1, mzl, mzh, pxl, pxh, v_out, g_out,
    va, vb, dd, gg, edge, hot, rs, xp, usl, ush, sems,
):
    iz, ix = info[0], info[1]
    k = KAPPA
    loads = [
        pltpu.make_async_copy(src, dst, sems.at[i])
        for i, (src, dst) in enumerate(
            (
                (s0, supply),
                (v1, vb.at[4:38, 0:32, :]),
                (g0, gg.at[:, 0:32, :]),
                (edge_in, edge),
                (d0, dd.at[:, 0:32, :]),
            )
        )
    ]
    for copy in loads:
        copy.start()

    for p in (1, 2, 39, 40):
        va[p] = jnp.zeros((40, 1024), F32)
    for p in (2, 3, 38, 39):
        vb[p] = jnp.zeros((40, 1024), F32)
    for p in (4, 37):
        vb[p, 32:40, :] = jnp.zeros((8, 1024), F32)

    sub8 = iota((8, 1024), 0)
    for t in range(NT):
        usl[0:64, lanes(t)] = xl[uptake_part(t)].astype(F32)
        ush[0:64, lanes(t)] = xh[uptake_part(t)].astype(F32)
        usl[64:72, lanes(t)] = xl[uptake_part(8)].astype(F32)[8 * t : 8 * t + 8]
        ush[64:72, lanes(t)] = xh[uptake_part(8)].astype(F32)[8 * t : 8 * t + 8]

    def set_halo(q, low, high, valid_z):
        gz = jnp.where(valid_z, OMEGA, 0.0)
        d = jnp.where(sub8 < 2, high, jnp.where(sub8 >= 6, low, 0.0)) + BASE
        dd[q, 32:40, :] = d
        omega = jnp.where(sub8 < 2, jnp.where(ix < nx - 1, gz, 0.0), jnp.where(sub8 >= 6, jnp.where(ix > 0, gz, 0.0), 0.0))
        gg[q, 32:40, :] = omega / d

    def halos(i):
        rows = pl.ds(pl.multiple_of(8 * i, 8), 8)
        low, high = usl[rows, :], ush[rows, :]
        for n in range(4):
            set_halo(4 * i + n + Q, shifted(low, 6 - 2 * n, 0), shifted(high, -2 * n, 0), True)

    loop(0, C // 4, halos)
    low, high = usl[64:72, :], ush[64:72, :]
    for n in range(4):
        exists = iz > 0 if n < 2 else iz < nz - 1
        set_halo(n if n < 2 else 32 + n, shifted(low, 6 - 2 * n, 0), shifted(high, -2 * n, 0), exists)

    blocks = [(ref, lanes(n)) for ref in (xl, xh) for n in range(3)]
    waiting = list(loads[0:3])
    for z, rows, cols, sums in scatter(blocks, hot):
        while waiting:
            waiting.pop().wait()
        supply[z : z + 16, rows, cols] = supply[z : z + 16, rows, cols] + sums
        g = gg[z + Q : z + Q + 16, rows, cols]
        vb[z + O : z + O + 16, rows, cols] = vb[z + O : z + O + 16, rows, cols] + g * sums
    loads[3].wait()

    def edges(z):
        vb[z + O, 32:40, :] = gg[z + Q, 32:40, :] * edge[z]

    loop(0, C, edges)

    loop(0, C, lambda z: sweep(vb, va, supply, gg, z, True), 2)
    loop(0, 4, lambda i: sweep(vb, va, supply, gg, jnp.where(i < 2, i - 2, i + C - 2), False))
    loads[4].wait()
    v_copy = pltpu.make_async_copy(va.at[3:39], v_out, sems.at[5])
    g_copy = pltpu.make_async_copy(gg, g_out, sems.at[6])
    v_copy.start()
    g_copy.start()

    def residual(z, sourced, edge):
        for t, here, sums in plane(va, z + O):
            r = k * sums
            if not edge:
                r = r - dd[z + Q, :, lanes(t)] * here
            if sourced:
                r = jnp.concatenate([r[0:32] + supply[z, :, lanes(t)], r[32:40]], axis=0)
            yield t, r

    def coarse(m, sourced):
        both = zip(residual(2 * m - 4, sourced, False), residual(2 * m - 3, sourced, False))
        for (t, first), (_, second) in both:
            xp[t, m, 0:20, :] = halve_rows(first + second, rs, t)

    loop(2, 18, lambda m: coarse(m, True))
    loop(0, 2, lambda i: coarse(1 + 17 * i, False))

    def outer(i):
        for t, r in residual(jnp.where(i == 0, -3, 34), False, True):
            xp[t, 19 * i, 0:20, :] = halve_rows(r, rs, t)

    loop(0, 2, outer)

    sub = iota((20, 8, 128), 1)
    for t, tile in enumerate(halve_lanes(xp, 20, 24)):
        last = tile[:, 16:24]
        last = jnp.where(sub < 2, last, jnp.where(sub >= 6, shifted(last, 4, 1), 0.0))
        c1[:, 0:16, lanes(t)] = tile[:, 0:16]
        c1[:, 16:24, lanes(t)] = last

    empty = jnp.zeros((1, 8, 1024), F32)
    blank = jnp.zeros((8, 1024), F32)
    edges = (
        (mzl, slice(0, 6), slice(0, 4), va[3:7], 0),
        (mzh, slice(14, 20), slice(12, 16), va[35:39], 31),
    )
    for ref, planes, rates, values, z in edges:
        source = c1[planes].reshape(144, 512)
        ref[0:80, 0:512] = source[0:80].astype(BF16)
        ref[0:64, 512:1024] = source[80:144].astype(BF16)
        ref[64:80, 512:1024] = jnp.zeros((16, 512), BF16)
        ref[80:144, 0:512] = r1[rates].reshape(64, 512).astype(BF16)
        ref[80:144, 512:768] = r2[...].astype(BF16)
        ref[80:144, 768:1024] = jnp.zeros((64, 256), BF16)
        level0 = jnp.concatenate([values, jnp.concatenate([supply[z : z + 1], empty], axis=1)], axis=0)
        ref[144:352, :] = jnp.concatenate([level0.reshape(200, 1024), blank], axis=0).astype(BF16)

    def sides(i):
        lows, highs = [], []
        for j in range(2):
            p = 4 * i + 2 * j + 3
            lows.append(pack_low(va[p], va[p + 1]))
            highs.append(pack_high(va[p], va[p + 1]))
        rows = pl.ds(pl.multiple_of(16 * i, 16), 16)
        pxl[rows, :] = jnp.concatenate(lows, axis=0).astype(BF16)
        pxh[rows, :] = jnp.concatenate(highs, axis=0).astype(BF16)

    loop(0, 9, sides)

    def sources(i):
        lows, highs = [], []
        for j in range(2):
            low, high = jnp.zeros((8, 1024), F32), jnp.zeros((8, 1024), F32)
            for n in range(8):
                z = 16 * i + 8 * j + n
                low = jnp.where(sub8 == n, shifted(supply[z, 0:8, :], n, 0), low)
                high = jnp.where(sub8 == n, shifted(supply[z, 24:32, :], n + 1, 0), high)
            lows.append(low)
            highs.append(high)
        rows = pl.ds(pl.multiple_of(16 * i + 144, 16), 16)
        pxl[rows, :] = jnp.concatenate(lows, axis=0).astype(BF16)
        pxh[rows, :] = jnp.concatenate(highs, axis=0).astype(BF16)

    loop(0, 2, sources)
    v_copy.wait()
    g_copy.wait()


def outer_rows(sub):
    return (sub < 2) | (sub >= 6)


def pack_pair(sub, a, b):
    return jnp.where(outer_rows(sub), a, shifted(b, 4, 0))


def pack_low(first, second):
    sub = iota((8, 1024), 0)
    a, b = [jnp.where(sub < 4, v[0:8], v[32:40]) for v in (first, second)]
    return pack_pair(sub, a, b)


def pack_high(first, second):
    sub = iota((8, 1024), 0)
    a, b = [jnp.where(sub >= 4, v[24:32], v[32:40]) for v in (first, second)]
    return pack_pair(sub, a, b)


def sides_kernel(pxl, pxh, mzl, mzh, r2, out_l, out_h):
    for ref, out in ((pxl, out_l), (pxh, out_h)):
        out[0:176, :] = ref[...]
        for n, rates in enumerate((mzl[80:144, 512:768], r2[...].astype(BF16), mzh[80:144, 512:768])):
            out[176:240, n * 256 : n * 256 + 256] = rates
        out[176:240, 768:1024] = jnp.zeros((64, 256), BF16)
    for message, start in ((mzl, 0), (mzh, 128)):
        planes = message[144:304, :].astype(F32).reshape(4, 40, 1024)
        rows = slice(start, start + 16)
        for ref, out, pack in ((pxl, out_l, pack_low), (pxh, out_h, pack_high)):
            added = [pack(planes[2 * i], planes[2 * i + 1]) for i in range(2)]
            out[rows, :] = (ref[rows, :].astype(F32) + jnp.concatenate(added, axis=0)).astype(BF16)


def in_three(sub, tiles, free, turns):
    spare = (sub == free) | (sub == free + 1)
    last = tiles[:, 3]
    parts = [jnp.where(spare, shifted(last, turn, 1), tiles[:, i]) for i, turn in enumerate(turns)]
    return jnp.stack(parts, axis=1)


def out_of_three(sub, parts, free, turns):
    last = None
    for i, turn in enumerate(turns):
        back = shifted(parts[:, i], -turn, 1)
        home = (free - turn) % 8
        here = (sub == home) | (sub == home + 1)
        last = jnp.where(here, back, 0.0 if last is None else last)
    return jnp.stack([parts[:, 0], parts[:, 1], parts[:, 2], last], axis=1)


HIGH_PACK = (2, (-2, 4, 2))
LOW_PACK = (4, (-2, 4, 2))


def merge_kernel(c1, r1, mzl, mzh, f1, q1, mxl, mxh):
    zeros = jnp.zeros((24, 512), F32)
    for p in (0, 1, 22, 23):
        f1[p] = zeros
    f1[2:22] = c1[...]
    for ref, planes in ((mzl, slice(0, 6)), (mzh, slice(18, 24))):
        parts = [ref[0:80, 0:512].astype(F32), ref[0:64, 512:1024].astype(F32)]
        f1[planes] = f1[planes] + jnp.concatenate(parts, axis=0).reshape(6, 24, 512)
    sub = iota((6, 8, 512), 1)
    first, last, halo = [f1[:, 8 * n : 8 * n + 8].reshape(6, 4, 8, 512) for n in range(3)]
    sub4 = iota((6, 4, 8, 512), 2)
    to_high = in_three(sub, jnp.where(sub4 >= 4, last, halo), *HIGH_PACK)
    to_low = in_three(sub, jnp.where(sub4 >= 4, halo, first), *LOW_PACK)
    mxh[0:144, :] = to_high.reshape(144, 512).astype(BF16)
    mxl[0:144, :] = to_low.reshape(144, 512).astype(BF16)
    q1[0:4] = mzl[80:144, 0:512].astype(F32).reshape(4, 16, 512)
    q1[4:20] = r1[...]
    q1[20:24] = mzh[80:144, 0:512].astype(F32).reshape(4, 16, 512)
    sub1 = iota((12, 8, 512), 1)
    first = q1[:, 0:8, :].reshape(12, 2, 8, 512)
    last = q1[:, 8:16, :].reshape(12, 2, 8, 512)
    mxl[144:240, :] = halves(sub1, first[:, 0], first[:, 1]).reshape(96, 512).astype(BF16)
    mxh[144:240, :] = uppers(sub1, last[:, 0], last[:, 1]).reshape(96, 512).astype(BF16)


def middle_kernel(nz, nx, info, f0, q_in, r2, mxl, mxh, f1, g1, v1, g2, g2l, g2h, q0, va, rs, xp):
    iz, ix = info[0], info[1]
    k = spread(1)
    base = 1.0 + 6.0 * k
    sub6 = iota((6, 8, 512), 1)
    low = out_of_three(sub6, mxl[0:144, :].astype(F32).reshape(6, 3, 8, 512), *HIGH_PACK).reshape(24, 8, 512)
    high = out_of_three(sub6, mxh[0:144, :].astype(F32).reshape(6, 3, 8, 512), *LOW_PACK).reshape(24, 8, 512)
    sub = iota((24, 8, 512), 1)
    f1[:, 0:8] = f0[:, 0:8] + jnp.where(sub < 2, low, 0.0)
    f1[:, 8:16] = f0[:, 8:16] + jnp.where(sub >= 6, high, 0.0)
    f1[:, 16:24] = f0[:, 16:24] + jnp.where(sub >= 4, low, high)
    low, high = [ref[144:240, :].astype(F32).reshape(12, 8, 512) for ref in (mxl, mxh)]
    sub12 = iota((12, 8, 512), 1)
    even = jnp.where(sub12 >= 4, shifted(low, 4, 1), high)
    odd = jnp.where(sub12 >= 4, low, shifted(high, 4, 1))
    q0[:, 0:16] = q_in[...]
    q0[:, 16:24] = jnp.stack([even, odd], axis=1).reshape(24, 8, 512)
    shape = (24, 24, 128)
    valid = inside(shape, 0, -4, None, iz, 16, nz) & inside(shape, 1, 0, 20, ix, 16, nx)
    for t in range(4):
        g = jnp.where(valid, OMEGA, 0.0) / (q0[:, :, lanes(t)] + base)
        g1[:, :, lanes(t)] = g
        va[:, :, lanes(t)] = g * f1[:, :, lanes(t)]
    v1[0] = va[0]
    v1[23] = va[23]

    def sweep(p):
        for t, here, sums in plane(va, p):
            v1[p, :, lanes(t)] = KEEP * here + g1[p, :, lanes(t)] * (f1[p, :, lanes(t)] + k * sums)

    loop(1, 23, sweep, 2)

    def residual(p):
        for t, here, sums in plane(v1, p):
            yield t, f1[p, :, lanes(t)] + k * sums - (q0[p, :, lanes(t)] + base) * here

    def coarse(m):
        for (t, first), (_, second) in zip(residual(2 * m + 4), residual(2 * m + 5)):
            xp[t, m] = halve_rows((first + second)[0:16], rs, t)

    loop(0, 8, coarse)
    for t, tile in enumerate(halve_lanes(xp, 8, 8)):
        g2[:, lanes(t)] = tile.reshape(64, 128)
        low, high = far_along_z(nz, iz, tile[0:4].reshape(32, 128), tile[4:8].reshape(32, 128))
        g2l[0:32, lanes(t)] = low
        g2h[0:32, lanes(t)] = high
    low, high = far_along_z(nz, iz, r2[0:32, :], r2[32:64, :])
    g2l[32:64, :] = low
    g2h[32:64, :] = high


def back_kernel(
    nz, nx, info, f1, g1, v1, vzl, vzh, vxl, vxh, own2, n2l, n2h, m2l, m2h, q_own, v_in, g_in, s_in,
    out,
    f2, q2, h2, a2, b2, rs, xp, xpr, wa, w1, zsl, zsh, vb, ws,
    v2, gg, supply, fsl, fsh, sems,
):
    iz, ix = info[0], info[1]
    matrix = doubling()
    level0 = [
        pltpu.make_async_copy(src, dst, sems.at[i])
        for i, (src, dst) in enumerate(((v_in, v2), (g_in, gg), (s_in, supply)))
    ]
    for copy in level0:
        copy.start()

    f2[:, 0:8, :] = own2[...]
    f2[:, 8:16, :] = n2h[0:256, :].astype(F32).reshape(32, 8, 256)
    f2[:, 16:24, :] = far_tile(m2l[0:128, :].astype(F32), m2h[0:128, :].astype(F32))
    f2[:, 24:32, :] = n2l[0:256, :].astype(F32).reshape(32, 8, 256)
    q2[:, 0:8, :] = q_own[...]
    q2[:, 16:24, :] = far_tile(m2l[128:256, :].astype(F32), m2h[128:256, :].astype(F32))
    for ref, rows in ((vxh, slice(8, 16)), (vxl, slice(24, 32))):
        for n in range(3):
            q2[8 * n + 4 : 8 * n + 12, rows, :] = ref[176:240, n * 256 : n * 256 + 256].astype(F32).reshape(8, 8, 256)
    for ref, rows in ((n2h, slice(8, 16)), (n2l, slice(24, 32))):
        outer = ref[256:320, :].astype(F32).reshape(8, 8, 256)
        q2[0:4, rows, :] = outer[0:4]
        q2[28:32, rows, :] = outer[4:8]

    k = spread(2)
    base = 1.0 + 6.0 * k
    shape = (32, 32, 128)
    valid = inside(shape, 0, -12, None, iz, 8, nz) & inside(shape, 1, 0, 20, ix, 8, nx)
    for t in range(2):
        g = jnp.where(valid, OMEGA, 0.0) / (q2[:, :, lanes(t)] + base)
        h2[:, :, lanes(t)] = g
        a2[:, :, lanes(t)] = g * f2[:, :, lanes(t)]
    b2[0] = a2[0]
    b2[31] = a2[31]

    def sweep2(src, dst):
        def body(p):
            for t, here, sums in plane(src, p):
                dst[p, :, lanes(t)] = KEEP * here + h2[p, :, lanes(t)] * (f2[p, :, lanes(t)] + k * sums)

        return body

    loop(1, 31, sweep2(a2, b2), 2)

    def coarse(m):
        total, rates = [0.0, 0.0], [0.0, 0.0]
        for j in range(2):
            p = 2 * m + j
            for t, here, sums in plane(b2, p):
                r = f2[p, :, lanes(t)] + k * sums - (q2[p, :, lanes(t)] + base) * here
                total[t] = total[t] + r
                rates[t] = rates[t] + q2[p, :, lanes(t)]
        for t in range(2):
            xp[t, m] = halve_rows(total[t], rs, t)
            xpr[t, m] = halve_rows(rates[t], rs, t + 2)

    for t in range(2):
        for m in (0, 15):
            xp[t, m] = jnp.zeros((16, 128), F32)
            xpr[t, m] = jnp.zeros((16, 128), F32)
    loop(1, 15, coarse)

    shape = (16, 16, 128)
    valid = inside(shape, 0, -6, None, iz, 4, nz) & inside(shape, 1, 0, 10, ix, 4, nx)
    k3 = spread(3)
    (source,) = halve_lanes(xp, 16, 16)
    (rates,) = halve_lanes(xpr, 16, 16)
    g = jnp.where(valid, OMEGA, 0.0) / (rates + (1.0 + 6.0 * k3))
    v = g * source
    lane = iota(shape, 2)
    for repeat in range(3):
        edge = jnp.zeros((1, 16, 128), F32)
        sums = jnp.concatenate([v[1:], edge], axis=0) + jnp.concatenate([edge, v[:-1]], axis=0)
        sums = sums + shifted(v, 1, 1) + shifted(v, -1, 1)
        sums = sums + jnp.where(lane == 0, 0.0, shifted(v, 1, 2)) + jnp.where(lane == 127, 0.0, shifted(v, -1, 2))
        v = KEEP * v + g * (source + k3 * sums)

    wide = split_dot(v[4:12].reshape(128, 128), matrix).reshape(8, 16, 256)
    for m in range(8):
        for t in range(2):
            part = wide[m, :, lanes(t)]
            rs[t, pl.ds(0, 16, stride=2), :] = part
            rs[t, pl.ds(1, 16, stride=2), :] = part
            for j in range(2):
                p = 8 + 2 * m + j
                b2[p, :, lanes(t)] = b2[p, :, lanes(t)] + rs[t, 0:32, :]
    loop(9, 23, sweep2(b2, a2), 2)
    loop(10, 22, sweep2(a2, b2), 2)

    w = b2[10:22]
    near, far = w[:, 8:16], w[:, 24:32]
    near = jnp.where(iota((12, 8, 256), 1) < 2, near, shifted(far, 4, 1))
    w = jnp.concatenate([w[:, 0:8], near], axis=1).reshape(192, 256)
    wide = [split_dot(w[:, lanes(t)], matrix) for t in range(2)]
    wide = jnp.concatenate(wide, axis=1).reshape(12, 16, 512)
    for m in range(12):
        for t in range(4):
            part = wide[m, :, lanes(t)]
            rs[t, pl.ds(0, 16, stride=2), :] = part
            rs[t, pl.ds(1, 16, stride=2), :] = part
            for j in range(2):
                p = 2 * m + j
                wa[p, :, lanes(t)] = v1[p, :, lanes(t)] + rs[t, 0:24, :]
    k1 = spread(1)

    def sweep1(src, dst):
        def body(p):
            for t, here, sums in plane(src, p):
                dst[p, :, lanes(t)] = KEEP * here + g1[p, :, lanes(t)] * (f1[p, :, lanes(t)] + k1 * sums)

        return body

    loop(2, 22, sweep1(wa, w1), 2)
    loop(3, 21, sweep1(w1, wa), 2)

    sub = iota((18, 8, 128), 1)
    for t in range(4):
        halo = wa[3:21, 16:24, lanes(t)]
        halo = jnp.where(sub < 2, halo, shifted(halo, 4, 1))
        w = jnp.concatenate([wa[3:21, 0:16, lanes(t)], halo], axis=1)
        ws[:, :, t * 256 : t * 256 + 256] = split_dot(w.reshape(432, 128), matrix).reshape(18, 24, 256)

    for copy in level0:
        copy.wait()
    zsl[...] = vzl[144:352, :].astype(F32)
    zsh[...] = vzh[144:352, :].astype(F32)
    for i in range(4):
        v2[i] = v2[i] + zsl[40 * i : 40 * i + 40, :]
        v2[32 + i] = v2[32 + i] + zsh[40 * i : 40 * i + 40, :]

    s8 = iota((8, 128), 0)

    outer = outer_rows(s8)

    def correct(i):
        rows = pl.ds(pl.multiple_of(16 * i, 16), 16)
        for t in range(NT):
            low = vxl[rows, lanes(t)].astype(F32)
            high = vxh[rows, lanes(t)].astype(F32)
            for n in range(2):
                part = ws[2 * i + n, :, lanes(t)]
                rs[t, pl.ds(0, 24, stride=2), :] = part
                rs[t, pl.ds(1, 24, stride=2), :] = part
                for j in range(2):
                    p = 4 * i + 2 * n + j
                    lo, hi = low[8 * n : 8 * n + 8], high[8 * n : 8 * n + 8]
                    if j:
                        lo, hi = shifted(lo, 4, 0), shifted(hi, 4, 0)
                    v2[p, 0:8, lanes(t)] = v2[p, 0:8, lanes(t)] + rs[t, 0:8, :] + jnp.where(s8 < 2, lo, 0.0)
                    v2[p, 8:24, lanes(t)] = v2[p, 8:24, lanes(t)] + rs[t, 8:24, :]
                    v2[p, 24:32, lanes(t)] = v2[p, 24:32, lanes(t)] + rs[t, 24:32, :] + jnp.where(s8 >= 6, hi, 0.0)
                    extra = jnp.where(outer, jnp.where(s8 >= 4, lo, hi), 0.0)
                    v2[p, 32:40, lanes(t)] = v2[p, 32:40, lanes(t)] + rs[t, 32:40, :] + extra

    loop(0, 9, correct)
    k0 = spread(0)

    def first(i):
        rows = pl.ds(pl.multiple_of(16 * i + 144, 16), 16)
        for t in range(NT):
            fsl[:, lanes(t)] = vxl[rows, lanes(t)].astype(F32)
            fsh[:, lanes(t)] = vxh[rows, lanes(t)].astype(F32)

        def step(j):
            z = 16 * i + j
            start = pl.multiple_of((j // 8) * 8, 8)
            turn = lax.rem(j, 8)
            for t, here, sums in plane(v2, z + 2):
                lo = pltpu.roll(fsl[pl.ds(start, 8), lanes(t)], 7 - turn, 0)
                hi = pltpu.roll(fsh[pl.ds(start, 8), lanes(t)], lax.rem(8 - turn, 8), 0)
                f = jnp.where(s8 == 7, lo, jnp.where(s8 == 0, hi, 0.0))
                g = gg[z + 2, :, lanes(t)]
                inner = k0 * sums
                vb[z + 1, 0:32, lanes(t)] = KEEP * here[0:32] + g[0:32] * (supply[z, :, lanes(t)] + inner[0:32])
                vb[z + 1, 32:40, lanes(t)] = KEEP * here[32:40] + g[32:40] * (f + inner[32:40])

        loop(0, 16, step, 2)

    loop(0, 2, first)
    for p, ref in ((1, zsl), (34, zsh)):
        for t, here, sums in plane(v2, p):
            g = gg[p, :, lanes(t)]
            vb[p - 1, :, lanes(t)] = KEEP * here + g * (ref[160:200, lanes(t)] + k0 * sums)

    def second(z):
        for t, here, sums in plane(vb, z + 1):
            g = gg[z + 2, 0:32, lanes(t)]
            out[z, :, lanes(t)] = KEEP * here[0:32] + g * (supply[z, :, lanes(t)] + k0 * sums[0:32])

    loop(0, C, second, 2)


VMEM = pl.BlockSpec(memory_space=pltpu.VMEM)
SMEM = pl.BlockSpec(memory_space=pltpu.SMEM)
ANY = pl.BlockSpec(memory_space=pl.ANY)


def call(kernel, outs, scratch, smem, args, out_specs=None, in_hbm=0):
    moved = sum(a.size * a.dtype.itemsize for a in list(args) + list(outs))
    return pl.pallas_call(
        kernel,
        out_shape=tuple(outs),
        in_specs=[SMEM] * smem + [VMEM] * (len(args) - smem - in_hbm) + [ANY] * in_hbm,
        out_specs=tuple(out_specs or [VMEM] * len(outs)),
        scratch_shapes=scratch,
        compiler_params=pltpu.CompilerParams(vmem_limit_bytes=58 * 2**20),
        cost_estimate=pl.CostEstimate(flops=20 * moved, bytes_accessed=moved, transcendentals=0),
    )(*args)


def shaped(shape, dtype=F32):
    return jax.ShapeDtypeStruct(shape, dtype)


def both_ways(to_low, to_high, axis, distance=1):
    count = lax.axis_size(axis)
    up = [(i, i + distance) for i in range(count - distance)]
    down = [(j, i) for i, j in up]
    return lax.ppermute(to_high, axis, up), lax.ppermute(to_low, axis, down)


def two_away(to_low, to_high):
    count = lax.axis_size("gz")
    if count != 4:
        return both_ways(to_low, to_high, "gz", 2)
    came = lax.ppermute(to_low, "gz", [(i, (i + 2) % 4) for i in range(4)])
    return came, came


def shards(density, uptake, brick_values, brick_ids, slot_counts):
    nz, nx = lax.axis_size("gz"), lax.axis_size("xy")
    info = jnp.stack([lax.axis_index("gz"), lax.axis_index("xy")]).astype(jnp.int32)
    scratch = pltpu.VMEM
    half = lambda *shape: shaped(shape, BF16)
    full = lambda *shape: shaped(shape, F32)

    own, zl, zh = call(
        lambda *refs: first_kernel(2 * nx, *refs),
        [half(BLOCK, 384), half(FIRST_ROWS, 384), half(FIRST_ROWS, 384)],
        [scratch((SLOTS, BRICK), F32), scratch((2, 2, C, 1024), F32), pltpu.SemaphoreType.DMA((2,))],
        2,
        (brick_ids, slot_counts, brick_values, uptake),
        in_hbm=1,
    )
    zl, zh = both_ways(zl, zh, "gz")
    r1, r2, uxl, uxh = call(
        rates_kernel,
        [full(16, 16, 512), full(64, 256), half(64, 1024), half(64, 1024)],
        [scratch((8, 32, 128), F32), scratch((8, 16, 16, 128), F32), scratch((4, 16, 128), F32), scratch((4, 8, 8, 128), F32)],
        0,
        (lax.optimization_barrier((uptake, own))[0],),
    )
    xl, xh = call(
        first_x_kernel,
        [half(FIRST_ROWS, 384), half(FIRST_ROWS, 384)],
        [],
        0,
        (own, uxl, uxh, zl, zh),
    )
    s0, g0, d0, v1, edge = call(
        lambda *refs: own_kernel(nz, *refs),
        [full(C, C, 1024), full(36, C, 1024), full(36, C, 1024), full(34, C, 1024), full(C, 8, 1024)],
        [scratch((42, 40, 1024), F32), scratch((1024, 384), BF16)],
        1,
        (info, density, uptake, own, zl, zh),
    )
    xl, xh = both_ways(xl, xh, "xy")

    supply, c1, mzl, mzh, pxl, pxh, v2, gg = call(
        lambda *refs: pre_kernel(nz, nx, *refs),
        [
            full(C, C, 1024),
            full(20, 24, 512),
            half(352, 1024),
            half(352, 1024),
            half(176, 1024),
            half(176, 1024),
            full(36, 40, 1024),
            full(36, 40, 1024),
        ],
        [
            scratch((42, 40, 1024), F32),
            scratch((42, 40, 1024), F32),
            scratch((36, 40, 1024), F32),
            scratch((36, 40, 1024), F32),
            scratch((C, 8, 1024), F32),
            scratch((1024, 768), BF16),
            scratch((8, 40, 128), F32),
            scratch((8, 20, 24, 128), F32),
            scratch((72, 1024), F32),
            scratch((72, 1024), F32),
            pltpu.SemaphoreType.DMA((7,)),
        ],
        1,
        (info, xl, xh, r1, r2, s0, g0, d0, v1, edge),
        [VMEM] * 6 + [ANY] * 2,
        in_hbm=5,
    )
    mzl, mzh = both_ways(mzl, mzh, "gz")
    f1, q1, mxl, mxh = call(
        merge_kernel,
        [full(24, 24, 512), full(24, 16, 512), half(240, 512), half(240, 512)],
        [],
        0,
        (c1, r1, mzl, mzh),
    )
    mxl, mxh = both_ways(mxl, mxh, "xy")
    pxl, pxh = call(
        sides_kernel,
        [half(240, 1024), half(240, 1024)],
        [],
        0,
        (pxl, pxh, mzl, mzh, r2),
    )
    vxl, vxh = both_ways(pxl, pxh, "xy")
    f1, pxl, pxh = lax.optimization_barrier((f1, pxl, pxh))
    f1, g1, v1, g2, g2l, g2h = call(
        lambda *refs: middle_kernel(nz, nx, *refs),
        [full(24, 24, 512), full(24, 24, 512), full(24, 24, 512), full(64, 256), full(64, 256), full(64, 256)],
        [scratch((24, 24, 512), F32), scratch((24, 24, 512), F32), scratch((4, 16, 128), F32), scratch((4, 8, 8, 128), F32)],
        1,
        (info, f1, q1, r2, mxl, mxh),
    )
    low, high = both_ways(g2, g2, "gz")
    low2, high2 = two_away(g2l, g2h)
    own2, q2, near, fl, fh = call(
        source_window_kernel,
        [full(32, 8, 256), full(32, 8, 256), half(320, 256), half(256, 256), half(256, 256)],
        [],
        0,
        (g2, low, high, low2, high2, r2, mzl, mzh),
    )
    nl, nh = both_ways(near, near, "xy")
    fl, fh = both_ways(fl, fh, "xy", 2)
    window2 = scratch((32, 32, 256), F32)
    window1 = scratch((24, 24, 512), F32)
    (concentration,) = call(
        lambda *refs: back_kernel(nz, nx, *refs),
        [full(C, C, 1024)],
        [
            window2, window2, window2, window2, window2,
            scratch((8, 48, 128), F32),
            scratch((2, 16, 16, 128), F32),
            scratch((2, 16, 16, 128), F32),
            window1, window1,
            scratch((208, 1024), F32),
            scratch((208, 1024), F32),
            scratch((34, 40, 1024), F32),
            scratch((18, 24, 1024), F32),
            scratch((36, 40, 1024), F32),
            scratch((36, 40, 1024), F32),
            scratch((C, C, 1024), F32),
            scratch((16, 1024), F32),
            scratch((16, 1024), F32),
            pltpu.SemaphoreType.DMA((3,)),
        ],
        1,
        (info, f1, g1, v1, mzl, mzh, vxl, vxh, own2, nl, nh, fl, fh, q2, v2, gg, supply),
        in_hbm=3,
    )
    return supply, concentration


def solution(mesh):
    return jax.shard_map(
        shards,
        mesh=mesh,
        in_specs=(
            P("gz", "xy", None),
            P("gz", "xy", None),
            P(("gz", "xy"), None),
            P(("gz", "xy")),
            P(("gz", "xy"), None),
        ),
        out_specs=(P("gz", "xy", None), P("gz", "xy", None)),
        check_vma=False,
    )
```

```python
import jax
import jax.numpy as jnp
from jax import lax
from jax.experimental import pallas as pl
from jax.experimental.pallas import tpu as pltpu
from jax.sharding import PartitionSpec as P

EDGE = 16
CAP = 8
BRICK = 4096
SLOTS = 72
KAPPA = 32.0
OMEGA = 0.8
KEEP = 1.0 - OMEGA

C = 32
NT = 8
F32 = jnp.float32
BF16 = jnp.bfloat16


def spread(level):
    return KAPPA / 4.0**level


def shifted(values, distance, axis):
    return pltpu.roll(values, distance % values.shape[axis], axis)


def iota(shape, dim):
    return lax.broadcasted_iota(jnp.int32, shape, dim)


def lanes(t):
    return slice(t * 128, (t + 1) * 128)


def plane(ref, p):
    count = ref.shape[2] // 128
    rows = ref.shape[1]
    lane = iota((rows, 128), 1)
    before, here = None, ref[p, :, lanes(0)]
    for t in range(count):
        after = ref[p, :, lanes(t + 1)] if t + 1 < count else None
        low = jnp.where(lane == 127, 0.0 if before is None else before, here)
        high = jnp.where(lane == 0, 0.0 if after is None else after, here)
        sums = shifted(low, 1, 1) + shifted(high, -1, 1)
        sums = sums + (shifted(here, 1, 0) + shifted(here, -1, 0))
        sums = sums + (ref[p - 1, :, lanes(t)] + ref[p + 1, :, lanes(t)])
        yield t, here, sums
        before, here = here, after


def loop(start, stop, body, unroll=1):
    def step(i, carry):
        body(i)
        return carry

    lax.fori_loop(start, stop, step, 0, unroll=unroll)


def split_dot(a, b):
    high = a.astype(BF16)
    low = (a - high.astype(F32)).astype(BF16)
    return jnp.dot(high, b, preferred_element_type=F32) + jnp.dot(low, b, preferred_element_type=F32)


def pooling():
    return jnp.where(iota((256, 128), 0) // 2 == iota((256, 128), 1), 0.125, 0.0).astype(BF16)


def doubling():
    return jnp.where(iota((128, 256), 1) // 2 == iota((128, 256), 0), 1.0, 0.0).astype(BF16)


def halve_rows(values, rs, t):
    rows = values.shape[0]
    rs[t, 0:rows, :] = values
    return rs[t, pl.ds(0, rows // 2, stride=2), :] + rs[t, pl.ds(1, rows // 2, stride=2), :]


def halve_lanes(xp, planes, rows):
    matrix = pooling()
    tiles = []
    for t in range(0, xp.shape[0], 2):
        pair = jnp.concatenate([xp[t].reshape(planes * rows, 128), xp[t + 1].reshape(planes * rows, 128)], axis=1)
        tiles.append(split_dot(pair, matrix).reshape(planes, rows, 128))
    return tiles


def inside(shape, dim, first, wrap, index, size, count):
    place = iota(shape, dim) + first
    if wrap is not None:
        place = jnp.where(place < wrap, place, place - shape[dim])
    place = place + index * size
    return (place >= 0) & (place < count * size)


BLOCK = 272
FIRST_ROWS = BLOCK + 3 * 64


def uptake_part(t):
    return slice(BLOCK + 64 * (t // 3), BLOCK + 64 * (t // 3) + 64), lanes(t % 3)


def transposed_bricks(bricks_x, ids, counts, bricks, xs, targets):
    xs[...] = bricks[...].astype(F32)
    row = iota((1, 8, 128), 1)
    group = iota((1, 8, 128), 2) // 16
    group16 = iota((16, 128), 1) // 16
    per_y = 64

    def block(j, out, part):
        start = pl.multiple_of(j * 8, 8)
        x = jnp.stack([xs[pl.ds(start, 8), lanes(k)] for k in range(32)])
        for s in (4, 2, 1):
            up = shifted(shifted(x, -s, 1), 16 * s, 2)
            down = shifted(shifted(x, s, 1), -16 * s, 2)
            row_bit = (row // s) % 2
            group_bit = (group // s) % 2
            x = jnp.where(row_bit == group_bit, x, jnp.where(row_bit == 0, up, down))
        x = jnp.where(group < counts[0, j], x, 0.0)
        out[0:256, part] = x.reshape(256, 128).astype(BF16)
        names = jnp.zeros((16, 128), jnp.int32)
        for e in range(CAP):
            number = ids[j * 8 + e]
            by = lax.rem(number, per_y)
            rest = lax.div(number, per_y)
            bx = lax.rem(rest, 2)
            bz = lax.rem(lax.div(rest, bricks_x), 2)
            names = jnp.where(group16 == e, (bz * 2 + bx) * per_y + by, names)
        out[256:272, part] = names.astype(F32).astype(BF16)

    for i, out in enumerate(targets):
        for d in range(3):
            block(3 * i + d, out, lanes(d))


def first_kernel(bricks_x, ids, counts, bricks, uptake, own, zl, zh, xs, edges, sems):
    copies = [pltpu.make_async_copy(uptake.at[pl.ds(30 * i, 2)], edges.at[i], sems.at[i]) for i in range(2)]
    for copy in copies:
        copy.start()
    transposed_bricks(bricks_x, ids, counts, bricks, xs, (zl, own, zh))
    for i, ref in enumerate((zl, zh)):
        copies[i].wait()
        for t in range(8):
            ref[uptake_part(t)] = edges[i, :, :, lanes(t)].reshape(64, 128).astype(BF16)
        ref[uptake_part(8)] = jnp.zeros((64, 128), BF16)


def rates_kernel(uptake, r1, r2, xl, xh, rs, xp, rs1, xp1):
    def pair(m):
        for t in range(NT):
            both = uptake[2 * m, :, lanes(t)] + uptake[2 * m + 1, :, lanes(t)]
            xp[t, m] = halve_rows(both, rs, t)

    loop(0, 16, pair)
    for t, tile in enumerate(halve_lanes(xp, 16, 16)):
        r1[:, :, lanes(t)] = tile

    def pair1(m):
        for t in range(4):
            both = r1[2 * m, :, lanes(t)] + r1[2 * m + 1, :, lanes(t)]
            xp1[t, m] = halve_rows(both, rs1, t)

    loop(0, 8, pair1)
    for t, tile in enumerate(halve_lanes(xp1, 8, 8)):
        r2[:, lanes(t)] = tile.reshape(64, 128)

    sub = iota((8, 1024), 0)

    def columns(i):
        lows, highs = [], []
        for j in range(2):
            low, high = jnp.zeros((8, 1024), F32), jnp.zeros((8, 1024), F32)
            for n in range(4):
                z = 8 * i + 4 * j + n
                low = jnp.where(sub // 2 == n, shifted(uptake[z, 0:8, :], 2 * n, 0), low)
                high = jnp.where(sub // 2 == n, shifted(uptake[z, 24:32, :], 2 * n + 2, 0), high)
            lows.append(low)
            highs.append(high)
        rows = pl.ds(pl.multiple_of(16 * i, 16), 16)
        xl[rows, :] = jnp.concatenate(lows, axis=0).astype(BF16)
        xh[rows, :] = jnp.concatenate(highs, axis=0).astype(BF16)

    loop(0, 4, columns)


def far_along_z(nz, iz, to_low, to_high):
    if nz != 4:
        return to_low, to_high
    one = jnp.where(iz < 2, to_high, to_low)
    return one, one


def halves(sub, first, second):
    return jnp.where(sub < 4, first, shifted(second, 4, 1))


def uppers(sub, first, second):
    return jnp.where(sub < 4, shifted(first, 4, 1), second)


def far_messages(window):
    planes, _, width = window.shape
    pairs = window.reshape(planes // 2, 2, 8, width)
    sub = iota((planes // 2, 8, width), 1)
    size = (planes * 4, width)
    return halves(sub, pairs[:, 0], pairs[:, 1]).reshape(size), uppers(sub, pairs[:, 0], pairs[:, 1]).reshape(size)


def far_tile(from_low, from_high):
    width = from_low.shape[-1]
    low, high = from_low.reshape(-1, 8, width), from_high.reshape(-1, 8, width)
    sub = iota(low.shape, 1)
    even = jnp.where(sub < 4, high, shifted(low, 4, 1))
    odd = jnp.where(sub < 4, shifted(high, 4, 1), low)
    return jnp.stack([even, odd], axis=1).reshape(-1, 8, width)


def first_x_kernel(own, uxl, uxh, zl, zh, xl, xh):
    for ref, d in ((xl, 0), (xh, 2)):
        for n, src in enumerate((own, zl, zh)):
            ref[0:BLOCK, lanes(n)] = src[0:BLOCK, lanes(d)]
    sub = iota((8, 128), 0)
    lows, highs = [], []
    for t in range(8):
        xl[uptake_part(t)] = uxl[:, lanes(t)]
        xh[uptake_part(t)] = uxh[:, lanes(t)]
        both = [ref[uptake_part(t)].astype(F32) for ref in (zl, zh)]
        planes = [both[0][0:32], both[0][32:64], both[1][0:32], both[1][32:64]]
        to_low, to_high = jnp.zeros((8, 128), F32), jnp.zeros((8, 128), F32)
        for n, p in enumerate(planes):
            here = sub // 2 == n
            to_low = jnp.where(here, shifted(p[0:8], 2 * n, 0), to_low)
            to_high = jnp.where(here, shifted(p[24:32], 2 * n + 2, 0), to_high)
        lows.append(to_low)
        highs.append(to_high)
    xl[uptake_part(8)] = jnp.concatenate(lows, axis=0).astype(BF16)
    xh[uptake_part(8)] = jnp.concatenate(highs, axis=0).astype(BF16)


def window_planes(own, low, high, low2, high2):
    parts = (low2, low, own, high, high2)
    return jnp.concatenate([a.reshape(-1, 8, 256) for a in parts], axis=0)


def source_window_kernel(own, low, high, low2, high2, r2, zl, zh, f2, q2, near, fl, fh):
    planes = window_planes(own[...], low[...], high[...], low2[0:32, :], high2[0:32, :])
    f2[...] = planes
    below, above = [ref[80:144, 512:768].astype(F32) for ref in (zl, zh)]
    rates = window_planes(r2[...], below, above, low2[32:64, :], high2[32:64, :])
    q2[...] = rates
    near[0:256, :] = planes.reshape(256, 256).astype(BF16)
    near[256:320, :] = jnp.concatenate([low2[32:64, :], high2[32:64, :]], axis=0).astype(BF16)
    for i, values in enumerate((planes, rates)):
        to_low, to_high = far_messages(values)
        fl[128 * i : 128 * i + 128, :] = to_low.astype(BF16)
        fh[128 * i : 128 * i + 128, :] = to_high.astype(BF16)


O = 5
Q = 2
BASE = 1.0 + 6.0 * KAPPA


def spots(blocks, hot):
    lane = iota((1, 128), 1)
    at_y = iota((1024, 128), 0)
    tiles = []
    for i, (ref, part) in enumerate(blocks):
        name = ref[256:272, part].astype(F32).astype(jnp.int32)[0:1]
        tiles.append(lax.shift_right_logical(name, 6))
        y = (name & 63) * 16 + (lane & 15)
        hot[:, lanes(i)] = jnp.where(at_y == y, 1.0, 0.0).astype(BF16)
    return tiles


def scatter(blocks, hot):
    tiles = spots(blocks, hot)
    for tile in range(4):
        bz, bx = tile // 2, tile % 2
        left = [
            jnp.where(tiles[i] == tile, ref[0:256, part].astype(F32), 0.0).astype(BF16)
            for i, (ref, part) in enumerate(blocks)
        ]
        left = jnp.concatenate(left, axis=1)
        for n in range(4):
            cols = slice(n * 256, (n + 1) * 256)
            sums = lax.dot_general(left, hot[cols, :], (((1,), (1,)), ((), ())), preferred_element_type=F32)
            yield 16 * bz, slice(16 * bx, 16 * bx + 16), cols, sums.reshape(16, 16, 256)


def sweep(src, dst, source, gg, z, sourced):
    for t, here, sums in plane(src, z + O):
        inner = KAPPA * sums
        g = gg[z + Q, :, lanes(t)]
        if sourced:
            body = inner[0:32] + source[z, :, lanes(t)]
            dst[z + O, 0:32, lanes(t)] = KEEP * here[0:32] + g[0:32] * body
            dst[z + O, 32:40, lanes(t)] = KEEP * here[32:40] + g[32:40] * inner[32:40]
        else:
            dst[z + O, :, lanes(t)] = KEEP * here + g * inner


def own_kernel(
    nz, info, own, zl, zh, density, uptake, s_out, g_out, v_out, edge_out,
    dens, upt, s0, g0, v1, edge, va, hot, sems,
):
    iz = info[0]
    loads = [pltpu.make_async_copy(density, dens, sems.at[0]), pltpu.make_async_copy(uptake, upt, sems.at[1])]
    stores = [
        pltpu.make_async_copy(src, dst, sems.at[2 + i])
        for i, (src, dst) in enumerate(((s0, s_out), (g0, g_out), (v1, v_out), (edge, edge_out)))
    ]
    for copy in loads:
        copy.start()
    for p in (3, 4, 37, 38):
        va[p] = jnp.zeros((40, 1024), F32)
    for n in range(4):
        ref, valid = (zl, iz > 0) if n < 2 else (zh, iz < nz - 1)
        q = n if n < 2 else 32 + n
        rows = slice(32 * (n % 2), 32 * (n % 2) + 32)
        for t in range(NT):
            g0[q, :, lanes(t)] = jnp.where(valid, OMEGA, 0.0) / (ref[uptake_part(t)].astype(F32)[rows] + BASE)

    blocks = [(ref, lanes(1)) for ref in (own, zl, zh)]
    waiting = list(loads[0:1])
    for z, rows, cols, sums in scatter(blocks, hot):
        while waiting:
            waiting.pop().wait()
        planes = slice(z, z + 16)
        s0[planes, rows, cols] = dens[planes, rows, cols] + sums
    stores[0].start()
    loads[1].wait()

    def own_plane(z):
        va[z + O, 0:32, :] = dens[z]
        va[z + O, 32:40, :] = jnp.zeros((8, 1024), F32)
        g0[z + Q] = OMEGA / (upt[z] + BASE)

    loop(0, C, own_plane)
    stores[1].start()

    def first(z):
        for t, here, sums in plane(va, z + O):
            inner = KAPPA * sums
            body = inner[0:32] + s0[z, :, lanes(t)]
            v1[z + 1, :, lanes(t)] = KEEP * here[0:32] + g0[z + Q, :, lanes(t)] * body
            edge[z, :, lanes(t)] = inner[32:40]

    loop(0, C, first, 2)
    for z in (-1, C):
        for t in range(NT):
            near = va[z + O + (1 if z < 0 else -1), 0:32, lanes(t)]
            v1[z + 1, :, lanes(t)] = g0[z + Q, :, lanes(t)] * (KAPPA * near)
    for copy in stores[2:]:
        copy.start()
    for copy in stores:
        copy.wait()


def pre_kernel(
    nz, nx, info, xl, xh, zl, zh, r1, r2, s0, g0, v1, edge_in, uptake,
    c1, mzl, mzh, vzl, vzh, pxl, pxh, v_out, g_out, s_out,
    va, vb, supply, upt, dh, gg, edge, hot, rs, xp, usl, ush, sems,
):
    iz, ix = info[0], info[1]
    k = KAPPA
    loads = [
        pltpu.make_async_copy(src, dst, sems.at[i])
        for i, (src, dst) in enumerate(
            (
                (s0, supply),
                (v1, vb.at[4:38, 0:32, :]),
                (g0, gg.at[:, 0:32, :]),
                (edge_in, edge),
                (uptake, upt),
            )
        )
    ]
    for copy in loads:
        copy.start()

    for p in (1, 2, 39, 40):
        va[p] = jnp.zeros((40, 1024), F32)
    for p in (2, 3, 38, 39):
        vb[p] = jnp.zeros((40, 1024), F32)
    for p in (4, 37):
        vb[p, 32:40, :] = jnp.zeros((8, 1024), F32)

    sub8 = iota((8, 1024), 0)
    for t in range(NT):
        usl[0:64, lanes(t)] = xl[uptake_part(t)].astype(F32)
        ush[0:64, lanes(t)] = xh[uptake_part(t)].astype(F32)
        usl[64:72, lanes(t)] = xl[uptake_part(8)].astype(F32)[8 * t : 8 * t + 8]
        ush[64:72, lanes(t)] = xh[uptake_part(8)].astype(F32)[8 * t : 8 * t + 8]

    def set_halo(q, low, high, valid_z):
        gz = jnp.where(valid_z, OMEGA, 0.0)
        d = jnp.where(sub8 < 2, high, jnp.where(sub8 >= 6, low, 0.0)) + BASE
        dh[q] = d
        omega = jnp.where(sub8 < 2, jnp.where(ix < nx - 1, gz, 0.0), jnp.where(sub8 >= 6, jnp.where(ix > 0, gz, 0.0), 0.0))
        gg[q, 32:40, :] = omega / d

    def halos(i):
        rows = pl.ds(pl.multiple_of(8 * i, 8), 8)
        low, high = usl[rows, :], ush[rows, :]
        for n in range(4):
            set_halo(4 * i + n + Q, shifted(low, 6 - 2 * n, 0), shifted(high, -2 * n, 0), True)

    loop(0, C // 4, halos)
    low, high = usl[64:72, :], ush[64:72, :]
    for n in range(4):
        exists = iz > 0 if n < 2 else iz < nz - 1
        set_halo(n if n < 2 else 32 + n, shifted(low, 6 - 2 * n, 0), shifted(high, -2 * n, 0), exists)

    blocks = [(ref, lanes(n)) for ref in (xl, xh) for n in range(3)]
    waiting = list(loads[0:3])
    for z, rows, cols, sums in scatter(blocks, hot):
        while waiting:
            waiting.pop().wait()
        supply[z : z + 16, rows, cols] = supply[z : z + 16, rows, cols] + sums
        g = gg[z + Q : z + Q + 16, rows, cols]
        vb[z + O : z + O + 16, rows, cols] = vb[z + O : z + O + 16, rows, cols] + g * sums
    loads[3].wait()

    s_copy = pltpu.make_async_copy(supply, s_out, sems.at[7])
    s_copy.start()

    def edges(z):
        vb[z + O, 32:40, :] = gg[z + Q, 32:40, :] * edge[z]

    loop(0, C, edges)

    loop(0, C, lambda z: sweep(vb, va, supply, gg, z, True), 2)
    loop(0, 4, lambda i: sweep(vb, va, supply, gg, jnp.where(i < 2, i - 2, i + C - 2), False))
    loads[4].wait()
    v_copy = pltpu.make_async_copy(va.at[3:39], v_out, sems.at[5])
    g_copy = pltpu.make_async_copy(gg, g_out, sems.at[6])
    v_copy.start()
    g_copy.start()

    def residual(z, rates, sourced):
        for t, here, sums in plane(va, z + O):
            r = k * sums
            if rates is not None:
                inner = r[0:32] - (rates(t) + BASE) * here[0:32]
                if sourced:
                    inner = inner + supply[z, :, lanes(t)]
                r = jnp.concatenate([inner, r[32:40] - dh[z + Q, :, lanes(t)] * here[32:40]], axis=0)
            yield t, r

    def coarse(m, zs, rates, sourced):
        parts = [residual(zs[i], rates[i], sourced) for i in range(2)]
        for (t, first), (_, second) in zip(*parts):
            xp[t, m, 0:20, :] = halve_rows(first + second, rs, t)

    def from_message(ref, n):
        return lambda t: ref[uptake_part(t)].astype(F32)[32 * n : 32 * n + 32]

    def inner(m):
        zs = (2 * m - 4, 2 * m - 3)
        coarse(m, zs, [lambda t, z=z: upt[z, :, lanes(t)] for z in zs], True)

    loop(2, 18, inner)
    for m, ref, z in ((1, zl, -2), (18, zh, C)):
        coarse(m, (z, z + 1), [from_message(ref, 0), from_message(ref, 1)], False)

    def outer(i):
        for t, r in residual(jnp.where(i == 0, -3, 34), None, False):
            xp[t, 19 * i, 0:20, :] = halve_rows(r, rs, t)

    loop(0, 2, outer)

    sub = iota((20, 8, 128), 1)
    for t, tile in enumerate(halve_lanes(xp, 20, 24)):
        last = tile[:, 16:24]
        last = jnp.where(sub < 2, last, jnp.where(sub >= 6, shifted(last, 4, 1), 0.0))
        c1[:, 0:16, lanes(t)] = tile[:, 0:16]
        c1[:, 16:24, lanes(t)] = last

    empty = jnp.zeros((1, 8, 1024), F32)
    blank = jnp.zeros((8, 1024), F32)
    edges = (
        (mzl, vzl, slice(0, 6), slice(0, 4), 3, 0),
        (mzh, vzh, slice(14, 20), slice(12, 16), 35, 31),
    )
    for ref, level0, planes, rates, p, z in edges:
        source = c1[planes].reshape(144, 512)
        ref[0:80, 0:512] = source[0:80].astype(BF16)
        ref[0:64, 512:1024] = source[80:144].astype(BF16)
        ref[64:80, 512:1024] = jnp.zeros((16, 512), BF16)
        ref[80:144, 0:512] = r1[rates].reshape(64, 512).astype(BF16)
        ref[80:144, 512:768] = r2[...].astype(BF16)
        corner = jnp.concatenate([pack_low(va[p], va[p + 1]), pack_low(va[p + 2], va[p + 3])], axis=0).astype(BF16)
        for n in range(4):
            ref[80 + 16 * n : 96 + 16 * n, 768:1024] = corner[:, n * 256 : n * 256 + 256]
        corner = jnp.concatenate([pack_high(va[p], va[p + 1]), pack_high(va[p + 2], va[p + 3])], axis=0).astype(BF16)
        ref[144:160, :] = corner
        values = jnp.concatenate([va[p : p + 4], jnp.concatenate([supply[z : z + 1], empty], axis=1)], axis=0)
        level0[...] = jnp.concatenate([values.reshape(200, 1024), blank], axis=0).astype(BF16)

    def sides(i):
        lows, highs = [], []
        for j in range(2):
            p = 4 * i + 2 * j + 3
            lows.append(pack_low(va[p], va[p + 1]))
            highs.append(pack_high(va[p], va[p + 1]))
        rows = pl.ds(pl.multiple_of(16 * i, 16), 16)
        pxl[rows, :] = jnp.concatenate(lows, axis=0).astype(BF16)
        pxh[rows, :] = jnp.concatenate(highs, axis=0).astype(BF16)

    loop(0, 9, sides)

    def sources(i):
        lows, highs = [], []
        for j in range(2):
            low, high = jnp.zeros((8, 1024), F32), jnp.zeros((8, 1024), F32)
            for n in range(8):
                z = 16 * i + 8 * j + n
                low = jnp.where(sub8 == n, shifted(supply[z, 0:8, :], n, 0), low)
                high = jnp.where(sub8 == n, shifted(supply[z, 24:32, :], n + 1, 0), high)
            lows.append(low)
            highs.append(high)
        rows = pl.ds(pl.multiple_of(16 * i + 144, 16), 16)
        pxl[rows, :] = jnp.concatenate(lows, axis=0).astype(BF16)
        pxh[rows, :] = jnp.concatenate(highs, axis=0).astype(BF16)

    loop(0, 2, sources)
    v_copy.wait()
    g_copy.wait()
    s_copy.wait()


def outer_rows(sub):
    return (sub < 2) | (sub >= 6)


def pack_pair(sub, a, b):
    return jnp.where(outer_rows(sub), a, shifted(b, 4, 0))


def pack_low(first, second):
    sub = iota((8, 1024), 0)
    a, b = [jnp.where(sub < 4, v[0:8], v[32:40]) for v in (first, second)]
    return pack_pair(sub, a, b)


def pack_high(first, second):
    sub = iota((8, 1024), 0)
    a, b = [jnp.where(sub >= 4, v[24:32], v[32:40]) for v in (first, second)]
    return pack_pair(sub, a, b)


def sides_kernel(pxl, pxh, mzl, mzh, r2, out_l, out_h):
    for ref, out in ((pxl, out_l), (pxh, out_h)):
        out[0:176, :] = ref[...]
        for n, rates in enumerate((mzl[80:144, 512:768], r2[...].astype(BF16), mzh[80:144, 512:768])):
            out[176:240, n * 256 : n * 256 + 256] = rates
        out[176:240, 768:1024] = jnp.zeros((64, 256), BF16)
    for message, start in ((mzl, 0), (mzh, 128)):
        low = jnp.concatenate([message[80 + 16 * n : 96 + 16 * n, 768:1024] for n in range(4)], axis=1)
        rows = slice(start, start + 16)
        for ref, out, corner in ((pxl, out_l, low), (pxh, out_h, message[144:160, :])):
            out[rows, :] = (ref[rows, :].astype(F32) + corner.astype(F32)).astype(BF16)


def in_three(sub, tiles, free, turns):
    spare = (sub == free) | (sub == free + 1)
    last = tiles[:, 3]
    parts = [jnp.where(spare, shifted(last, turn, 1), tiles[:, i]) for i, turn in enumerate(turns)]
    return jnp.stack(parts, axis=1)


def out_of_three(sub, parts, free, turns):
    last = None
    for i, turn in enumerate(turns):
        back = shifted(parts[:, i], -turn, 1)
        home = (free - turn) % 8
        here = (sub == home) | (sub == home + 1)
        last = jnp.where(here, back, 0.0 if last is None else last)
    return jnp.stack([parts[:, 0], parts[:, 1], parts[:, 2], last], axis=1)


HIGH_PACK = (2, (-2, 4, 2))
LOW_PACK = (4, (-2, 4, 2))


def merge_kernel(c1, r1, mzl, mzh, f1, q1, mxl, mxh):
    zeros = jnp.zeros((24, 512), F32)
    for p in (0, 1, 22, 23):
        f1[p] = zeros
    f1[2:22] = c1[...]
    for ref, planes in ((mzl, slice(0, 6)), (mzh, slice(18, 24))):
        parts = [ref[0:80, 0:512].astype(F32), ref[0:64, 512:1024].astype(F32)]
        f1[planes] = f1[planes] + jnp.concatenate(parts, axis=0).reshape(6, 24, 512)
    sub = iota((6, 8, 512), 1)
    first, last, halo = [f1[:, 8 * n : 8 * n + 8].reshape(6, 4, 8, 512) for n in range(3)]
    sub4 = iota((6, 4, 8, 512), 2)
    to_high = in_three(sub, jnp.where(sub4 >= 4, last, halo), *HIGH_PACK)
    to_low = in_three(sub, jnp.where(sub4 >= 4, halo, first), *LOW_PACK)
    mxh[0:144, :] = to_high.reshape(144, 512).astype(BF16)
    mxl[0:144, :] = to_low.reshape(144, 512).astype(BF16)
    q1[0:4] = mzl[80:144, 0:512].astype(F32).reshape(4, 16, 512)
    q1[4:20] = r1[...]
    q1[20:24] = mzh[80:144, 0:512].astype(F32).reshape(4, 16, 512)
    sub1 = iota((12, 8, 512), 1)
    first = q1[:, 0:8, :].reshape(12, 2, 8, 512)
    last = q1[:, 8:16, :].reshape(12, 2, 8, 512)
    mxl[144:240, :] = halves(sub1, first[:, 0], first[:, 1]).reshape(96, 512).astype(BF16)
    mxh[144:240, :] = uppers(sub1, last[:, 0], last[:, 1]).reshape(96, 512).astype(BF16)


def middle_kernel(nz, nx, info, f0, q_in, r2, mxl, mxh, f1, g1, v1, g2, g2l, g2h, q0, va, rs, xp):
    iz, ix = info[0], info[1]
    k = spread(1)
    base = 1.0 + 6.0 * k
    sub6 = iota((6, 8, 512), 1)
    low = out_of_three(sub6, mxl[0:144, :].astype(F32).reshape(6, 3, 8, 512), *HIGH_PACK).reshape(24, 8, 512)
    high = out_of_three(sub6, mxh[0:144, :].astype(F32).reshape(6, 3, 8, 512), *LOW_PACK).reshape(24, 8, 512)
    sub = iota((24, 8, 512), 1)
    f1[:, 0:8] = f0[:, 0:8] + jnp.where(sub < 2, low, 0.0)
    f1[:, 8:16] = f0[:, 8:16] + jnp.where(sub >= 6, high, 0.0)
    f1[:, 16:24] = f0[:, 16:24] + jnp.where(sub >= 4, low, high)
    low, high = [ref[144:240, :].astype(F32).reshape(12, 8, 512) for ref in (mxl, mxh)]
    sub12 = iota((12, 8, 512), 1)
    even = jnp.where(sub12 >= 4, shifted(low, 4, 1), high)
    odd = jnp.where(sub12 >= 4, low, shifted(high, 4, 1))
    q0[:, 0:16] = q_in[...]
    q0[:, 16:24] = jnp.stack([even, odd], axis=1).reshape(24, 8, 512)
    shape = (24, 24, 128)
    valid = inside(shape, 0, -4, None, iz, 16, nz) & inside(shape, 1, 0, 20, ix, 16, nx)
    for t in range(4):
        g = jnp.where(valid, OMEGA, 0.0) / (q0[:, :, lanes(t)] + base)
        g1[:, :, lanes(t)] = g
        va[:, :, lanes(t)] = g * f1[:, :, lanes(t)]
    v1[0] = va[0]
    v1[23] = va[23]

    def sweep(p):
        for t, here, sums in plane(va, p):
            v1[p, :, lanes(t)] = KEEP * here + g1[p, :, lanes(t)] * (f1[p, :, lanes(t)] + k * sums)

    loop(1, 23, sweep, 2)

    def residual(p):
        for t, here, sums in plane(v1, p):
            yield t, f1[p, :, lanes(t)] + k * sums - (q0[p, :, lanes(t)] + base) * here

    def coarse(m):
        for (t, first), (_, second) in zip(residual(2 * m + 4), residual(2 * m + 5)):
            xp[t, m] = halve_rows((first + second)[0:16], rs, t)

    loop(0, 8, coarse)
    for t, tile in enumerate(halve_lanes(xp, 8, 8)):
        g2[:, lanes(t)] = tile.reshape(64, 128)
        low, high = far_along_z(nz, iz, tile[0:4].reshape(32, 128), tile[4:8].reshape(32, 128))
        g2l[0:32, lanes(t)] = low
        g2h[0:32, lanes(t)] = high
    low, high = far_along_z(nz, iz, r2[0:32, :], r2[32:64, :])
    g2l[32:64, :] = low
    g2h[32:64, :] = high


def back_kernel(
    nz, nx, info, f1, g1, v1, vzl, vzh, vxl, vxh, own2, n2l, n2h, m2l, m2h, q_own, v_in, g_in, s_in,
    out_hbm,
    f2, q2, h2, a2, b2, rs, xp, xpr, wa, w1, zsl, zsh, vb, ws,
    v2, gg, supply, fsl, fsh, out, sems,
):
    iz, ix = info[0], info[1]
    matrix = doubling()
    level0 = [
        pltpu.make_async_copy(src, dst, sems.at[i])
        for i, (src, dst) in enumerate(((v_in, v2), (g_in, gg), (s_in, supply)))
    ]
    for copy in level0:
        copy.start()

    f2[:, 0:8, :] = own2[...]
    f2[:, 8:16, :] = n2h[0:256, :].astype(F32).reshape(32, 8, 256)
    f2[:, 16:24, :] = far_tile(m2l[0:128, :].astype(F32), m2h[0:128, :].astype(F32))
    f2[:, 24:32, :] = n2l[0:256, :].astype(F32).reshape(32, 8, 256)
    q2[:, 0:8, :] = q_own[...]
    q2[:, 16:24, :] = far_tile(m2l[128:256, :].astype(F32), m2h[128:256, :].astype(F32))
    for ref, rows in ((vxh, slice(8, 16)), (vxl, slice(24, 32))):
        for n in range(3):
            q2[8 * n + 4 : 8 * n + 12, rows, :] = ref[176:240, n * 256 : n * 256 + 256].astype(F32).reshape(8, 8, 256)
    for ref, rows in ((n2h, slice(8, 16)), (n2l, slice(24, 32))):
        outer = ref[256:320, :].astype(F32).reshape(8, 8, 256)
        q2[0:4, rows, :] = outer[0:4]
        q2[28:32, rows, :] = outer[4:8]

    k = spread(2)
    base = 1.0 + 6.0 * k
    shape = (32, 32, 128)
    valid = inside(shape, 0, -12, None, iz, 8, nz) & inside(shape, 1, 0, 20, ix, 8, nx)
    for t in range(2):
        g = jnp.where(valid, OMEGA, 0.0) / (q2[:, :, lanes(t)] + base)
        h2[:, :, lanes(t)] = g
        a2[:, :, lanes(t)] = g * f2[:, :, lanes(t)]
    b2[0] = a2[0]
    b2[31] = a2[31]

    def sweep2(src, dst):
        def body(p):
            for t, here, sums in plane(src, p):
                dst[p, :, lanes(t)] = KEEP * here + h2[p, :, lanes(t)] * (f2[p, :, lanes(t)] + k * sums)

        return body

    loop(1, 31, sweep2(a2, b2), 2)

    def coarse(m):
        total, rates = [0.0, 0.0], [0.0, 0.0]
        for j in range(2):
            p = 2 * m + j
            for t, here, sums in plane(b2, p):
                r = f2[p, :, lanes(t)] + k * sums - (q2[p, :, lanes(t)] + base) * here
                total[t] = total[t] + r
                rates[t] = rates[t] + q2[p, :, lanes(t)]
        for t in range(2):
            xp[t, m] = halve_rows(total[t], rs, t)
            xpr[t, m] = halve_rows(rates[t], rs, t + 2)

    for t in range(2):
        for m in (0, 15):
            xp[t, m] = jnp.zeros((16, 128), F32)
            xpr[t, m] = jnp.zeros((16, 128), F32)
    loop(1, 15, coarse)

    shape = (16, 16, 128)
    valid = inside(shape, 0, -6, None, iz, 4, nz) & inside(shape, 1, 0, 10, ix, 4, nx)
    k3 = spread(3)
    (source,) = halve_lanes(xp, 16, 16)
    (rates,) = halve_lanes(xpr, 16, 16)
    g = jnp.where(valid, OMEGA, 0.0) / (rates + (1.0 + 6.0 * k3))
    v = g * source
    lane = iota(shape, 2)
    for repeat in range(3):
        edge = jnp.zeros((1, 16, 128), F32)
        sums = jnp.concatenate([v[1:], edge], axis=0) + jnp.concatenate([edge, v[:-1]], axis=0)
        sums = sums + shifted(v, 1, 1) + shifted(v, -1, 1)
        sums = sums + jnp.where(lane == 0, 0.0, shifted(v, 1, 2)) + jnp.where(lane == 127, 0.0, shifted(v, -1, 2))
        v = KEEP * v + g * (source + k3 * sums)

    wide = split_dot(v[4:12].reshape(128, 128), matrix).reshape(8, 16, 256)
    for m in range(8):
        for t in range(2):
            part = wide[m, :, lanes(t)]
            rs[t, pl.ds(0, 16, stride=2), :] = part
            rs[t, pl.ds(1, 16, stride=2), :] = part
            for j in range(2):
                p = 8 + 2 * m + j
                b2[p, :, lanes(t)] = b2[p, :, lanes(t)] + rs[t, 0:32, :]
    loop(9, 23, sweep2(b2, a2), 2)
    loop(10, 22, sweep2(a2, b2), 2)

    w = b2[10:22]
    near, far = w[:, 8:16], w[:, 24:32]
    near = jnp.where(iota((12, 8, 256), 1) < 2, near, shifted(far, 4, 1))
    w = jnp.concatenate([w[:, 0:8], near], axis=1).reshape(192, 256)
    wide = [split_dot(w[:, lanes(t)], matrix) for t in range(2)]
    wide = jnp.concatenate(wide, axis=1).reshape(12, 16, 512)
    for m in range(12):
        for t in range(4):
            part = wide[m, :, lanes(t)]
            rs[t, pl.ds(0, 16, stride=2), :] = part
            rs[t, pl.ds(1, 16, stride=2), :] = part
            for j in range(2):
                p = 2 * m + j
                wa[p, :, lanes(t)] = v1[p, :, lanes(t)] + rs[t, 0:24, :]
    k1 = spread(1)

    def sweep1(src, dst):
        def body(p):
            for t, here, sums in plane(src, p):
                dst[p, :, lanes(t)] = KEEP * here + g1[p, :, lanes(t)] * (f1[p, :, lanes(t)] + k1 * sums)

        return body

    loop(2, 22, sweep1(wa, w1), 2)
    loop(3, 21, sweep1(w1, wa), 2)

    sub = iota((18, 8, 128), 1)
    for t in range(4):
        halo = wa[3:21, 16:24, lanes(t)]
        halo = jnp.where(sub < 2, halo, shifted(halo, 4, 1))
        w = jnp.concatenate([wa[3:21, 0:16, lanes(t)], halo], axis=1)
        ws[:, :, t * 256 : t * 256 + 256] = split_dot(w.reshape(432, 128), matrix).reshape(18, 24, 256)

    for copy in level0:
        copy.wait()
    zsl[...] = vzl[...].astype(F32)
    zsh[...] = vzh[...].astype(F32)
    for i in range(4):
        v2[i] = v2[i] + zsl[40 * i : 40 * i + 40, :]
        v2[32 + i] = v2[32 + i] + zsh[40 * i : 40 * i + 40, :]

    s8 = iota((8, 128), 0)

    outer = outer_rows(s8)

    def correct(i):
        rows = pl.ds(pl.multiple_of(16 * i, 16), 16)
        for t in range(NT):
            low = vxl[rows, lanes(t)].astype(F32)
            high = vxh[rows, lanes(t)].astype(F32)
            for n in range(2):
                part = ws[2 * i + n, :, lanes(t)]
                rs[t, pl.ds(0, 24, stride=2), :] = part
                rs[t, pl.ds(1, 24, stride=2), :] = part
                for j in range(2):
                    p = 4 * i + 2 * n + j
                    lo, hi = low[8 * n : 8 * n + 8], high[8 * n : 8 * n + 8]
                    if j:
                        lo, hi = shifted(lo, 4, 0), shifted(hi, 4, 0)
                    v2[p, 0:8, lanes(t)] = v2[p, 0:8, lanes(t)] + rs[t, 0:8, :] + jnp.where(s8 < 2, lo, 0.0)
                    v2[p, 8:24, lanes(t)] = v2[p, 8:24, lanes(t)] + rs[t, 8:24, :]
                    v2[p, 24:32, lanes(t)] = v2[p, 24:32, lanes(t)] + rs[t, 24:32, :] + jnp.where(s8 >= 6, hi, 0.0)
                    extra = jnp.where(outer, jnp.where(s8 >= 4, lo, hi), 0.0)
                    v2[p, 32:40, lanes(t)] = v2[p, 32:40, lanes(t)] + rs[t, 32:40, :] + extra

    loop(0, 9, correct)
    k0 = spread(0)

    def first(i):
        rows = pl.ds(pl.multiple_of(16 * i + 144, 16), 16)
        for t in range(NT):
            fsl[:, lanes(t)] = vxl[rows, lanes(t)].astype(F32)
            fsh[:, lanes(t)] = vxh[rows, lanes(t)].astype(F32)

        def step(j):
            z = 16 * i + j
            start = pl.multiple_of((j // 8) * 8, 8)
            turn = lax.rem(j, 8)
            for t, here, sums in plane(v2, z + 2):
                lo = pltpu.roll(fsl[pl.ds(start, 8), lanes(t)], 7 - turn, 0)
                hi = pltpu.roll(fsh[pl.ds(start, 8), lanes(t)], lax.rem(8 - turn, 8), 0)
                f = jnp.where(s8 == 7, lo, jnp.where(s8 == 0, hi, 0.0))
                g = gg[z + 2, :, lanes(t)]
                inner = k0 * sums
                vb[z + 1, 0:32, lanes(t)] = KEEP * here[0:32] + g[0:32] * (supply[z, :, lanes(t)] + inner[0:32])
                vb[z + 1, 32:40, lanes(t)] = KEEP * here[32:40] + g[32:40] * (f + inner[32:40])

        loop(0, 16, step, 2)

    loop(0, 2, first)
    for p, ref in ((1, zsl), (34, zsh)):
        for t, here, sums in plane(v2, p):
            g = gg[p, :, lanes(t)]
            vb[p - 1, :, lanes(t)] = KEEP * here + g * (ref[160:200, lanes(t)] + k0 * sums)

    def second(z):
        for t, here, sums in plane(vb, z + 1):
            g = gg[z + 2, 0:32, lanes(t)]
            out[z, :, lanes(t)] = KEEP * here[0:32] + g * (supply[z, :, lanes(t)] + k0 * sums[0:32])

    stores = []
    for i in range(4):
        part = pl.ds(8 * i, 8)
        loop(8 * i, 8 * i + 8, second, 2)
        stores.append(pltpu.make_async_copy(out.at[part], out_hbm.at[part], sems.at[3 + i]))
        stores[i].start()
    for copy in stores:
        copy.wait()


VMEM = pl.BlockSpec(memory_space=pltpu.VMEM)
SMEM = pl.BlockSpec(memory_space=pltpu.SMEM)
ANY = pl.BlockSpec(memory_space=pl.ANY)


def call(kernel, outs, scratch, smem, args, out_specs=None, in_hbm=0):
    moved = sum(a.size * a.dtype.itemsize for a in list(args) + list(outs))
    return pl.pallas_call(
        kernel,
        out_shape=tuple(outs),
        in_specs=[SMEM] * smem + [VMEM] * (len(args) - smem - in_hbm) + [ANY] * in_hbm,
        out_specs=tuple(out_specs or [VMEM] * len(outs)),
        scratch_shapes=scratch,
        compiler_params=pltpu.CompilerParams(vmem_limit_bytes=58 * 2**20),
        cost_estimate=pl.CostEstimate(flops=20 * moved, bytes_accessed=moved, transcendentals=0),
    )(*args)


def shaped(shape, dtype=F32):
    return jax.ShapeDtypeStruct(shape, dtype)


def both_ways(to_low, to_high, axis, distance=1):
    count = lax.axis_size(axis)
    up = [(i, i + distance) for i in range(count - distance)]
    down = [(j, i) for i, j in up]
    return lax.ppermute(to_high, axis, up), lax.ppermute(to_low, axis, down)


def two_away(to_low, to_high):
    count = lax.axis_size("gz")
    if count != 4:
        return both_ways(to_low, to_high, "gz", 2)
    came = lax.ppermute(to_low, "gz", [(i, (i + 2) % 4) for i in range(4)])
    return came, came


def shards(density, uptake, brick_values, brick_ids, slot_counts):
    nz, nx = lax.axis_size("gz"), lax.axis_size("xy")
    info = jnp.stack([lax.axis_index("gz"), lax.axis_index("xy")]).astype(jnp.int32)
    scratch = pltpu.VMEM
    half = lambda *shape: shaped(shape, BF16)
    full = lambda *shape: shaped(shape, F32)

    own, zl, zh = call(
        lambda *refs: first_kernel(2 * nx, *refs),
        [half(BLOCK, 384), half(FIRST_ROWS, 384), half(FIRST_ROWS, 384)],
        [scratch((SLOTS, BRICK), F32), scratch((2, 2, C, 1024), F32), pltpu.SemaphoreType.DMA((2,))],
        2,
        (brick_ids, slot_counts, brick_values, uptake),
        in_hbm=1,
    )
    zl, zh = both_ways(zl, zh, "gz")
    r1, r2, uxl, uxh = call(
        rates_kernel,
        [full(16, 16, 512), full(64, 256), half(64, 1024), half(64, 1024)],
        [scratch((8, 32, 128), F32), scratch((8, 16, 16, 128), F32), scratch((4, 16, 128), F32), scratch((4, 8, 8, 128), F32)],
        0,
        (lax.optimization_barrier((uptake, own))[0],),
    )
    xl, xh = call(
        first_x_kernel,
        [half(FIRST_ROWS, 384), half(FIRST_ROWS, 384)],
        [],
        0,
        (own, uxl, uxh, zl, zh),
    )
    s0, g0, v1, edge = call(
        lambda *refs: own_kernel(nz, *refs),
        [full(C, C, 1024), full(36, C, 1024), full(34, C, 1024), full(C, 8, 1024)],
        [
            scratch((C, C, 1024), F32),
            scratch((C, C, 1024), F32),
            scratch((C, C, 1024), F32),
            scratch((36, C, 1024), F32),
            scratch((34, C, 1024), F32),
            scratch((C, 8, 1024), F32),
            scratch((42, 40, 1024), F32),
            scratch((1024, 384), BF16),
            pltpu.SemaphoreType.DMA((6,)),
        ],
        1,
        (info, own, zl, zh, density, uptake),
        [ANY] * 4,
        in_hbm=2,
    )
    xl, xh = both_ways(xl, xh, "xy")

    c1, mzl, mzh, vzl, vzh, pxl, pxh, v2, gg, supply = call(
        lambda *refs: pre_kernel(nz, nx, *refs),
        [
            full(20, 24, 512),
            half(160, 1024),
            half(160, 1024),
            half(208, 1024),
            half(208, 1024),
            half(176, 1024),
            half(176, 1024),
            full(36, 40, 1024),
            full(36, 40, 1024),
            full(C, C, 1024),
        ],
        [
            scratch((42, 40, 1024), F32),
            scratch((42, 40, 1024), F32),
            scratch((C, C, 1024), F32),
            scratch((C, C, 1024), F32),
            scratch((36, 8, 1024), F32),
            scratch((36, 40, 1024), F32),
            scratch((C, 8, 1024), F32),
            scratch((1024, 768), BF16),
            scratch((8, 40, 128), F32),
            scratch((8, 20, 24, 128), F32),
            scratch((72, 1024), F32),
            scratch((72, 1024), F32),
            pltpu.SemaphoreType.DMA((8,)),
        ],
        1,
        (info, xl, xh, zl, zh, r1, r2, s0, g0, v1, edge, uptake),
        [VMEM] * 7 + [ANY] * 3,
        in_hbm=5,
    )
    mzl, mzh = both_ways(mzl, mzh, "gz")
    f1, q1, mxl, mxh = call(
        merge_kernel,
        [full(24, 24, 512), full(24, 16, 512), half(240, 512), half(240, 512)],
        [],
        0,
        (c1, r1, mzl, mzh),
    )
    mxl, mxh = both_ways(mxl, mxh, "xy")
    vzl, vzh, f1 = lax.optimization_barrier((vzl, vzh, f1))
    vzl, vzh = both_ways(vzl, vzh, "gz")
    vzl, vzh, pxl, pxh = lax.optimization_barrier((vzl, vzh, pxl, pxh))
    pxl, pxh = call(
        sides_kernel,
        [half(240, 1024), half(240, 1024)],
        [],
        0,
        (pxl, pxh, mzl, mzh, r2),
    )
    vxl, vxh = both_ways(pxl, pxh, "xy")
    f1, pxl, pxh = lax.optimization_barrier((f1, pxl, pxh))
    f1, g1, v1, g2, g2l, g2h = call(
        lambda *refs: middle_kernel(nz, nx, *refs),
        [full(24, 24, 512), full(24, 24, 512), full(24, 24, 512), full(64, 256), full(64, 256), full(64, 256)],
        [scratch((24, 24, 512), F32), scratch((24, 24, 512), F32), scratch((4, 16, 128), F32), scratch((4, 8, 8, 128), F32)],
        1,
        (info, f1, q1, r2, mxl, mxh),
    )
    low, high = both_ways(g2, g2, "gz")
    low2, high2 = two_away(g2l, g2h)
    own2, q2, near, fl, fh = call(
        source_window_kernel,
        [full(32, 8, 256), full(32, 8, 256), half(320, 256), half(256, 256), half(256, 256)],
        [],
        0,
        (g2, low, high, low2, high2, r2, mzl, mzh),
    )
    nl, nh = both_ways(near, near, "xy")
    fl, fh = both_ways(fl, fh, "xy", 2)
    window2 = scratch((32, 32, 256), F32)
    window1 = scratch((24, 24, 512), F32)
    (concentration,) = call(
        lambda *refs: back_kernel(nz, nx, *refs),
        [full(C, C, 1024)],
        [
            window2, window2, window2, window2, window2,
            scratch((8, 48, 128), F32),
            scratch((2, 16, 16, 128), F32),
            scratch((2, 16, 16, 128), F32),
            window1, window1,
            scratch((208, 1024), F32),
            scratch((208, 1024), F32),
            scratch((34, 40, 1024), F32),
            scratch((18, 24, 1024), F32),
            scratch((36, 40, 1024), F32),
            scratch((36, 40, 1024), F32),
            scratch((C, C, 1024), F32),
            scratch((16, 1024), F32),
            scratch((16, 1024), F32),
            scratch((C, C, 1024), F32),
            pltpu.SemaphoreType.DMA((7,)),
        ],
        1,
        (info, f1, g1, v1, vzl, vzh, vxl, vxh, own2, nl, nh, fl, fh, q2, v2, gg, supply),
        [ANY],
        in_hbm=3,
    )
    return supply, concentration


def solution(mesh):
    return jax.shard_map(
        shards,
        mesh=mesh,
        in_specs=(
            P("gz", "xy", None),
            P("gz", "xy", None),
            P(("gz", "xy"), None),
            P(("gz", "xy")),
            P(("gz", "xy"), None),
        ),
        out_specs=(P("gz", "xy", None), P("gz", "xy", None)),
        check_vma=False,
    )
```

```python
import jax
import jax.numpy as jnp
from jax import lax
from jax.experimental import pallas as pl
from jax.experimental.pallas import tpu as pltpu
from jax.sharding import PartitionSpec as P

EDGE = 16
CAP = 8
BRICK = 4096
SLOTS = 72
KAPPA = 32.0
OMEGA = 0.8
KEEP = 1.0 - OMEGA

C = 32
NT = 8
F32 = jnp.float32
BF16 = jnp.bfloat16


def spread(level):
    return KAPPA / 4.0**level


def shifted(values, distance, axis):
    return pltpu.roll(values, distance % values.shape[axis], axis)


def iota(shape, dim):
    return lax.broadcasted_iota(jnp.int32, shape, dim)


def lanes(t):
    return slice(t * 128, (t + 1) * 128)


def plane(ref, p):
    count = ref.shape[2] // 128
    rows = ref.shape[1]
    lane = iota((rows, 128), 1)
    before, here = None, ref[p, :, lanes(0)]
    for t in range(count):
        after = ref[p, :, lanes(t + 1)] if t + 1 < count else None
        low = jnp.where(lane == 127, 0.0 if before is None else before, here)
        high = jnp.where(lane == 0, 0.0 if after is None else after, here)
        sums = shifted(low, 1, 1) + shifted(high, -1, 1)
        sums = sums + (shifted(here, 1, 0) + shifted(here, -1, 0))
        sums = sums + (ref[p - 1, :, lanes(t)] + ref[p + 1, :, lanes(t)])
        yield t, here, sums
        before, here = here, after


def loop(start, stop, body, unroll=1):
    def step(i, carry):
        body(i)
        return carry

    lax.fori_loop(start, stop, step, 0, unroll=unroll)


def split_dot(a, b):
    high = a.astype(BF16)
    low = (a - high.astype(F32)).astype(BF16)
    return jnp.dot(high, b, preferred_element_type=F32) + jnp.dot(low, b, preferred_element_type=F32)


def pooling():
    return jnp.where(iota((256, 128), 0) // 2 == iota((256, 128), 1), 0.125, 0.0).astype(BF16)


def doubling():
    return jnp.where(iota((128, 256), 1) // 2 == iota((128, 256), 0), 1.0, 0.0).astype(BF16)


def halve_rows(values, rs, t):
    rows = values.shape[0]
    rs[t, 0:rows, :] = values
    return rs[t, pl.ds(0, rows // 2, stride=2), :] + rs[t, pl.ds(1, rows // 2, stride=2), :]


def halve_lanes(xp, planes, rows):
    matrix = pooling()
    tiles = []
    for t in range(0, xp.shape[0], 2):
        pair = jnp.concatenate([xp[t].reshape(planes * rows, 128), xp[t + 1].reshape(planes * rows, 128)], axis=1)
        tiles.append(split_dot(pair, matrix).reshape(planes, rows, 128))
    return tiles


def inside(shape, dim, first, wrap, index, size, count):
    place = iota(shape, dim) + first
    if wrap is not None:
        place = jnp.where(place < wrap, place, place - shape[dim])
    place = place + index * size
    return (place >= 0) & (place < count * size)


BLOCK = 272
FIRST_ROWS = BLOCK + 3 * 64


def uptake_part(t):
    return slice(BLOCK + 64 * (t // 3), BLOCK + 64 * (t // 3) + 64), lanes(t % 3)


def transposed_bricks(bricks_x, ids, counts, bricks, xs, targets):
    xs[...] = bricks[...].astype(F32)
    row = iota((1, 8, 128), 1)
    group = iota((1, 8, 128), 2) // 16
    group16 = iota((16, 128), 1) // 16
    per_y = 64

    def block(j, out, part):
        start = pl.multiple_of(j * 8, 8)
        x = jnp.stack([xs[pl.ds(start, 8), lanes(k)] for k in range(32)])
        for s in (4, 2, 1):
            up = shifted(shifted(x, -s, 1), 16 * s, 2)
            down = shifted(shifted(x, s, 1), -16 * s, 2)
            row_bit = (row // s) % 2
            group_bit = (group // s) % 2
            x = jnp.where(row_bit == group_bit, x, jnp.where(row_bit == 0, up, down))
        x = jnp.where(group < counts[0, j], x, 0.0)
        out[0:256, part] = x.reshape(256, 128).astype(BF16)
        names = jnp.zeros((16, 128), jnp.int32)
        for e in range(CAP):
            number = ids[j * 8 + e]
            by = lax.rem(number, per_y)
            rest = lax.div(number, per_y)
            bx = lax.rem(rest, 2)
            bz = lax.rem(lax.div(rest, bricks_x), 2)
            names = jnp.where(group16 == e, (bz * 2 + bx) * per_y + by, names)
        out[256:272, part] = names.astype(F32).astype(BF16)

    for i, out in enumerate(targets):
        for d in range(3):
            block(3 * i + d, out, lanes(d))


def first_kernel(bricks_x, ids, counts, bricks, uptake, own, zl, zh, xs, edges, sems):
    copies = [pltpu.make_async_copy(uptake.at[pl.ds(30 * i, 2)], edges.at[i], sems.at[i]) for i in range(2)]
    for copy in copies:
        copy.start()
    transposed_bricks(bricks_x, ids, counts, bricks, xs, (zl, own, zh))
    for i, ref in enumerate((zl, zh)):
        copies[i].wait()
        for t in range(8):
            ref[uptake_part(t)] = edges[i, :, :, lanes(t)].reshape(64, 128).astype(BF16)
        ref[uptake_part(8)] = jnp.zeros((64, 128), BF16)


def rates_kernel(uptake, r1, r2, xl, xh, rs, xp, rs1, xp1):
    def pair(m):
        for t in range(NT):
            both = uptake[2 * m, :, lanes(t)] + uptake[2 * m + 1, :, lanes(t)]
            xp[t, m] = halve_rows(both, rs, t)

    loop(0, 16, pair)
    for t, tile in enumerate(halve_lanes(xp, 16, 16)):
        r1[:, :, lanes(t)] = tile

    def pair1(m):
        for t in range(4):
            both = r1[2 * m, :, lanes(t)] + r1[2 * m + 1, :, lanes(t)]
            xp1[t, m] = halve_rows(both, rs1, t)

    loop(0, 8, pair1)
    for t, tile in enumerate(halve_lanes(xp1, 8, 8)):
        r2[:, lanes(t)] = tile.reshape(64, 128)

    sub = iota((8, 1024), 0)

    def columns(i):
        lows, highs = [], []
        for j in range(2):
            low, high = jnp.zeros((8, 1024), F32), jnp.zeros((8, 1024), F32)
            for n in range(4):
                z = 8 * i + 4 * j + n
                low = jnp.where(sub // 2 == n, shifted(uptake[z, 0:8, :], 2 * n, 0), low)
                high = jnp.where(sub // 2 == n, shifted(uptake[z, 24:32, :], 2 * n + 2, 0), high)
            lows.append(low)
            highs.append(high)
        rows = pl.ds(pl.multiple_of(16 * i, 16), 16)
        xl[rows, :] = jnp.concatenate(lows, axis=0).astype(BF16)
        xh[rows, :] = jnp.concatenate(highs, axis=0).astype(BF16)

    loop(0, 4, columns)


def far_along_z(nz, iz, to_low, to_high):
    if nz != 4:
        return to_low, to_high
    one = jnp.where(iz < 2, to_high, to_low)
    return one, one


def halves(sub, first, second):
    return jnp.where(sub < 4, first, shifted(second, 4, 1))


def uppers(sub, first, second):
    return jnp.where(sub < 4, shifted(first, 4, 1), second)


def far_messages(window):
    planes, _, width = window.shape
    pairs = window.reshape(planes // 2, 2, 8, width)
    sub = iota((planes // 2, 8, width), 1)
    size = (planes * 4, width)
    return halves(sub, pairs[:, 0], pairs[:, 1]).reshape(size), uppers(sub, pairs[:, 0], pairs[:, 1]).reshape(size)


def far_tile(from_low, from_high):
    width = from_low.shape[-1]
    low, high = from_low.reshape(-1, 8, width), from_high.reshape(-1, 8, width)
    sub = iota(low.shape, 1)
    even = jnp.where(sub < 4, high, shifted(low, 4, 1))
    odd = jnp.where(sub < 4, shifted(high, 4, 1), low)
    return jnp.stack([even, odd], axis=1).reshape(-1, 8, width)


def first_x_kernel(own, uxl, uxh, zl, zh, xl, xh):
    for ref, d in ((xl, 0), (xh, 2)):
        for n, src in enumerate((own, zl, zh)):
            ref[0:BLOCK, lanes(n)] = src[0:BLOCK, lanes(d)]
    sub = iota((8, 128), 0)
    lows, highs = [], []
    for t in range(8):
        xl[uptake_part(t)] = uxl[:, lanes(t)]
        xh[uptake_part(t)] = uxh[:, lanes(t)]
        both = [ref[uptake_part(t)].astype(F32) for ref in (zl, zh)]
        planes = [both[0][0:32], both[0][32:64], both[1][0:32], both[1][32:64]]
        to_low, to_high = jnp.zeros((8, 128), F32), jnp.zeros((8, 128), F32)
        for n, p in enumerate(planes):
            here = sub // 2 == n
            to_low = jnp.where(here, shifted(p[0:8], 2 * n, 0), to_low)
            to_high = jnp.where(here, shifted(p[24:32], 2 * n + 2, 0), to_high)
        lows.append(to_low)
        highs.append(to_high)
    xl[uptake_part(8)] = jnp.concatenate(lows, axis=0).astype(BF16)
    xh[uptake_part(8)] = jnp.concatenate(highs, axis=0).astype(BF16)


def window_planes(own, low, high, low2, high2):
    parts = (low2, low, own, high, high2)
    return jnp.concatenate([a.reshape(-1, 8, 256) for a in parts], axis=0)


def source_window_kernel(own, low, high, low2, high2, r2, zl, zh, f2, q2, near, fl, fh):
    planes = window_planes(own[...], low[...], high[...], low2[0:32, :], high2[0:32, :])
    f2[...] = planes
    below, above = [ref[80:144, 512:768].astype(F32) for ref in (zl, zh)]
    rates = window_planes(r2[...], below, above, low2[32:64, :], high2[32:64, :])
    q2[...] = rates
    near[0:256, :] = planes.reshape(256, 256).astype(BF16)
    near[256:320, :] = jnp.concatenate([low2[32:64, :], high2[32:64, :]], axis=0).astype(BF16)
    for i, values in enumerate((planes, rates)):
        to_low, to_high = far_messages(values)
        fl[128 * i : 128 * i + 128, :] = to_low.astype(BF16)
        fh[128 * i : 128 * i + 128, :] = to_high.astype(BF16)


O = 5
Q = 2
BASE = 1.0 + 6.0 * KAPPA


def scatter(blocks, hot, left):
    lane = iota((128, 128), 1)
    for i, (ref, part) in enumerate(blocks):
        name = ref[256:272, part].astype(F32).astype(jnp.int32)[0:1]
        tiles = lax.shift_right_logical(name, 6)
        at_y = (name & 63) * 16 + (lane[0:1] & 15)
        at_y = jnp.broadcast_to(at_y.astype(F32), (128, 128)).T.astype(jnp.int32)
        for t in range(NT):
            hot[128 * i : 128 * i + 128, lanes(t)] = jnp.where(at_y == lane + 128 * t, 1.0, 0.0).astype(BF16)
        values = ref[0:256, part].astype(F32)
        for tile in range(4):
            left[256 * tile : 256 * tile + 256, lanes(i)] = jnp.where(tiles == tile, values, 0.0).astype(BF16)
    for n in range(4):
        cols = slice(n * 256, (n + 1) * 256)
        sums = jnp.dot(left[...], hot[:, cols], preferred_element_type=F32)
        for tile in range(4):
            bz, bx = tile // 2, tile % 2
            yield 16 * bz, slice(16 * bx, 16 * bx + 16), cols, sums[256 * tile : 256 * tile + 256].reshape(16, 16, 256)


def sweep(src, dst, source, gg, z, sourced):
    for t, here, sums in plane(src, z + O):
        inner = KAPPA * sums
        g = gg[z + Q, :, lanes(t)]
        if sourced:
            body = inner[0:32] + source[z, :, lanes(t)]
            dst[z + O, 0:32, lanes(t)] = KEEP * here[0:32] + g[0:32] * body
            dst[z + O, 32:40, lanes(t)] = KEEP * here[32:40] + g[32:40] * inner[32:40]
        else:
            dst[z + O, :, lanes(t)] = KEEP * here + g * inner


def own_kernel(
    nz, info, own, zl, zh, density, uptake, s_out, g_out, v_out, edge_out,
    dens, upt, s0, g0, v1, edge, va, hot, left, sems,
):
    iz = info[0]
    loads = [pltpu.make_async_copy(density, dens, sems.at[0]), pltpu.make_async_copy(uptake, upt, sems.at[1])]
    stores = [
        pltpu.make_async_copy(src, dst, sems.at[2 + i])
        for i, (src, dst) in enumerate(((s0, s_out), (g0, g_out), (v1, v_out), (edge, edge_out)))
    ]
    for copy in loads:
        copy.start()
    for p in (3, 4, 37, 38):
        va[p] = jnp.zeros((40, 1024), F32)
    for n in range(4):
        ref, valid = (zl, iz > 0) if n < 2 else (zh, iz < nz - 1)
        q = n if n < 2 else 32 + n
        rows = slice(32 * (n % 2), 32 * (n % 2) + 32)
        for t in range(NT):
            g0[q, :, lanes(t)] = jnp.where(valid, OMEGA, 0.0) / (ref[uptake_part(t)].astype(F32)[rows] + BASE)

    blocks = [(ref, lanes(1)) for ref in (own, zl, zh)]
    waiting = list(loads[0:1])
    for z, rows, cols, sums in scatter(blocks, hot, left):
        while waiting:
            waiting.pop().wait()
        planes = slice(z, z + 16)
        s0[planes, rows, cols] = dens[planes, rows, cols] + sums
    stores[0].start()
    loads[1].wait()

    def own_plane(z):
        va[z + O, 0:32, :] = dens[z]
        va[z + O, 32:40, :] = jnp.zeros((8, 1024), F32)
        g0[z + Q] = OMEGA / (upt[z] + BASE)

    loop(0, C, own_plane)
    stores[1].start()

    def first(z):
        for t, here, sums in plane(va, z + O):
            inner = KAPPA * sums
            body = inner[0:32] + s0[z, :, lanes(t)]
            v1[z + 1, :, lanes(t)] = KEEP * here[0:32] + g0[z + Q, :, lanes(t)] * body
            edge[z, :, lanes(t)] = inner[32:40]

    loop(0, C, first, 2)
    for z in (-1, C):
        for t in range(NT):
            near = va[z + O + (1 if z < 0 else -1), 0:32, lanes(t)]
            v1[z + 1, :, lanes(t)] = g0[z + Q, :, lanes(t)] * (KAPPA * near)
    for copy in stores[2:]:
        copy.start()
    for copy in stores:
        copy.wait()


def pre_kernel(
    nz, nx, info, xl, xh, zl, zh, r1, r2, s0, g0, v1, edge_in, uptake,
    c1, mzl, mzh, vzl, vzh, pxl, pxh, v_out, g_out, s_out,
    va, vb, supply, upt, dh, gg, edge, hot, left, rs, xp, usl, ush, sems,
):
    iz, ix = info[0], info[1]
    k = KAPPA
    loads = [
        pltpu.make_async_copy(src, dst, sems.at[i])
        for i, (src, dst) in enumerate(
            (
                (s0, supply),
                (v1, vb.at[4:38, 0:32, :]),
                (g0, gg.at[:, 0:32, :]),
                (edge_in, edge),
                (uptake, upt),
            )
        )
    ]
    for copy in loads:
        copy.start()

    for p in (1, 2, 39, 40):
        va[p] = jnp.zeros((40, 1024), F32)
    for p in (2, 3, 38, 39):
        vb[p] = jnp.zeros((40, 1024), F32)
    for p in (4, 37):
        vb[p, 32:40, :] = jnp.zeros((8, 1024), F32)

    sub8 = iota((8, 1024), 0)
    for t in range(NT):
        usl[0:64, lanes(t)] = xl[uptake_part(t)].astype(F32)
        ush[0:64, lanes(t)] = xh[uptake_part(t)].astype(F32)
        usl[64:72, lanes(t)] = xl[uptake_part(8)].astype(F32)[8 * t : 8 * t + 8]
        ush[64:72, lanes(t)] = xh[uptake_part(8)].astype(F32)[8 * t : 8 * t + 8]

    def set_halo(q, low, high, valid_z):
        gz = jnp.where(valid_z, OMEGA, 0.0)
        d = jnp.where(sub8 < 2, high, jnp.where(sub8 >= 6, low, 0.0)) + BASE
        dh[q] = d
        omega = jnp.where(sub8 < 2, jnp.where(ix < nx - 1, gz, 0.0), jnp.where(sub8 >= 6, jnp.where(ix > 0, gz, 0.0), 0.0))
        gg[q, 32:40, :] = omega / d

    def halos(i):
        rows = pl.ds(pl.multiple_of(8 * i, 8), 8)
        low, high = usl[rows, :], ush[rows, :]
        for n in range(4):
            set_halo(4 * i + n + Q, shifted(low, 6 - 2 * n, 0), shifted(high, -2 * n, 0), True)

    loop(0, C // 4, halos)
    low, high = usl[64:72, :], ush[64:72, :]
    for n in range(4):
        exists = iz > 0 if n < 2 else iz < nz - 1
        set_halo(n if n < 2 else 32 + n, shifted(low, 6 - 2 * n, 0), shifted(high, -2 * n, 0), exists)

    blocks = [(ref, lanes(n)) for ref in (xl, xh) for n in range(3)]
    waiting = list(loads[0:3])
    for z, rows, cols, sums in scatter(blocks, hot, left):
        while waiting:
            waiting.pop().wait()
        supply[z : z + 16, rows, cols] = supply[z : z + 16, rows, cols] + sums
        g = gg[z + Q : z + Q + 16, rows, cols]
        vb[z + O : z + O + 16, rows, cols] = vb[z + O : z + O + 16, rows, cols] + g * sums
    loads[3].wait()

    s_copy = pltpu.make_async_copy(supply, s_out, sems.at[7])
    s_copy.start()

    def edges(z):
        vb[z + O, 32:40, :] = gg[z + Q, 32:40, :] * edge[z]

    loop(0, C, edges)

    loop(0, C, lambda z: sweep(vb, va, supply, gg, z, True), 2)
    loop(0, 4, lambda i: sweep(vb, va, supply, gg, jnp.where(i < 2, i - 2, i + C - 2), False))
    loads[4].wait()
    v_copy = pltpu.make_async_copy(va.at[3:39], v_out, sems.at[5])
    g_copy = pltpu.make_async_copy(gg, g_out, sems.at[6])
    v_copy.start()
    g_copy.start()

    def residual(z, rates, sourced):
        for t, here, sums in plane(va, z + O):
            r = k * sums
            if rates is not None:
                inner = r[0:32] - (rates(t) + BASE) * here[0:32]
                if sourced:
                    inner = inner + supply[z, :, lanes(t)]
                r = jnp.concatenate([inner, r[32:40] - dh[z + Q, :, lanes(t)] * here[32:40]], axis=0)
            yield t, r

    def coarse(m, zs, rates, sourced):
        parts = [residual(zs[i], rates[i], sourced) for i in range(2)]
        for (t, first), (_, second) in zip(*parts):
            xp[t, m, 0:20, :] = halve_rows(first + second, rs, t)

    def from_message(ref, n):
        return lambda t: ref[uptake_part(t)].astype(F32)[32 * n : 32 * n + 32]

    def inner(m):
        zs = (2 * m - 4, 2 * m - 3)
        coarse(m, zs, [lambda t, z=z: upt[z, :, lanes(t)] for z in zs], True)

    loop(2, 18, inner)
    for m, ref, z in ((1, zl, -2), (18, zh, C)):
        coarse(m, (z, z + 1), [from_message(ref, 0), from_message(ref, 1)], False)

    def outer(i):
        for t, r in residual(jnp.where(i == 0, -3, 34), None, False):
            xp[t, 19 * i, 0:20, :] = halve_rows(r, rs, t)

    loop(0, 2, outer)

    sub = iota((20, 8, 128), 1)
    for t, tile in enumerate(halve_lanes(xp, 20, 24)):
        last = tile[:, 16:24]
        last = jnp.where(sub < 2, last, jnp.where(sub >= 6, shifted(last, 4, 1), 0.0))
        c1[:, 0:16, lanes(t)] = tile[:, 0:16]
        c1[:, 16:24, lanes(t)] = last

    empty = jnp.zeros((1, 8, 1024), F32)
    blank = jnp.zeros((8, 1024), F32)
    edges = (
        (mzl, vzl, slice(0, 6), slice(0, 4), 3, 0),
        (mzh, vzh, slice(14, 20), slice(12, 16), 35, 31),
    )
    for ref, level0, planes, rates, p, z in edges:
        source = c1[planes].reshape(144, 512)
        ref[0:80, 0:512] = source[0:80].astype(BF16)
        ref[0:64, 512:1024] = source[80:144].astype(BF16)
        ref[64:80, 512:1024] = jnp.zeros((16, 512), BF16)
        ref[80:144, 0:512] = r1[rates].reshape(64, 512).astype(BF16)
        ref[80:144, 512:768] = r2[...].astype(BF16)
        corner = jnp.concatenate([pack_low(va[p], va[p + 1]), pack_low(va[p + 2], va[p + 3])], axis=0).astype(BF16)
        for n in range(4):
            ref[80 + 16 * n : 96 + 16 * n, 768:1024] = corner[:, n * 256 : n * 256 + 256]
        corner = jnp.concatenate([pack_high(va[p], va[p + 1]), pack_high(va[p + 2], va[p + 3])], axis=0).astype(BF16)
        ref[144:160, :] = corner
        values = jnp.concatenate([va[p : p + 4], jnp.concatenate([supply[z : z + 1], empty], axis=1)], axis=0)
        level0[...] = jnp.concatenate([values.reshape(200, 1024), blank], axis=0).astype(BF16)

    def sides(i):
        lows, highs = [], []
        for j in range(2):
            p = 4 * i + 2 * j + 3
            lows.append(pack_low(va[p], va[p + 1]))
            highs.append(pack_high(va[p], va[p + 1]))
        rows = pl.ds(pl.multiple_of(16 * i, 16), 16)
        pxl[rows, :] = jnp.concatenate(lows, axis=0).astype(BF16)
        pxh[rows, :] = jnp.concatenate(highs, axis=0).astype(BF16)

    loop(0, 9, sides)

    def sources(i):
        lows, highs = [], []
        for j in range(2):
            low, high = jnp.zeros((8, 1024), F32), jnp.zeros((8, 1024), F32)
            for n in range(8):
                z = 16 * i + 8 * j + n
                low = jnp.where(sub8 == n, shifted(supply[z, 0:8, :], n, 0), low)
                high = jnp.where(sub8 == n, shifted(supply[z, 24:32, :], n + 1, 0), high)
            lows.append(low)
            highs.append(high)
        rows = pl.ds(pl.multiple_of(16 * i + 144, 16), 16)
        pxl[rows, :] = jnp.concatenate(lows, axis=0).astype(BF16)
        pxh[rows, :] = jnp.concatenate(highs, axis=0).astype(BF16)

    loop(0, 2, sources)
    v_copy.wait()
    g_copy.wait()
    s_copy.wait()


def outer_rows(sub):
    return (sub < 2) | (sub >= 6)


def pack_pair(sub, a, b):
    return jnp.where(outer_rows(sub), a, shifted(b, 4, 0))


def pack_low(first, second):
    sub = iota((8, 1024), 0)
    a, b = [jnp.where(sub < 4, v[0:8], v[32:40]) for v in (first, second)]
    return pack_pair(sub, a, b)


def pack_high(first, second):
    sub = iota((8, 1024), 0)
    a, b = [jnp.where(sub >= 4, v[24:32], v[32:40]) for v in (first, second)]
    return pack_pair(sub, a, b)


def sides_kernel(pxl, pxh, mzl, mzh, r2, out_l, out_h):
    for ref, out in ((pxl, out_l), (pxh, out_h)):
        out[0:176, :] = ref[...]
        for n, rates in enumerate((mzl[80:144, 512:768], r2[...].astype(BF16), mzh[80:144, 512:768])):
            out[176:240, n * 256 : n * 256 + 256] = rates
        out[176:240, 768:1024] = jnp.zeros((64, 256), BF16)
    for message, start in ((mzl, 0), (mzh, 128)):
        low = jnp.concatenate([message[80 + 16 * n : 96 + 16 * n, 768:1024] for n in range(4)], axis=1)
        rows = slice(start, start + 16)
        for ref, out, corner in ((pxl, out_l, low), (pxh, out_h, message[144:160, :])):
            out[rows, :] = (ref[rows, :].astype(F32) + corner.astype(F32)).astype(BF16)


def in_three(sub, tiles, free, turns):
    spare = (sub == free) | (sub == free + 1)
    last = tiles[:, 3]
    parts = [jnp.where(spare, shifted(last, turn, 1), tiles[:, i]) for i, turn in enumerate(turns)]
    return jnp.stack(parts, axis=1)


def out_of_three(sub, parts, free, turns):
    last = None
    for i, turn in enumerate(turns):
        back = shifted(parts[:, i], -turn, 1)
        home = (free - turn) % 8
        here = (sub == home) | (sub == home + 1)
        last = jnp.where(here, back, 0.0 if last is None else last)
    return jnp.stack([parts[:, 0], parts[:, 1], parts[:, 2], last], axis=1)


HIGH_PACK = (2, (-2, 4, 2))
LOW_PACK = (4, (-2, 4, 2))


def merge_kernel(c1, r1, mzl, mzh, f1, q1, mxl, mxh):
    zeros = jnp.zeros((24, 512), F32)
    for p in (0, 1, 22, 23):
        f1[p] = zeros
    f1[2:22] = c1[...]
    for ref, planes in ((mzl, slice(0, 6)), (mzh, slice(18, 24))):
        parts = [ref[0:80, 0:512].astype(F32), ref[0:64, 512:1024].astype(F32)]
        f1[planes] = f1[planes] + jnp.concatenate(parts, axis=0).reshape(6, 24, 512)
    sub = iota((6, 8, 512), 1)
    first, last, halo = [f1[:, 8 * n : 8 * n + 8].reshape(6, 4, 8, 512) for n in range(3)]
    sub4 = iota((6, 4, 8, 512), 2)
    to_high = in_three(sub, jnp.where(sub4 >= 4, last, halo), *HIGH_PACK)
    to_low = in_three(sub, jnp.where(sub4 >= 4, halo, first), *LOW_PACK)
    mxh[0:144, :] = to_high.reshape(144, 512).astype(BF16)
    mxl[0:144, :] = to_low.reshape(144, 512).astype(BF16)
    q1[0:4] = mzl[80:144, 0:512].astype(F32).reshape(4, 16, 512)
    q1[4:20] = r1[...]
    q1[20:24] = mzh[80:144, 0:512].astype(F32).reshape(4, 16, 512)
    sub1 = iota((12, 8, 512), 1)
    first = q1[:, 0:8, :].reshape(12, 2, 8, 512)
    last = q1[:, 8:16, :].reshape(12, 2, 8, 512)
    mxl[144:240, :] = halves(sub1, first[:, 0], first[:, 1]).reshape(96, 512).astype(BF16)
    mxh[144:240, :] = uppers(sub1, last[:, 0], last[:, 1]).reshape(96, 512).astype(BF16)


def middle_kernel(nz, nx, info, f0, q_in, r2, mxl, mxh, f1, g1, v1, g2, g2l, g2h, q0, va, rs, xp):
    iz, ix = info[0], info[1]
    k = spread(1)
    base = 1.0 + 6.0 * k
    sub6 = iota((6, 8, 512), 1)
    low = out_of_three(sub6, mxl[0:144, :].astype(F32).reshape(6, 3, 8, 512), *HIGH_PACK).reshape(24, 8, 512)
    high = out_of_three(sub6, mxh[0:144, :].astype(F32).reshape(6, 3, 8, 512), *LOW_PACK).reshape(24, 8, 512)
    sub = iota((24, 8, 512), 1)
    f1[:, 0:8] = f0[:, 0:8] + jnp.where(sub < 2, low, 0.0)
    f1[:, 8:16] = f0[:, 8:16] + jnp.where(sub >= 6, high, 0.0)
    f1[:, 16:24] = f0[:, 16:24] + jnp.where(sub >= 4, low, high)
    low, high = [ref[144:240, :].astype(F32).reshape(12, 8, 512) for ref in (mxl, mxh)]
    sub12 = iota((12, 8, 512), 1)
    even = jnp.where(sub12 >= 4, shifted(low, 4, 1), high)
    odd = jnp.where(sub12 >= 4, low, shifted(high, 4, 1))
    q0[:, 0:16] = q_in[...]
    q0[:, 16:24] = jnp.stack([even, odd], axis=1).reshape(24, 8, 512)
    shape = (24, 24, 128)
    valid = inside(shape, 0, -4, None, iz, 16, nz) & inside(shape, 1, 0, 20, ix, 16, nx)
    for t in range(4):
        g = jnp.where(valid, OMEGA, 0.0) / (q0[:, :, lanes(t)] + base)
        g1[:, :, lanes(t)] = g
        va[:, :, lanes(t)] = g * f1[:, :, lanes(t)]
    v1[0] = va[0]
    v1[23] = va[23]

    def sweep(p):
        for t, here, sums in plane(va, p):
            v1[p, :, lanes(t)] = KEEP * here + g1[p, :, lanes(t)] * (f1[p, :, lanes(t)] + k * sums)

    loop(1, 23, sweep, 2)

    def residual(p):
        for t, here, sums in plane(v1, p):
            yield t, f1[p, :, lanes(t)] + k * sums - (q0[p, :, lanes(t)] + base) * here

    def coarse(m):
        for (t, first), (_, second) in zip(residual(2 * m + 4), residual(2 * m + 5)):
            xp[t, m] = halve_rows((first + second)[0:16], rs, t)

    loop(0, 8, coarse)
    for t, tile in enumerate(halve_lanes(xp, 8, 8)):
        g2[:, lanes(t)] = tile.reshape(64, 128)
        low, high = far_along_z(nz, iz, tile[0:4].reshape(32, 128), tile[4:8].reshape(32, 128))
        g2l[0:32, lanes(t)] = low
        g2h[0:32, lanes(t)] = high
    low, high = far_along_z(nz, iz, r2[0:32, :], r2[32:64, :])
    g2l[32:64, :] = low
    g2h[32:64, :] = high


def back_kernel(
    nz, nx, info, f1, g1, v1, vzl, vzh, vxl, vxh, own2, n2l, n2h, m2l, m2h, q_own, v_in, g_in, s_in,
    out_hbm,
    f2, q2, h2, a2, b2, rs, xp, xpr, wa, w1, zsl, zsh, vb, ws,
    v2, gg, supply, fsl, fsh, out, sems,
):
    iz, ix = info[0], info[1]
    matrix = doubling()
    level0 = [
        pltpu.make_async_copy(src, dst, sems.at[i])
        for i, (src, dst) in enumerate(((v_in, v2), (g_in, gg), (s_in, supply)))
    ]
    for copy in level0:
        copy.start()

    f2[:, 0:8, :] = own2[...]
    f2[:, 8:16, :] = n2h[0:256, :].astype(F32).reshape(32, 8, 256)
    f2[:, 16:24, :] = far_tile(m2l[0:128, :].astype(F32), m2h[0:128, :].astype(F32))
    f2[:, 24:32, :] = n2l[0:256, :].astype(F32).reshape(32, 8, 256)
    q2[:, 0:8, :] = q_own[...]
    q2[:, 16:24, :] = far_tile(m2l[128:256, :].astype(F32), m2h[128:256, :].astype(F32))
    for ref, rows in ((vxh, slice(8, 16)), (vxl, slice(24, 32))):
        for n in range(3):
            q2[8 * n + 4 : 8 * n + 12, rows, :] = ref[176:240, n * 256 : n * 256 + 256].astype(F32).reshape(8, 8, 256)
    for ref, rows in ((n2h, slice(8, 16)), (n2l, slice(24, 32))):
        outer = ref[256:320, :].astype(F32).reshape(8, 8, 256)
        q2[0:4, rows, :] = outer[0:4]
        q2[28:32, rows, :] = outer[4:8]

    k = spread(2)
    base = 1.0 + 6.0 * k
    shape = (32, 32, 128)
    valid = inside(shape, 0, -12, None, iz, 8, nz) & inside(shape, 1, 0, 20, ix, 8, nx)
    for t in range(2):
        g = jnp.where(valid, OMEGA, 0.0) / (q2[:, :, lanes(t)] + base)
        h2[:, :, lanes(t)] = g
        a2[:, :, lanes(t)] = g * f2[:, :, lanes(t)]
    b2[0] = a2[0]
    b2[31] = a2[31]

    def sweep2(src, dst):
        def body(p):
            for t, here, sums in plane(src, p):
                dst[p, :, lanes(t)] = KEEP * here + h2[p, :, lanes(t)] * (f2[p, :, lanes(t)] + k * sums)

        return body

    loop(1, 31, sweep2(a2, b2), 2)

    def coarse(m):
        total, rates = [0.0, 0.0], [0.0, 0.0]
        for j in range(2):
            p = 2 * m + j
            for t, here, sums in plane(b2, p):
                r = f2[p, :, lanes(t)] + k * sums - (q2[p, :, lanes(t)] + base) * here
                total[t] = total[t] + r
                rates[t] = rates[t] + q2[p, :, lanes(t)]
        for t in range(2):
            xp[t, m] = halve_rows(total[t], rs, t)
            xpr[t, m] = halve_rows(rates[t], rs, t + 2)

    for t in range(2):
        for m in (0, 15):
            xp[t, m] = jnp.zeros((16, 128), F32)
            xpr[t, m] = jnp.zeros((16, 128), F32)
    loop(1, 15, coarse)

    shape = (16, 16, 128)
    valid = inside(shape, 0, -6, None, iz, 4, nz) & inside(shape, 1, 0, 10, ix, 4, nx)
    k3 = spread(3)
    (source,) = halve_lanes(xp, 16, 16)
    (rates,) = halve_lanes(xpr, 16, 16)
    g = jnp.where(valid, OMEGA, 0.0) / (rates + (1.0 + 6.0 * k3))
    v = g * source
    lane = iota(shape, 2)
    for repeat in range(3):
        edge = jnp.zeros((1, 16, 128), F32)
        sums = jnp.concatenate([v[1:], edge], axis=0) + jnp.concatenate([edge, v[:-1]], axis=0)
        sums = sums + shifted(v, 1, 1) + shifted(v, -1, 1)
        sums = sums + jnp.where(lane == 0, 0.0, shifted(v, 1, 2)) + jnp.where(lane == 127, 0.0, shifted(v, -1, 2))
        v = KEEP * v + g * (source + k3 * sums)

    wide = split_dot(v[4:12].reshape(128, 128), matrix).reshape(8, 16, 256)
    for m in range(8):
        for t in range(2):
            part = wide[m, :, lanes(t)]
            rs[t, pl.ds(0, 16, stride=2), :] = part
            rs[t, pl.ds(1, 16, stride=2), :] = part
            for j in range(2):
                p = 8 + 2 * m + j
                b2[p, :, lanes(t)] = b2[p, :, lanes(t)] + rs[t, 0:32, :]
    loop(9, 23, sweep2(b2, a2), 2)
    loop(10, 22, sweep2(a2, b2), 2)

    w = b2[10:22]
    near, far = w[:, 8:16], w[:, 24:32]
    near = jnp.where(iota((12, 8, 256), 1) < 2, near, shifted(far, 4, 1))
    w = jnp.concatenate([w[:, 0:8], near], axis=1).reshape(192, 256)
    wide = [split_dot(w[:, lanes(t)], matrix) for t in range(2)]
    wide = jnp.concatenate(wide, axis=1).reshape(12, 16, 512)
    for m in range(12):
        for t in range(4):
            part = wide[m, :, lanes(t)]
            rs[t, pl.ds(0, 16, stride=2), :] = part
            rs[t, pl.ds(1, 16, stride=2), :] = part
            for j in range(2):
                p = 2 * m + j
                wa[p, :, lanes(t)] = v1[p, :, lanes(t)] + rs[t, 0:24, :]
    k1 = spread(1)

    def sweep1(src, dst):
        def body(p):
            for t, here, sums in plane(src, p):
                dst[p, :, lanes(t)] = KEEP * here + g1[p, :, lanes(t)] * (f1[p, :, lanes(t)] + k1 * sums)

        return body

    loop(2, 22, sweep1(wa, w1), 2)
    loop(3, 21, sweep1(w1, wa), 2)

    sub = iota((18, 8, 128), 1)
    for t in range(4):
        halo = wa[3:21, 16:24, lanes(t)]
        halo = jnp.where(sub < 2, halo, shifted(halo, 4, 1))
        w = jnp.concatenate([wa[3:21, 0:16, lanes(t)], halo], axis=1)
        ws[:, :, t * 256 : t * 256 + 256] = split_dot(w.reshape(432, 128), matrix).reshape(18, 24, 256)

    for copy in level0:
        copy.wait()
    zsl[...] = vzl[...].astype(F32)
    zsh[...] = vzh[...].astype(F32)
    for i in range(4):
        v2[i] = v2[i] + zsl[40 * i : 40 * i + 40, :]
        v2[32 + i] = v2[32 + i] + zsh[40 * i : 40 * i + 40, :]

    s8 = iota((8, 128), 0)

    outer = outer_rows(s8)

    def correct(i):
        rows = pl.ds(pl.multiple_of(16 * i, 16), 16)
        for t in range(NT):
            low = vxl[rows, lanes(t)].astype(F32)
            high = vxh[rows, lanes(t)].astype(F32)
            for n in range(2):
                part = ws[2 * i + n, :, lanes(t)]
                rs[t, pl.ds(0, 24, stride=2), :] = part
                rs[t, pl.ds(1, 24, stride=2), :] = part
                for j in range(2):
                    p = 4 * i + 2 * n + j
                    lo, hi = low[8 * n : 8 * n + 8], high[8 * n : 8 * n + 8]
                    if j:
                        lo, hi = shifted(lo, 4, 0), shifted(hi, 4, 0)
                    v2[p, 0:8, lanes(t)] = v2[p, 0:8, lanes(t)] + rs[t, 0:8, :] + jnp.where(s8 < 2, lo, 0.0)
                    v2[p, 8:24, lanes(t)] = v2[p, 8:24, lanes(t)] + rs[t, 8:24, :]
                    v2[p, 24:32, lanes(t)] = v2[p, 24:32, lanes(t)] + rs[t, 24:32, :] + jnp.where(s8 >= 6, hi, 0.0)
                    extra = jnp.where(outer, jnp.where(s8 >= 4, lo, hi), 0.0)
                    v2[p, 32:40, lanes(t)] = v2[p, 32:40, lanes(t)] + rs[t, 32:40, :] + extra

    loop(0, 9, correct)
    k0 = spread(0)

    def first(i):
        rows = pl.ds(pl.multiple_of(16 * i + 144, 16), 16)
        for t in range(NT):
            fsl[:, lanes(t)] = vxl[rows, lanes(t)].astype(F32)
            fsh[:, lanes(t)] = vxh[rows, lanes(t)].astype(F32)

        def step(j):
            z = 16 * i + j
            start = pl.multiple_of((j // 8) * 8, 8)
            turn = lax.rem(j, 8)
            for t, here, sums in plane(v2, z + 2):
                lo = pltpu.roll(fsl[pl.ds(start, 8), lanes(t)], 7 - turn, 0)
                hi = pltpu.roll(fsh[pl.ds(start, 8), lanes(t)], lax.rem(8 - turn, 8), 0)
                f = jnp.where(s8 == 7, lo, jnp.where(s8 == 0, hi, 0.0))
                g = gg[z + 2, :, lanes(t)]
                inner = k0 * sums
                vb[z + 1, 0:32, lanes(t)] = KEEP * here[0:32] + g[0:32] * (supply[z, :, lanes(t)] + inner[0:32])
                vb[z + 1, 32:40, lanes(t)] = KEEP * here[32:40] + g[32:40] * (f + inner[32:40])

        loop(0, 16, step, 2)

    loop(0, 2, first)
    for p, ref in ((1, zsl), (34, zsh)):
        for t, here, sums in plane(v2, p):
            g = gg[p, :, lanes(t)]
            vb[p - 1, :, lanes(t)] = KEEP * here + g * (ref[160:200, lanes(t)] + k0 * sums)

    def second(z):
        for t, here, sums in plane(vb, z + 1):
            g = gg[z + 2, 0:32, lanes(t)]
            out[z, :, lanes(t)] = KEEP * here[0:32] + g * (supply[z, :, lanes(t)] + k0 * sums[0:32])

    stores = []
    for i in range(4):
        part = pl.ds(8 * i, 8)
        loop(8 * i, 8 * i + 8, second, 2)
        stores.append(pltpu.make_async_copy(out.at[part], out_hbm.at[part], sems.at[3 + i]))
        stores[i].start()
    for copy in stores:
        copy.wait()


VMEM = pl.BlockSpec(memory_space=pltpu.VMEM)
SMEM = pl.BlockSpec(memory_space=pltpu.SMEM)
ANY = pl.BlockSpec(memory_space=pl.ANY)


def call(kernel, outs, scratch, smem, args, out_specs=None, in_hbm=0):
    moved = sum(a.size * a.dtype.itemsize for a in list(args) + list(outs))
    return pl.pallas_call(
        kernel,
        out_shape=tuple(outs),
        in_specs=[SMEM] * smem + [VMEM] * (len(args) - smem - in_hbm) + [ANY] * in_hbm,
        out_specs=tuple(out_specs or [VMEM] * len(outs)),
        scratch_shapes=scratch,
        compiler_params=pltpu.CompilerParams(vmem_limit_bytes=58 * 2**20),
        cost_estimate=pl.CostEstimate(flops=20 * moved, bytes_accessed=moved, transcendentals=0),
    )(*args)


def shaped(shape, dtype=F32):
    return jax.ShapeDtypeStruct(shape, dtype)


def both_ways(to_low, to_high, axis, distance=1):
    count = lax.axis_size(axis)
    up = [(i, i + distance) for i in range(count - distance)]
    down = [(j, i) for i, j in up]
    return lax.ppermute(to_high, axis, up), lax.ppermute(to_low, axis, down)


def two_away(to_low, to_high):
    count = lax.axis_size("gz")
    if count != 4:
        return both_ways(to_low, to_high, "gz", 2)
    came = lax.ppermute(to_low, "gz", [(i, (i + 2) % 4) for i in range(4)])
    return came, came


def shards(density, uptake, brick_values, brick_ids, slot_counts):
    nz, nx = lax.axis_size("gz"), lax.axis_size("xy")
    info = jnp.stack([lax.axis_index("gz"), lax.axis_index("xy")]).astype(jnp.int32)
    scratch = pltpu.VMEM
    half = lambda *shape: shaped(shape, BF16)
    full = lambda *shape: shaped(shape, F32)

    own, zl, zh = call(
        lambda *refs: first_kernel(2 * nx, *refs),
        [half(BLOCK, 384), half(FIRST_ROWS, 384), half(FIRST_ROWS, 384)],
        [scratch((SLOTS, BRICK), F32), scratch((2, 2, C, 1024), F32), pltpu.SemaphoreType.DMA((2,))],
        2,
        (brick_ids, slot_counts, brick_values, uptake),
        in_hbm=1,
    )
    zl, zh = both_ways(zl, zh, "gz")
    r1, r2, uxl, uxh = call(
        rates_kernel,
        [full(16, 16, 512), full(64, 256), half(64, 1024), half(64, 1024)],
        [scratch((8, 32, 128), F32), scratch((8, 16, 16, 128), F32), scratch((4, 16, 128), F32), scratch((4, 8, 8, 128), F32)],
        0,
        (lax.optimization_barrier((uptake, own))[0],),
    )
    xl, xh = call(
        first_x_kernel,
        [half(FIRST_ROWS, 384), half(FIRST_ROWS, 384)],
        [],
        0,
        (own, uxl, uxh, zl, zh),
    )
    s0, g0, v1, edge = call(
        lambda *refs: own_kernel(nz, *refs),
        [full(C, C, 1024), full(36, C, 1024), full(34, C, 1024), full(C, 8, 1024)],
        [
            scratch((C, C, 1024), F32),
            scratch((C, C, 1024), F32),
            scratch((C, C, 1024), F32),
            scratch((36, C, 1024), F32),
            scratch((34, C, 1024), F32),
            scratch((C, 8, 1024), F32),
            scratch((42, 40, 1024), F32),
            scratch((384, 1024), BF16),
            scratch((1024, 384), BF16),
            pltpu.SemaphoreType.DMA((6,)),
        ],
        1,
        (info, own, zl, zh, density, uptake),
        [ANY] * 4,
        in_hbm=2,
    )
    xl, xh = both_ways(xl, xh, "xy")

    c1, mzl, mzh, vzl, vzh, pxl, pxh, v2, gg, supply = call(
        lambda *refs: pre_kernel(nz, nx, *refs),
        [
            full(20, 24, 512),
            half(160, 1024),
            half(160, 1024),
            half(208, 1024),
            half(208, 1024),
            half(176, 1024),
            half(176, 1024),
            full(36, 40, 1024),
            full(36, 40, 1024),
            full(C, C, 1024),
        ],
        [
            scratch((42, 40, 1024), F32),
            scratch((42, 40, 1024), F32),
            scratch((C, C, 1024), F32),
            scratch((C, C, 1024), F32),
            scratch((36, 8, 1024), F32),
            scratch((36, 40, 1024), F32),
            scratch((C, 8, 1024), F32),
            scratch((768, 1024), BF16),
            scratch((1024, 768), BF16),
            scratch((8, 40, 128), F32),
            scratch((8, 20, 24, 128), F32),
            scratch((72, 1024), F32),
            scratch((72, 1024), F32),
            pltpu.SemaphoreType.DMA((8,)),
        ],
        1,
        (info, xl, xh, zl, zh, r1, r2, s0, g0, v1, edge, uptake),
        [VMEM] * 7 + [ANY] * 3,
        in_hbm=5,
    )
    mzl, mzh = both_ways(mzl, mzh, "gz")
    f1, q1, mxl, mxh = call(
        merge_kernel,
        [full(24, 24, 512), full(24, 16, 512), half(240, 512), half(240, 512)],
        [],
        0,
        (c1, r1, mzl, mzh),
    )
    mxl, mxh = both_ways(mxl, mxh, "xy")
    pxl, pxh, f1 = lax.optimization_barrier((pxl, pxh, f1))
    pxl, pxh = call(
        sides_kernel,
        [half(240, 1024), half(240, 1024)],
        [],
        0,
        (pxl, pxh, mzl, mzh, r2),
    )
    vzl, vzh, pxl, pxh, f1 = lax.optimization_barrier((vzl, vzh, pxl, pxh, f1))
    vzl, vzh = both_ways(vzl, vzh, "gz")
    f1, g1, v1, g2, g2l, g2h = call(
        lambda *refs: middle_kernel(nz, nx, *refs),
        [full(24, 24, 512), full(24, 24, 512), full(24, 24, 512), full(64, 256), full(64, 256), full(64, 256)],
        [scratch((24, 24, 512), F32), scratch((24, 24, 512), F32), scratch((4, 16, 128), F32), scratch((4, 8, 8, 128), F32)],
        1,
        (info, f1, q1, r2, mxl, mxh),
    )
    pxl, pxh, g2 = lax.optimization_barrier((pxl, pxh, g2))
    vxl, vxh = both_ways(pxl, pxh, "xy")
    low, high = both_ways(g2, g2, "gz")
    low2, high2 = two_away(g2l, g2h)
    own2, q2, near, fl, fh = call(
        source_window_kernel,
        [full(32, 8, 256), full(32, 8, 256), half(320, 256), half(256, 256), half(256, 256)],
        [],
        0,
        (g2, low, high, low2, high2, r2, mzl, mzh),
    )
    nl, nh = both_ways(near, near, "xy")
    fl, fh = both_ways(fl, fh, "xy", 2)
    window2 = scratch((32, 32, 256), F32)
    window1 = scratch((24, 24, 512), F32)
    (concentration,) = call(
        lambda *refs: back_kernel(nz, nx, *refs),
        [full(C, C, 1024)],
        [
            window2, window2, window2, window2, window2,
            scratch((8, 48, 128), F32),
            scratch((2, 16, 16, 128), F32),
            scratch((2, 16, 16, 128), F32),
            window1, window1,
            scratch((208, 1024), F32),
            scratch((208, 1024), F32),
            scratch((34, 40, 1024), F32),
            scratch((18, 24, 1024), F32),
            scratch((36, 40, 1024), F32),
            scratch((36, 40, 1024), F32),
            scratch((C, C, 1024), F32),
            scratch((16, 1024), F32),
            scratch((16, 1024), F32),
            scratch((C, C, 1024), F32),
            pltpu.SemaphoreType.DMA((7,)),
        ],
        1,
        (info, f1, g1, v1, vzl, vzh, vxl, vxh, own2, nl, nh, fl, fh, q2, v2, gg, supply),
        [ANY],
        in_hbm=3,
    )
    return supply, concentration


def solution(mesh):
    return jax.shard_map(
        shards,
        mesh=mesh,
        in_specs=(
            P("gz", "xy", None),
            P("gz", "xy", None),
            P(("gz", "xy"), None),
            P(("gz", "xy")),
            P(("gz", "xy"), None),
        ),
        out_specs=(P("gz", "xy", None), P("gz", "xy", None)),
        check_vma=False,
    )
```

```python
import jax
import jax.numpy as jnp
from jax import lax
from jax.experimental import pallas as pl
from jax.experimental.pallas import tpu as pltpu
from jax.sharding import PartitionSpec as P

EDGE = 16
CAP = 8
BRICK = 4096
SLOTS = 72
KAPPA = 32.0
OMEGA = 0.8
KEEP = 1.0 - OMEGA

C = 32
NT = 8
F32 = jnp.float32
BF16 = jnp.bfloat16


def spread(level):
    return KAPPA / 4.0**level


def shifted(values, distance, axis):
    return pltpu.roll(values, distance % values.shape[axis], axis)


def iota(shape, dim):
    return lax.broadcasted_iota(jnp.int32, shape, dim)


def lanes(t):
    return slice(t * 128, (t + 1) * 128)


def plane(ref, p):
    count = ref.shape[2] // 128
    rows = ref.shape[1]
    lane = iota((rows, 128), 1)
    before, here = None, ref[p, :, lanes(0)]
    for t in range(count):
        after = ref[p, :, lanes(t + 1)] if t + 1 < count else None
        low = jnp.where(lane == 127, 0.0 if before is None else before, here)
        high = jnp.where(lane == 0, 0.0 if after is None else after, here)
        sums = shifted(low, 1, 1) + shifted(high, -1, 1)
        sums = sums + (shifted(here, 1, 0) + shifted(here, -1, 0))
        sums = sums + (ref[p - 1, :, lanes(t)] + ref[p + 1, :, lanes(t)])
        yield t, here, sums
        before, here = here, after


def loop(start, stop, body, unroll=1):
    def step(i, carry):
        body(i)
        return carry

    lax.fori_loop(start, stop, step, 0, unroll=unroll)


def split_dot(a, b):
    high = a.astype(BF16)
    low = (a - high.astype(F32)).astype(BF16)
    return jnp.dot(high, b, preferred_element_type=F32) + jnp.dot(low, b, preferred_element_type=F32)


def pooling():
    return jnp.where(iota((256, 128), 0) // 2 == iota((256, 128), 1), 0.125, 0.0).astype(BF16)


def doubling():
    return jnp.where(iota((128, 256), 1) // 2 == iota((128, 256), 0), 1.0, 0.0).astype(BF16)


def halve_rows(values, rs, t):
    rows = values.shape[0]
    rs[t, 0:rows, :] = values
    return rs[t, pl.ds(0, rows // 2, stride=2), :] + rs[t, pl.ds(1, rows // 2, stride=2), :]


def halve_lanes(xp, planes, rows):
    matrix = pooling()
    tiles = []
    for t in range(0, xp.shape[0], 2):
        pair = jnp.concatenate([xp[t].reshape(planes * rows, 128), xp[t + 1].reshape(planes * rows, 128)], axis=1)
        tiles.append(split_dot(pair, matrix).reshape(planes, rows, 128))
    return tiles


def inside(shape, dim, first, wrap, index, size, count):
    place = iota(shape, dim) + first
    if wrap is not None:
        place = jnp.where(place < wrap, place, place - shape[dim])
    place = place + index * size
    return (place >= 0) & (place < count * size)


BLOCK = 272
X_ROWS = BLOCK + 3 * 64
Z_ROWS = BLOCK + 5 * 64


def uptake_part(t):
    return slice(BLOCK + 64 * (t // 3), BLOCK + 64 * (t // 3) + 64), lanes(t % 3)


def transposed_bricks(bricks_x, ids, counts, bricks, xs, targets):
    xs[...] = bricks[...].astype(F32)
    row = iota((1, 8, 128), 1)
    group = iota((1, 8, 128), 2) // 16
    group16 = iota((16, 128), 1) // 16
    per_y = 64

    def block(j, out, part):
        start = pl.multiple_of(j * 8, 8)
        x = jnp.stack([xs[pl.ds(start, 8), lanes(k)] for k in range(32)])
        for s in (4, 2, 1):
            up = shifted(shifted(x, -s, 1), 16 * s, 2)
            down = shifted(shifted(x, s, 1), -16 * s, 2)
            row_bit = (row // s) % 2
            group_bit = (group // s) % 2
            x = jnp.where(row_bit == group_bit, x, jnp.where(row_bit == 0, up, down))
        x = jnp.where(group < counts[0, j], x, 0.0)
        out[0:256, part] = x.reshape(256, 128).astype(BF16)
        names = jnp.zeros((16, 128), jnp.int32)
        for e in range(CAP):
            number = ids[j * 8 + e]
            by = lax.rem(number, per_y)
            rest = lax.div(number, per_y)
            bx = lax.rem(rest, 2)
            bz = lax.rem(lax.div(rest, bricks_x), 2)
            names = jnp.where(group16 == e, (bz * 2 + bx) * per_y + by, names)
        out[256:272, part] = names.astype(F32).astype(BF16)

    for i, out in enumerate(targets):
        for d in range(3):
            block(3 * i + d, out, lanes(d))


def first_kernel(bricks_x, ids, counts, bricks, uptake_in, own, r1, r2, zl, zh, xl, xh, rs, xp, rs1, xp1, xs, uptake, sems):
    load = pltpu.make_async_copy(uptake_in, uptake, sems.at[0])
    load.start()
    transposed_bricks(bricks_x, ids, counts, bricks, xs, (zl, own, zh))
    load.wait()

    def pair(m):
        for t in range(NT):
            both = uptake[2 * m, :, lanes(t)] + uptake[2 * m + 1, :, lanes(t)]
            xp[t, m] = halve_rows(both, rs, t)

    loop(0, 16, pair)
    for t, tile in enumerate(halve_lanes(xp, 16, 16)):
        r1[:, :, lanes(t)] = tile

    def pair1(m):
        for t in range(4):
            both = r1[2 * m, :, lanes(t)] + r1[2 * m + 1, :, lanes(t)]
            xp1[t, m] = halve_rows(both, rs1, t)

    loop(0, 8, pair1)
    for t, tile in enumerate(halve_lanes(xp1, 8, 8)):
        r2[:, lanes(t)] = tile.reshape(64, 128)
    for ref, u, r in ((zl, slice(0, 2), slice(0, 4)), (zh, slice(30, 32), slice(12, 16))):
        for t in range(8):
            ref[uptake_part(t)] = uptake[u, :, lanes(t)].reshape(64, 128).astype(BF16)
        for t in range(4):
            ref[uptake_part(8 + t)] = r1[r, :, lanes(t)].reshape(64, 128).astype(BF16)
        for t in range(2):
            ref[uptake_part(12 + t)] = r2[:, lanes(t)].astype(BF16)
        ref[uptake_part(14)] = jnp.zeros((64, 128), BF16)

    sub = iota((8, 1024), 0)

    def columns(i):
        lows, highs = [], []
        for j in range(2):
            low, high = jnp.zeros((8, 1024), F32), jnp.zeros((8, 1024), F32)
            for n in range(4):
                z = 8 * i + 4 * j + n
                low = jnp.where(sub // 2 == n, shifted(uptake[z, 0:8, :], 2 * n, 0), low)
                high = jnp.where(sub // 2 == n, shifted(uptake[z, 24:32, :], 2 * n + 2, 0), high)
            lows.append(low)
            highs.append(high)
        rows = pl.ds(pl.multiple_of(16 * i, 16), 16)
        xl[rows, :] = jnp.concatenate(lows, axis=0).astype(BF16)
        xh[rows, :] = jnp.concatenate(highs, axis=0).astype(BF16)

    loop(0, 4, columns)


def far_along_z(nz, iz, to_low, to_high):
    if nz != 4:
        return to_low, to_high
    one = jnp.where(iz < 2, to_high, to_low)
    return one, one


def halves(sub, first, second):
    return jnp.where(sub < 4, first, shifted(second, 4, 1))


def uppers(sub, first, second):
    return jnp.where(sub < 4, shifted(first, 4, 1), second)


def far_messages(window):
    planes, _, width = window.shape
    pairs = window.reshape(planes // 2, 2, 8, width)
    sub = iota((planes // 2, 8, width), 1)
    size = (planes * 4, width)
    return halves(sub, pairs[:, 0], pairs[:, 1]).reshape(size), uppers(sub, pairs[:, 0], pairs[:, 1]).reshape(size)


def far_tile(from_low, from_high):
    width = from_low.shape[-1]
    low, high = from_low.reshape(-1, 8, width), from_high.reshape(-1, 8, width)
    sub = iota(low.shape, 1)
    even = jnp.where(sub < 4, high, shifted(low, 4, 1))
    odd = jnp.where(sub < 4, shifted(high, 4, 1), low)
    return jnp.stack([even, odd], axis=1).reshape(-1, 8, width)


def first_x_kernel(own, r1, uxl, uxh, zl, zh, q1, xl, xh):
    q1[4:20] = r1[...]
    for ref, planes in ((zl, slice(0, 4)), (zh, slice(20, 24))):
        for t in range(4):
            q1[planes, :, lanes(t)] = ref[uptake_part(8 + t)].astype(F32).reshape(4, 16, 128)
    for ref, d in ((xl, 0), (xh, 2)):
        for n, src in enumerate((own, zl, zh)):
            ref[0:BLOCK, lanes(n)] = src[0:BLOCK, lanes(d)]
    sub = iota((8, 128), 0)
    lows, highs = [], []
    for t in range(8):
        xl[uptake_part(t)] = uxl[:, lanes(t)]
        xh[uptake_part(t)] = uxh[:, lanes(t)]
        both = [ref[uptake_part(t)].astype(F32) for ref in (zl, zh)]
        planes = [both[0][0:32], both[0][32:64], both[1][0:32], both[1][32:64]]
        to_low, to_high = jnp.zeros((8, 128), F32), jnp.zeros((8, 128), F32)
        for n, p in enumerate(planes):
            here = sub // 2 == n
            to_low = jnp.where(here, shifted(p[0:8], 2 * n, 0), to_low)
            to_high = jnp.where(here, shifted(p[24:32], 2 * n + 2, 0), to_high)
        lows.append(to_low)
        highs.append(to_high)
    xl[uptake_part(8)] = jnp.concatenate(lows, axis=0).astype(BF16)
    xh[uptake_part(8)] = jnp.concatenate(highs, axis=0).astype(BF16)


FAR = 80


def source_window_kernel(nz, info, own, zl, zh, z2l, z2h, r2, firstl, firsth, f2, q2, near, fl, fh):
    iz = info[0]
    zeros = jnp.zeros((10, 8, 256), F32)
    f2[0:10] = zeros
    f2[22:32] = zeros
    f2[10:22] = own[...].reshape(12, 8, 256)
    for ref, planes in ((zl, slice(2, 14)), (zh, slice(18, 30))):
        part = jnp.concatenate([ref[240:288, 0:256], ref[240:288, 256:512]], axis=0).astype(F32)
        f2[planes] = f2[planes] + part.reshape(12, 8, 256)
    for ref, planes, exists in ((z2l, slice(0, 6), iz >= 2), (z2h, slice(26, 32), iz < nz - 2)):
        part = jnp.where(exists, ref[0:48, :].astype(F32), 0.0)
        f2[planes] = f2[planes] + part.reshape(6, 8, 256)
    q2[0:4] = z2l[48:80, :].astype(F32).reshape(4, 8, 256)
    q2[28:32] = z2h[48:80, :].astype(F32).reshape(4, 8, 256)
    q2[12:20] = r2[...].reshape(8, 8, 256)
    for ref, planes in ((firstl, slice(4, 12)), (firsth, slice(20, 28))):
        for t in range(2):
            q2[planes, :, lanes(t)] = ref[uptake_part(12 + t)].astype(F32).reshape(8, 8, 128)
    near[0:256, :] = f2[...].reshape(256, 256).astype(BF16)
    near[256:288, :] = z2l[48:80, :]
    near[288:320, :] = z2h[48:80, :]
    for i, ref in enumerate((f2, q2)):
        to_low, to_high = far_messages(ref[...])
        fl[128 * i : 128 * i + 128, :] = to_low.astype(BF16)
        fh[128 * i : 128 * i + 128, :] = to_high.astype(BF16)


O = 5
Q = 2
BASE = 1.0 + 6.0 * KAPPA


def scatter(blocks, hot, left):
    lane = iota((128, 128), 1)
    for i, (ref, part) in enumerate(blocks):
        name = ref[256:272, part].astype(F32).astype(jnp.int32)[0:1]
        tiles = lax.shift_right_logical(name, 6)
        at_y = (name & 63) * 16 + (lane[0:1] & 15)
        at_y = jnp.broadcast_to(at_y.astype(F32), (128, 128)).T.astype(jnp.int32)
        for t in range(NT):
            hot[128 * i : 128 * i + 128, lanes(t)] = jnp.where(at_y == lane + 128 * t, 1.0, 0.0).astype(BF16)
        values = ref[0:256, part].astype(F32)
        for tile in range(4):
            left[256 * tile : 256 * tile + 256, lanes(i)] = jnp.where(tiles == tile, values, 0.0).astype(BF16)
    for n in range(4):
        cols = slice(n * 256, (n + 1) * 256)
        sums = jnp.dot(left[...], hot[:, cols], preferred_element_type=F32)
        for tile in range(4):
            bz, bx = tile // 2, tile % 2
            yield 16 * bz, slice(16 * bx, 16 * bx + 16), cols, sums[256 * tile : 256 * tile + 256].reshape(16, 16, 256)


def sweep(src, dst, source, gg, z, sourced):
    for t, here, sums in plane(src, z + O):
        inner = KAPPA * sums
        g = gg[z + Q, :, lanes(t)]
        if sourced:
            body = inner[0:32] + source[z, :, lanes(t)]
            dst[z + O, 0:32, lanes(t)] = KEEP * here[0:32] + g[0:32] * body
            dst[z + O, 32:40, lanes(t)] = KEEP * here[32:40] + g[32:40] * inner[32:40]
        else:
            dst[z + O, :, lanes(t)] = KEEP * here + g * inner


def own_kernel(
    nz, info, own, zl, zh, density, uptake, s_out, g_out, v_out, edge_out,
    dens, upt, s0, g0, v1, edge, va, hot, left, sems,
):
    iz = info[0]
    loads = [pltpu.make_async_copy(density, dens, sems.at[0]), pltpu.make_async_copy(uptake, upt, sems.at[1])]
    stores = [
        pltpu.make_async_copy(src, dst, sems.at[2 + i])
        for i, (src, dst) in enumerate(((s0, s_out), (g0, g_out), (v1, v_out), (edge, edge_out)))
    ]
    for copy in loads:
        copy.start()
    for p in (3, 4, 37, 38):
        va[p] = jnp.zeros((40, 1024), F32)
    for n in range(4):
        ref, valid = (zl, iz > 0) if n < 2 else (zh, iz < nz - 1)
        q = n if n < 2 else 32 + n
        rows = slice(32 * (n % 2), 32 * (n % 2) + 32)
        for t in range(NT):
            g0[q, :, lanes(t)] = jnp.where(valid, OMEGA, 0.0) / (ref[uptake_part(t)].astype(F32)[rows] + BASE)

    blocks = [(ref, lanes(1)) for ref in (own, zl, zh)]
    waiting = list(loads[0:1])
    for z, rows, cols, sums in scatter(blocks, hot, left):
        while waiting:
            waiting.pop().wait()
        planes = slice(z, z + 16)
        s0[planes, rows, cols] = dens[planes, rows, cols] + sums
    stores[0].start()
    loads[1].wait()

    def own_plane(z):
        va[z + O, 0:32, :] = dens[z]
        va[z + O, 32:40, :] = jnp.zeros((8, 1024), F32)
        g0[z + Q] = OMEGA / (upt[z] + BASE)

    loop(0, C, own_plane)
    stores[1].start()

    def first(z):
        for t, here, sums in plane(va, z + O):
            inner = KAPPA * sums
            body = inner[0:32] + s0[z, :, lanes(t)]
            v1[z + 1, :, lanes(t)] = KEEP * here[0:32] + g0[z + Q, :, lanes(t)] * body
            edge[z, :, lanes(t)] = inner[32:40]

    loop(0, C, first, 2)
    for z in (-1, C):
        for t in range(NT):
            near = va[z + O + (1 if z < 0 else -1), 0:32, lanes(t)]
            v1[z + 1, :, lanes(t)] = g0[z + Q, :, lanes(t)] * (KAPPA * near)
    for copy in stores[2:]:
        copy.start()
    for copy in stores:
        copy.wait()


def pre_kernel(
    nz, nx, info, xl, xh, zl, zh, q1, s0, g0, v1, edge_in, uptake,
    c1, mxl, mxh, vzl, vzh, pxl, pxh, v_out, g_out, s_out,
    va, vb, supply, upt, dh, gg, edge, hot, left, rs, xp, usl, ush, sems,
):
    iz, ix = info[0], info[1]
    k = KAPPA
    loads = [
        pltpu.make_async_copy(src, dst, sems.at[i])
        for i, (src, dst) in enumerate(
            (
                (s0, supply),
                (v1, vb.at[4:38, 0:32, :]),
                (g0, gg.at[:, 0:32, :]),
                (edge_in, edge),
                (uptake, upt),
            )
        )
    ]
    for copy in loads:
        copy.start()

    for p in (1, 2, 39, 40):
        va[p] = jnp.zeros((40, 1024), F32)
    for p in (2, 3, 38, 39):
        vb[p] = jnp.zeros((40, 1024), F32)
    for p in (4, 37):
        vb[p, 32:40, :] = jnp.zeros((8, 1024), F32)

    sub8 = iota((8, 1024), 0)
    for t in range(NT):
        usl[0:64, lanes(t)] = xl[uptake_part(t)].astype(F32)
        ush[0:64, lanes(t)] = xh[uptake_part(t)].astype(F32)
        usl[64:72, lanes(t)] = xl[uptake_part(8)].astype(F32)[8 * t : 8 * t + 8]
        ush[64:72, lanes(t)] = xh[uptake_part(8)].astype(F32)[8 * t : 8 * t + 8]

    def set_halo(q, low, high, valid_z):
        gz = jnp.where(valid_z, OMEGA, 0.0)
        d = jnp.where(sub8 < 2, high, jnp.where(sub8 >= 6, low, 0.0)) + BASE
        dh[q] = d
        omega = jnp.where(sub8 < 2, jnp.where(ix < nx - 1, gz, 0.0), jnp.where(sub8 >= 6, jnp.where(ix > 0, gz, 0.0), 0.0))
        gg[q, 32:40, :] = omega / d

    def halos(i):
        rows = pl.ds(pl.multiple_of(8 * i, 8), 8)
        low, high = usl[rows, :], ush[rows, :]
        for n in range(4):
            set_halo(4 * i + n + Q, shifted(low, 6 - 2 * n, 0), shifted(high, -2 * n, 0), True)

    loop(0, C // 4, halos)
    low, high = usl[64:72, :], ush[64:72, :]
    for n in range(4):
        exists = iz > 0 if n < 2 else iz < nz - 1
        set_halo(n if n < 2 else 32 + n, shifted(low, 6 - 2 * n, 0), shifted(high, -2 * n, 0), exists)

    blocks = [(ref, lanes(n)) for ref in (xl, xh) for n in range(3)]
    waiting = list(loads[0:3])
    for z, rows, cols, sums in scatter(blocks, hot, left):
        while waiting:
            waiting.pop().wait()
        supply[z : z + 16, rows, cols] = supply[z : z + 16, rows, cols] + sums
        g = gg[z + Q : z + Q + 16, rows, cols]
        vb[z + O : z + O + 16, rows, cols] = vb[z + O : z + O + 16, rows, cols] + g * sums
    loads[3].wait()

    s_copy = pltpu.make_async_copy(supply, s_out, sems.at[7])
    s_copy.start()

    def edges(z):
        vb[z + O, 32:40, :] = gg[z + Q, 32:40, :] * edge[z]

    loop(0, C, edges)

    loop(0, C, lambda z: sweep(vb, va, supply, gg, z, True), 2)
    loop(0, 4, lambda i: sweep(vb, va, supply, gg, jnp.where(i < 2, i - 2, i + C - 2), False))
    loads[4].wait()
    v_copy = pltpu.make_async_copy(va.at[3:39], v_out, sems.at[5])
    g_copy = pltpu.make_async_copy(gg, g_out, sems.at[6])
    v_copy.start()
    g_copy.start()

    def residual(z, rates, sourced):
        for t, here, sums in plane(va, z + O):
            r = k * sums
            if rates is not None:
                inner = r[0:32] - (rates(t) + BASE) * here[0:32]
                if sourced:
                    inner = inner + supply[z, :, lanes(t)]
                r = jnp.concatenate([inner, r[32:40] - dh[z + Q, :, lanes(t)] * here[32:40]], axis=0)
            yield t, r

    def coarse(m, zs, rates, sourced):
        parts = [residual(zs[i], rates[i], sourced) for i in range(2)]
        for (t, first), (_, second) in zip(*parts):
            xp[t, m, 0:20, :] = halve_rows(first + second, rs, t)

    def from_message(ref, n):
        return lambda t: ref[uptake_part(t)].astype(F32)[32 * n : 32 * n + 32]

    def inner(m):
        zs = (2 * m - 4, 2 * m - 3)
        coarse(m, zs, [lambda t, z=z: upt[z, :, lanes(t)] for z in zs], True)

    loop(2, 18, inner)
    for m, ref, z in ((1, zl, -2), (18, zh, C)):
        coarse(m, (z, z + 1), [from_message(ref, 0), from_message(ref, 1)], False)

    def outer(i):
        for t, r in residual(jnp.where(i == 0, -3, 34), None, False):
            xp[t, 19 * i, 0:20, :] = halve_rows(r, rs, t)

    loop(0, 2, outer)

    sub = iota((20, 8, 128), 1)
    for t, tile in enumerate(halve_lanes(xp, 20, 24)):
        last = tile[:, 16:24]
        last = jnp.where(sub < 2, last, jnp.where(sub >= 6, shifted(last, 4, 1), 0.0))
        c1[:, 0:16, lanes(t)] = tile[:, 0:16]
        c1[:, 16:24, lanes(t)] = last

    empty = jnp.zeros((1, 8, 1024), F32)
    blank = jnp.zeros((8, 1024), F32)
    sub1 = iota((5, 8, 512), 1)
    first, last, halo = [c1[:, 8 * n : 8 * n + 8].reshape(5, 4, 8, 512) for n in range(3)]
    sub4 = iota((5, 4, 8, 512), 2)
    to_high = in_three(sub1, jnp.where(sub4 >= 4, last, halo), *HIGH_PACK)
    to_low = in_three(sub1, jnp.where(sub4 >= 4, halo, first), *LOW_PACK)
    sub1 = iota((12, 8, 512), 1)
    first = q1[:, 0:8, :].reshape(12, 2, 8, 512)
    last = q1[:, 8:16, :].reshape(12, 2, 8, 512)
    low_rates = halves(sub1, first[:, 0], first[:, 1]).reshape(96, 512)
    high_rates = uppers(sub1, last[:, 0], last[:, 1]).reshape(96, 512)
    filler = jnp.zeros((8, 512), F32)
    for ref, sources, rates in ((mxl, to_low, low_rates), (mxh, to_high, high_rates)):
        ref[0:128, :] = jnp.concatenate([sources.reshape(120, 512), filler], axis=0).astype(BF16)
        ref[128:224, :] = rates.astype(BF16)

    for level0, p, z in ((vzl, 3, 0), (vzh, 35, 31)):
        values = jnp.concatenate([va[p : p + 4], jnp.concatenate([supply[z : z + 1], empty], axis=1)], axis=0)
        level0[0:208, :] = jnp.concatenate([values.reshape(200, 1024), blank], axis=0).astype(BF16)
        for i, pack in enumerate((pack_low, pack_high)):
            corner = jnp.concatenate([pack(va[p], va[p + 1]), pack(va[p + 2], va[p + 3])], axis=0)
            level0[208 + 16 * i : 224 + 16 * i, :] = corner.astype(BF16)

    def sides(i):
        lows, highs = [], []
        for j in range(2):
            p = 4 * i + 2 * j + 3
            lows.append(pack_low(va[p], va[p + 1]))
            highs.append(pack_high(va[p], va[p + 1]))
        rows = pl.ds(pl.multiple_of(16 * i, 16), 16)
        pxl[rows, :] = jnp.concatenate(lows, axis=0).astype(BF16)
        pxh[rows, :] = jnp.concatenate(highs, axis=0).astype(BF16)

    loop(0, 9, sides)

    def sources(i):
        lows, highs = [], []
        for j in range(2):
            low, high = jnp.zeros((8, 1024), F32), jnp.zeros((8, 1024), F32)
            for n in range(8):
                z = 16 * i + 8 * j + n
                low = jnp.where(sub8 == n, shifted(supply[z, 0:8, :], n, 0), low)
                high = jnp.where(sub8 == n, shifted(supply[z, 24:32, :], n + 1, 0), high)
            lows.append(low)
            highs.append(high)
        rows = pl.ds(pl.multiple_of(16 * i + 144, 16), 16)
        pxl[rows, :] = jnp.concatenate(lows, axis=0).astype(BF16)
        pxh[rows, :] = jnp.concatenate(highs, axis=0).astype(BF16)

    loop(0, 2, sources)
    v_copy.wait()
    g_copy.wait()
    s_copy.wait()


def outer_rows(sub):
    return (sub < 2) | (sub >= 6)


def pack_pair(sub, a, b):
    return jnp.where(outer_rows(sub), a, shifted(b, 4, 0))


def pack_low(first, second):
    sub = iota((8, 1024), 0)
    a, b = [jnp.where(sub < 4, v[0:8], v[32:40]) for v in (first, second)]
    return pack_pair(sub, a, b)


def pack_high(first, second):
    sub = iota((8, 1024), 0)
    a, b = [jnp.where(sub >= 4, v[24:32], v[32:40]) for v in (first, second)]
    return pack_pair(sub, a, b)


def sides_kernel(pxl, pxh, vzl, vzh, firstl, firsth, r2, out_l, out_h):
    for ref, out in ((pxl, out_l), (pxh, out_h)):
        out[0:176, :] = ref[...]
        for t in range(2):
            out[176:240, lanes(t)] = firstl[uptake_part(12 + t)]
            out[176:240, lanes(2 + t)] = r2[:, lanes(t)].astype(BF16)
            out[176:240, lanes(4 + t)] = firsth[uptake_part(12 + t)]
        out[176:240, 768:1024] = jnp.zeros((64, 256), BF16)
    for message, start in ((vzl, 0), (vzh, 128)):
        rows = slice(start, start + 16)
        for i, (ref, out) in enumerate(((pxl, out_l), (pxh, out_h))):
            corner = message[208 + 16 * i : 224 + 16 * i, :]
            out[rows, :] = (ref[rows, :].astype(F32) + corner.astype(F32)).astype(BF16)


def in_three(sub, tiles, free, turns):
    spare = (sub == free) | (sub == free + 1)
    last = tiles[:, 3]
    parts = [jnp.where(spare, shifted(last, turn, 1), tiles[:, i]) for i, turn in enumerate(turns)]
    return jnp.stack(parts, axis=1)


def out_of_three(sub, parts, free, turns):
    last = None
    for i, turn in enumerate(turns):
        back = shifted(parts[:, i], -turn, 1)
        home = (free - turn) % 8
        here = (sub == home) | (sub == home + 1)
        last = jnp.where(here, back, 0.0 if last is None else last)
    return jnp.stack([parts[:, 0], parts[:, 1], parts[:, 2], last], axis=1)


HIGH_PACK = (2, (-2, 4, 2))
LOW_PACK = (4, (-2, 4, 2))


def middle_kernel(nz, nx, info, c1, q_in, r2, mxl, mxh, f1, g1, v1, g2, z1l, z1h, z2l, z2h, q0, va, vv, rs, xp):
    iz, ix = info[0], info[1]
    k = spread(1)
    base = 1.0 + 6.0 * k
    sub5 = iota((5, 8, 512), 1)
    low = out_of_three(sub5, mxl[0:128, :].astype(F32)[0:120].reshape(5, 3, 8, 512), *HIGH_PACK).reshape(20, 8, 512)
    high = out_of_three(sub5, mxh[0:128, :].astype(F32)[0:120].reshape(5, 3, 8, 512), *LOW_PACK).reshape(20, 8, 512)
    sub = iota((20, 8, 512), 1)
    for p in (0, 1, 22, 23):
        f1[p] = jnp.zeros((24, 512), F32)
    f1[2:22, 0:8] = c1[:, 0:8] + jnp.where(sub < 2, low, 0.0)
    f1[2:22, 8:16] = c1[:, 8:16] + jnp.where(sub >= 6, high, 0.0)
    f1[2:22, 16:24] = c1[:, 16:24] + jnp.where(sub >= 4, low, high)
    low, high = [ref[128:224, :].astype(F32).reshape(12, 8, 512) for ref in (mxl, mxh)]
    sub12 = iota((12, 8, 512), 1)
    even = jnp.where(sub12 >= 4, shifted(low, 4, 1), high)
    odd = jnp.where(sub12 >= 4, low, shifted(high, 4, 1))
    q0[:, 0:16] = q_in[...]
    q0[:, 16:24] = jnp.stack([even, odd], axis=1).reshape(24, 8, 512)
    shape = (24, 24, 128)
    valid = inside(shape, 0, -4, None, iz, 16, nz) & inside(shape, 1, 0, 20, ix, 16, nx)
    for t in range(4):
        g = jnp.where(valid, OMEGA, 0.0) / (q0[:, :, lanes(t)] + base)
        g1[:, :, lanes(t)] = g
        va[:, :, lanes(t)] = g * f1[:, :, lanes(t)]
    for p in (0, 1, 24, 25):
        vv[p] = jnp.zeros((24, 512), F32)

    def sweep(p):
        for t, here, sums in plane(va, p):
            vv[p + 1, :, lanes(t)] = KEEP * here + g1[p, :, lanes(t)] * (f1[p, :, lanes(t)] + k * sums)

    loop(1, 23, sweep, 2)
    v1[...] = vv[1:25]

    def residual(p):
        for t, here, sums in plane(vv, p + 1):
            yield t, f1[p, :, lanes(t)] + k * sums - (q0[p, :, lanes(t)] + base) * here

    def coarse(m):
        for (t, first), (_, second) in zip(residual(2 * m), residual(2 * m + 1)):
            xp[t, m] = halve_rows((first + second)[0:16], rs, t)

    loop(0, 12, coarse)
    for t, tile in enumerate(halve_lanes(xp, 12, 8)):
        g2[:, lanes(t)] = tile.reshape(96, 128)
        for ref in (z1l, z1h):
            ref[240:288, lanes(t)] = tile[0:6].reshape(48, 128).astype(BF16)
            ref[240:288, lanes(2 + t)] = tile[6:12].reshape(48, 128).astype(BF16)
    for ref, p in ((z1l, 2), (z1h, 18)):
        ref[0:144, :] = vv[p : p + 6].reshape(144, 512).astype(BF16)
        ref[144:240, :] = f1[p : p + 4].reshape(96, 512).astype(BF16)
    low, high = far_along_z(nz, iz, g2[0:48, :], g2[48:96, :])
    z2l[0:48, :] = low.astype(BF16)
    z2h[0:48, :] = high.astype(BF16)
    low, high = far_along_z(nz, iz, r2[0:32, :], r2[32:64, :])
    z2l[48:80, :] = low.astype(BF16)
    z2h[48:80, :] = high.astype(BF16)


def back_kernel(
    nz, nx, info, f_in, g1, v1, z1l, z1h, vzl, vzh, vxl, vxh, own2, n2l, n2h, m2l, m2h, q_own, v_in, g_in, s_in,
    out_hbm,
    f2, q2, h2, a2, b2, rs, xp, xpr, wa, w1, zsl, zsh, vb, ws,
    v2, gg, supply, fsl, fsh, out, f1, sems,
):
    iz, ix = info[0], info[1]
    matrix = doubling()
    level0 = [
        pltpu.make_async_copy(src, dst, sems.at[i])
        for i, (src, dst) in enumerate(((v_in, v2), (g_in, gg), (s_in, supply)))
    ]
    for copy in level0:
        copy.start()

    f1[...] = f_in[...]
    wa[...] = v1[...]
    for ref, p in ((z1l, 1), (z1h, 17)):
        wa[p : p + 6] = wa[p : p + 6] + ref[0:144, :].astype(F32).reshape(6, 24, 512)
        f1[p + 1 : p + 5] = f1[p + 1 : p + 5] + ref[144:240, :].astype(F32).reshape(4, 24, 512)

    f2[:, 0:8, :] = own2[...]
    f2[:, 8:16, :] = n2h[0:256, :].astype(F32).reshape(32, 8, 256)
    f2[:, 16:24, :] = far_tile(m2l[0:128, :].astype(F32), m2h[0:128, :].astype(F32))
    f2[:, 24:32, :] = n2l[0:256, :].astype(F32).reshape(32, 8, 256)
    q2[:, 0:8, :] = q_own[...]
    q2[:, 16:24, :] = far_tile(m2l[128:256, :].astype(F32), m2h[128:256, :].astype(F32))
    for ref, rows in ((vxh, slice(8, 16)), (vxl, slice(24, 32))):
        for n in range(3):
            q2[8 * n + 4 : 8 * n + 12, rows, :] = ref[176:240, n * 256 : n * 256 + 256].astype(F32).reshape(8, 8, 256)
    for ref, rows in ((n2h, slice(8, 16)), (n2l, slice(24, 32))):
        outer = ref[256:320, :].astype(F32).reshape(8, 8, 256)
        q2[0:4, rows, :] = outer[0:4]
        q2[28:32, rows, :] = outer[4:8]

    k = spread(2)
    base = 1.0 + 6.0 * k
    shape = (32, 32, 128)
    valid = inside(shape, 0, -12, None, iz, 8, nz) & inside(shape, 1, 0, 20, ix, 8, nx)
    for t in range(2):
        g = jnp.where(valid, OMEGA, 0.0) / (q2[:, :, lanes(t)] + base)
        h2[:, :, lanes(t)] = g
        a2[:, :, lanes(t)] = g * f2[:, :, lanes(t)]
    b2[0] = a2[0]
    b2[31] = a2[31]

    def sweep2(src, dst):
        def body(p):
            for t, here, sums in plane(src, p):
                dst[p, :, lanes(t)] = KEEP * here + h2[p, :, lanes(t)] * (f2[p, :, lanes(t)] + k * sums)

        return body

    loop(1, 31, sweep2(a2, b2), 2)

    def coarse(m):
        total, rates = [0.0, 0.0], [0.0, 0.0]
        for j in range(2):
            p = 2 * m + j
            for t, here, sums in plane(b2, p):
                r = f2[p, :, lanes(t)] + k * sums - (q2[p, :, lanes(t)] + base) * here
                total[t] = total[t] + r
                rates[t] = rates[t] + q2[p, :, lanes(t)]
        for t in range(2):
            xp[t, m] = halve_rows(total[t], rs, t)
            xpr[t, m] = halve_rows(rates[t], rs, t + 2)

    for t in range(2):
        for m in (0, 15):
            xp[t, m] = jnp.zeros((16, 128), F32)
            xpr[t, m] = jnp.zeros((16, 128), F32)
    loop(1, 15, coarse)

    shape = (16, 16, 128)
    valid = inside(shape, 0, -6, None, iz, 4, nz) & inside(shape, 1, 0, 10, ix, 4, nx)
    k3 = spread(3)
    (source,) = halve_lanes(xp, 16, 16)
    (rates,) = halve_lanes(xpr, 16, 16)
    g = jnp.where(valid, OMEGA, 0.0) / (rates + (1.0 + 6.0 * k3))
    v = g * source
    lane = iota(shape, 2)
    for repeat in range(3):
        edge = jnp.zeros((1, 16, 128), F32)
        sums = jnp.concatenate([v[1:], edge], axis=0) + jnp.concatenate([edge, v[:-1]], axis=0)
        sums = sums + shifted(v, 1, 1) + shifted(v, -1, 1)
        sums = sums + jnp.where(lane == 0, 0.0, shifted(v, 1, 2)) + jnp.where(lane == 127, 0.0, shifted(v, -1, 2))
        v = KEEP * v + g * (source + k3 * sums)

    wide = split_dot(v[4:12].reshape(128, 128), matrix).reshape(8, 16, 256)
    for m in range(8):
        for t in range(2):
            part = wide[m, :, lanes(t)]
            rs[t, pl.ds(0, 16, stride=2), :] = part
            rs[t, pl.ds(1, 16, stride=2), :] = part
            for j in range(2):
                p = 8 + 2 * m + j
                b2[p, :, lanes(t)] = b2[p, :, lanes(t)] + rs[t, 0:32, :]
    loop(9, 23, sweep2(b2, a2), 2)
    loop(10, 22, sweep2(a2, b2), 2)

    w = b2[10:22]
    near, far = w[:, 8:16], w[:, 24:32]
    near = jnp.where(iota((12, 8, 256), 1) < 2, near, shifted(far, 4, 1))
    w = jnp.concatenate([w[:, 0:8], near], axis=1).reshape(192, 256)
    wide = [split_dot(w[:, lanes(t)], matrix) for t in range(2)]
    wide = jnp.concatenate(wide, axis=1).reshape(12, 16, 512)
    for m in range(12):
        for t in range(4):
            part = wide[m, :, lanes(t)]
            rs[t, pl.ds(0, 16, stride=2), :] = part
            rs[t, pl.ds(1, 16, stride=2), :] = part
            for j in range(2):
                p = 2 * m + j
                wa[p, :, lanes(t)] = wa[p, :, lanes(t)] + rs[t, 0:24, :]
    k1 = spread(1)

    def sweep1(src, dst):
        def body(p):
            for t, here, sums in plane(src, p):
                dst[p, :, lanes(t)] = KEEP * here + g1[p, :, lanes(t)] * (f1[p, :, lanes(t)] + k1 * sums)

        return body

    loop(2, 22, sweep1(wa, w1), 2)
    loop(3, 21, sweep1(w1, wa), 2)

    sub = iota((18, 8, 128), 1)
    for t in range(4):
        halo = wa[3:21, 16:24, lanes(t)]
        halo = jnp.where(sub < 2, halo, shifted(halo, 4, 1))
        w = jnp.concatenate([wa[3:21, 0:16, lanes(t)], halo], axis=1)
        ws[:, :, t * 256 : t * 256 + 256] = split_dot(w.reshape(432, 128), matrix).reshape(18, 24, 256)

    for copy in level0:
        copy.wait()
    zsl[...] = vzl[0:208, :].astype(F32)
    zsh[...] = vzh[0:208, :].astype(F32)
    for i in range(4):
        v2[i] = v2[i] + zsl[40 * i : 40 * i + 40, :]
        v2[32 + i] = v2[32 + i] + zsh[40 * i : 40 * i + 40, :]

    s8 = iota((8, 128), 0)

    outer = outer_rows(s8)

    def correct(i):
        rows = pl.ds(pl.multiple_of(16 * i, 16), 16)
        for t in range(NT):
            low = vxl[rows, lanes(t)].astype(F32)
            high = vxh[rows, lanes(t)].astype(F32)
            for n in range(2):
                part = ws[2 * i + n, :, lanes(t)]
                rs[t, pl.ds(0, 24, stride=2), :] = part
                rs[t, pl.ds(1, 24, stride=2), :] = part
                for j in range(2):
                    p = 4 * i + 2 * n + j
                    lo, hi = low[8 * n : 8 * n + 8], high[8 * n : 8 * n + 8]
                    if j:
                        lo, hi = shifted(lo, 4, 0), shifted(hi, 4, 0)
                    v2[p, 0:8, lanes(t)] = v2[p, 0:8, lanes(t)] + rs[t, 0:8, :] + jnp.where(s8 < 2, lo, 0.0)
                    v2[p, 8:24, lanes(t)] = v2[p, 8:24, lanes(t)] + rs[t, 8:24, :]
                    v2[p, 24:32, lanes(t)] = v2[p, 24:32, lanes(t)] + rs[t, 24:32, :] + jnp.where(s8 >= 6, hi, 0.0)
                    extra = jnp.where(outer, jnp.where(s8 >= 4, lo, hi), 0.0)
                    v2[p, 32:40, lanes(t)] = v2[p, 32:40, lanes(t)] + rs[t, 32:40, :] + extra

    loop(0, 9, correct)
    k0 = spread(0)

    def first(i):
        rows = pl.ds(pl.multiple_of(16 * i + 144, 16), 16)
        for t in range(NT):
            fsl[:, lanes(t)] = vxl[rows, lanes(t)].astype(F32)
            fsh[:, lanes(t)] = vxh[rows, lanes(t)].astype(F32)

        def step(j):
            z = 16 * i + j
            start = pl.multiple_of((j // 8) * 8, 8)
            turn = lax.rem(j, 8)
            for t, here, sums in plane(v2, z + 2):
                lo = pltpu.roll(fsl[pl.ds(start, 8), lanes(t)], 7 - turn, 0)
                hi = pltpu.roll(fsh[pl.ds(start, 8), lanes(t)], lax.rem(8 - turn, 8), 0)
                f = jnp.where(s8 == 7, lo, jnp.where(s8 == 0, hi, 0.0))
                g = gg[z + 2, :, lanes(t)]
                inner = k0 * sums
                vb[z + 1, 0:32, lanes(t)] = KEEP * here[0:32] + g[0:32] * (supply[z, :, lanes(t)] + inner[0:32])
                vb[z + 1, 32:40, lanes(t)] = KEEP * here[32:40] + g[32:40] * (f + inner[32:40])

        loop(0, 16, step, 2)

    loop(0, 2, first)
    for p, ref in ((1, zsl), (34, zsh)):
        for t, here, sums in plane(v2, p):
            g = gg[p, :, lanes(t)]
            vb[p - 1, :, lanes(t)] = KEEP * here + g * (ref[160:200, lanes(t)] + k0 * sums)

    def second(z):
        for t, here, sums in plane(vb, z + 1):
            g = gg[z + 2, 0:32, lanes(t)]
            out[z, :, lanes(t)] = KEEP * here[0:32] + g * (supply[z, :, lanes(t)] + k0 * sums[0:32])

    stores = []
    for i in range(4):
        part = pl.ds(8 * i, 8)
        loop(8 * i, 8 * i + 8, second, 2)
        stores.append(pltpu.make_async_copy(out.at[part], out_hbm.at[part], sems.at[3 + i]))
        stores[i].start()
    for copy in stores:
        copy.wait()


VMEM = pl.BlockSpec(memory_space=pltpu.VMEM)
SMEM = pl.BlockSpec(memory_space=pltpu.SMEM)
ANY = pl.BlockSpec(memory_space=pl.ANY)


def call(kernel, outs, scratch, smem, args, out_specs=None, in_hbm=0):
    moved = sum(a.size * a.dtype.itemsize for a in list(args) + list(outs))
    return pl.pallas_call(
        kernel,
        out_shape=tuple(outs),
        in_specs=[SMEM] * smem + [VMEM] * (len(args) - smem - in_hbm) + [ANY] * in_hbm,
        out_specs=tuple(out_specs or [VMEM] * len(outs)),
        scratch_shapes=scratch,
        compiler_params=pltpu.CompilerParams(vmem_limit_bytes=58 * 2**20),
        cost_estimate=pl.CostEstimate(flops=20 * moved, bytes_accessed=moved, transcendentals=0),
    )(*args)


def shaped(shape, dtype=F32):
    return jax.ShapeDtypeStruct(shape, dtype)


def both_ways(to_low, to_high, axis, distance=1):
    count = lax.axis_size(axis)
    up = [(i, i + distance) for i in range(count - distance)]
    down = [(j, i) for i, j in up]
    return lax.ppermute(to_high, axis, up), lax.ppermute(to_low, axis, down)


def two_away(to_low, to_high):
    count = lax.axis_size("gz")
    if count != 4:
        return both_ways(to_low, to_high, "gz", 2)
    came = lax.ppermute(to_low, "gz", [(i, (i + 2) % 4) for i in range(4)])
    return came, came


def shards(density, uptake, brick_values, brick_ids, slot_counts):
    nz, nx = lax.axis_size("gz"), lax.axis_size("xy")
    info = jnp.stack([lax.axis_index("gz"), lax.axis_index("xy")]).astype(jnp.int32)
    scratch = pltpu.VMEM
    half = lambda *shape: shaped(shape, BF16)
    full = lambda *shape: shaped(shape, F32)

    own, r1, r2, zl, zh, uxl, uxh = call(
        lambda *refs: first_kernel(2 * nx, *refs),
        [
            half(BLOCK, 384), full(16, 16, 512), full(64, 256), half(Z_ROWS, 384), half(Z_ROWS, 384),
            half(64, 1024), half(64, 1024),
        ],
        [
            scratch((8, 32, 128), F32), scratch((8, 16, 16, 128), F32), scratch((4, 16, 128), F32),
            scratch((4, 8, 8, 128), F32), scratch((SLOTS, BRICK), F32), scratch((C, C, 1024), F32),
            pltpu.SemaphoreType.DMA((1,)),
        ],
        2,
        (brick_ids, slot_counts, brick_values, uptake),
        in_hbm=1,
    )
    zl, zh = both_ways(zl, zh, "gz")
    q1, xl, xh = call(
        first_x_kernel,
        [full(24, 16, 512), half(X_ROWS, 384), half(X_ROWS, 384)],
        [],
        0,
        (own, r1, uxl, uxh, zl, zh),
    )
    s0, g0, v1, edge = call(
        lambda *refs: own_kernel(nz, *refs),
        [full(C, C, 1024), full(36, C, 1024), full(34, C, 1024), full(C, 8, 1024)],
        [
            scratch((C, C, 1024), F32),
            scratch((C, C, 1024), F32),
            scratch((C, C, 1024), F32),
            scratch((36, C, 1024), F32),
            scratch((34, C, 1024), F32),
            scratch((C, 8, 1024), F32),
            scratch((42, 40, 1024), F32),
            scratch((384, 1024), BF16),
            scratch((1024, 384), BF16),
            pltpu.SemaphoreType.DMA((6,)),
        ],
        1,
        (info, own, zl, zh, density, uptake),
        [ANY] * 4,
        in_hbm=2,
    )
    xl, xh = both_ways(xl, xh, "xy")

    c1, mxl, mxh, vzl, vzh, pxl, pxh, v2, gg, supply = call(
        lambda *refs: pre_kernel(nz, nx, *refs),
        [
            full(20, 24, 512),
            half(224, 512),
            half(224, 512),
            half(240, 1024),
            half(240, 1024),
            half(176, 1024),
            half(176, 1024),
            full(36, 40, 1024),
            full(36, 40, 1024),
            full(C, C, 1024),
        ],
        [
            scratch((42, 40, 1024), F32),
            scratch((42, 40, 1024), F32),
            scratch((C, C, 1024), F32),
            scratch((C, C, 1024), F32),
            scratch((36, 8, 1024), F32),
            scratch((36, 40, 1024), F32),
            scratch((C, 8, 1024), F32),
            scratch((768, 1024), BF16),
            scratch((1024, 768), BF16),
            scratch((8, 40, 128), F32),
            scratch((8, 20, 24, 128), F32),
            scratch((72, 1024), F32),
            scratch((72, 1024), F32),
            pltpu.SemaphoreType.DMA((8,)),
        ],
        1,
        (info, xl, xh, zl, zh, q1, s0, g0, v1, edge, uptake),
        [VMEM] * 7 + [ANY] * 3,
        in_hbm=5,
    )
    mxl, mxh = both_ways(mxl, mxh, "xy")
    vzl, vzh = both_ways(vzl, vzh, "gz")
    pxl, pxh = call(
        sides_kernel,
        [half(240, 1024), half(240, 1024)],
        [],
        0,
        (pxl, pxh, vzl, vzh, zl, zh, r2),
    )
    c1, mxl, mxh, pxl, pxh = lax.optimization_barrier((c1, mxl, mxh, pxl, pxh))
    vxl, vxh = both_ways(pxl, pxh, "xy")
    f1, g1, v1, g2, z1l, z1h, z2l, z2h = call(
        lambda *refs: middle_kernel(nz, nx, *refs),
        [
            full(24, 24, 512), full(24, 24, 512), full(24, 24, 512), full(96, 256),
            half(288, 512), half(288, 512), half(FAR, 256), half(FAR, 256),
        ],
        [
            scratch((24, 24, 512), F32), scratch((24, 24, 512), F32), scratch((26, 24, 512), F32),
            scratch((4, 16, 128), F32), scratch((4, 12, 8, 128), F32),
        ],
        1,
        (info, c1, q1, r2, mxl, mxh),
    )
    z1l, z1h = both_ways(z1l, z1h, "gz")
    z2l, z2h = two_away(z2l, z2h)
    own2, q2, near, fl, fh = call(
        lambda *refs: source_window_kernel(nz, *refs),
        [full(32, 8, 256), full(32, 8, 256), half(320, 256), half(256, 256), half(256, 256)],
        [],
        1,
        (info, g2, z1l, z1h, z2l, z2h, r2, zl, zh),
    )
    nl, nh = both_ways(near, near, "xy")
    fl, fh = both_ways(fl, fh, "xy", 2)
    window2 = scratch((32, 32, 256), F32)
    window1 = scratch((24, 24, 512), F32)
    (concentration,) = call(
        lambda *refs: back_kernel(nz, nx, *refs),
        [full(C, C, 1024)],
        [
            window2, window2, window2, window2, window2,
            scratch((8, 48, 128), F32),
            scratch((2, 16, 16, 128), F32),
            scratch((2, 16, 16, 128), F32),
            window1, window1,
            scratch((208, 1024), F32),
            scratch((208, 1024), F32),
            scratch((34, 40, 1024), F32),
            scratch((18, 24, 1024), F32),
            scratch((36, 40, 1024), F32),
            scratch((36, 40, 1024), F32),
            scratch((C, C, 1024), F32),
            scratch((16, 1024), F32),
            scratch((16, 1024), F32),
            scratch((C, C, 1024), F32),
            window1,
            pltpu.SemaphoreType.DMA((7,)),
        ],
        1,
        (info, f1, g1, v1, z1l, z1h, vzl, vzh, vxl, vxh, own2, nl, nh, fl, fh, q2, v2, gg, supply),
        [ANY],
        in_hbm=3,
    )
    return supply, concentration


def solution(mesh):
    return jax.shard_map(
        shards,
        mesh=mesh,
        in_specs=(
            P("gz", "xy", None),
            P("gz", "xy", None),
            P(("gz", "xy"), None),
            P(("gz", "xy")),
            P(("gz", "xy"), None),
        ),
        out_specs=(P("gz", "xy", None), P("gz", "xy", None)),
        check_vma=False,
    )
```

```python
import jax
import jax.numpy as jnp
from jax import lax
from jax.experimental import pallas as pl
from jax.experimental.pallas import tpu as pltpu
from jax.sharding import PartitionSpec as P

EDGE = 16
CAP = 8
BRICK = 4096
SLOTS = 72
KAPPA = 32.0
OMEGA = 0.8
KEEP = 1.0 - OMEGA

C = 32
NT = 8
F32 = jnp.float32
BF16 = jnp.bfloat16


def spread(level):
    return KAPPA / 4.0**level


def shifted(values, distance, axis):
    return pltpu.roll(values, distance % values.shape[axis], axis)


def iota(shape, dim):
    return lax.broadcasted_iota(jnp.int32, shape, dim)


def lanes(t):
    return slice(t * 128, (t + 1) * 128)


def plane(ref, p):
    count = ref.shape[2] // 128
    rows = ref.shape[1]
    lane = iota((rows, 128), 1)
    before, here = None, ref[p, :, lanes(0)]
    for t in range(count):
        after = ref[p, :, lanes(t + 1)] if t + 1 < count else None
        low = jnp.where(lane == 127, 0.0 if before is None else before, here)
        high = jnp.where(lane == 0, 0.0 if after is None else after, here)
        sums = shifted(low, 1, 1) + shifted(high, -1, 1)
        sums = sums + (shifted(here, 1, 0) + shifted(here, -1, 0))
        sums = sums + (ref[p - 1, :, lanes(t)] + ref[p + 1, :, lanes(t)])
        yield t, here, sums
        before, here = here, after


def loop(start, stop, body, unroll=1):
    def step(i, carry):
        body(i)
        return carry

    lax.fori_loop(start, stop, step, 0, unroll=unroll)


def split_dot(a, b):
    high = a.astype(BF16)
    low = (a - high.astype(F32)).astype(BF16)
    return jnp.dot(high, b, preferred_element_type=F32) + jnp.dot(low, b, preferred_element_type=F32)


def pooling():
    return jnp.where(iota((256, 128), 0) // 2 == iota((256, 128), 1), 0.125, 0.0).astype(BF16)


def doubling():
    return jnp.where(iota((128, 256), 1) // 2 == iota((128, 256), 0), 1.0, 0.0).astype(BF16)


def halve_rows(values, rs, t):
    rows = values.shape[0]
    rs[t, 0:rows, :] = values
    return rs[t, pl.ds(0, rows // 2, stride=2), :] + rs[t, pl.ds(1, rows // 2, stride=2), :]


def halve_lanes(xp, planes, rows):
    matrix = pooling()
    tiles = []
    for t in range(0, xp.shape[0], 2):
        pair = jnp.concatenate([xp[t].reshape(planes * rows, 128), xp[t + 1].reshape(planes * rows, 128)], axis=1)
        tiles.append(split_dot(pair, matrix).reshape(planes, rows, 128))
    return tiles


def inside(shape, dim, first, wrap, index, size, count):
    place = iota(shape, dim) + first
    if wrap is not None:
        place = jnp.where(place < wrap, place, place - shape[dim])
    place = place + index * size
    return (place >= 0) & (place < count * size)


BLOCK = 272
X_ROWS = BLOCK + 3 * 64
Z_ROWS = BLOCK + 5 * 64


def uptake_part(t):
    return slice(BLOCK + 64 * (t // 3), BLOCK + 64 * (t // 3) + 64), lanes(t % 3)


def transposed_bricks(bricks_x, ids, counts, bricks, xs, targets):
    xs[...] = bricks[...].astype(F32)
    row = iota((1, 8, 128), 1)
    group = iota((1, 8, 128), 2) // 16
    group16 = iota((16, 128), 1) // 16
    per_y = 64

    def block(j, out, part):
        start = pl.multiple_of(j * 8, 8)
        x = jnp.stack([xs[pl.ds(start, 8), lanes(k)] for k in range(32)])
        for s in (4, 2, 1):
            up = shifted(shifted(x, -s, 1), 16 * s, 2)
            down = shifted(shifted(x, s, 1), -16 * s, 2)
            row_bit = (row // s) % 2
            group_bit = (group // s) % 2
            x = jnp.where(row_bit == group_bit, x, jnp.where(row_bit == 0, up, down))
        x = jnp.where(group < counts[0, j], x, 0.0)
        out[0:256, part] = x.reshape(256, 128).astype(BF16)
        names = jnp.zeros((16, 128), jnp.int32)
        for e in range(CAP):
            number = ids[j * 8 + e]
            by = lax.rem(number, per_y)
            rest = lax.div(number, per_y)
            bx = lax.rem(rest, 2)
            bz = lax.rem(lax.div(rest, bricks_x), 2)
            names = jnp.where(group16 == e, (bz * 2 + bx) * per_y + by, names)
        out[256:272, part] = names.astype(F32).astype(BF16)

    for i, out in enumerate(targets):
        for d in range(3):
            block(3 * i + d, out, lanes(d))


def first_kernel(bricks_x, ids, counts, bricks, uptake_in, own, r1, r2, zl, zh, xl, xh, rs, xp, rs1, xp1, xs, uptake, sems):
    load = pltpu.make_async_copy(uptake_in, uptake, sems.at[0])
    load.start()
    transposed_bricks(bricks_x, ids, counts, bricks, xs, (zl, own, zh))
    load.wait()

    def pair(m):
        for t in range(NT):
            both = uptake[2 * m, :, lanes(t)] + uptake[2 * m + 1, :, lanes(t)]
            xp[t, m] = halve_rows(both, rs, t)

    loop(0, 16, pair)
    for t, tile in enumerate(halve_lanes(xp, 16, 16)):
        r1[:, :, lanes(t)] = tile

    def pair1(m):
        for t in range(4):
            both = r1[2 * m, :, lanes(t)] + r1[2 * m + 1, :, lanes(t)]
            xp1[t, m] = halve_rows(both, rs1, t)

    loop(0, 8, pair1)
    for t, tile in enumerate(halve_lanes(xp1, 8, 8)):
        r2[:, lanes(t)] = tile.reshape(64, 128)
    for ref, u, r in ((zl, slice(0, 2), slice(0, 4)), (zh, slice(30, 32), slice(12, 16))):
        for t in range(8):
            ref[uptake_part(t)] = uptake[u, :, lanes(t)].reshape(64, 128).astype(BF16)
        for t in range(4):
            ref[uptake_part(8 + t)] = r1[r, :, lanes(t)].reshape(64, 128).astype(BF16)
        for t in range(2):
            ref[uptake_part(12 + t)] = r2[:, lanes(t)].astype(BF16)
        ref[uptake_part(14)] = jnp.zeros((64, 128), BF16)

    sub = iota((8, 1024), 0)

    def columns(i):
        lows, highs = [], []
        for j in range(2):
            low, high = jnp.zeros((8, 1024), F32), jnp.zeros((8, 1024), F32)
            for n in range(4):
                z = 8 * i + 4 * j + n
                low = jnp.where(sub // 2 == n, shifted(uptake[z, 0:8, :], 2 * n, 0), low)
                high = jnp.where(sub // 2 == n, shifted(uptake[z, 24:32, :], 2 * n + 2, 0), high)
            lows.append(low)
            highs.append(high)
        rows = pl.ds(pl.multiple_of(16 * i, 16), 16)
        xl[rows, :] = jnp.concatenate(lows, axis=0).astype(BF16)
        xh[rows, :] = jnp.concatenate(highs, axis=0).astype(BF16)

    loop(0, 4, columns)


def far_along_z(nz, iz, to_low, to_high):
    if nz != 4:
        return to_low, to_high
    one = jnp.where(iz < 2, to_high, to_low)
    return one, one


def halves(sub, first, second):
    return jnp.where(sub < 4, first, shifted(second, 4, 1))


def uppers(sub, first, second):
    return jnp.where(sub < 4, shifted(first, 4, 1), second)


def far_messages(window):
    planes, _, width = window.shape
    pairs = window.reshape(planes // 2, 2, 8, width)
    sub = iota((planes // 2, 8, width), 1)
    size = (planes * 4, width)
    return halves(sub, pairs[:, 0], pairs[:, 1]).reshape(size), uppers(sub, pairs[:, 0], pairs[:, 1]).reshape(size)


def far_tile(from_low, from_high):
    width = from_low.shape[-1]
    low, high = from_low.reshape(-1, 8, width), from_high.reshape(-1, 8, width)
    sub = iota(low.shape, 1)
    even = jnp.where(sub < 4, high, shifted(low, 4, 1))
    odd = jnp.where(sub < 4, shifted(high, 4, 1), low)
    return jnp.stack([even, odd], axis=1).reshape(-1, 8, width)


def first_x_kernel(own, r1, uxl, uxh, zl, zh, q1, xl, xh):
    q1[4:20] = r1[...]
    for ref, planes in ((zl, slice(0, 4)), (zh, slice(20, 24))):
        for t in range(4):
            q1[planes, :, lanes(t)] = ref[uptake_part(8 + t)].astype(F32).reshape(4, 16, 128)
    for ref, d in ((xl, 0), (xh, 2)):
        for n, src in enumerate((own, zl, zh)):
            ref[0:BLOCK, lanes(n)] = src[0:BLOCK, lanes(d)]
    sub = iota((8, 128), 0)
    lows, highs = [], []
    for t in range(8):
        xl[uptake_part(t)] = uxl[:, lanes(t)]
        xh[uptake_part(t)] = uxh[:, lanes(t)]
        both = [ref[uptake_part(t)].astype(F32) for ref in (zl, zh)]
        planes = [both[0][0:32], both[0][32:64], both[1][0:32], both[1][32:64]]
        to_low, to_high = jnp.zeros((8, 128), F32), jnp.zeros((8, 128), F32)
        for n, p in enumerate(planes):
            here = sub // 2 == n
            to_low = jnp.where(here, shifted(p[0:8], 2 * n, 0), to_low)
            to_high = jnp.where(here, shifted(p[24:32], 2 * n + 2, 0), to_high)
        lows.append(to_low)
        highs.append(to_high)
    xl[uptake_part(8)] = jnp.concatenate(lows, axis=0).astype(BF16)
    xh[uptake_part(8)] = jnp.concatenate(highs, axis=0).astype(BF16)


FAR = 80


def source_window_kernel(nz, info, own, zl, zh, z2l, z2h, r2, firstl, firsth, f2, q2, nl, nh, fl, fh):
    iz = info[0]
    zeros = jnp.zeros((10, 8, 256), F32)
    f2[0:10] = zeros
    f2[22:32] = zeros
    f2[10:22] = own[...].reshape(12, 8, 256)
    for ref, planes in ((zl, slice(2, 14)), (zh, slice(18, 30))):
        part = jnp.concatenate([ref[240:288, 0:256], ref[240:288, 256:512]], axis=0).astype(F32)
        f2[planes] = f2[planes] + part.reshape(12, 8, 256)
    for ref, planes, exists in ((z2l, slice(0, 6), iz >= 2), (z2h, slice(26, 32), iz < nz - 2)):
        part = jnp.where(exists, ref[0:48, :].astype(F32), 0.0)
        f2[planes] = f2[planes] + part.reshape(6, 8, 256)
    q2[0:4] = z2l[48:80, :].astype(F32).reshape(4, 8, 256)
    q2[28:32] = z2h[48:80, :].astype(F32).reshape(4, 8, 256)
    q2[12:20] = r2[...].reshape(8, 8, 256)
    for ref, planes in ((firstl, slice(4, 12)), (firsth, slice(20, 28))):
        for t in range(2):
            q2[planes, :, lanes(t)] = ref[uptake_part(12 + t)].astype(F32).reshape(8, 8, 128)
    for i, near in enumerate((nl, nh)):
        near[0:256, :] = f2[...].reshape(256, 256).astype(BF16)
        near[256:288, :] = z2l[48:80, :]
        near[288:320, :] = z2h[48:80, :]
        for n in range(4):
            rows = slice(288 + 32 * (n // 2) + 16 * i, 304 + 32 * (n // 2) + 16 * i)
            cols = slice(256 * (n % 2), 256 * (n % 2) + 256)
            near[320 + 32 * n : 336 + 32 * n, :] = zl[rows, cols]
            near[336 + 32 * n : 352 + 32 * n, :] = zh[rows, cols]
    for i, ref in enumerate((f2, q2)):
        to_low, to_high = far_messages(ref[...])
        fl[128 * i : 128 * i + 128, :] = to_low.astype(BF16)
        fh[128 * i : 128 * i + 128, :] = to_high.astype(BF16)


O = 5
Q = 2
BASE = 1.0 + 6.0 * KAPPA


def scatter(blocks, hot, left):
    lane = iota((128, 128), 1)
    for i, (ref, part) in enumerate(blocks):
        name = ref[256:272, part].astype(F32).astype(jnp.int32)[0:1]
        tiles = lax.shift_right_logical(name, 6)
        at_y = (name & 63) * 16 + (lane[0:1] & 15)
        at_y = jnp.broadcast_to(at_y.astype(F32), (128, 128)).T.astype(jnp.int32)
        for t in range(NT):
            hot[128 * i : 128 * i + 128, lanes(t)] = jnp.where(at_y == lane + 128 * t, 1.0, 0.0).astype(BF16)
        values = ref[0:256, part].astype(F32)
        for tile in range(4):
            left[256 * tile : 256 * tile + 256, lanes(i)] = jnp.where(tiles == tile, values, 0.0).astype(BF16)
    for n in range(4):
        cols = slice(n * 256, (n + 1) * 256)
        sums = jnp.dot(left[...], hot[:, cols], preferred_element_type=F32)
        for tile in range(4):
            bz, bx = tile // 2, tile % 2
            yield 16 * bz, slice(16 * bx, 16 * bx + 16), cols, sums[256 * tile : 256 * tile + 256].reshape(16, 16, 256)


def sweep(src, dst, source, gg, z, sourced):
    for t, here, sums in plane(src, z + O):
        inner = KAPPA * sums
        g = gg[z + Q, :, lanes(t)]
        if sourced:
            body = inner[0:32] + source[z, :, lanes(t)]
            dst[z + O, 0:32, lanes(t)] = KEEP * here[0:32] + g[0:32] * body
            dst[z + O, 32:40, lanes(t)] = KEEP * here[32:40] + g[32:40] * inner[32:40]
        else:
            dst[z + O, :, lanes(t)] = KEEP * here + g * inner


def own_kernel(
    nz, info, own, zl, zh, density, uptake, s_out, g_out, v_out, edge_out,
    dens, upt, s0, g0, v1, edge, va, hot, left, sems,
):
    iz = info[0]
    loads = [pltpu.make_async_copy(density, dens, sems.at[0]), pltpu.make_async_copy(uptake, upt, sems.at[1])]
    stores = [
        pltpu.make_async_copy(src, dst, sems.at[2 + i])
        for i, (src, dst) in enumerate(((s0, s_out), (g0, g_out), (v1, v_out), (edge, edge_out)))
    ]
    for copy in loads:
        copy.start()
    for p in (3, 4, 37, 38):
        va[p] = jnp.zeros((40, 1024), F32)
    for n in range(4):
        ref, valid = (zl, iz > 0) if n < 2 else (zh, iz < nz - 1)
        q = n if n < 2 else 32 + n
        rows = slice(32 * (n % 2), 32 * (n % 2) + 32)
        for t in range(NT):
            g0[q, :, lanes(t)] = jnp.where(valid, OMEGA, 0.0) / (ref[uptake_part(t)].astype(F32)[rows] + BASE)

    blocks = [(ref, lanes(1)) for ref in (own, zl, zh)]
    waiting = list(loads[0:1])
    for z, rows, cols, sums in scatter(blocks, hot, left):
        while waiting:
            waiting.pop().wait()
        planes = slice(z, z + 16)
        s0[planes, rows, cols] = dens[planes, rows, cols] + sums
    stores[0].start()
    loads[1].wait()

    def own_plane(z):
        va[z + O, 0:32, :] = dens[z]
        va[z + O, 32:40, :] = jnp.zeros((8, 1024), F32)
        g0[z + Q] = OMEGA / (upt[z] + BASE)

    loop(0, C, own_plane)
    stores[1].start()

    def first(z):
        for t, here, sums in plane(va, z + O):
            inner = KAPPA * sums
            body = inner[0:32] + s0[z, :, lanes(t)]
            v1[z + 1, :, lanes(t)] = KEEP * here[0:32] + g0[z + Q, :, lanes(t)] * body
            edge[z, :, lanes(t)] = inner[32:40]

    loop(0, C, first, 2)
    for z in (-1, C):
        for t in range(NT):
            near = va[z + O + (1 if z < 0 else -1), 0:32, lanes(t)]
            v1[z + 1, :, lanes(t)] = g0[z + Q, :, lanes(t)] * (KAPPA * near)
    for copy in stores[2:]:
        copy.start()
    for copy in stores:
        copy.wait()


def pre_kernel(
    nz, nx, info, xl, xh, zl, zh, q1, r2, s0, g0, v1, edge_in, uptake,
    c1, mxl, mxh, vzl, vzh, pxl, pxh, cnl, cnh, v_out, g_out, s_out,
    va, vb, supply, upt, dh, gg, edge, hot, left, rs, xp, usl, ush, sems,
):
    iz, ix = info[0], info[1]
    k = KAPPA
    loads = [
        pltpu.make_async_copy(src, dst, sems.at[i])
        for i, (src, dst) in enumerate(
            (
                (s0, supply),
                (v1, vb.at[4:38, 0:32, :]),
                (g0, gg.at[:, 0:32, :]),
                (edge_in, edge),
                (uptake, upt),
            )
        )
    ]
    for copy in loads:
        copy.start()

    for p in (1, 2, 39, 40):
        va[p] = jnp.zeros((40, 1024), F32)
    for p in (2, 3, 38, 39):
        vb[p] = jnp.zeros((40, 1024), F32)
    for p in (4, 37):
        vb[p, 32:40, :] = jnp.zeros((8, 1024), F32)

    sub8 = iota((8, 1024), 0)
    for t in range(NT):
        usl[0:64, lanes(t)] = xl[uptake_part(t)].astype(F32)
        ush[0:64, lanes(t)] = xh[uptake_part(t)].astype(F32)
        usl[64:72, lanes(t)] = xl[uptake_part(8)].astype(F32)[8 * t : 8 * t + 8]
        ush[64:72, lanes(t)] = xh[uptake_part(8)].astype(F32)[8 * t : 8 * t + 8]

    def set_halo(q, low, high, valid_z):
        gz = jnp.where(valid_z, OMEGA, 0.0)
        d = jnp.where(sub8 < 2, high, jnp.where(sub8 >= 6, low, 0.0)) + BASE
        dh[q] = d
        omega = jnp.where(sub8 < 2, jnp.where(ix < nx - 1, gz, 0.0), jnp.where(sub8 >= 6, jnp.where(ix > 0, gz, 0.0), 0.0))
        gg[q, 32:40, :] = omega / d

    def halos(i):
        rows = pl.ds(pl.multiple_of(8 * i, 8), 8)
        low, high = usl[rows, :], ush[rows, :]
        for n in range(4):
            set_halo(4 * i + n + Q, shifted(low, 6 - 2 * n, 0), shifted(high, -2 * n, 0), True)

    loop(0, C // 4, halos)
    low, high = usl[64:72, :], ush[64:72, :]
    for n in range(4):
        exists = iz > 0 if n < 2 else iz < nz - 1
        set_halo(n if n < 2 else 32 + n, shifted(low, 6 - 2 * n, 0), shifted(high, -2 * n, 0), exists)

    blocks = [(ref, lanes(n)) for ref in (xl, xh) for n in range(3)]
    waiting = list(loads[0:3])
    for z, rows, cols, sums in scatter(blocks, hot, left):
        while waiting:
            waiting.pop().wait()
        supply[z : z + 16, rows, cols] = supply[z : z + 16, rows, cols] + sums
        g = gg[z + Q : z + Q + 16, rows, cols]
        vb[z + O : z + O + 16, rows, cols] = vb[z + O : z + O + 16, rows, cols] + g * sums
    loads[3].wait()

    s_copy = pltpu.make_async_copy(supply, s_out, sems.at[7])
    s_copy.start()

    def edges(z):
        vb[z + O, 32:40, :] = gg[z + Q, 32:40, :] * edge[z]

    loop(0, C, edges)

    loop(0, C, lambda z: sweep(vb, va, supply, gg, z, True), 2)
    loop(0, 4, lambda i: sweep(vb, va, supply, gg, jnp.where(i < 2, i - 2, i + C - 2), False))
    loads[4].wait()
    v_copy = pltpu.make_async_copy(va.at[3:39], v_out, sems.at[5])
    g_copy = pltpu.make_async_copy(gg, g_out, sems.at[6])
    v_copy.start()
    g_copy.start()

    def residual(z, rates, sourced):
        for t, here, sums in plane(va, z + O):
            r = k * sums
            if rates is not None:
                inner = r[0:32] - (rates(t) + BASE) * here[0:32]
                if sourced:
                    inner = inner + supply[z, :, lanes(t)]
                r = jnp.concatenate([inner, r[32:40] - dh[z + Q, :, lanes(t)] * here[32:40]], axis=0)
            yield t, r

    def coarse(m, zs, rates, sourced):
        parts = [residual(zs[i], rates[i], sourced) for i in range(2)]
        for (t, first), (_, second) in zip(*parts):
            xp[t, m, 0:20, :] = halve_rows(first + second, rs, t)

    def from_message(ref, n):
        return lambda t: ref[uptake_part(t)].astype(F32)[32 * n : 32 * n + 32]

    def inner(m):
        zs = (2 * m - 4, 2 * m - 3)
        coarse(m, zs, [lambda t, z=z: upt[z, :, lanes(t)] for z in zs], True)

    loop(2, 18, inner)
    for m, ref, z in ((1, zl, -2), (18, zh, C)):
        coarse(m, (z, z + 1), [from_message(ref, 0), from_message(ref, 1)], False)

    def outer(i):
        for t, r in residual(jnp.where(i == 0, -3, 34), None, False):
            xp[t, 19 * i, 0:20, :] = halve_rows(r, rs, t)

    loop(0, 2, outer)

    sub = iota((20, 8, 128), 1)
    for t, tile in enumerate(halve_lanes(xp, 20, 24)):
        last = tile[:, 16:24]
        last = jnp.where(sub < 2, last, jnp.where(sub >= 6, shifted(last, 4, 1), 0.0))
        c1[:, 0:16, lanes(t)] = tile[:, 0:16]
        c1[:, 16:24, lanes(t)] = last

    empty = jnp.zeros((1, 8, 1024), F32)
    blank = jnp.zeros((8, 1024), F32)
    sub1 = iota((5, 8, 512), 1)
    first, last, halo = [c1[:, 8 * n : 8 * n + 8].reshape(5, 4, 8, 512) for n in range(3)]
    sub4 = iota((5, 4, 8, 512), 2)
    to_high = in_three(sub1, jnp.where(sub4 >= 4, last, halo), *HIGH_PACK)
    to_low = in_three(sub1, jnp.where(sub4 >= 4, halo, first), *LOW_PACK)
    sub1 = iota((12, 8, 512), 1)
    first = q1[:, 0:8, :].reshape(12, 2, 8, 512)
    last = q1[:, 8:16, :].reshape(12, 2, 8, 512)
    low_rates = halves(sub1, first[:, 0], first[:, 1]).reshape(96, 512)
    high_rates = uppers(sub1, last[:, 0], last[:, 1]).reshape(96, 512)
    filler = jnp.zeros((8, 512), F32)
    for ref, sources, rates in ((mxl, to_low, low_rates), (mxh, to_high, high_rates)):
        ref[0:128, :] = jnp.concatenate([sources.reshape(120, 512), filler], axis=0).astype(BF16)
        ref[128:224, :] = rates.astype(BF16)

    for level0, corners, p, z in ((vzl, cnl, 3, 0), (vzh, cnh, 35, 31)):
        values = jnp.concatenate([va[p : p + 4], jnp.concatenate([supply[z : z + 1], empty], axis=1)], axis=0)
        level0[...] = jnp.concatenate([values.reshape(200, 1024), blank], axis=0).astype(BF16)
        for i, pack in enumerate((pack_low, pack_high)):
            corner = jnp.concatenate([pack(va[p], va[p + 1]), pack(va[p + 2], va[p + 3])], axis=0)
            corners[16 * i : 16 * i + 16, :] = corner.astype(BF16)

    def sides(i):
        lows, highs = [], []
        for j in range(2):
            p = 4 * i + 2 * j + 3
            lows.append(pack_low(va[p], va[p + 1]))
            highs.append(pack_high(va[p], va[p + 1]))
        rows = pl.ds(pl.multiple_of(16 * i, 16), 16)
        pxl[rows, :] = jnp.concatenate(lows, axis=0).astype(BF16)
        pxh[rows, :] = jnp.concatenate(highs, axis=0).astype(BF16)

    loop(0, 9, sides)

    def sources(i):
        lows, highs = [], []
        for j in range(2):
            low, high = jnp.zeros((8, 1024), F32), jnp.zeros((8, 1024), F32)
            for n in range(8):
                z = 16 * i + 8 * j + n
                low = jnp.where(sub8 == n, shifted(supply[z, 0:8, :], n, 0), low)
                high = jnp.where(sub8 == n, shifted(supply[z, 24:32, :], n + 1, 0), high)
            lows.append(low)
            highs.append(high)
        rows = pl.ds(pl.multiple_of(16 * i + 144, 16), 16)
        pxl[rows, :] = jnp.concatenate(lows, axis=0).astype(BF16)
        pxh[rows, :] = jnp.concatenate(highs, axis=0).astype(BF16)

    loop(0, 2, sources)
    for ref in (pxl, pxh):
        for t in range(2):
            ref[176:240, lanes(t)] = zl[uptake_part(12 + t)]
            ref[176:240, lanes(2 + t)] = r2[:, lanes(t)].astype(BF16)
            ref[176:240, lanes(4 + t)] = zh[uptake_part(12 + t)]
        ref[176:240, 768:1024] = jnp.zeros((64, 256), BF16)
    v_copy.wait()
    g_copy.wait()
    s_copy.wait()


def outer_rows(sub):
    return (sub < 2) | (sub >= 6)


def pack_pair(sub, a, b):
    return jnp.where(outer_rows(sub), a, shifted(b, 4, 0))


def pack_low(first, second):
    sub = iota((8, 1024), 0)
    a, b = [jnp.where(sub < 4, v[0:8], v[32:40]) for v in (first, second)]
    return pack_pair(sub, a, b)


def pack_high(first, second):
    sub = iota((8, 1024), 0)
    a, b = [jnp.where(sub >= 4, v[24:32], v[32:40]) for v in (first, second)]
    return pack_pair(sub, a, b)


def in_three(sub, tiles, free, turns):
    spare = (sub == free) | (sub == free + 1)
    last = tiles[:, 3]
    parts = [jnp.where(spare, shifted(last, turn, 1), tiles[:, i]) for i, turn in enumerate(turns)]
    return jnp.stack(parts, axis=1)


def out_of_three(sub, parts, free, turns):
    last = None
    for i, turn in enumerate(turns):
        back = shifted(parts[:, i], -turn, 1)
        home = (free - turn) % 8
        here = (sub == home) | (sub == home + 1)
        last = jnp.where(here, back, 0.0 if last is None else last)
    return jnp.stack([parts[:, 0], parts[:, 1], parts[:, 2], last], axis=1)


HIGH_PACK = (2, (-2, 4, 2))
LOW_PACK = (4, (-2, 4, 2))


def middle_kernel(nz, nx, info, c1, q_in, r2, cnl, cnh, mxl, mxh, f1, g1, v1, g2, z1l, z1h, z2l, z2h, q0, va, vv, rs, xp):
    iz, ix = info[0], info[1]
    k = spread(1)
    base = 1.0 + 6.0 * k
    sub5 = iota((5, 8, 512), 1)
    low = out_of_three(sub5, mxl[0:128, :].astype(F32)[0:120].reshape(5, 3, 8, 512), *HIGH_PACK).reshape(20, 8, 512)
    high = out_of_three(sub5, mxh[0:128, :].astype(F32)[0:120].reshape(5, 3, 8, 512), *LOW_PACK).reshape(20, 8, 512)
    sub = iota((20, 8, 512), 1)
    for p in (0, 1, 22, 23):
        f1[p] = jnp.zeros((24, 512), F32)
    f1[2:22, 0:8] = c1[:, 0:8] + jnp.where(sub < 2, low, 0.0)
    f1[2:22, 8:16] = c1[:, 8:16] + jnp.where(sub >= 6, high, 0.0)
    f1[2:22, 16:24] = c1[:, 16:24] + jnp.where(sub >= 4, low, high)
    low, high = [ref[128:224, :].astype(F32).reshape(12, 8, 512) for ref in (mxl, mxh)]
    sub12 = iota((12, 8, 512), 1)
    even = jnp.where(sub12 >= 4, shifted(low, 4, 1), high)
    odd = jnp.where(sub12 >= 4, low, shifted(high, 4, 1))
    q0[:, 0:16] = q_in[...]
    q0[:, 16:24] = jnp.stack([even, odd], axis=1).reshape(24, 8, 512)
    shape = (24, 24, 128)
    valid = inside(shape, 0, -4, None, iz, 16, nz) & inside(shape, 1, 0, 20, ix, 16, nx)
    for t in range(4):
        g = jnp.where(valid, OMEGA, 0.0) / (q0[:, :, lanes(t)] + base)
        g1[:, :, lanes(t)] = g
        va[:, :, lanes(t)] = g * f1[:, :, lanes(t)]
    for p in (0, 1, 24, 25):
        vv[p] = jnp.zeros((24, 512), F32)

    def sweep(p):
        for t, here, sums in plane(va, p):
            vv[p + 1, :, lanes(t)] = KEEP * here + g1[p, :, lanes(t)] * (f1[p, :, lanes(t)] + k * sums)

    loop(1, 23, sweep, 2)
    v1[...] = vv[1:25]

    def residual(p):
        for t, here, sums in plane(vv, p + 1):
            yield t, f1[p, :, lanes(t)] + k * sums - (q0[p, :, lanes(t)] + base) * here

    def coarse(m):
        for (t, first), (_, second) in zip(residual(2 * m), residual(2 * m + 1)):
            xp[t, m] = halve_rows((first + second)[0:16], rs, t)

    loop(0, 12, coarse)
    for t, tile in enumerate(halve_lanes(xp, 12, 8)):
        g2[:, lanes(t)] = tile.reshape(96, 128)
        for ref in (z1l, z1h):
            ref[240:288, lanes(t)] = tile[0:6].reshape(48, 128).astype(BF16)
            ref[240:288, lanes(2 + t)] = tile[6:12].reshape(48, 128).astype(BF16)
    for ref, corners in ((z1l, cnl), (z1h, cnh)):
        ref[288:320, :] = corners[:, 0:512]
        ref[320:352, :] = corners[:, 512:1024]
    for ref, p in ((z1l, 2), (z1h, 18)):
        ref[0:144, :] = vv[p : p + 6].reshape(144, 512).astype(BF16)
        ref[144:240, :] = f1[p : p + 4].reshape(96, 512).astype(BF16)
    low, high = far_along_z(nz, iz, g2[0:48, :], g2[48:96, :])
    z2l[0:48, :] = low.astype(BF16)
    z2h[0:48, :] = high.astype(BF16)
    low, high = far_along_z(nz, iz, r2[0:32, :], r2[32:64, :])
    z2l[48:80, :] = low.astype(BF16)
    z2h[48:80, :] = high.astype(BF16)


def back_kernel(
    nz, nx, info, f_in, g1, v1, z1l, z1h, vzl, vzh, vxl_in, vxh_in, own2, n2l, n2h, m2l, m2h, q_own, v_in, g_in, s_in,
    out_hbm,
    f2, q2, h2, a2, b2, rs, xp, xpr, wa, w1, zsl, zsh, vb, ws,
    v2, gg, supply, fsl, fsh, out, f1, vxl, vxh, sems,
):
    iz, ix = info[0], info[1]
    matrix = doubling()
    level0 = [
        pltpu.make_async_copy(src, dst, sems.at[i])
        for i, (src, dst) in enumerate(((v_in, v2), (g_in, gg), (s_in, supply)))
    ]
    for copy in level0:
        copy.start()

    f1[...] = f_in[...]
    wa[...] = v1[...]
    for ref, p in ((z1l, 1), (z1h, 17)):
        wa[p : p + 6] = wa[p : p + 6] + ref[0:144, :].astype(F32).reshape(6, 24, 512)
        f1[p + 1 : p + 5] = f1[p + 1 : p + 5] + ref[144:240, :].astype(F32).reshape(4, 24, 512)

    f2[:, 0:8, :] = own2[...]
    f2[:, 8:16, :] = n2h[0:256, :].astype(F32).reshape(32, 8, 256)
    f2[:, 16:24, :] = far_tile(m2l[0:128, :].astype(F32), m2h[0:128, :].astype(F32))
    f2[:, 24:32, :] = n2l[0:256, :].astype(F32).reshape(32, 8, 256)
    q2[:, 0:8, :] = q_own[...]
    q2[:, 16:24, :] = far_tile(m2l[128:256, :].astype(F32), m2h[128:256, :].astype(F32))
    for ref, rows in ((vxh_in, slice(8, 16)), (vxl_in, slice(24, 32))):
        for n in range(3):
            q2[8 * n + 4 : 8 * n + 12, rows, :] = ref[176:240, n * 256 : n * 256 + 256].astype(F32).reshape(8, 8, 256)
    for ref, rows in ((n2h, slice(8, 16)), (n2l, slice(24, 32))):
        outer = ref[256:320, :].astype(F32).reshape(8, 8, 256)
        q2[0:4, rows, :] = outer[0:4]
        q2[28:32, rows, :] = outer[4:8]

    k = spread(2)
    base = 1.0 + 6.0 * k
    shape = (32, 32, 128)
    valid = inside(shape, 0, -12, None, iz, 8, nz) & inside(shape, 1, 0, 20, ix, 8, nx)
    for t in range(2):
        g = jnp.where(valid, OMEGA, 0.0) / (q2[:, :, lanes(t)] + base)
        h2[:, :, lanes(t)] = g
        a2[:, :, lanes(t)] = g * f2[:, :, lanes(t)]
    b2[0] = a2[0]
    b2[31] = a2[31]

    def sweep2(src, dst):
        def body(p):
            for t, here, sums in plane(src, p):
                dst[p, :, lanes(t)] = KEEP * here + h2[p, :, lanes(t)] * (f2[p, :, lanes(t)] + k * sums)

        return body

    loop(1, 31, sweep2(a2, b2), 2)

    def coarse(m):
        total, rates = [0.0, 0.0], [0.0, 0.0]
        for j in range(2):
            p = 2 * m + j
            for t, here, sums in plane(b2, p):
                r = f2[p, :, lanes(t)] + k * sums - (q2[p, :, lanes(t)] + base) * here
                total[t] = total[t] + r
                rates[t] = rates[t] + q2[p, :, lanes(t)]
        for t in range(2):
            xp[t, m] = halve_rows(total[t], rs, t)
            xpr[t, m] = halve_rows(rates[t], rs, t + 2)

    for t in range(2):
        for m in (0, 15):
            xp[t, m] = jnp.zeros((16, 128), F32)
            xpr[t, m] = jnp.zeros((16, 128), F32)
    loop(1, 15, coarse)

    shape = (16, 16, 128)
    valid = inside(shape, 0, -6, None, iz, 4, nz) & inside(shape, 1, 0, 10, ix, 4, nx)
    k3 = spread(3)
    (source,) = halve_lanes(xp, 16, 16)
    (rates,) = halve_lanes(xpr, 16, 16)
    g = jnp.where(valid, OMEGA, 0.0) / (rates + (1.0 + 6.0 * k3))
    v = g * source
    lane = iota(shape, 2)
    for repeat in range(3):
        edge = jnp.zeros((1, 16, 128), F32)
        sums = jnp.concatenate([v[1:], edge], axis=0) + jnp.concatenate([edge, v[:-1]], axis=0)
        sums = sums + shifted(v, 1, 1) + shifted(v, -1, 1)
        sums = sums + jnp.where(lane == 0, 0.0, shifted(v, 1, 2)) + jnp.where(lane == 127, 0.0, shifted(v, -1, 2))
        v = KEEP * v + g * (source + k3 * sums)

    wide = split_dot(v[4:12].reshape(128, 128), matrix).reshape(8, 16, 256)
    for m in range(8):
        for t in range(2):
            part = wide[m, :, lanes(t)]
            rs[t, pl.ds(0, 16, stride=2), :] = part
            rs[t, pl.ds(1, 16, stride=2), :] = part
            for j in range(2):
                p = 8 + 2 * m + j
                b2[p, :, lanes(t)] = b2[p, :, lanes(t)] + rs[t, 0:32, :]
    loop(9, 23, sweep2(b2, a2), 2)
    loop(10, 22, sweep2(a2, b2), 2)

    w = b2[10:22]
    near, far = w[:, 8:16], w[:, 24:32]
    near = jnp.where(iota((12, 8, 256), 1) < 2, near, shifted(far, 4, 1))
    w = jnp.concatenate([w[:, 0:8], near], axis=1).reshape(192, 256)
    wide = [split_dot(w[:, lanes(t)], matrix) for t in range(2)]
    wide = jnp.concatenate(wide, axis=1).reshape(12, 16, 512)
    for m in range(12):
        for t in range(4):
            part = wide[m, :, lanes(t)]
            rs[t, pl.ds(0, 16, stride=2), :] = part
            rs[t, pl.ds(1, 16, stride=2), :] = part
            for j in range(2):
                p = 2 * m + j
                wa[p, :, lanes(t)] = wa[p, :, lanes(t)] + rs[t, 0:24, :]
    k1 = spread(1)

    def sweep1(src, dst):
        def body(p):
            for t, here, sums in plane(src, p):
                dst[p, :, lanes(t)] = KEEP * here + g1[p, :, lanes(t)] * (f1[p, :, lanes(t)] + k1 * sums)

        return body

    loop(2, 22, sweep1(wa, w1), 2)
    loop(3, 21, sweep1(w1, wa), 2)

    sub = iota((18, 8, 128), 1)
    for t in range(4):
        halo = wa[3:21, 16:24, lanes(t)]
        halo = jnp.where(sub < 2, halo, shifted(halo, 4, 1))
        w = jnp.concatenate([wa[3:21, 0:16, lanes(t)], halo], axis=1)
        ws[:, :, t * 256 : t * 256 + 256] = split_dot(w.reshape(432, 128), matrix).reshape(18, 24, 256)

    for copy in level0:
        copy.wait()
    zsl[...] = vzl[...].astype(F32)
    zsh[...] = vzh[...].astype(F32)
    for ref, src, near in ((vxl, vxl_in, n2l), (vxh, vxh_in, n2h)):
        ref[...] = src[0:176, :]
        for n in range(4):
            cols = slice(256 * n, 256 * n + 256)
            for i, rows in enumerate((slice(0, 16), slice(128, 144))):
                corner = near[320 + 32 * n + 16 * i : 336 + 32 * n + 16 * i, :].astype(F32)
                ref[rows, cols] = (src[rows, cols].astype(F32) + corner).astype(BF16)
    for i in range(4):
        v2[i] = v2[i] + zsl[40 * i : 40 * i + 40, :]
        v2[32 + i] = v2[32 + i] + zsh[40 * i : 40 * i + 40, :]

    s8 = iota((8, 128), 0)

    outer = outer_rows(s8)

    def correct(i):
        rows = pl.ds(pl.multiple_of(16 * i, 16), 16)
        for t in range(NT):
            low = vxl[rows, lanes(t)].astype(F32)
            high = vxh[rows, lanes(t)].astype(F32)
            for n in range(2):
                part = ws[2 * i + n, :, lanes(t)]
                rs[t, pl.ds(0, 24, stride=2), :] = part
                rs[t, pl.ds(1, 24, stride=2), :] = part
                for j in range(2):
                    p = 4 * i + 2 * n + j
                    lo, hi = low[8 * n : 8 * n + 8], high[8 * n : 8 * n + 8]
                    if j:
                        lo, hi = shifted(lo, 4, 0), shifted(hi, 4, 0)
                    v2[p, 0:8, lanes(t)] = v2[p, 0:8, lanes(t)] + rs[t, 0:8, :] + jnp.where(s8 < 2, lo, 0.0)
                    v2[p, 8:24, lanes(t)] = v2[p, 8:24, lanes(t)] + rs[t, 8:24, :]
                    v2[p, 24:32, lanes(t)] = v2[p, 24:32, lanes(t)] + rs[t, 24:32, :] + jnp.where(s8 >= 6, hi, 0.0)
                    extra = jnp.where(outer, jnp.where(s8 >= 4, lo, hi), 0.0)
                    v2[p, 32:40, lanes(t)] = v2[p, 32:40, lanes(t)] + rs[t, 32:40, :] + extra

    loop(0, 9, correct)
    k0 = spread(0)

    def first(i):
        rows = pl.ds(pl.multiple_of(16 * i + 144, 16), 16)
        for t in range(NT):
            fsl[:, lanes(t)] = vxl[rows, lanes(t)].astype(F32)
            fsh[:, lanes(t)] = vxh[rows, lanes(t)].astype(F32)

        def step(j):
            z = 16 * i + j
            start = pl.multiple_of((j // 8) * 8, 8)
            turn = lax.rem(j, 8)
            for t, here, sums in plane(v2, z + 2):
                lo = pltpu.roll(fsl[pl.ds(start, 8), lanes(t)], 7 - turn, 0)
                hi = pltpu.roll(fsh[pl.ds(start, 8), lanes(t)], lax.rem(8 - turn, 8), 0)
                f = jnp.where(s8 == 7, lo, jnp.where(s8 == 0, hi, 0.0))
                g = gg[z + 2, :, lanes(t)]
                inner = k0 * sums
                vb[z + 1, 0:32, lanes(t)] = KEEP * here[0:32] + g[0:32] * (supply[z, :, lanes(t)] + inner[0:32])
                vb[z + 1, 32:40, lanes(t)] = KEEP * here[32:40] + g[32:40] * (f + inner[32:40])

        loop(0, 16, step, 2)

    loop(0, 2, first)
    for p, ref in ((1, zsl), (34, zsh)):
        for t, here, sums in plane(v2, p):
            g = gg[p, :, lanes(t)]
            vb[p - 1, :, lanes(t)] = KEEP * here + g * (ref[160:200, lanes(t)] + k0 * sums)

    def second(z):
        for t, here, sums in plane(vb, z + 1):
            g = gg[z + 2, 0:32, lanes(t)]
            out[z, :, lanes(t)] = KEEP * here[0:32] + g * (supply[z, :, lanes(t)] + k0 * sums[0:32])

    stores = []
    for i in range(4):
        part = pl.ds(8 * i, 8)
        loop(8 * i, 8 * i + 8, second, 2)
        stores.append(pltpu.make_async_copy(out.at[part], out_hbm.at[part], sems.at[3 + i]))
        stores[i].start()
    for copy in stores:
        copy.wait()


VMEM = pl.BlockSpec(memory_space=pltpu.VMEM)
SMEM = pl.BlockSpec(memory_space=pltpu.SMEM)
ANY = pl.BlockSpec(memory_space=pl.ANY)


def call(kernel, outs, scratch, smem, args, out_specs=None, in_hbm=0):
    moved = sum(a.size * a.dtype.itemsize for a in list(args) + list(outs))
    return pl.pallas_call(
        kernel,
        out_shape=tuple(outs),
        in_specs=[SMEM] * smem + [VMEM] * (len(args) - smem - in_hbm) + [ANY] * in_hbm,
        out_specs=tuple(out_specs or [VMEM] * len(outs)),
        scratch_shapes=scratch,
        compiler_params=pltpu.CompilerParams(vmem_limit_bytes=58 * 2**20),
        cost_estimate=pl.CostEstimate(flops=20 * moved, bytes_accessed=moved, transcendentals=0),
    )(*args)


def shaped(shape, dtype=F32):
    return jax.ShapeDtypeStruct(shape, dtype)


def both_ways(to_low, to_high, axis, distance=1):
    count = lax.axis_size(axis)
    up = [(i, i + distance) for i in range(count - distance)]
    down = [(j, i) for i, j in up]
    return lax.ppermute(to_high, axis, up), lax.ppermute(to_low, axis, down)


def two_away(to_low, to_high):
    count = lax.axis_size("gz")
    if count != 4:
        return both_ways(to_low, to_high, "gz", 2)
    came = lax.ppermute(to_low, "gz", [(i, (i + 2) % 4) for i in range(4)])
    return came, came


def shards(density, uptake, brick_values, brick_ids, slot_counts):
    nz, nx = lax.axis_size("gz"), lax.axis_size("xy")
    info = jnp.stack([lax.axis_index("gz"), lax.axis_index("xy")]).astype(jnp.int32)
    scratch = pltpu.VMEM
    half = lambda *shape: shaped(shape, BF16)
    full = lambda *shape: shaped(shape, F32)

    own, r1, r2, zl, zh, uxl, uxh = call(
        lambda *refs: first_kernel(2 * nx, *refs),
        [
            half(BLOCK, 384), full(16, 16, 512), full(64, 256), half(Z_ROWS, 384), half(Z_ROWS, 384),
            half(64, 1024), half(64, 1024),
        ],
        [
            scratch((8, 32, 128), F32), scratch((8, 16, 16, 128), F32), scratch((4, 16, 128), F32),
            scratch((4, 8, 8, 128), F32), scratch((SLOTS, BRICK), F32), scratch((C, C, 1024), F32),
            pltpu.SemaphoreType.DMA((1,)),
        ],
        2,
        (brick_ids, slot_counts, brick_values, uptake),
        in_hbm=1,
    )
    zl, zh = both_ways(zl, zh, "gz")
    q1, xl, xh = call(
        first_x_kernel,
        [full(24, 16, 512), half(X_ROWS, 384), half(X_ROWS, 384)],
        [],
        0,
        (own, r1, uxl, uxh, zl, zh),
    )
    s0, g0, v1, edge = call(
        lambda *refs: own_kernel(nz, *refs),
        [full(C, C, 1024), full(36, C, 1024), full(34, C, 1024), full(C, 8, 1024)],
        [
            scratch((C, C, 1024), F32),
            scratch((C, C, 1024), F32),
            scratch((C, C, 1024), F32),
            scratch((36, C, 1024), F32),
            scratch((34, C, 1024), F32),
            scratch((C, 8, 1024), F32),
            scratch((42, 40, 1024), F32),
            scratch((384, 1024), BF16),
            scratch((1024, 384), BF16),
            pltpu.SemaphoreType.DMA((6,)),
        ],
        1,
        (info, own, zl, zh, density, uptake),
        [ANY] * 4,
        in_hbm=2,
    )
    xl, xh = both_ways(xl, xh, "xy")

    c1, mxl, mxh, vzl, vzh, pxl, pxh, cnl, cnh, v2, gg, supply = call(
        lambda *refs: pre_kernel(nz, nx, *refs),
        [
            full(20, 24, 512),
            half(224, 512),
            half(224, 512),
            half(208, 1024),
            half(208, 1024),
            half(240, 1024),
            half(240, 1024),
            half(32, 1024),
            half(32, 1024),
            full(36, 40, 1024),
            full(36, 40, 1024),
            full(C, C, 1024),
        ],
        [
            scratch((42, 40, 1024), F32),
            scratch((42, 40, 1024), F32),
            scratch((C, C, 1024), F32),
            scratch((C, C, 1024), F32),
            scratch((36, 8, 1024), F32),
            scratch((36, 40, 1024), F32),
            scratch((C, 8, 1024), F32),
            scratch((768, 1024), BF16),
            scratch((1024, 768), BF16),
            scratch((8, 40, 128), F32),
            scratch((8, 20, 24, 128), F32),
            scratch((72, 1024), F32),
            scratch((72, 1024), F32),
            pltpu.SemaphoreType.DMA((8,)),
        ],
        1,
        (info, xl, xh, zl, zh, q1, r2, s0, g0, v1, edge, uptake),
        [VMEM] * 9 + [ANY] * 3,
        in_hbm=5,
    )
    mxl, mxh = both_ways(mxl, mxh, "xy")
    vzl, vzh = both_ways(vzl, vzh, "gz")
    pxl, pxh, vzl, vzh, c1 = lax.optimization_barrier((pxl, pxh, vzl, vzh, c1))
    vxl, vxh = both_ways(pxl, pxh, "xy")
    f1, g1, v1, g2, z1l, z1h, z2l, z2h = call(
        lambda *refs: middle_kernel(nz, nx, *refs),
        [
            full(24, 24, 512), full(24, 24, 512), full(24, 24, 512), full(96, 256),
            half(352, 512), half(352, 512), half(FAR, 256), half(FAR, 256),
        ],
        [
            scratch((24, 24, 512), F32), scratch((24, 24, 512), F32), scratch((26, 24, 512), F32),
            scratch((4, 16, 128), F32), scratch((4, 12, 8, 128), F32),
        ],
        1,
        (info, c1, q1, r2, cnl, cnh, mxl, mxh),
    )
    z1l, z1h = both_ways(z1l, z1h, "gz")
    z2l, z2h = two_away(z2l, z2h)
    g2, vxl, vxh = lax.optimization_barrier((g2, vxl, vxh))
    own2, q2, nl, nh, fl, fh = call(
        lambda *refs: source_window_kernel(nz, *refs),
        [full(32, 8, 256), full(32, 8, 256), half(448, 256), half(448, 256), half(256, 256), half(256, 256)],
        [],
        1,
        (info, g2, z1l, z1h, z2l, z2h, r2, zl, zh),
    )
    nl, nh = both_ways(nl, nh, "xy")
    fl, fh = both_ways(fl, fh, "xy", 2)
    window2 = scratch((32, 32, 256), F32)
    window1 = scratch((24, 24, 512), F32)
    (concentration,) = call(
        lambda *refs: back_kernel(nz, nx, *refs),
        [full(C, C, 1024)],
        [
            window2, window2, window2, window2, window2,
            scratch((8, 48, 128), F32),
            scratch((2, 16, 16, 128), F32),
            scratch((2, 16, 16, 128), F32),
            window1, window1,
            scratch((208, 1024), F32),
            scratch((208, 1024), F32),
            scratch((34, 40, 1024), F32),
            scratch((18, 24, 1024), F32),
            scratch((36, 40, 1024), F32),
            scratch((36, 40, 1024), F32),
            scratch((C, C, 1024), F32),
            scratch((16, 1024), F32),
            scratch((16, 1024), F32),
            scratch((C, C, 1024), F32),
            window1,
            scratch((176, 1024), BF16),
            scratch((176, 1024), BF16),
            pltpu.SemaphoreType.DMA((7,)),
        ],
        1,
        (info, f1, g1, v1, z1l, z1h, vzl, vzh, vxl, vxh, own2, nl, nh, fl, fh, q2, v2, gg, supply),
        [ANY],
        in_hbm=3,
    )
    return supply, concentration


def solution(mesh):
    return jax.shard_map(
        shards,
        mesh=mesh,
        in_specs=(
            P("gz", "xy", None),
            P("gz", "xy", None),
            P(("gz", "xy"), None),
            P(("gz", "xy")),
            P(("gz", "xy"), None),
        ),
        out_specs=(P("gz", "xy", None), P("gz", "xy", None)),
        check_vma=False,
    )
```

```python
import jax
import jax.numpy as jnp
from jax import lax
from jax.experimental import pallas as pl
from jax.experimental.pallas import tpu as pltpu
from jax.sharding import PartitionSpec as P

EDGE = 16
CAP = 8
BRICK = 4096
SLOTS = 72
KAPPA = 32.0
OMEGA = 0.8
KEEP = 1.0 - OMEGA

C = 32
NT = 8
F32 = jnp.float32
BF16 = jnp.bfloat16


def spread(level):
    return KAPPA / 4.0**level


def shifted(values, distance, axis):
    return pltpu.roll(values, distance % values.shape[axis], axis)


def iota(shape, dim):
    return lax.broadcasted_iota(jnp.int32, shape, dim)


def lanes(t):
    return slice(t * 128, (t + 1) * 128)


def plane(ref, p):
    count = ref.shape[2] // 128
    rows = ref.shape[1]
    lane = iota((rows, 128), 1)
    before, here = None, ref[p, :, lanes(0)]
    for t in range(count):
        after = ref[p, :, lanes(t + 1)] if t + 1 < count else None
        low = jnp.where(lane == 127, 0.0 if before is None else before, here)
        high = jnp.where(lane == 0, 0.0 if after is None else after, here)
        sums = shifted(low, 1, 1) + shifted(high, -1, 1)
        sums = sums + (shifted(here, 1, 0) + shifted(here, -1, 0))
        sums = sums + (ref[p - 1, :, lanes(t)] + ref[p + 1, :, lanes(t)])
        yield t, here, sums
        before, here = here, after


def loop(start, stop, body, unroll=1):
    def step(i, carry):
        body(i)
        return carry

    lax.fori_loop(start, stop, step, 0, unroll=unroll)


def split_dot(a, b):
    high = a.astype(BF16)
    low = (a - high.astype(F32)).astype(BF16)
    return jnp.dot(high, b, preferred_element_type=F32) + jnp.dot(low, b, preferred_element_type=F32)


def pooling():
    return jnp.where(iota((256, 128), 0) // 2 == iota((256, 128), 1), 0.125, 0.0).astype(BF16)


def doubling():
    return jnp.where(iota((128, 256), 1) // 2 == iota((128, 256), 0), 1.0, 0.0).astype(BF16)


def halve_rows(values, rs, t):
    rows = values.shape[0]
    rs[t, 0:rows, :] = values
    return rs[t, pl.ds(0, rows // 2, stride=2), :] + rs[t, pl.ds(1, rows // 2, stride=2), :]


def halve_lanes(xp, planes, rows):
    matrix = pooling()
    tiles = []
    for t in range(0, xp.shape[0], 2):
        pair = jnp.concatenate([xp[t].reshape(planes * rows, 128), xp[t + 1].reshape(planes * rows, 128)], axis=1)
        tiles.append(split_dot(pair, matrix).reshape(planes, rows, 128))
    return tiles


def inside(shape, dim, first, wrap, index, size, count):
    place = iota(shape, dim) + first
    if wrap is not None:
        place = jnp.where(place < wrap, place, place - shape[dim])
    place = place + index * size
    return (place >= 0) & (place < count * size)


BLOCK = 272
X_ROWS = BLOCK + 3 * 64
Z_ROWS = BLOCK + 5 * 64


def uptake_part(t):
    return slice(BLOCK + 64 * (t // 3), BLOCK + 64 * (t // 3) + 64), lanes(t % 3)


def transposed_bricks(bricks_x, ids, counts, bricks, xs, targets):
    xs[...] = bricks[...].astype(F32)
    row = iota((1, 8, 128), 1)
    group = iota((1, 8, 128), 2) // 16
    group16 = iota((16, 128), 1) // 16
    per_y = 64

    def block(j, out, part):
        start = pl.multiple_of(j * 8, 8)
        x = jnp.stack([xs[pl.ds(start, 8), lanes(k)] for k in range(32)])
        for s in (4, 2, 1):
            up = shifted(shifted(x, -s, 1), 16 * s, 2)
            down = shifted(shifted(x, s, 1), -16 * s, 2)
            row_bit = (row // s) % 2
            group_bit = (group // s) % 2
            x = jnp.where(row_bit == group_bit, x, jnp.where(row_bit == 0, up, down))
        x = jnp.where(group < counts[0, j], x, 0.0)
        out[0:256, part] = x.reshape(256, 128).astype(BF16)
        names = jnp.zeros((16, 128), jnp.int32)
        for e in range(CAP):
            number = ids[j * 8 + e]
            by = lax.rem(number, per_y)
            rest = lax.div(number, per_y)
            bx = lax.rem(rest, 2)
            bz = lax.rem(lax.div(rest, bricks_x), 2)
            names = jnp.where(group16 == e, (bz * 2 + bx) * per_y + by, names)
        out[256:272, part] = names.astype(F32).astype(BF16)

    for i, out in enumerate(targets):
        for d in range(3):
            block(3 * i + d, out, lanes(d))


def first_kernel(bricks_x, ids, counts, bricks, uptake_in, own, r1, r2, zl, zh, xl, xh, rs, xp, rs1, xp1, xs, uptake, sems):
    load = pltpu.make_async_copy(uptake_in, uptake, sems.at[0])
    load.start()
    transposed_bricks(bricks_x, ids, counts, bricks, xs, (zl, own, zh))
    load.wait()

    def pair(m):
        for t in range(NT):
            both = uptake[2 * m, :, lanes(t)] + uptake[2 * m + 1, :, lanes(t)]
            xp[t, m] = halve_rows(both, rs, t)

    loop(0, 16, pair)
    for t, tile in enumerate(halve_lanes(xp, 16, 16)):
        r1[:, :, lanes(t)] = tile

    def pair1(m):
        for t in range(4):
            both = r1[2 * m, :, lanes(t)] + r1[2 * m + 1, :, lanes(t)]
            xp1[t, m] = halve_rows(both, rs1, t)

    loop(0, 8, pair1)
    for t, tile in enumerate(halve_lanes(xp1, 8, 8)):
        r2[:, lanes(t)] = tile.reshape(64, 128)
    for ref, u, r in ((zl, slice(0, 2), slice(0, 4)), (zh, slice(30, 32), slice(12, 16))):
        for t in range(8):
            ref[uptake_part(t)] = uptake[u, :, lanes(t)].reshape(64, 128).astype(BF16)
        for t in range(4):
            ref[uptake_part(8 + t)] = r1[r, :, lanes(t)].reshape(64, 128).astype(BF16)
        for t in range(2):
            ref[uptake_part(12 + t)] = r2[:, lanes(t)].astype(BF16)
        ref[uptake_part(14)] = jnp.zeros((64, 128), BF16)

    sub = iota((8, 1024), 0)

    def columns(i):
        lows, highs = [], []
        for j in range(2):
            low, high = jnp.zeros((8, 1024), F32), jnp.zeros((8, 1024), F32)
            for n in range(4):
                z = 8 * i + 4 * j + n
                low = jnp.where(sub // 2 == n, shifted(uptake[z, 0:8, :], 2 * n, 0), low)
                high = jnp.where(sub // 2 == n, shifted(uptake[z, 24:32, :], 2 * n + 2, 0), high)
            lows.append(low)
            highs.append(high)
        rows = pl.ds(pl.multiple_of(16 * i, 16), 16)
        xl[rows, :] = jnp.concatenate(lows, axis=0).astype(BF16)
        xh[rows, :] = jnp.concatenate(highs, axis=0).astype(BF16)

    loop(0, 4, columns)


def far_along_z(nz, iz, to_low, to_high):
    if nz != 4:
        return to_low, to_high
    one = jnp.where(iz < 2, to_high, to_low)
    return one, one


def halves(sub, first, second):
    return jnp.where(sub < 4, first, shifted(second, 4, 1))


def uppers(sub, first, second):
    return jnp.where(sub < 4, shifted(first, 4, 1), second)


def far_messages(window):
    planes, _, width = window.shape
    pairs = window.reshape(planes // 2, 2, 8, width)
    sub = iota((planes // 2, 8, width), 1)
    size = (planes * 4, width)
    return halves(sub, pairs[:, 0], pairs[:, 1]).reshape(size), uppers(sub, pairs[:, 0], pairs[:, 1]).reshape(size)


def far_tile(from_low, from_high):
    width = from_low.shape[-1]
    low, high = from_low.reshape(-1, 8, width), from_high.reshape(-1, 8, width)
    sub = iota(low.shape, 1)
    even = jnp.where(sub < 4, high, shifted(low, 4, 1))
    odd = jnp.where(sub < 4, shifted(high, 4, 1), low)
    return jnp.stack([even, odd], axis=1).reshape(-1, 8, width)


def first_x_kernel(own, r1, uxl, uxh, zl, zh, q1, xl, xh):
    q1[4:20] = r1[...]
    for ref, planes in ((zl, slice(0, 4)), (zh, slice(20, 24))):
        for t in range(4):
            q1[planes, :, lanes(t)] = ref[uptake_part(8 + t)].astype(F32).reshape(4, 16, 128)
    for ref, d in ((xl, 0), (xh, 2)):
        for n, src in enumerate((own, zl, zh)):
            ref[0:BLOCK, lanes(n)] = src[0:BLOCK, lanes(d)]
    sub = iota((8, 128), 0)
    lows, highs = [], []
    for t in range(8):
        xl[uptake_part(t)] = uxl[:, lanes(t)]
        xh[uptake_part(t)] = uxh[:, lanes(t)]
        both = [ref[uptake_part(t)].astype(F32) for ref in (zl, zh)]
        planes = [both[0][0:32], both[0][32:64], both[1][0:32], both[1][32:64]]
        to_low, to_high = jnp.zeros((8, 128), F32), jnp.zeros((8, 128), F32)
        for n, p in enumerate(planes):
            here = sub // 2 == n
            to_low = jnp.where(here, shifted(p[0:8], 2 * n, 0), to_low)
            to_high = jnp.where(here, shifted(p[24:32], 2 * n + 2, 0), to_high)
        lows.append(to_low)
        highs.append(to_high)
    xl[uptake_part(8)] = jnp.concatenate(lows, axis=0).astype(BF16)
    xh[uptake_part(8)] = jnp.concatenate(highs, axis=0).astype(BF16)


FAR = 80


def source_window_kernel(nz, own, zl, zh, z2l, z2h, r2, firstl, firsth, f2, q2, nl, nh, fl, fh):
    iz = lax.axis_index("gz")
    zeros = jnp.zeros((10, 8, 256), F32)
    f2[0:10] = zeros
    f2[22:32] = zeros
    f2[10:22] = own[...].reshape(12, 8, 256)
    for ref, planes in ((zl, slice(2, 14)), (zh, slice(18, 30))):
        part = jnp.concatenate([ref[240:288, 0:256], ref[240:288, 256:512]], axis=0).astype(F32)
        f2[planes] = f2[planes] + part.reshape(12, 8, 256)
    for ref, planes, exists in ((z2l, slice(0, 6), iz >= 2), (z2h, slice(26, 32), iz < nz - 2)):
        part = jnp.where(exists, ref[0:48, :].astype(F32), 0.0)
        f2[planes] = f2[planes] + part.reshape(6, 8, 256)
    q2[0:4] = z2l[48:80, :].astype(F32).reshape(4, 8, 256)
    q2[28:32] = z2h[48:80, :].astype(F32).reshape(4, 8, 256)
    q2[12:20] = r2[...].reshape(8, 8, 256)
    for ref, planes in ((firstl, slice(4, 12)), (firsth, slice(20, 28))):
        for t in range(2):
            q2[planes, :, lanes(t)] = ref[uptake_part(12 + t)].astype(F32).reshape(8, 8, 128)
    for i, near in enumerate((nl, nh)):
        near[0:256, :] = f2[...].reshape(256, 256).astype(BF16)
        near[256:288, :] = z2l[48:80, :]
        near[288:320, :] = z2h[48:80, :]
        for n in range(4):
            rows = slice(288 + 32 * (n // 2) + 16 * i, 304 + 32 * (n // 2) + 16 * i)
            cols = slice(256 * (n % 2), 256 * (n % 2) + 256)
            near[320 + 32 * n : 336 + 32 * n, :] = zl[rows, cols]
            near[336 + 32 * n : 352 + 32 * n, :] = zh[rows, cols]
    for i, ref in enumerate((f2, q2)):
        to_low, to_high = far_messages(ref[...])
        fl[128 * i : 128 * i + 128, :] = to_low.astype(BF16)
        fh[128 * i : 128 * i + 128, :] = to_high.astype(BF16)


O = 5
Q = 2
BASE = 1.0 + 6.0 * KAPPA


def scatter(blocks, hot, left):
    lane = iota((128, 128), 1)
    for i, (ref, part) in enumerate(blocks):
        name = ref[256:272, part].astype(F32).astype(jnp.int32)[0:1]
        tiles = lax.shift_right_logical(name, 6)
        at_y = (name & 63) * 16 + (lane[0:1] & 15)
        at_y = jnp.broadcast_to(at_y.astype(F32), (128, 128)).T.astype(jnp.int32)
        for t in range(NT):
            hot[128 * i : 128 * i + 128, lanes(t)] = jnp.where(at_y == lane + 128 * t, 1.0, 0.0).astype(BF16)
        values = ref[0:256, part].astype(F32)
        for tile in range(4):
            left[256 * tile : 256 * tile + 256, lanes(i)] = jnp.where(tiles == tile, values, 0.0).astype(BF16)
    for n in range(4):
        cols = slice(n * 256, (n + 1) * 256)
        sums = jnp.dot(left[...], hot[:, cols], preferred_element_type=F32)
        for tile in range(4):
            bz, bx = tile // 2, tile % 2
            yield 16 * bz, slice(16 * bx, 16 * bx + 16), cols, sums[256 * tile : 256 * tile + 256].reshape(16, 16, 256)


def sweep(src, dst, source, gg, z, sourced):
    for t, here, sums in plane(src, z + O):
        inner = KAPPA * sums
        g = gg[z + Q, :, lanes(t)]
        if sourced:
            body = inner[0:32] + source[z, :, lanes(t)]
            dst[z + O, 0:32, lanes(t)] = KEEP * here[0:32] + g[0:32] * body
            dst[z + O, 32:40, lanes(t)] = KEEP * here[32:40] + g[32:40] * inner[32:40]
        else:
            dst[z + O, :, lanes(t)] = KEEP * here + g * inner


def own_kernel(
    nz, own, zl, zh, density, uptake, s_out, g_out, v_out, edge_out,
    dens, upt, s0, g0, v1, edge, va, hot, left, sems,
):
    iz = lax.axis_index("gz")
    loads = [pltpu.make_async_copy(density, dens, sems.at[0]), pltpu.make_async_copy(uptake, upt, sems.at[1])]
    stores = [
        pltpu.make_async_copy(src, dst, sems.at[2 + i])
        for i, (src, dst) in enumerate(((s0, s_out), (g0, g_out), (v1, v_out), (edge, edge_out)))
    ]
    for copy in loads:
        copy.start()
    for p in (3, 4, 37, 38):
        va[p] = jnp.zeros((40, 1024), F32)
    for n in range(4):
        ref, valid = (zl, iz > 0) if n < 2 else (zh, iz < nz - 1)
        q = n if n < 2 else 32 + n
        rows = slice(32 * (n % 2), 32 * (n % 2) + 32)
        for t in range(NT):
            g0[q, :, lanes(t)] = jnp.where(valid, OMEGA, 0.0) / (ref[uptake_part(t)].astype(F32)[rows] + BASE)

    blocks = [(ref, lanes(1)) for ref in (own, zl, zh)]
    waiting = list(loads[0:1])
    for z, rows, cols, sums in scatter(blocks, hot, left):
        while waiting:
            waiting.pop().wait()
        planes = slice(z, z + 16)
        s0[planes, rows, cols] = dens[planes, rows, cols] + sums
    stores[0].start()
    loads[1].wait()

    def own_plane(z):
        va[z + O, 0:32, :] = dens[z]
        va[z + O, 32:40, :] = jnp.zeros((8, 1024), F32)
        g0[z + Q] = OMEGA / (upt[z] + BASE)

    loop(0, C, own_plane)
    stores[1].start()

    def first(z):
        for t, here, sums in plane(va, z + O):
            inner = KAPPA * sums
            body = inner[0:32] + s0[z, :, lanes(t)]
            v1[z + 1, :, lanes(t)] = KEEP * here[0:32] + g0[z + Q, :, lanes(t)] * body
            edge[z, :, lanes(t)] = inner[32:40]

    loop(0, C, first, 2)
    for z in (-1, C):
        for t in range(NT):
            near = va[z + O + (1 if z < 0 else -1), 0:32, lanes(t)]
            v1[z + 1, :, lanes(t)] = g0[z + Q, :, lanes(t)] * (KAPPA * near)
    for copy in stores[2:]:
        copy.start()
    for copy in stores:
        copy.wait()


def pre_kernel(
    nz, nx, xl, xh, zl, zh, q1, s0, g0, v1, edge_in, uptake,
    c1, mxl, mxh, v_out, g_out, s_out,
    va, vb, supply, upt, dh, gg, edge, hot, left, rs, xp, usl, ush, sems,
):
    iz, ix = lax.axis_index("gz"), lax.axis_index("xy")
    k = KAPPA
    loads = [
        pltpu.make_async_copy(src, dst, sems.at[i])
        for i, (src, dst) in enumerate(
            (
                (s0, supply),
                (v1, vb.at[4:38, 0:32, :]),
                (g0, gg.at[:, 0:32, :]),
                (edge_in, edge),
                (uptake, upt),
            )
        )
    ]
    for copy in loads:
        copy.start()

    for p in (1, 2, 39, 40):
        va[p] = jnp.zeros((40, 1024), F32)
    for p in (2, 3, 38, 39):
        vb[p] = jnp.zeros((40, 1024), F32)
    for p in (4, 37):
        vb[p, 32:40, :] = jnp.zeros((8, 1024), F32)

    sub8 = iota((8, 1024), 0)
    for t in range(NT):
        usl[0:64, lanes(t)] = xl[uptake_part(t)].astype(F32)
        ush[0:64, lanes(t)] = xh[uptake_part(t)].astype(F32)
        usl[64:72, lanes(t)] = xl[uptake_part(8)].astype(F32)[8 * t : 8 * t + 8]
        ush[64:72, lanes(t)] = xh[uptake_part(8)].astype(F32)[8 * t : 8 * t + 8]

    def set_halo(q, low, high, valid_z):
        gz = jnp.where(valid_z, OMEGA, 0.0)
        d = jnp.where(sub8 < 2, high, jnp.where(sub8 >= 6, low, 0.0)) + BASE
        dh[q] = d
        omega = jnp.where(sub8 < 2, jnp.where(ix < nx - 1, gz, 0.0), jnp.where(sub8 >= 6, jnp.where(ix > 0, gz, 0.0), 0.0))
        gg[q, 32:40, :] = omega / d

    def halos(i):
        rows = pl.ds(pl.multiple_of(8 * i, 8), 8)
        low, high = usl[rows, :], ush[rows, :]
        for n in range(4):
            set_halo(4 * i + n + Q, shifted(low, 6 - 2 * n, 0), shifted(high, -2 * n, 0), True)

    loop(0, C // 4, halos)
    low, high = usl[64:72, :], ush[64:72, :]
    for n in range(4):
        exists = iz > 0 if n < 2 else iz < nz - 1
        set_halo(n if n < 2 else 32 + n, shifted(low, 6 - 2 * n, 0), shifted(high, -2 * n, 0), exists)

    blocks = [(ref, lanes(n)) for ref in (xl, xh) for n in range(3)]
    waiting = list(loads[0:3])
    for z, rows, cols, sums in scatter(blocks, hot, left):
        while waiting:
            waiting.pop().wait()
        supply[z : z + 16, rows, cols] = supply[z : z + 16, rows, cols] + sums
        g = gg[z + Q : z + Q + 16, rows, cols]
        vb[z + O : z + O + 16, rows, cols] = vb[z + O : z + O + 16, rows, cols] + g * sums
    loads[3].wait()

    s_copy = pltpu.make_async_copy(supply, s_out, sems.at[7])
    s_copy.start()

    def edges(z):
        vb[z + O, 32:40, :] = gg[z + Q, 32:40, :] * edge[z]

    loop(0, C, edges)

    loop(0, C, lambda z: sweep(vb, va, supply, gg, z, True), 2)
    loop(0, 4, lambda i: sweep(vb, va, supply, gg, jnp.where(i < 2, i - 2, i + C - 2), False))
    loads[4].wait()
    v_copy = pltpu.make_async_copy(va.at[3:39], v_out, sems.at[5])
    g_copy = pltpu.make_async_copy(gg, g_out, sems.at[6])
    v_copy.start()
    g_copy.start()

    def residual(z, rates, sourced):
        for t, here, sums in plane(va, z + O):
            r = k * sums
            if rates is not None:
                inner = r[0:32] - (rates(t) + BASE) * here[0:32]
                if sourced:
                    inner = inner + supply[z, :, lanes(t)]
                r = jnp.concatenate([inner, r[32:40] - dh[z + Q, :, lanes(t)] * here[32:40]], axis=0)
            yield t, r

    def coarse(m, zs, rates, sourced):
        parts = [residual(zs[i], rates[i], sourced) for i in range(2)]
        for (t, first), (_, second) in zip(*parts):
            xp[t, m, 0:20, :] = halve_rows(first + second, rs, t)

    def from_message(ref, n):
        return lambda t: ref[uptake_part(t)].astype(F32)[32 * n : 32 * n + 32]

    def inner(m):
        zs = (2 * m - 4, 2 * m - 3)
        coarse(m, zs, [lambda t, z=z: upt[z, :, lanes(t)] for z in zs], True)

    loop(2, 18, inner)
    for m, ref, z in ((1, zl, -2), (18, zh, C)):
        coarse(m, (z, z + 1), [from_message(ref, 0), from_message(ref, 1)], False)

    def outer(i):
        for t, r in residual(jnp.where(i == 0, -3, 34), None, False):
            xp[t, 19 * i, 0:20, :] = halve_rows(r, rs, t)

    loop(0, 2, outer)

    sub = iota((20, 8, 128), 1)
    for t, tile in enumerate(halve_lanes(xp, 20, 24)):
        last = tile[:, 16:24]
        last = jnp.where(sub < 2, last, jnp.where(sub >= 6, shifted(last, 4, 1), 0.0))
        c1[:, 0:16, lanes(t)] = tile[:, 0:16]
        c1[:, 16:24, lanes(t)] = last

    sub1 = iota((5, 8, 512), 1)
    first, last, halo = [c1[:, 8 * n : 8 * n + 8].reshape(5, 4, 8, 512) for n in range(3)]
    sub4 = iota((5, 4, 8, 512), 2)
    to_high = in_three(sub1, jnp.where(sub4 >= 4, last, halo), *HIGH_PACK)
    to_low = in_three(sub1, jnp.where(sub4 >= 4, halo, first), *LOW_PACK)
    sub1 = iota((12, 8, 512), 1)
    first = q1[:, 0:8, :].reshape(12, 2, 8, 512)
    last = q1[:, 8:16, :].reshape(12, 2, 8, 512)
    low_rates = halves(sub1, first[:, 0], first[:, 1]).reshape(96, 512)
    high_rates = uppers(sub1, last[:, 0], last[:, 1]).reshape(96, 512)
    filler = jnp.zeros((8, 512), F32)
    for ref, sources, rates in ((mxl, to_low, low_rates), (mxh, to_high, high_rates)):
        ref[0:128, :] = jnp.concatenate([sources.reshape(120, 512), filler], axis=0).astype(BF16)
        ref[128:224, :] = rates.astype(BF16)

    v_copy.wait()
    g_copy.wait()
    s_copy.wait()


def edges_kernel(r2, zl, zh, v_in, s_in, vzl, vzh, pxl, pxh, cnl, cnh, vx, vz, sx, sz, sems):
    copies = [
        (v_in.at[:, 0:8, :], vx.at[:, 0:8, :]),
        (v_in.at[:, 24:40, :], vx.at[:, 8:24, :]),
        (v_in.at[0:4], vz.at[0]),
        (v_in.at[32:36], vz.at[1]),
        (s_in.at[:, 0:8, :], sx.at[:, 0:8, :]),
        (s_in.at[:, 24:32, :], sx.at[:, 8:16, :]),
        (s_in.at[0], sz.at[0]),
        (s_in.at[31], sz.at[1]),
    ]
    copies = [pltpu.make_async_copy(src, dst, sems.at[i]) for i, (src, dst) in enumerate(copies)]
    for copy in copies:
        copy.start()
    sub8 = iota((8, 1024), 0)
    for ref in (pxl, pxh):
        for t in range(2):
            ref[176:240, lanes(t)] = zl[uptake_part(12 + t)]
            ref[176:240, lanes(2 + t)] = r2[:, lanes(t)].astype(BF16)
            ref[176:240, lanes(4 + t)] = zh[uptake_part(12 + t)]
        ref[176:240, 768:1024] = jnp.zeros((64, 256), BF16)
    for copy in copies:
        copy.wait()

    for i, (level0, corners) in enumerate(((vzl, cnl), (vzh, cnh))):
        level0[0:160, :] = vz[i].reshape(160, 1024).astype(BF16)
        last = jnp.concatenate([sz[i], jnp.zeros((16, 1024), F32)], axis=0)
        level0[160:208, :] = last.astype(BF16)
        planes = [vz[i, n] for n in range(4)]
        low = [pack_low((v[0:8], v[32:40]), (w[0:8], w[32:40])) for v, w in (planes[0:2], planes[2:4])]
        high = [pack_high((v[24:32], v[32:40]), (w[24:32], w[32:40])) for v, w in (planes[0:2], planes[2:4])]
        corners[...] = jnp.concatenate(low + high, axis=0).astype(BF16)

    def sides(i):
        lows, highs = [], []
        for j in range(2):
            p = 4 * i + 2 * j
            v, w = vx[p], vx[p + 1]
            lows.append(pack_low((v[0:8], v[16:24]), (w[0:8], w[16:24])))
            highs.append(pack_high((v[8:16], v[16:24]), (w[8:16], w[16:24])))
        rows = pl.ds(pl.multiple_of(16 * i, 16), 16)
        pxl[rows, :] = jnp.concatenate(lows, axis=0).astype(BF16)
        pxh[rows, :] = jnp.concatenate(highs, axis=0).astype(BF16)

    loop(0, 9, sides)

    def sources(i):
        lows, highs = [], []
        for j in range(2):
            low, high = jnp.zeros((8, 1024), F32), jnp.zeros((8, 1024), F32)
            for n in range(8):
                z = 16 * i + 8 * j + n
                low = jnp.where(sub8 == n, shifted(sx[z, 0:8, :], n, 0), low)
                high = jnp.where(sub8 == n, shifted(sx[z, 8:16, :], n + 1, 0), high)
            lows.append(low)
            highs.append(high)
        rows = pl.ds(pl.multiple_of(16 * i + 144, 16), 16)
        pxl[rows, :] = jnp.concatenate(lows, axis=0).astype(BF16)
        pxh[rows, :] = jnp.concatenate(highs, axis=0).astype(BF16)

    loop(0, 2, sources)


def outer_rows(sub):
    return (sub < 2) | (sub >= 6)


def pack_pair(sub, a, b):
    return jnp.where(outer_rows(sub), a, shifted(b, 4, 0))


def pack_low(first, second):
    sub = iota((8, 1024), 0)
    a, b = [jnp.where(sub < 4, near, halo) for near, halo in (first, second)]
    return pack_pair(sub, a, b)


def pack_high(first, second):
    sub = iota((8, 1024), 0)
    a, b = [jnp.where(sub >= 4, near, halo) for near, halo in (first, second)]
    return pack_pair(sub, a, b)


def in_three(sub, tiles, free, turns):
    spare = (sub == free) | (sub == free + 1)
    last = tiles[:, 3]
    parts = [jnp.where(spare, shifted(last, turn, 1), tiles[:, i]) for i, turn in enumerate(turns)]
    return jnp.stack(parts, axis=1)


def out_of_three(sub, parts, free, turns):
    last = None
    for i, turn in enumerate(turns):
        back = shifted(parts[:, i], -turn, 1)
        home = (free - turn) % 8
        here = (sub == home) | (sub == home + 1)
        last = jnp.where(here, back, 0.0 if last is None else last)
    return jnp.stack([parts[:, 0], parts[:, 1], parts[:, 2], last], axis=1)


HIGH_PACK = (2, (-2, 4, 2))
LOW_PACK = (4, (-2, 4, 2))


def middle_kernel(nz, nx, c1, q_in, r2, cnl, cnh, mxl, mxh, f1, g1, v1, g2, z1l, z1h, z2l, z2h, q0, va, vv, rs, xp):
    iz, ix = lax.axis_index("gz"), lax.axis_index("xy")
    k = spread(1)
    base = 1.0 + 6.0 * k
    sub5 = iota((5, 8, 512), 1)
    low = out_of_three(sub5, mxl[0:128, :].astype(F32)[0:120].reshape(5, 3, 8, 512), *HIGH_PACK).reshape(20, 8, 512)
    high = out_of_three(sub5, mxh[0:128, :].astype(F32)[0:120].reshape(5, 3, 8, 512), *LOW_PACK).reshape(20, 8, 512)
    sub = iota((20, 8, 512), 1)
    for p in (0, 1, 22, 23):
        f1[p] = jnp.zeros((24, 512), F32)
    f1[2:22, 0:8] = c1[:, 0:8] + jnp.where(sub < 2, low, 0.0)
    f1[2:22, 8:16] = c1[:, 8:16] + jnp.where(sub >= 6, high, 0.0)
    f1[2:22, 16:24] = c1[:, 16:24] + jnp.where(sub >= 4, low, high)
    low, high = [ref[128:224, :].astype(F32).reshape(12, 8, 512) for ref in (mxl, mxh)]
    sub12 = iota((12, 8, 512), 1)
    even = jnp.where(sub12 >= 4, shifted(low, 4, 1), high)
    odd = jnp.where(sub12 >= 4, low, shifted(high, 4, 1))
    q0[:, 0:16] = q_in[...]
    q0[:, 16:24] = jnp.stack([even, odd], axis=1).reshape(24, 8, 512)
    shape = (24, 24, 128)
    valid = inside(shape, 0, -4, None, iz, 16, nz) & inside(shape, 1, 0, 20, ix, 16, nx)
    for t in range(4):
        g = jnp.where(valid, OMEGA, 0.0) / (q0[:, :, lanes(t)] + base)
        g1[:, :, lanes(t)] = g
        va[:, :, lanes(t)] = g * f1[:, :, lanes(t)]
    for p in (0, 1, 24, 25):
        vv[p] = jnp.zeros((24, 512), F32)

    def sweep(p):
        for t, here, sums in plane(va, p):
            vv[p + 1, :, lanes(t)] = KEEP * here + g1[p, :, lanes(t)] * (f1[p, :, lanes(t)] + k * sums)

    loop(1, 23, sweep, 2)
    v1[...] = vv[1:25]

    def residual(p):
        for t, here, sums in plane(vv, p + 1):
            yield t, f1[p, :, lanes(t)] + k * sums - (q0[p, :, lanes(t)] + base) * here

    def coarse(m):
        for (t, first), (_, second) in zip(residual(2 * m), residual(2 * m + 1)):
            xp[t, m] = halve_rows((first + second)[0:16], rs, t)

    loop(0, 12, coarse)
    for t, tile in enumerate(halve_lanes(xp, 12, 8)):
        g2[:, lanes(t)] = tile.reshape(96, 128)
        for ref in (z1l, z1h):
            ref[240:288, lanes(t)] = tile[0:6].reshape(48, 128).astype(BF16)
            ref[240:288, lanes(2 + t)] = tile[6:12].reshape(48, 128).astype(BF16)
    for ref, corners in ((z1l, cnl), (z1h, cnh)):
        ref[288:320, :] = corners[:, 0:512]
        ref[320:352, :] = corners[:, 512:1024]
    for ref, p in ((z1l, 2), (z1h, 18)):
        ref[0:144, :] = vv[p : p + 6].reshape(144, 512).astype(BF16)
        ref[144:240, :] = f1[p : p + 4].reshape(96, 512).astype(BF16)
    low, high = far_along_z(nz, iz, g2[0:48, :], g2[48:96, :])
    z2l[0:48, :] = low.astype(BF16)
    z2h[0:48, :] = high.astype(BF16)
    low, high = far_along_z(nz, iz, r2[0:32, :], r2[32:64, :])
    z2l[48:80, :] = low.astype(BF16)
    z2h[48:80, :] = high.astype(BF16)


def back_kernel(
    nz, nx, f_in, g1, v1, z1l, z1h, vzl, vzh, vxl_in, vxh_in, own2, n2l, n2h, m2l, m2h, q_own, v_in, g_in, s_in,
    out_hbm,
    f2, q2, h2, a2, b2, rs, xp, xpr, wa, w1, zsl, zsh, vb, ws,
    v2, gg, supply, fsl, fsh, out, f1, vxl, vxh, sems,
):
    iz, ix = lax.axis_index("gz"), lax.axis_index("xy")
    matrix = doubling()
    level0 = [
        pltpu.make_async_copy(src, dst, sems.at[i])
        for i, (src, dst) in enumerate(((v_in, v2), (g_in, gg), (s_in, supply)))
    ]
    for copy in level0:
        copy.start()

    f1[...] = f_in[...]
    wa[...] = v1[...]
    for ref, p in ((z1l, 1), (z1h, 17)):
        wa[p : p + 6] = wa[p : p + 6] + ref[0:144, :].astype(F32).reshape(6, 24, 512)
        f1[p + 1 : p + 5] = f1[p + 1 : p + 5] + ref[144:240, :].astype(F32).reshape(4, 24, 512)

    f2[:, 0:8, :] = own2[...]
    f2[:, 8:16, :] = n2h[0:256, :].astype(F32).reshape(32, 8, 256)
    f2[:, 16:24, :] = far_tile(m2l[0:128, :].astype(F32), m2h[0:128, :].astype(F32))
    f2[:, 24:32, :] = n2l[0:256, :].astype(F32).reshape(32, 8, 256)
    q2[:, 0:8, :] = q_own[...]
    q2[:, 16:24, :] = far_tile(m2l[128:256, :].astype(F32), m2h[128:256, :].astype(F32))
    for ref, rows in ((vxh_in, slice(8, 16)), (vxl_in, slice(24, 32))):
        for n in range(3):
            q2[8 * n + 4 : 8 * n + 12, rows, :] = ref[176:240, n * 256 : n * 256 + 256].astype(F32).reshape(8, 8, 256)
    for ref, rows in ((n2h, slice(8, 16)), (n2l, slice(24, 32))):
        outer = ref[256:320, :].astype(F32).reshape(8, 8, 256)
        q2[0:4, rows, :] = outer[0:4]
        q2[28:32, rows, :] = outer[4:8]

    k = spread(2)
    base = 1.0 + 6.0 * k
    shape = (32, 32, 128)
    valid = inside(shape, 0, -12, None, iz, 8, nz) & inside(shape, 1, 0, 20, ix, 8, nx)
    for t in range(2):
        g = jnp.where(valid, OMEGA, 0.0) / (q2[:, :, lanes(t)] + base)
        h2[:, :, lanes(t)] = g
        a2[:, :, lanes(t)] = g * f2[:, :, lanes(t)]
    b2[0] = a2[0]
    b2[31] = a2[31]

    def sweep2(src, dst):
        def body(p):
            for t, here, sums in plane(src, p):
                dst[p, :, lanes(t)] = KEEP * here + h2[p, :, lanes(t)] * (f2[p, :, lanes(t)] + k * sums)

        return body

    loop(1, 31, sweep2(a2, b2), 2)

    def coarse(m):
        total, rates = [0.0, 0.0], [0.0, 0.0]
        for j in range(2):
            p = 2 * m + j
            for t, here, sums in plane(b2, p):
                r = f2[p, :, lanes(t)] + k * sums - (q2[p, :, lanes(t)] + base) * here
                total[t] = total[t] + r
                rates[t] = rates[t] + q2[p, :, lanes(t)]
        for t in range(2):
            xp[t, m] = halve_rows(total[t], rs, t)
            xpr[t, m] = halve_rows(rates[t], rs, t + 2)

    for t in range(2):
        for m in (0, 15):
            xp[t, m] = jnp.zeros((16, 128), F32)
            xpr[t, m] = jnp.zeros((16, 128), F32)
    loop(1, 15, coarse)

    shape = (16, 16, 128)
    valid = inside(shape, 0, -6, None, iz, 4, nz) & inside(shape, 1, 0, 10, ix, 4, nx)
    k3 = spread(3)
    (source,) = halve_lanes(xp, 16, 16)
    (rates,) = halve_lanes(xpr, 16, 16)
    g = jnp.where(valid, OMEGA, 0.0) / (rates + (1.0 + 6.0 * k3))
    v = g * source
    lane = iota(shape, 2)
    for repeat in range(3):
        edge = jnp.zeros((1, 16, 128), F32)
        sums = jnp.concatenate([v[1:], edge], axis=0) + jnp.concatenate([edge, v[:-1]], axis=0)
        sums = sums + shifted(v, 1, 1) + shifted(v, -1, 1)
        sums = sums + jnp.where(lane == 0, 0.0, shifted(v, 1, 2)) + jnp.where(lane == 127, 0.0, shifted(v, -1, 2))
        v = KEEP * v + g * (source + k3 * sums)

    wide = split_dot(v[4:12].reshape(128, 128), matrix).reshape(8, 16, 256)
    for m in range(8):
        for t in range(2):
            part = wide[m, :, lanes(t)]
            rs[t, pl.ds(0, 16, stride=2), :] = part
            rs[t, pl.ds(1, 16, stride=2), :] = part
            for j in range(2):
                p = 8 + 2 * m + j
                b2[p, :, lanes(t)] = b2[p, :, lanes(t)] + rs[t, 0:32, :]
    loop(9, 23, sweep2(b2, a2), 2)
    loop(10, 22, sweep2(a2, b2), 2)

    w = b2[10:22]
    near, far = w[:, 8:16], w[:, 24:32]
    near = jnp.where(iota((12, 8, 256), 1) < 2, near, shifted(far, 4, 1))
    w = jnp.concatenate([w[:, 0:8], near], axis=1).reshape(192, 256)
    wide = [split_dot(w[:, lanes(t)], matrix) for t in range(2)]
    wide = jnp.concatenate(wide, axis=1).reshape(12, 16, 512)
    for m in range(12):
        for t in range(4):
            part = wide[m, :, lanes(t)]
            rs[t, pl.ds(0, 16, stride=2), :] = part
            rs[t, pl.ds(1, 16, stride=2), :] = part
            for j in range(2):
                p = 2 * m + j
                wa[p, :, lanes(t)] = wa[p, :, lanes(t)] + rs[t, 0:24, :]
    k1 = spread(1)

    def sweep1(src, dst):
        def body(p):
            for t, here, sums in plane(src, p):
                dst[p, :, lanes(t)] = KEEP * here + g1[p, :, lanes(t)] * (f1[p, :, lanes(t)] + k1 * sums)

        return body

    loop(2, 22, sweep1(wa, w1), 2)
    loop(3, 21, sweep1(w1, wa), 2)

    sub = iota((18, 8, 128), 1)
    for t in range(4):
        halo = wa[3:21, 16:24, lanes(t)]
        halo = jnp.where(sub < 2, halo, shifted(halo, 4, 1))
        w = jnp.concatenate([wa[3:21, 0:16, lanes(t)], halo], axis=1)
        ws[:, :, t * 256 : t * 256 + 256] = split_dot(w.reshape(432, 128), matrix).reshape(18, 24, 256)

    for copy in level0:
        copy.wait()
    zsl[...] = vzl[...].astype(F32)
    zsh[...] = vzh[...].astype(F32)
    for ref, src, near in ((vxl, vxl_in, n2l), (vxh, vxh_in, n2h)):
        ref[...] = src[0:176, :]
        for n in range(4):
            cols = slice(256 * n, 256 * n + 256)
            for i, rows in enumerate((slice(0, 16), slice(128, 144))):
                corner = near[320 + 32 * n + 16 * i : 336 + 32 * n + 16 * i, :].astype(F32)
                ref[rows, cols] = (src[rows, cols].astype(F32) + corner).astype(BF16)
    for i in range(4):
        v2[i] = v2[i] + zsl[40 * i : 40 * i + 40, :]
        v2[32 + i] = v2[32 + i] + zsh[40 * i : 40 * i + 40, :]

    s8 = iota((8, 128), 0)

    outer = outer_rows(s8)

    def correct(i):
        rows = pl.ds(pl.multiple_of(16 * i, 16), 16)
        for t in range(NT):
            low = vxl[rows, lanes(t)].astype(F32)
            high = vxh[rows, lanes(t)].astype(F32)
            for n in range(2):
                part = ws[2 * i + n, :, lanes(t)]
                rs[t, pl.ds(0, 24, stride=2), :] = part
                rs[t, pl.ds(1, 24, stride=2), :] = part
                for j in range(2):
                    p = 4 * i + 2 * n + j
                    lo, hi = low[8 * n : 8 * n + 8], high[8 * n : 8 * n + 8]
                    if j:
                        lo, hi = shifted(lo, 4, 0), shifted(hi, 4, 0)
                    v2[p, 0:8, lanes(t)] = v2[p, 0:8, lanes(t)] + rs[t, 0:8, :] + jnp.where(s8 < 2, lo, 0.0)
                    v2[p, 8:24, lanes(t)] = v2[p, 8:24, lanes(t)] + rs[t, 8:24, :]
                    v2[p, 24:32, lanes(t)] = v2[p, 24:32, lanes(t)] + rs[t, 24:32, :] + jnp.where(s8 >= 6, hi, 0.0)
                    extra = jnp.where(outer, jnp.where(s8 >= 4, lo, hi), 0.0)
                    v2[p, 32:40, lanes(t)] = v2[p, 32:40, lanes(t)] + rs[t, 32:40, :] + extra

    loop(0, 9, correct)
    k0 = spread(0)

    def first(i):
        rows = pl.ds(pl.multiple_of(16 * i + 144, 16), 16)
        for t in range(NT):
            fsl[:, lanes(t)] = vxl[rows, lanes(t)].astype(F32)
            fsh[:, lanes(t)] = vxh[rows, lanes(t)].astype(F32)

        def step(j):
            z = 16 * i + j
            start = pl.multiple_of((j // 8) * 8, 8)
            turn = lax.rem(j, 8)
            for t, here, sums in plane(v2, z + 2):
                lo = pltpu.roll(fsl[pl.ds(start, 8), lanes(t)], 7 - turn, 0)
                hi = pltpu.roll(fsh[pl.ds(start, 8), lanes(t)], lax.rem(8 - turn, 8), 0)
                f = jnp.where(s8 == 7, lo, jnp.where(s8 == 0, hi, 0.0))
                g = gg[z + 2, :, lanes(t)]
                inner = k0 * sums
                vb[z + 1, 0:32, lanes(t)] = KEEP * here[0:32] + g[0:32] * (supply[z, :, lanes(t)] + inner[0:32])
                vb[z + 1, 32:40, lanes(t)] = KEEP * here[32:40] + g[32:40] * (f + inner[32:40])

        loop(0, 16, step, 2)

    loop(0, 2, first)
    for p, ref in ((1, zsl), (34, zsh)):
        for t, here, sums in plane(v2, p):
            g = gg[p, :, lanes(t)]
            vb[p - 1, :, lanes(t)] = KEEP * here + g * (ref[160:200, lanes(t)] + k0 * sums)

    def second(z):
        for t, here, sums in plane(vb, z + 1):
            g = gg[z + 2, 0:32, lanes(t)]
            out[z, :, lanes(t)] = KEEP * here[0:32] + g * (supply[z, :, lanes(t)] + k0 * sums[0:32])

    stores = []
    for i in range(4):
        part = pl.ds(8 * i, 8)
        loop(8 * i, 8 * i + 8, second, 2)
        stores.append(pltpu.make_async_copy(out.at[part], out_hbm.at[part], sems.at[3 + i]))
        stores[i].start()
    for copy in stores:
        copy.wait()


VMEM = pl.BlockSpec(memory_space=pltpu.VMEM)
SMEM = pl.BlockSpec(memory_space=pltpu.SMEM)
ANY = pl.BlockSpec(memory_space=pl.ANY)


def call(kernel, outs, scratch, smem, args, out_specs=None, in_hbm=0):
    moved = sum(a.size * a.dtype.itemsize for a in list(args) + list(outs))
    return pl.pallas_call(
        kernel,
        out_shape=tuple(outs),
        in_specs=[SMEM] * smem + [VMEM] * (len(args) - smem - in_hbm) + [ANY] * in_hbm,
        out_specs=tuple(out_specs or [VMEM] * len(outs)),
        scratch_shapes=scratch,
        compiler_params=pltpu.CompilerParams(vmem_limit_bytes=58 * 2**20),
        cost_estimate=pl.CostEstimate(flops=20 * moved, bytes_accessed=moved, transcendentals=0),
    )(*args)


def shaped(shape, dtype=F32):
    return jax.ShapeDtypeStruct(shape, dtype)


def both_ways(to_low, to_high, axis, distance=1):
    count = lax.axis_size(axis)
    up = [(i, i + distance) for i in range(count - distance)]
    down = [(j, i) for i, j in up]
    return lax.ppermute(to_high, axis, up), lax.ppermute(to_low, axis, down)


def two_away(to_low, to_high):
    count = lax.axis_size("gz")
    if count != 4:
        return both_ways(to_low, to_high, "gz", 2)
    came = lax.ppermute(to_low, "gz", [(i, (i + 2) % 4) for i in range(4)])
    return came, came


def shards(density, uptake, brick_values, brick_ids, slot_counts):
    nz, nx = lax.axis_size("gz"), lax.axis_size("xy")
    scratch = pltpu.VMEM
    half = lambda *shape: shaped(shape, BF16)
    full = lambda *shape: shaped(shape, F32)

    own, r1, r2, zl, zh, uxl, uxh = call(
        lambda *refs: first_kernel(2 * nx, *refs),
        [
            half(BLOCK, 384), full(16, 16, 512), full(64, 256), half(Z_ROWS, 384), half(Z_ROWS, 384),
            half(64, 1024), half(64, 1024),
        ],
        [
            scratch((8, 32, 128), F32), scratch((8, 16, 16, 128), F32), scratch((4, 16, 128), F32),
            scratch((4, 8, 8, 128), F32), scratch((SLOTS, BRICK), F32), scratch((C, C, 1024), F32),
            pltpu.SemaphoreType.DMA((1,)),
        ],
        2,
        (brick_ids, slot_counts, brick_values, uptake),
        in_hbm=1,
    )
    zl, zh = both_ways(zl, zh, "gz")
    q1, xl, xh = call(
        first_x_kernel,
        [full(24, 16, 512), half(X_ROWS, 384), half(X_ROWS, 384)],
        [],
        0,
        (own, r1, uxl, uxh, zl, zh),
    )
    s0, g0, v1, edge = call(
        lambda *refs: own_kernel(nz, *refs),
        [full(C, C, 1024), full(36, C, 1024), full(34, C, 1024), full(C, 8, 1024)],
        [
            scratch((C, C, 1024), F32),
            scratch((C, C, 1024), F32),
            scratch((C, C, 1024), F32),
            scratch((36, C, 1024), F32),
            scratch((34, C, 1024), F32),
            scratch((C, 8, 1024), F32),
            scratch((42, 40, 1024), F32),
            scratch((384, 1024), BF16),
            scratch((1024, 384), BF16),
            pltpu.SemaphoreType.DMA((6,)),
        ],
        0,
        (own, zl, zh, density, uptake),
        [ANY] * 4,
        in_hbm=2,
    )
    xl, xh = both_ways(xl, xh, "xy")

    c1, mxl, mxh, v2, gg, supply = call(
        lambda *refs: pre_kernel(nz, nx, *refs),
        [
            full(20, 24, 512),
            half(224, 512),
            half(224, 512),
            full(36, 40, 1024),
            full(36, 40, 1024),
            full(C, C, 1024),
        ],
        [
            scratch((42, 40, 1024), F32),
            scratch((42, 40, 1024), F32),
            scratch((C, C, 1024), F32),
            scratch((C, C, 1024), F32),
            scratch((36, 8, 1024), F32),
            scratch((36, 40, 1024), F32),
            scratch((C, 8, 1024), F32),
            scratch((768, 1024), BF16),
            scratch((1024, 768), BF16),
            scratch((8, 40, 128), F32),
            scratch((8, 20, 24, 128), F32),
            scratch((72, 1024), F32),
            scratch((72, 1024), F32),
            pltpu.SemaphoreType.DMA((8,)),
        ],
        0,
        (xl, xh, zl, zh, q1, s0, g0, v1, edge, uptake),
        [VMEM] * 3 + [ANY] * 3,
        in_hbm=5,
    )
    mxl, mxh = both_ways(mxl, mxh, "xy")
    vzl, vzh, pxl, pxh, cnl, cnh = call(
        edges_kernel,
        [
            half(208, 1024), half(208, 1024), half(240, 1024), half(240, 1024), half(32, 1024), half(32, 1024),
        ],
        [
            scratch((36, 24, 1024), F32), scratch((2, 4, 40, 1024), F32), scratch((C, 16, 1024), F32),
            scratch((2, C, 1024), F32), pltpu.SemaphoreType.DMA((8,)),
        ],
        0,
        (r2, zl, zh, v2, supply),
        in_hbm=2,
    )
    pxl, pxh, vzl, vzh, c1 = lax.optimization_barrier((pxl, pxh, vzl, vzh, c1))
    pxl, pxh, mxl, mxh = lax.optimization_barrier((pxl, pxh, mxl, mxh))
    vxl, vxh = both_ways(pxl, pxh, "xy")
    f1, g1, v1, g2, z1l, z1h, z2l, z2h = call(
        lambda *refs: middle_kernel(nz, nx, *refs),
        [
            full(24, 24, 512), full(24, 24, 512), full(24, 24, 512), full(96, 256),
            half(352, 512), half(352, 512), half(FAR, 256), half(FAR, 256),
        ],
        [
            scratch((24, 24, 512), F32), scratch((24, 24, 512), F32), scratch((26, 24, 512), F32),
            scratch((4, 16, 128), F32), scratch((4, 12, 8, 128), F32),
        ],
        0,
        (c1, q1, r2, cnl, cnh, mxl, mxh),
    )
    z1l, z1h = both_ways(z1l, z1h, "gz")
    z2l, z2h = two_away(z2l, z2h)
    g2, vxl, vxh = lax.optimization_barrier((g2, vxl, vxh))
    own2, q2, nl, nh, fl, fh = call(
        lambda *refs: source_window_kernel(nz, *refs),
        [full(32, 8, 256), full(32, 8, 256), half(448, 256), half(448, 256), half(256, 256), half(256, 256)],
        [],
        0,
        (g2, z1l, z1h, z2l, z2h, r2, zl, zh),
    )
    vzl, vzh, nl, nh, fl, fh = lax.optimization_barrier((vzl, vzh, nl, nh, fl, fh))
    nl, nh = both_ways(nl, nh, "xy")
    vzl, vzh = both_ways(vzl, vzh, "gz")
    fl, fh = both_ways(fl, fh, "xy", 2)
    window2 = scratch((32, 32, 256), F32)
    window1 = scratch((24, 24, 512), F32)
    (concentration,) = call(
        lambda *refs: back_kernel(nz, nx, *refs),
        [full(C, C, 1024)],
        [
            window2, window2, window2, window2, window2,
            scratch((8, 48, 128), F32),
            scratch((2, 16, 16, 128), F32),
            scratch((2, 16, 16, 128), F32),
            window1, window1,
            scratch((208, 1024), F32),
            scratch((208, 1024), F32),
            scratch((34, 40, 1024), F32),
            scratch((18, 24, 1024), F32),
            scratch((36, 40, 1024), F32),
            scratch((36, 40, 1024), F32),
            scratch((C, C, 1024), F32),
            scratch((16, 1024), F32),
            scratch((16, 1024), F32),
            scratch((C, C, 1024), F32),
            window1,
            scratch((176, 1024), BF16),
            scratch((176, 1024), BF16),
            pltpu.SemaphoreType.DMA((7,)),
        ],
        0,
        (f1, g1, v1, z1l, z1h, vzl, vzh, vxl, vxh, own2, nl, nh, fl, fh, q2, v2, gg, supply),
        [ANY],
        in_hbm=3,
    )
    return supply, concentration


def solution(mesh):
    return jax.shard_map(
        shards,
        mesh=mesh,
        in_specs=(
            P("gz", "xy", None),
            P("gz", "xy", None),
            P(("gz", "xy"), None),
            P(("gz", "xy")),
            P(("gz", "xy"), None),
        ),
        out_specs=(P("gz", "xy", None), P("gz", "xy", None)),
        check_vma=False,
    )
```

```python
import jax
import jax.numpy as jnp
from jax import lax
from jax.experimental import pallas as pl
from jax.experimental.pallas import tpu as pltpu
from jax.sharding import PartitionSpec as P

EDGE = 16
CAP = 8
BRICK = 4096
SLOTS = 72
KAPPA = 32.0
OMEGA = 0.8
KEEP = 1.0 - OMEGA

C = 32
NT = 8
F32 = jnp.float32
BF16 = jnp.bfloat16


def spread(level):
    return KAPPA / 4.0**level


def shifted(values, distance, axis):
    return pltpu.roll(values, distance % values.shape[axis], axis)


def iota(shape, dim):
    return lax.broadcasted_iota(jnp.int32, shape, dim)


def lanes(t):
    return slice(t * 128, (t + 1) * 128)


def plane(ref, p):
    count = ref.shape[2] // 128
    rows = ref.shape[1]
    lane = iota((rows, 128), 1)
    before, here = None, ref[p, :, lanes(0)]
    for t in range(count):
        after = ref[p, :, lanes(t + 1)] if t + 1 < count else None
        low = jnp.where(lane == 127, 0.0 if before is None else before, here)
        high = jnp.where(lane == 0, 0.0 if after is None else after, here)
        sums = shifted(low, 1, 1) + shifted(high, -1, 1)
        sums = sums + (shifted(here, 1, 0) + shifted(here, -1, 0))
        sums = sums + (ref[p - 1, :, lanes(t)] + ref[p + 1, :, lanes(t)])
        yield t, here, sums
        before, here = here, after


def loop(start, stop, body, unroll=1):
    def step(i, carry):
        body(i)
        return carry

    lax.fori_loop(start, stop, step, 0, unroll=unroll)


def split_dot(a, b):
    high = a.astype(BF16)
    low = (a - high.astype(F32)).astype(BF16)
    return jnp.dot(high, b, preferred_element_type=F32) + jnp.dot(low, b, preferred_element_type=F32)


def pooling():
    return jnp.where(iota((256, 128), 0) // 2 == iota((256, 128), 1), 0.125, 0.0).astype(BF16)


def doubling():
    return jnp.where(iota((128, 256), 1) // 2 == iota((128, 256), 0), 1.0, 0.0).astype(BF16)


def halve_rows(values, rs, t):
    rows = values.shape[0]
    rs[t, 0:rows, :] = values
    return rs[t, pl.ds(0, rows // 2, stride=2), :] + rs[t, pl.ds(1, rows // 2, stride=2), :]


def halve_lanes(xp, planes, rows):
    matrix = pooling()
    tiles = []
    for t in range(0, xp.shape[0], 2):
        pair = jnp.concatenate([xp[t].reshape(planes * rows, 128), xp[t + 1].reshape(planes * rows, 128)], axis=1)
        tiles.append(split_dot(pair, matrix).reshape(planes, rows, 128))
    return tiles


def inside(shape, dim, first, wrap, index, size, count):
    place = iota(shape, dim) + first
    if wrap is not None:
        place = jnp.where(place < wrap, place, place - shape[dim])
    place = place + index * size
    return (place >= 0) & (place < count * size)


BLOCK = 272
X_ROWS = BLOCK + 3 * 64
Z_ROWS = BLOCK + 5 * 64


def uptake_part(t):
    return slice(BLOCK + 64 * (t // 3), BLOCK + 64 * (t // 3) + 64), lanes(t % 3)


def transposed_bricks(bricks_x, ids, counts, bricks, xs, targets):
    xs[...] = bricks[...].astype(F32)
    row = iota((1, 8, 128), 1)
    group = iota((1, 8, 128), 2) // 16
    group16 = iota((16, 128), 1) // 16
    per_y = 64

    def block(j, out, part):
        start = pl.multiple_of(j * 8, 8)
        x = jnp.stack([xs[pl.ds(start, 8), lanes(k)] for k in range(32)])
        for s in (4, 2, 1):
            up = shifted(shifted(x, -s, 1), 16 * s, 2)
            down = shifted(shifted(x, s, 1), -16 * s, 2)
            row_bit = (row // s) % 2
            group_bit = (group // s) % 2
            x = jnp.where(row_bit == group_bit, x, jnp.where(row_bit == 0, up, down))
        x = jnp.where(group < counts[0, j], x, 0.0)
        out[0:256, part] = x.reshape(256, 128).astype(BF16)
        names = jnp.zeros((16, 128), jnp.int32)
        for e in range(CAP):
            number = ids[j * 8 + e]
            by = lax.rem(number, per_y)
            rest = lax.div(number, per_y)
            bx = lax.rem(rest, 2)
            bz = lax.rem(lax.div(rest, bricks_x), 2)
            names = jnp.where(group16 == e, (bz * 2 + bx) * per_y + by, names)
        out[256:272, part] = names.astype(F32).astype(BF16)

    for i, out in enumerate(targets):
        for d in range(3):
            block(3 * i + d, out, lanes(d))


def first_kernel(bricks_x, ids, counts, bricks, uptake_in, own, r1, r2, zl, zh, xl, xh, rs, xp, rs1, xp1, xs, uptake, sems):
    load = pltpu.make_async_copy(uptake_in, uptake, sems.at[0])
    load.start()
    transposed_bricks(bricks_x, ids, counts, bricks, xs, (zl, own, zh))
    load.wait()

    def pair(m):
        for t in range(NT):
            both = uptake[2 * m, :, lanes(t)] + uptake[2 * m + 1, :, lanes(t)]
            xp[t, m] = halve_rows(both, rs, t)

    loop(0, 16, pair)
    for t, tile in enumerate(halve_lanes(xp, 16, 16)):
        r1[:, :, lanes(t)] = tile

    def pair1(m):
        for t in range(4):
            both = r1[2 * m, :, lanes(t)] + r1[2 * m + 1, :, lanes(t)]
            xp1[t, m] = halve_rows(both, rs1, t)

    loop(0, 8, pair1)
    for t, tile in enumerate(halve_lanes(xp1, 8, 8)):
        r2[:, lanes(t)] = tile.reshape(64, 128)
    for ref, u, r in ((zl, slice(0, 2), slice(0, 4)), (zh, slice(30, 32), slice(12, 16))):
        for t in range(8):
            ref[uptake_part(t)] = uptake[u, :, lanes(t)].reshape(64, 128).astype(BF16)
        for t in range(4):
            ref[uptake_part(8 + t)] = r1[r, :, lanes(t)].reshape(64, 128).astype(BF16)
        for t in range(2):
            ref[uptake_part(12 + t)] = r2[:, lanes(t)].astype(BF16)
        ref[uptake_part(14)] = jnp.zeros((64, 128), BF16)

    sub = iota((8, 1024), 0)

    def columns(i):
        lows, highs = [], []
        for j in range(2):
            low, high = jnp.zeros((8, 1024), F32), jnp.zeros((8, 1024), F32)
            for n in range(4):
                z = 8 * i + 4 * j + n
                low = jnp.where(sub // 2 == n, shifted(uptake[z, 0:8, :], 2 * n, 0), low)
                high = jnp.where(sub // 2 == n, shifted(uptake[z, 24:32, :], 2 * n + 2, 0), high)
            lows.append(low)
            highs.append(high)
        rows = pl.ds(pl.multiple_of(16 * i, 16), 16)
        xl[rows, :] = jnp.concatenate(lows, axis=0).astype(BF16)
        xh[rows, :] = jnp.concatenate(highs, axis=0).astype(BF16)

    loop(0, 4, columns)


def far_along_z(nz, iz, to_low, to_high):
    if nz != 4:
        return to_low, to_high
    one = jnp.where(iz < 2, to_high, to_low)
    return one, one


def halves(sub, first, second):
    return jnp.where(sub < 4, first, shifted(second, 4, 1))


def uppers(sub, first, second):
    return jnp.where(sub < 4, shifted(first, 4, 1), second)


def far_messages(window):
    planes, _, width = window.shape
    pairs = window.reshape(planes // 2, 2, 8, width)
    sub = iota((planes // 2, 8, width), 1)
    size = (planes * 4, width)
    return halves(sub, pairs[:, 0], pairs[:, 1]).reshape(size), uppers(sub, pairs[:, 0], pairs[:, 1]).reshape(size)


def far_tile(from_low, from_high):
    width = from_low.shape[-1]
    low, high = from_low.reshape(-1, 8, width), from_high.reshape(-1, 8, width)
    sub = iota(low.shape, 1)
    even = jnp.where(sub < 4, high, shifted(low, 4, 1))
    odd = jnp.where(sub < 4, shifted(high, 4, 1), low)
    return jnp.stack([even, odd], axis=1).reshape(-1, 8, width)


def first_x_kernel(own, r1, uxl, uxh, zl, zh, q1, xl, xh):
    q1[4:20] = r1[...]
    for ref, planes in ((zl, slice(0, 4)), (zh, slice(20, 24))):
        for t in range(4):
            q1[planes, :, lanes(t)] = ref[uptake_part(8 + t)].astype(F32).reshape(4, 16, 128)
    for ref, d in ((xl, 0), (xh, 2)):
        for n, src in enumerate((own, zl, zh)):
            ref[0:BLOCK, lanes(n)] = src[0:BLOCK, lanes(d)]
    sub = iota((8, 128), 0)
    lows, highs = [], []
    for t in range(8):
        xl[uptake_part(t)] = uxl[:, lanes(t)]
        xh[uptake_part(t)] = uxh[:, lanes(t)]
        both = [ref[uptake_part(t)].astype(F32) for ref in (zl, zh)]
        planes = [both[0][0:32], both[0][32:64], both[1][0:32], both[1][32:64]]
        to_low, to_high = jnp.zeros((8, 128), F32), jnp.zeros((8, 128), F32)
        for n, p in enumerate(planes):
            here = sub // 2 == n
            to_low = jnp.where(here, shifted(p[0:8], 2 * n, 0), to_low)
            to_high = jnp.where(here, shifted(p[24:32], 2 * n + 2, 0), to_high)
        lows.append(to_low)
        highs.append(to_high)
    xl[uptake_part(8)] = jnp.concatenate(lows, axis=0).astype(BF16)
    xh[uptake_part(8)] = jnp.concatenate(highs, axis=0).astype(BF16)


FAR = 80


def source_window_kernel(nz, own, zl, zh, z2l, z2h, r2, firstl, firsth, f2, q2, nl, nh, fl, fh):
    iz = lax.axis_index("gz")
    zeros = jnp.zeros((10, 8, 256), F32)
    f2[0:10] = zeros
    f2[22:32] = zeros
    f2[10:22] = own[...].reshape(12, 8, 256)
    for ref, planes in ((zl, slice(2, 14)), (zh, slice(18, 30))):
        part = jnp.concatenate([ref[240:288, 0:256], ref[240:288, 256:512]], axis=0).astype(F32)
        f2[planes] = f2[planes] + part.reshape(12, 8, 256)
    for ref, planes, exists in ((z2l, slice(0, 6), iz >= 2), (z2h, slice(26, 32), iz < nz - 2)):
        part = jnp.where(exists, ref[0:48, :].astype(F32), 0.0)
        f2[planes] = f2[planes] + part.reshape(6, 8, 256)
    q2[0:4] = z2l[48:80, :].astype(F32).reshape(4, 8, 256)
    q2[28:32] = z2h[48:80, :].astype(F32).reshape(4, 8, 256)
    q2[12:20] = r2[...].reshape(8, 8, 256)
    for ref, planes in ((firstl, slice(4, 12)), (firsth, slice(20, 28))):
        for t in range(2):
            q2[planes, :, lanes(t)] = ref[uptake_part(12 + t)].astype(F32).reshape(8, 8, 128)
    for i, near in enumerate((nl, nh)):
        near[0:256, :] = f2[...].reshape(256, 256).astype(BF16)
        near[256:288, :] = z2l[48:80, :]
        near[288:320, :] = z2h[48:80, :]
        for n in range(4):
            rows = slice(288 + 32 * (n // 2) + 16 * i, 304 + 32 * (n // 2) + 16 * i)
            cols = slice(256 * (n % 2), 256 * (n % 2) + 256)
            near[320 + 32 * n : 336 + 32 * n, :] = zl[rows, cols]
            near[336 + 32 * n : 352 + 32 * n, :] = zh[rows, cols]
    for i, ref in enumerate((f2, q2)):
        to_low, to_high = far_messages(ref[...])
        fl[128 * i : 128 * i + 128, :] = to_low.astype(BF16)
        fh[128 * i : 128 * i + 128, :] = to_high.astype(BF16)


O = 5
Q = 2
BASE = 1.0 + 6.0 * KAPPA


def scatter(blocks, hot, left):
    lane = iota((128, 128), 1)
    for i, (ref, part) in enumerate(blocks):
        name = ref[256:272, part].astype(F32).astype(jnp.int32)[0:1]
        tiles = lax.shift_right_logical(name, 6)
        at_y = (name & 63) * 16 + (lane[0:1] & 15)
        at_y = jnp.broadcast_to(at_y.astype(F32), (128, 128)).T.astype(jnp.int32)
        for t in range(NT):
            hot[128 * i : 128 * i + 128, lanes(t)] = jnp.where(at_y == lane + 128 * t, 1.0, 0.0).astype(BF16)
        values = ref[0:256, part].astype(F32)
        for tile in range(4):
            left[256 * tile : 256 * tile + 256, lanes(i)] = jnp.where(tiles == tile, values, 0.0).astype(BF16)
    for n in range(4):
        cols = slice(n * 256, (n + 1) * 256)
        sums = jnp.dot(left[...], hot[:, cols], preferred_element_type=F32)
        for tile in range(4):
            bz, bx = tile // 2, tile % 2
            yield 16 * bz, slice(16 * bx, 16 * bx + 16), cols, sums[256 * tile : 256 * tile + 256].reshape(16, 16, 256)


def sweep(src, dst, source, gg, z, sourced):
    for t, here, sums in plane(src, z + O):
        inner = KAPPA * sums
        g = gg[z + Q, :, lanes(t)]
        if sourced:
            body = inner[0:32] + source[z, :, lanes(t)]
            dst[z + O, 0:32, lanes(t)] = KEEP * here[0:32] + g[0:32] * body
            dst[z + O, 32:40, lanes(t)] = KEEP * here[32:40] + g[32:40] * inner[32:40]
        else:
            dst[z + O, :, lanes(t)] = KEEP * here + g * inner


def own_kernel(
    nz, own, zl, zh, density, uptake, s_out, g_out, v_out, edge_out,
    dens, upt, s0, g0, v1, edge, va, hot, left, sems,
):
    iz = lax.axis_index("gz")
    loads = [pltpu.make_async_copy(density, dens, sems.at[0]), pltpu.make_async_copy(uptake, upt, sems.at[1])]
    stores = [
        pltpu.make_async_copy(src, dst, sems.at[2 + i])
        for i, (src, dst) in enumerate(((s0, s_out), (g0, g_out), (v1, v_out), (edge, edge_out)))
    ]
    for copy in loads:
        copy.start()
    for p in (3, 4, 37, 38):
        va[p] = jnp.zeros((40, 1024), F32)
    for n in range(4):
        ref, valid = (zl, iz > 0) if n < 2 else (zh, iz < nz - 1)
        q = n if n < 2 else 32 + n
        rows = slice(32 * (n % 2), 32 * (n % 2) + 32)
        for t in range(NT):
            g0[q, :, lanes(t)] = jnp.where(valid, OMEGA, 0.0) / (ref[uptake_part(t)].astype(F32)[rows] + BASE)

    blocks = [(ref, lanes(1)) for ref in (own, zl, zh)]
    waiting = list(loads[0:1])
    for z, rows, cols, sums in scatter(blocks, hot, left):
        while waiting:
            waiting.pop().wait()
        planes = slice(z, z + 16)
        s0[planes, rows, cols] = dens[planes, rows, cols] + sums
    stores[0].start()
    loads[1].wait()

    def own_plane(z):
        va[z + O, 0:32, :] = dens[z]
        va[z + O, 32:40, :] = jnp.zeros((8, 1024), F32)
        g0[z + Q] = OMEGA / (upt[z] + BASE)

    loop(0, C, own_plane)
    stores[1].start()

    def first(z):
        for t, here, sums in plane(va, z + O):
            inner = KAPPA * sums
            body = inner[0:32] + s0[z, :, lanes(t)]
            v1[z + 1, :, lanes(t)] = KEEP * here[0:32] + g0[z + Q, :, lanes(t)] * body
            edge[z, :, lanes(t)] = inner[32:40]

    loop(0, C, first, 2)
    for z in (-1, C):
        for t in range(NT):
            near = va[z + O + (1 if z < 0 else -1), 0:32, lanes(t)]
            v1[z + 1, :, lanes(t)] = g0[z + Q, :, lanes(t)] * (KAPPA * near)
    for copy in stores[2:]:
        copy.start()
    for copy in stores:
        copy.wait()


def pre_kernel(
    nz, nx, xl, xh, zl, zh, q1, s0, g0, v1, edge_in, uptake,
    c1, mxl, mxh, v_out, g_out, s_out,
    va, vb, supply, upt, dh, gg, edge, hot, left, rs, xp, usl, ush, sems,
):
    iz, ix = lax.axis_index("gz"), lax.axis_index("xy")
    k = KAPPA
    loads = [
        pltpu.make_async_copy(src, dst, sems.at[i])
        for i, (src, dst) in enumerate(
            (
                (s0, supply),
                (v1, vb.at[4:38, 0:32, :]),
                (g0, gg.at[:, 0:32, :]),
                (edge_in, edge),
                (uptake, upt),
            )
        )
    ]
    for copy in loads:
        copy.start()

    for p in (1, 2, 39, 40):
        va[p] = jnp.zeros((40, 1024), F32)
    for p in (2, 3, 38, 39):
        vb[p] = jnp.zeros((40, 1024), F32)
    for p in (4, 37):
        vb[p, 32:40, :] = jnp.zeros((8, 1024), F32)

    sub8 = iota((8, 1024), 0)
    for t in range(NT):
        usl[0:64, lanes(t)] = xl[uptake_part(t)].astype(F32)
        ush[0:64, lanes(t)] = xh[uptake_part(t)].astype(F32)
        usl[64:72, lanes(t)] = xl[uptake_part(8)].astype(F32)[8 * t : 8 * t + 8]
        ush[64:72, lanes(t)] = xh[uptake_part(8)].astype(F32)[8 * t : 8 * t + 8]

    def set_halo(q, low, high, valid_z):
        gz = jnp.where(valid_z, OMEGA, 0.0)
        d = jnp.where(sub8 < 2, high, jnp.where(sub8 >= 6, low, 0.0)) + BASE
        dh[q] = d
        omega = jnp.where(sub8 < 2, jnp.where(ix < nx - 1, gz, 0.0), jnp.where(sub8 >= 6, jnp.where(ix > 0, gz, 0.0), 0.0))
        gg[q, 32:40, :] = omega / d

    def halos(i):
        rows = pl.ds(pl.multiple_of(8 * i, 8), 8)
        low, high = usl[rows, :], ush[rows, :]
        for n in range(4):
            set_halo(4 * i + n + Q, shifted(low, 6 - 2 * n, 0), shifted(high, -2 * n, 0), True)

    loop(0, C // 4, halos)
    low, high = usl[64:72, :], ush[64:72, :]
    for n in range(4):
        exists = iz > 0 if n < 2 else iz < nz - 1
        set_halo(n if n < 2 else 32 + n, shifted(low, 6 - 2 * n, 0), shifted(high, -2 * n, 0), exists)

    blocks = [(ref, lanes(n)) for ref in (xl, xh) for n in range(3)]
    waiting = list(loads[0:3])
    for z, rows, cols, sums in scatter(blocks, hot, left):
        while waiting:
            waiting.pop().wait()
        supply[z : z + 16, rows, cols] = supply[z : z + 16, rows, cols] + sums
        g = gg[z + Q : z + Q + 16, rows, cols]
        vb[z + O : z + O + 16, rows, cols] = vb[z + O : z + O + 16, rows, cols] + g * sums
    loads[3].wait()

    s_copy = pltpu.make_async_copy(supply, s_out, sems.at[7])
    s_copy.start()

    def edges(z):
        vb[z + O, 32:40, :] = gg[z + Q, 32:40, :] * edge[z]

    loop(0, C, edges)

    loop(0, C, lambda z: sweep(vb, va, supply, gg, z, True), 2)
    loop(0, 4, lambda i: sweep(vb, va, supply, gg, jnp.where(i < 2, i - 2, i + C - 2), False))
    loads[4].wait()
    v_copy = pltpu.make_async_copy(va.at[3:39], v_out, sems.at[5])
    g_copy = pltpu.make_async_copy(gg, g_out, sems.at[6])
    v_copy.start()
    g_copy.start()

    def residual(z, rates, sourced):
        for t, here, sums in plane(va, z + O):
            r = k * sums
            if rates is not None:
                inner = r[0:32] - (rates(t) + BASE) * here[0:32]
                if sourced:
                    inner = inner + supply[z, :, lanes(t)]
                r = jnp.concatenate([inner, r[32:40] - dh[z + Q, :, lanes(t)] * here[32:40]], axis=0)
            yield t, r

    def coarse(m, zs, rates, sourced):
        parts = [residual(zs[i], rates[i], sourced) for i in range(2)]
        for (t, first), (_, second) in zip(*parts):
            xp[t, m, 0:20, :] = halve_rows(first + second, rs, t)

    def from_message(ref, n):
        return lambda t: ref[uptake_part(t)].astype(F32)[32 * n : 32 * n + 32]

    def inner(m):
        zs = (2 * m - 4, 2 * m - 3)
        coarse(m, zs, [lambda t, z=z: upt[z, :, lanes(t)] for z in zs], True)

    loop(2, 18, inner)
    for m, ref, z in ((1, zl, -2), (18, zh, C)):
        coarse(m, (z, z + 1), [from_message(ref, 0), from_message(ref, 1)], False)

    def outer(i):
        for t, r in residual(jnp.where(i == 0, -3, 34), None, False):
            xp[t, 19 * i, 0:20, :] = halve_rows(r, rs, t)

    loop(0, 2, outer)

    sub = iota((20, 8, 128), 1)
    for t, tile in enumerate(halve_lanes(xp, 20, 24)):
        last = tile[:, 16:24]
        last = jnp.where(sub < 2, last, jnp.where(sub >= 6, shifted(last, 4, 1), 0.0))
        c1[:, 0:16, lanes(t)] = tile[:, 0:16]
        c1[:, 16:24, lanes(t)] = last

    sub1 = iota((5, 8, 512), 1)
    first, last, halo = [c1[:, 8 * n : 8 * n + 8].reshape(5, 4, 8, 512) for n in range(3)]
    sub4 = iota((5, 4, 8, 512), 2)
    to_high = in_three(sub1, jnp.where(sub4 >= 4, last, halo), *HIGH_PACK)
    to_low = in_three(sub1, jnp.where(sub4 >= 4, halo, first), *LOW_PACK)
    sub1 = iota((12, 8, 512), 1)
    first = q1[:, 0:8, :].reshape(12, 2, 8, 512)
    last = q1[:, 8:16, :].reshape(12, 2, 8, 512)
    low_rates = halves(sub1, first[:, 0], first[:, 1]).reshape(96, 512)
    high_rates = uppers(sub1, last[:, 0], last[:, 1]).reshape(96, 512)
    filler = jnp.zeros((8, 512), F32)
    for ref, sources, rates in ((mxl, to_low, low_rates), (mxh, to_high, high_rates)):
        ref[0:128, :] = jnp.concatenate([sources.reshape(120, 512), filler], axis=0).astype(BF16)
        ref[128:224, :] = rates.astype(BF16)

    v_copy.wait()
    g_copy.wait()
    s_copy.wait()


def edges_kernel(r2, zl, zh, v_in, s_in, vzl, vzh, pxl, pxh, cnl, cnh, vx, vz, sx, sz, sems):
    copies = [
        (v_in.at[:, 0:8, :], vx.at[:, 0:8, :]),
        (v_in.at[:, 24:40, :], vx.at[:, 8:24, :]),
        (v_in.at[0:4], vz.at[0]),
        (v_in.at[32:36], vz.at[1]),
        (s_in.at[:, 0:8, :], sx.at[:, 0:8, :]),
        (s_in.at[:, 24:32, :], sx.at[:, 8:16, :]),
        (s_in.at[0], sz.at[0]),
        (s_in.at[31], sz.at[1]),
    ]
    copies = [pltpu.make_async_copy(src, dst, sems.at[i]) for i, (src, dst) in enumerate(copies)]
    for copy in copies:
        copy.start()
    sub8 = iota((8, 1024), 0)
    for ref in (pxl, pxh):
        for t in range(2):
            ref[176:240, lanes(t)] = zl[uptake_part(12 + t)]
            ref[176:240, lanes(2 + t)] = r2[:, lanes(t)].astype(BF16)
            ref[176:240, lanes(4 + t)] = zh[uptake_part(12 + t)]
        ref[176:240, 768:1024] = jnp.zeros((64, 256), BF16)
    for copy in copies:
        copy.wait()

    for i, (level0, corners) in enumerate(((vzl, cnl), (vzh, cnh))):
        level0[0:160, :] = vz[i].reshape(160, 1024).astype(BF16)
        last = jnp.concatenate([sz[i], jnp.zeros((16, 1024), F32)], axis=0)
        level0[160:208, :] = last.astype(BF16)
        planes = [vz[i, n] for n in range(4)]
        low = [pack_low((v[0:8], v[32:40]), (w[0:8], w[32:40])) for v, w in (planes[0:2], planes[2:4])]
        high = [pack_high((v[24:32], v[32:40]), (w[24:32], w[32:40])) for v, w in (planes[0:2], planes[2:4])]
        corners[...] = jnp.concatenate(low + high, axis=0).astype(BF16)

    def sides(i):
        lows, highs = [], []
        for j in range(2):
            p = 4 * i + 2 * j
            v, w = vx[p], vx[p + 1]
            lows.append(pack_low((v[0:8], v[16:24]), (w[0:8], w[16:24])))
            highs.append(pack_high((v[8:16], v[16:24]), (w[8:16], w[16:24])))
        rows = pl.ds(pl.multiple_of(16 * i, 16), 16)
        pxl[rows, :] = jnp.concatenate(lows, axis=0).astype(BF16)
        pxh[rows, :] = jnp.concatenate(highs, axis=0).astype(BF16)

    loop(0, 9, sides)

    def sources(i):
        lows, highs = [], []
        for j in range(2):
            low, high = jnp.zeros((8, 1024), F32), jnp.zeros((8, 1024), F32)
            for n in range(8):
                z = 16 * i + 8 * j + n
                low = jnp.where(sub8 == n, shifted(sx[z, 0:8, :], n, 0), low)
                high = jnp.where(sub8 == n, shifted(sx[z, 8:16, :], n + 1, 0), high)
            lows.append(low)
            highs.append(high)
        rows = pl.ds(pl.multiple_of(16 * i + 144, 16), 16)
        pxl[rows, :] = jnp.concatenate(lows, axis=0).astype(BF16)
        pxh[rows, :] = jnp.concatenate(highs, axis=0).astype(BF16)

    loop(0, 2, sources)


def outer_rows(sub):
    return (sub < 2) | (sub >= 6)


def pack_pair(sub, a, b):
    return jnp.where(outer_rows(sub), a, shifted(b, 4, 0))


def pack_low(first, second):
    sub = iota((8, 1024), 0)
    a, b = [jnp.where(sub < 4, near, halo) for near, halo in (first, second)]
    return pack_pair(sub, a, b)


def pack_high(first, second):
    sub = iota((8, 1024), 0)
    a, b = [jnp.where(sub >= 4, near, halo) for near, halo in (first, second)]
    return pack_pair(sub, a, b)


def in_three(sub, tiles, free, turns):
    spare = (sub == free) | (sub == free + 1)
    last = tiles[:, 3]
    parts = [jnp.where(spare, shifted(last, turn, 1), tiles[:, i]) for i, turn in enumerate(turns)]
    return jnp.stack(parts, axis=1)


def out_of_three(sub, parts, free, turns):
    last = None
    for i, turn in enumerate(turns):
        back = shifted(parts[:, i], -turn, 1)
        home = (free - turn) % 8
        here = (sub == home) | (sub == home + 1)
        last = jnp.where(here, back, 0.0 if last is None else last)
    return jnp.stack([parts[:, 0], parts[:, 1], parts[:, 2], last], axis=1)


HIGH_PACK = (2, (-2, 4, 2))
LOW_PACK = (4, (-2, 4, 2))


def middle_kernel(nz, nx, c1, q_in, r2, cnl, cnh, vzl, vzh, mxl, mxh, f1, g1, v1, g2, z1l, z1h, z2l, z2h, q0, va, vv, rs, xp):
    iz, ix = lax.axis_index("gz"), lax.axis_index("xy")
    k = spread(1)
    base = 1.0 + 6.0 * k
    sub5 = iota((5, 8, 512), 1)
    low = out_of_three(sub5, mxl[0:128, :].astype(F32)[0:120].reshape(5, 3, 8, 512), *HIGH_PACK).reshape(20, 8, 512)
    high = out_of_three(sub5, mxh[0:128, :].astype(F32)[0:120].reshape(5, 3, 8, 512), *LOW_PACK).reshape(20, 8, 512)
    sub = iota((20, 8, 512), 1)
    for p in (0, 1, 22, 23):
        f1[p] = jnp.zeros((24, 512), F32)
    f1[2:22, 0:8] = c1[:, 0:8] + jnp.where(sub < 2, low, 0.0)
    f1[2:22, 8:16] = c1[:, 8:16] + jnp.where(sub >= 6, high, 0.0)
    f1[2:22, 16:24] = c1[:, 16:24] + jnp.where(sub >= 4, low, high)
    low, high = [ref[128:224, :].astype(F32).reshape(12, 8, 512) for ref in (mxl, mxh)]
    sub12 = iota((12, 8, 512), 1)
    even = jnp.where(sub12 >= 4, shifted(low, 4, 1), high)
    odd = jnp.where(sub12 >= 4, low, shifted(high, 4, 1))
    q0[:, 0:16] = q_in[...]
    q0[:, 16:24] = jnp.stack([even, odd], axis=1).reshape(24, 8, 512)
    shape = (24, 24, 128)
    valid = inside(shape, 0, -4, None, iz, 16, nz) & inside(shape, 1, 0, 20, ix, 16, nx)
    for t in range(4):
        g = jnp.where(valid, OMEGA, 0.0) / (q0[:, :, lanes(t)] + base)
        g1[:, :, lanes(t)] = g
        va[:, :, lanes(t)] = g * f1[:, :, lanes(t)]
    for p in (0, 1, 24, 25):
        vv[p] = jnp.zeros((24, 512), F32)

    def sweep(p):
        for t, here, sums in plane(va, p):
            vv[p + 1, :, lanes(t)] = KEEP * here + g1[p, :, lanes(t)] * (f1[p, :, lanes(t)] + k * sums)

    loop(1, 23, sweep, 2)
    v1[...] = vv[1:25]

    def residual(p):
        for t, here, sums in plane(vv, p + 1):
            yield t, f1[p, :, lanes(t)] + k * sums - (q0[p, :, lanes(t)] + base) * here

    def coarse(m):
        for (t, first), (_, second) in zip(residual(2 * m), residual(2 * m + 1)):
            xp[t, m] = halve_rows((first + second)[0:16], rs, t)

    loop(0, 12, coarse)
    for t, tile in enumerate(halve_lanes(xp, 12, 8)):
        g2[:, lanes(t)] = tile.reshape(96, 128)
        for ref in (z1l, z1h):
            ref[240:288, lanes(t)] = tile[0:6].reshape(48, 128).astype(BF16)
            ref[240:288, lanes(2 + t)] = tile[6:12].reshape(48, 128).astype(BF16)
    for ref, corners, level0 in ((z1l, cnl, vzl), (z1h, cnh, vzh)):
        ref[288:320, :] = corners[:, 0:512]
        ref[320:352, :] = corners[:, 512:1024]
        ref[352:560, :] = level0[:, 0:512]
        ref[560:768, :] = level0[:, 512:1024]
    for ref, p in ((z1l, 2), (z1h, 18)):
        ref[0:144, :] = vv[p : p + 6].reshape(144, 512).astype(BF16)
        ref[144:240, :] = f1[p : p + 4].reshape(96, 512).astype(BF16)
    low, high = far_along_z(nz, iz, g2[0:48, :], g2[48:96, :])
    z2l[0:48, :] = low.astype(BF16)
    z2h[0:48, :] = high.astype(BF16)
    low, high = far_along_z(nz, iz, r2[0:32, :], r2[32:64, :])
    z2l[48:80, :] = low.astype(BF16)
    z2h[48:80, :] = high.astype(BF16)


def back_kernel(
    nz, nx, f_in, g1, v1, z1l, z1h, vxl_in, vxh_in, own2, n2l, n2h, m2l, m2h, q_own, v_in, g_in, s_in,
    out_hbm,
    f2, q2, h2, a2, b2, rs, xp, xpr, wa, w1, zsl, zsh, vb, ws,
    v2, gg, supply, fsl, fsh, out, f1, vxl, vxh, sems,
):
    iz, ix = lax.axis_index("gz"), lax.axis_index("xy")
    matrix = doubling()
    level0 = [
        pltpu.make_async_copy(src, dst, sems.at[i])
        for i, (src, dst) in enumerate(((v_in, v2), (g_in, gg), (s_in, supply)))
    ]
    for copy in level0:
        copy.start()

    f1[...] = f_in[...]
    wa[...] = v1[...]
    for ref, p in ((z1l, 1), (z1h, 17)):
        wa[p : p + 6] = wa[p : p + 6] + ref[0:144, :].astype(F32).reshape(6, 24, 512)
        f1[p + 1 : p + 5] = f1[p + 1 : p + 5] + ref[144:240, :].astype(F32).reshape(4, 24, 512)

    f2[:, 0:8, :] = own2[...]
    f2[:, 8:16, :] = n2h[0:256, :].astype(F32).reshape(32, 8, 256)
    f2[:, 16:24, :] = far_tile(m2l[0:128, :].astype(F32), m2h[0:128, :].astype(F32))
    f2[:, 24:32, :] = n2l[0:256, :].astype(F32).reshape(32, 8, 256)
    q2[:, 0:8, :] = q_own[...]
    q2[:, 16:24, :] = far_tile(m2l[128:256, :].astype(F32), m2h[128:256, :].astype(F32))
    for ref, rows in ((vxh_in, slice(8, 16)), (vxl_in, slice(24, 32))):
        for n in range(3):
            q2[8 * n + 4 : 8 * n + 12, rows, :] = ref[176:240, n * 256 : n * 256 + 256].astype(F32).reshape(8, 8, 256)
    for ref, rows in ((n2h, slice(8, 16)), (n2l, slice(24, 32))):
        outer = ref[256:320, :].astype(F32).reshape(8, 8, 256)
        q2[0:4, rows, :] = outer[0:4]
        q2[28:32, rows, :] = outer[4:8]

    k = spread(2)
    base = 1.0 + 6.0 * k
    shape = (32, 32, 128)
    valid = inside(shape, 0, -12, None, iz, 8, nz) & inside(shape, 1, 0, 20, ix, 8, nx)
    for t in range(2):
        g = jnp.where(valid, OMEGA, 0.0) / (q2[:, :, lanes(t)] + base)
        h2[:, :, lanes(t)] = g
        a2[:, :, lanes(t)] = g * f2[:, :, lanes(t)]
    b2[0] = a2[0]
    b2[31] = a2[31]

    def sweep2(src, dst):
        def body(p):
            for t, here, sums in plane(src, p):
                dst[p, :, lanes(t)] = KEEP * here + h2[p, :, lanes(t)] * (f2[p, :, lanes(t)] + k * sums)

        return body

    loop(1, 31, sweep2(a2, b2), 2)

    def coarse(m):
        total, rates = [0.0, 0.0], [0.0, 0.0]
        for j in range(2):
            p = 2 * m + j
            for t, here, sums in plane(b2, p):
                r = f2[p, :, lanes(t)] + k * sums - (q2[p, :, lanes(t)] + base) * here
                total[t] = total[t] + r
                rates[t] = rates[t] + q2[p, :, lanes(t)]
        for t in range(2):
            xp[t, m] = halve_rows(total[t], rs, t)
            xpr[t, m] = halve_rows(rates[t], rs, t + 2)

    for t in range(2):
        for m in (0, 15):
            xp[t, m] = jnp.zeros((16, 128), F32)
            xpr[t, m] = jnp.zeros((16, 128), F32)
    loop(1, 15, coarse)

    shape = (16, 16, 128)
    valid = inside(shape, 0, -6, None, iz, 4, nz) & inside(shape, 1, 0, 10, ix, 4, nx)
    k3 = spread(3)
    (source,) = halve_lanes(xp, 16, 16)
    (rates,) = halve_lanes(xpr, 16, 16)
    g = jnp.where(valid, OMEGA, 0.0) / (rates + (1.0 + 6.0 * k3))
    v = g * source
    lane = iota(shape, 2)
    for repeat in range(3):
        edge = jnp.zeros((1, 16, 128), F32)
        sums = jnp.concatenate([v[1:], edge], axis=0) + jnp.concatenate([edge, v[:-1]], axis=0)
        sums = sums + shifted(v, 1, 1) + shifted(v, -1, 1)
        sums = sums + jnp.where(lane == 0, 0.0, shifted(v, 1, 2)) + jnp.where(lane == 127, 0.0, shifted(v, -1, 2))
        v = KEEP * v + g * (source + k3 * sums)

    wide = split_dot(v[4:12].reshape(128, 128), matrix).reshape(8, 16, 256)
    for m in range(8):
        for t in range(2):
            part = wide[m, :, lanes(t)]
            rs[t, pl.ds(0, 16, stride=2), :] = part
            rs[t, pl.ds(1, 16, stride=2), :] = part
            for j in range(2):
                p = 8 + 2 * m + j
                b2[p, :, lanes(t)] = b2[p, :, lanes(t)] + rs[t, 0:32, :]
    loop(9, 23, sweep2(b2, a2), 2)
    loop(10, 22, sweep2(a2, b2), 2)

    w = b2[10:22]
    near, far = w[:, 8:16], w[:, 24:32]
    near = jnp.where(iota((12, 8, 256), 1) < 2, near, shifted(far, 4, 1))
    w = jnp.concatenate([w[:, 0:8], near], axis=1).reshape(192, 256)
    wide = [split_dot(w[:, lanes(t)], matrix) for t in range(2)]
    wide = jnp.concatenate(wide, axis=1).reshape(12, 16, 512)
    for m in range(12):
        for t in range(4):
            part = wide[m, :, lanes(t)]
            rs[t, pl.ds(0, 16, stride=2), :] = part
            rs[t, pl.ds(1, 16, stride=2), :] = part
            for j in range(2):
                p = 2 * m + j
                wa[p, :, lanes(t)] = wa[p, :, lanes(t)] + rs[t, 0:24, :]
    k1 = spread(1)

    def sweep1(src, dst):
        def body(p):
            for t, here, sums in plane(src, p):
                dst[p, :, lanes(t)] = KEEP * here + g1[p, :, lanes(t)] * (f1[p, :, lanes(t)] + k1 * sums)

        return body

    loop(2, 22, sweep1(wa, w1), 2)
    loop(3, 21, sweep1(w1, wa), 2)

    sub = iota((18, 8, 128), 1)
    for t in range(4):
        halo = wa[3:21, 16:24, lanes(t)]
        halo = jnp.where(sub < 2, halo, shifted(halo, 4, 1))
        w = jnp.concatenate([wa[3:21, 0:16, lanes(t)], halo], axis=1)
        ws[:, :, t * 256 : t * 256 + 256] = split_dot(w.reshape(432, 128), matrix).reshape(18, 24, 256)

    for copy in level0:
        copy.wait()
    for ref, message in ((zsl, z1l), (zsh, z1h)):
        ref[:, 0:512] = message[352:560, :].astype(F32)
        ref[:, 512:1024] = message[560:768, :].astype(F32)
    for ref, src, near in ((vxl, vxl_in, n2l), (vxh, vxh_in, n2h)):
        ref[...] = src[0:176, :]
        for n in range(4):
            cols = slice(256 * n, 256 * n + 256)
            for i, rows in enumerate((slice(0, 16), slice(128, 144))):
                corner = near[320 + 32 * n + 16 * i : 336 + 32 * n + 16 * i, :].astype(F32)
                ref[rows, cols] = (src[rows, cols].astype(F32) + corner).astype(BF16)
    for i in range(4):
        v2[i] = v2[i] + zsl[40 * i : 40 * i + 40, :]
        v2[32 + i] = v2[32 + i] + zsh[40 * i : 40 * i + 40, :]

    s8 = iota((8, 128), 0)

    outer = outer_rows(s8)

    def correct(i):
        rows = pl.ds(pl.multiple_of(16 * i, 16), 16)
        for t in range(NT):
            low = vxl[rows, lanes(t)].astype(F32)
            high = vxh[rows, lanes(t)].astype(F32)
            for n in range(2):
                part = ws[2 * i + n, :, lanes(t)]
                rs[t, pl.ds(0, 24, stride=2), :] = part
                rs[t, pl.ds(1, 24, stride=2), :] = part
                for j in range(2):
                    p = 4 * i + 2 * n + j
                    lo, hi = low[8 * n : 8 * n + 8], high[8 * n : 8 * n + 8]
                    if j:
                        lo, hi = shifted(lo, 4, 0), shifted(hi, 4, 0)
                    v2[p, 0:8, lanes(t)] = v2[p, 0:8, lanes(t)] + rs[t, 0:8, :] + jnp.where(s8 < 2, lo, 0.0)
                    v2[p, 8:24, lanes(t)] = v2[p, 8:24, lanes(t)] + rs[t, 8:24, :]
                    v2[p, 24:32, lanes(t)] = v2[p, 24:32, lanes(t)] + rs[t, 24:32, :] + jnp.where(s8 >= 6, hi, 0.0)
                    extra = jnp.where(outer, jnp.where(s8 >= 4, lo, hi), 0.0)
                    v2[p, 32:40, lanes(t)] = v2[p, 32:40, lanes(t)] + rs[t, 32:40, :] + extra

    loop(0, 9, correct)
    k0 = spread(0)

    def first(i):
        rows = pl.ds(pl.multiple_of(16 * i + 144, 16), 16)
        for t in range(NT):
            fsl[:, lanes(t)] = vxl[rows, lanes(t)].astype(F32)
            fsh[:, lanes(t)] = vxh[rows, lanes(t)].astype(F32)

        def step(j):
            z = 16 * i + j
            start = pl.multiple_of((j // 8) * 8, 8)
            turn = lax.rem(j, 8)
            for t, here, sums in plane(v2, z + 2):
                lo = pltpu.roll(fsl[pl.ds(start, 8), lanes(t)], 7 - turn, 0)
                hi = pltpu.roll(fsh[pl.ds(start, 8), lanes(t)], lax.rem(8 - turn, 8), 0)
                f = jnp.where(s8 == 7, lo, jnp.where(s8 == 0, hi, 0.0))
                g = gg[z + 2, :, lanes(t)]
                inner = k0 * sums
                vb[z + 1, 0:32, lanes(t)] = KEEP * here[0:32] + g[0:32] * (supply[z, :, lanes(t)] + inner[0:32])
                vb[z + 1, 32:40, lanes(t)] = KEEP * here[32:40] + g[32:40] * (f + inner[32:40])

        loop(0, 16, step, 2)

    loop(0, 2, first)
    for p, ref in ((1, zsl), (34, zsh)):
        for t, here, sums in plane(v2, p):
            g = gg[p, :, lanes(t)]
            vb[p - 1, :, lanes(t)] = KEEP * here + g * (ref[160:200, lanes(t)] + k0 * sums)

    def second(z):
        for t, here, sums in plane(vb, z + 1):
            g = gg[z + 2, 0:32, lanes(t)]
            out[z, :, lanes(t)] = KEEP * here[0:32] + g * (supply[z, :, lanes(t)] + k0 * sums[0:32])

    stores = []
    for i in range(4):
        part = pl.ds(8 * i, 8)
        loop(8 * i, 8 * i + 8, second, 2)
        stores.append(pltpu.make_async_copy(out.at[part], out_hbm.at[part], sems.at[3 + i]))
        stores[i].start()
    for copy in stores:
        copy.wait()


VMEM = pl.BlockSpec(memory_space=pltpu.VMEM)
SMEM = pl.BlockSpec(memory_space=pltpu.SMEM)
ANY = pl.BlockSpec(memory_space=pl.ANY)


def call(kernel, outs, scratch, smem, args, out_specs=None, in_hbm=0):
    moved = sum(a.size * a.dtype.itemsize for a in list(args) + list(outs))
    return pl.pallas_call(
        kernel,
        out_shape=tuple(outs),
        in_specs=[SMEM] * smem + [VMEM] * (len(args) - smem - in_hbm) + [ANY] * in_hbm,
        out_specs=tuple(out_specs or [VMEM] * len(outs)),
        scratch_shapes=scratch,
        compiler_params=pltpu.CompilerParams(vmem_limit_bytes=58 * 2**20),
        cost_estimate=pl.CostEstimate(flops=20 * moved, bytes_accessed=moved, transcendentals=0),
    )(*args)


def shaped(shape, dtype=F32):
    return jax.ShapeDtypeStruct(shape, dtype)


def both_ways(to_low, to_high, axis, distance=1):
    count = lax.axis_size(axis)
    up = [(i, i + distance) for i in range(count - distance)]
    down = [(j, i) for i, j in up]
    return lax.ppermute(to_high, axis, up), lax.ppermute(to_low, axis, down)


def two_away(to_low, to_high):
    count = lax.axis_size("gz")
    if count != 4:
        return both_ways(to_low, to_high, "gz", 2)
    came = lax.ppermute(to_low, "gz", [(i, (i + 2) % 4) for i in range(4)])
    return came, came


def shards(density, uptake, brick_values, brick_ids, slot_counts):
    nz, nx = lax.axis_size("gz"), lax.axis_size("xy")
    scratch = pltpu.VMEM
    half = lambda *shape: shaped(shape, BF16)
    full = lambda *shape: shaped(shape, F32)

    own, r1, r2, zl, zh, uxl, uxh = call(
        lambda *refs: first_kernel(2 * nx, *refs),
        [
            half(BLOCK, 384), full(16, 16, 512), full(64, 256), half(Z_ROWS, 384), half(Z_ROWS, 384),
            half(64, 1024), half(64, 1024),
        ],
        [
            scratch((8, 32, 128), F32), scratch((8, 16, 16, 128), F32), scratch((4, 16, 128), F32),
            scratch((4, 8, 8, 128), F32), scratch((SLOTS, BRICK), F32), scratch((C, C, 1024), F32),
            pltpu.SemaphoreType.DMA((1,)),
        ],
        2,
        (brick_ids, slot_counts, brick_values, uptake),
        in_hbm=1,
    )
    zl, zh = both_ways(zl, zh, "gz")
    q1, xl, xh = call(
        first_x_kernel,
        [full(24, 16, 512), half(X_ROWS, 384), half(X_ROWS, 384)],
        [],
        0,
        (own, r1, uxl, uxh, zl, zh),
    )
    s0, g0, v1, edge = call(
        lambda *refs: own_kernel(nz, *refs),
        [full(C, C, 1024), full(36, C, 1024), full(34, C, 1024), full(C, 8, 1024)],
        [
            scratch((C, C, 1024), F32),
            scratch((C, C, 1024), F32),
            scratch((C, C, 1024), F32),
            scratch((36, C, 1024), F32),
            scratch((34, C, 1024), F32),
            scratch((C, 8, 1024), F32),
            scratch((42, 40, 1024), F32),
            scratch((384, 1024), BF16),
            scratch((1024, 384), BF16),
            pltpu.SemaphoreType.DMA((6,)),
        ],
        0,
        (own, zl, zh, density, uptake),
        [ANY] * 4,
        in_hbm=2,
    )
    xl, xh = both_ways(xl, xh, "xy")

    c1, mxl, mxh, v2, gg, supply = call(
        lambda *refs: pre_kernel(nz, nx, *refs),
        [
            full(20, 24, 512),
            half(224, 512),
            half(224, 512),
            full(36, 40, 1024),
            full(36, 40, 1024),
            full(C, C, 1024),
        ],
        [
            scratch((42, 40, 1024), F32),
            scratch((42, 40, 1024), F32),
            scratch((C, C, 1024), F32),
            scratch((C, C, 1024), F32),
            scratch((36, 8, 1024), F32),
            scratch((36, 40, 1024), F32),
            scratch((C, 8, 1024), F32),
            scratch((768, 1024), BF16),
            scratch((1024, 768), BF16),
            scratch((8, 40, 128), F32),
            scratch((8, 20, 24, 128), F32),
            scratch((72, 1024), F32),
            scratch((72, 1024), F32),
            pltpu.SemaphoreType.DMA((8,)),
        ],
        0,
        (xl, xh, zl, zh, q1, s0, g0, v1, edge, uptake),
        [VMEM] * 3 + [ANY] * 3,
        in_hbm=5,
    )
    mxl, mxh = both_ways(mxl, mxh, "xy")
    vzl, vzh, pxl, pxh, cnl, cnh = call(
        edges_kernel,
        [
            half(208, 1024), half(208, 1024), half(240, 1024), half(240, 1024), half(32, 1024), half(32, 1024),
        ],
        [
            scratch((36, 24, 1024), F32), scratch((2, 4, 40, 1024), F32), scratch((C, 16, 1024), F32),
            scratch((2, C, 1024), F32), pltpu.SemaphoreType.DMA((8,)),
        ],
        0,
        (r2, zl, zh, v2, supply),
        in_hbm=2,
    )
    pxl, pxh, mxl, mxh = lax.optimization_barrier((pxl, pxh, mxl, mxh))
    vxl, vxh = both_ways(pxl, pxh, "xy")
    f1, g1, v1, g2, z1l, z1h, z2l, z2h = call(
        lambda *refs: middle_kernel(nz, nx, *refs),
        [
            full(24, 24, 512), full(24, 24, 512), full(24, 24, 512), full(96, 256),
            half(768, 512), half(768, 512), half(FAR, 256), half(FAR, 256),
        ],
        [
            scratch((24, 24, 512), F32), scratch((24, 24, 512), F32), scratch((26, 24, 512), F32),
            scratch((4, 16, 128), F32), scratch((4, 12, 8, 128), F32),
        ],
        0,
        (c1, q1, r2, cnl, cnh, vzl, vzh, mxl, mxh),
    )
    z1l, z1h = both_ways(z1l, z1h, "gz")
    z2l, z2h = two_away(z2l, z2h)
    own2, q2, nl, nh, fl, fh = call(
        lambda *refs: source_window_kernel(nz, *refs),
        [full(32, 8, 256), full(32, 8, 256), half(448, 256), half(448, 256), half(256, 256), half(256, 256)],
        [],
        0,
        (g2, z1l, z1h, z2l, z2h, r2, zl, zh),
    )
    nl, nh = both_ways(nl, nh, "xy")
    fl, fh = both_ways(fl, fh, "xy", 2)
    window2 = scratch((32, 32, 256), F32)
    window1 = scratch((24, 24, 512), F32)
    (concentration,) = call(
        lambda *refs: back_kernel(nz, nx, *refs),
        [full(C, C, 1024)],
        [
            window2, window2, window2, window2, window2,
            scratch((8, 48, 128), F32),
            scratch((2, 16, 16, 128), F32),
            scratch((2, 16, 16, 128), F32),
            window1, window1,
            scratch((208, 1024), F32),
            scratch((208, 1024), F32),
            scratch((34, 40, 1024), F32),
            scratch((18, 24, 1024), F32),
            scratch((36, 40, 1024), F32),
            scratch((36, 40, 1024), F32),
            scratch((C, C, 1024), F32),
            scratch((16, 1024), F32),
            scratch((16, 1024), F32),
            scratch((C, C, 1024), F32),
            window1,
            scratch((176, 1024), BF16),
            scratch((176, 1024), BF16),
            pltpu.SemaphoreType.DMA((7,)),
        ],
        0,
        (f1, g1, v1, z1l, z1h, vxl, vxh, own2, nl, nh, fl, fh, q2, v2, gg, supply),
        [ANY],
        in_hbm=3,
    )
    return supply, concentration


def solution(mesh):
    return jax.shard_map(
        shards,
        mesh=mesh,
        in_specs=(
            P("gz", "xy", None),
            P("gz", "xy", None),
            P(("gz", "xy"), None),
            P(("gz", "xy")),
            P(("gz", "xy"), None),
        ),
        out_specs=(P("gz", "xy", None), P("gz", "xy", None)),
        check_vma=False,
    )
```

```python
import jax
import jax.numpy as jnp
from jax import lax
from jax.experimental import pallas as pl
from jax.experimental.pallas import tpu as pltpu
from jax.sharding import PartitionSpec as P

EDGE = 16
CAP = 8
BRICK = 4096
SLOTS = 72
KAPPA = 32.0
OMEGA = 0.8
KEEP = 1.0 - OMEGA

C = 32
NT = 8
F32 = jnp.float32
BF16 = jnp.bfloat16


def spread(level):
    return KAPPA / 4.0**level


def shifted(values, distance, axis):
    return pltpu.roll(values, distance % values.shape[axis], axis)


def iota(shape, dim):
    return lax.broadcasted_iota(jnp.int32, shape, dim)


def lanes(t):
    return slice(t * 128, (t + 1) * 128)


def plane(ref, p):
    count = ref.shape[2] // 128
    rows = ref.shape[1]
    lane = iota((rows, 128), 1)
    before, here = None, ref[p, :, lanes(0)]
    for t in range(count):
        after = ref[p, :, lanes(t + 1)] if t + 1 < count else None
        low = jnp.where(lane == 127, 0.0 if before is None else before, here)
        high = jnp.where(lane == 0, 0.0 if after is None else after, here)
        sums = shifted(low, 1, 1) + shifted(high, -1, 1)
        sums = sums + (shifted(here, 1, 0) + shifted(here, -1, 0))
        sums = sums + (ref[p - 1, :, lanes(t)] + ref[p + 1, :, lanes(t)])
        yield t, here, sums
        before, here = here, after


def loop(start, stop, body, unroll=1):
    def step(i, carry):
        body(i)
        return carry

    lax.fori_loop(start, stop, step, 0, unroll=unroll)


def split_dot(a, b):
    high = a.astype(BF16)
    low = (a - high.astype(F32)).astype(BF16)
    return jnp.dot(high, b, preferred_element_type=F32) + jnp.dot(low, b, preferred_element_type=F32)


def pooling():
    return jnp.where(iota((256, 128), 0) // 2 == iota((256, 128), 1), 0.125, 0.0).astype(BF16)


def doubling():
    return jnp.where(iota((128, 256), 1) // 2 == iota((128, 256), 0), 1.0, 0.0).astype(BF16)


def halve_rows(values, rs, t):
    rows = values.shape[0]
    rs[t, 0:rows, :] = values
    return rs[t, pl.ds(0, rows // 2, stride=2), :] + rs[t, pl.ds(1, rows // 2, stride=2), :]


def halve_lanes(xp, planes, rows):
    matrix = pooling()
    tiles = []
    for t in range(0, xp.shape[0], 2):
        pair = jnp.concatenate([xp[t].reshape(planes * rows, 128), xp[t + 1].reshape(planes * rows, 128)], axis=1)
        tiles.append(split_dot(pair, matrix).reshape(planes, rows, 128))
    return tiles


def inside(shape, dim, first, wrap, index, size, count):
    place = iota(shape, dim) + first
    if wrap is not None:
        place = jnp.where(place < wrap, place, place - shape[dim])
    place = place + index * size
    return (place >= 0) & (place < count * size)


BLOCK = 272
X_ROWS = BLOCK + 3 * 64 + 2 * 64
Z_ROWS = BLOCK + 5 * 64


def uptake_part(t):
    return slice(BLOCK + 64 * (t // 3), BLOCK + 64 * (t // 3) + 64), lanes(t % 3)


def rates2_part(n, t):
    k = 3 * t + n
    first = BLOCK + 3 * 64 + 64 * (k % 2)
    return slice(first, first + 64), lanes(k // 2)


def transposed_bricks(bricks_x, ids, counts, bricks, xs, targets):
    xs[...] = bricks[...].astype(F32)
    row = iota((1, 8, 128), 1)
    group = iota((1, 8, 128), 2) // 16
    group16 = iota((16, 128), 1) // 16
    per_y = 64

    def block(j, out, part):
        start = pl.multiple_of(j * 8, 8)
        x = jnp.stack([xs[pl.ds(start, 8), lanes(k)] for k in range(32)])
        for s in (4, 2, 1):
            up = shifted(shifted(x, -s, 1), 16 * s, 2)
            down = shifted(shifted(x, s, 1), -16 * s, 2)
            row_bit = (row // s) % 2
            group_bit = (group // s) % 2
            x = jnp.where(row_bit == group_bit, x, jnp.where(row_bit == 0, up, down))
        x = jnp.where(group < counts[0, j], x, 0.0)
        out[0:256, part] = x.reshape(256, 128).astype(BF16)
        names = jnp.zeros((16, 128), jnp.int32)
        for e in range(CAP):
            number = ids[j * 8 + e]
            by = lax.rem(number, per_y)
            rest = lax.div(number, per_y)
            bx = lax.rem(rest, 2)
            bz = lax.rem(lax.div(rest, bricks_x), 2)
            names = jnp.where(group16 == e, (bz * 2 + bx) * per_y + by, names)
        out[256:272, part] = names.astype(F32).astype(BF16)

    for i, out in enumerate(targets):
        for d in range(3):
            block(3 * i + d, out, lanes(d))


def first_kernel(bricks_x, ids, counts, bricks, uptake_in, own, r1, r2, zl, zh, xl, xh, rs, xp, rs1, xp1, xs, uptake, sems):
    load = pltpu.make_async_copy(uptake_in, uptake, sems.at[0])
    load.start()
    transposed_bricks(bricks_x, ids, counts, bricks, xs, (zl, own, zh))
    load.wait()

    def pair(m):
        for t in range(NT):
            both = uptake[2 * m, :, lanes(t)] + uptake[2 * m + 1, :, lanes(t)]
            xp[t, m] = halve_rows(both, rs, t)

    loop(0, 16, pair)
    for t, tile in enumerate(halve_lanes(xp, 16, 16)):
        r1[:, :, lanes(t)] = tile

    def pair1(m):
        for t in range(4):
            both = r1[2 * m, :, lanes(t)] + r1[2 * m + 1, :, lanes(t)]
            xp1[t, m] = halve_rows(both, rs1, t)

    loop(0, 8, pair1)
    for t, tile in enumerate(halve_lanes(xp1, 8, 8)):
        r2[:, lanes(t)] = tile.reshape(64, 128)
    for ref, u, r in ((zl, slice(0, 2), slice(0, 4)), (zh, slice(30, 32), slice(12, 16))):
        for t in range(8):
            ref[uptake_part(t)] = uptake[u, :, lanes(t)].reshape(64, 128).astype(BF16)
        for t in range(4):
            ref[uptake_part(8 + t)] = r1[r, :, lanes(t)].reshape(64, 128).astype(BF16)
        for t in range(2):
            ref[uptake_part(12 + t)] = r2[:, lanes(t)].astype(BF16)
        ref[uptake_part(14)] = jnp.zeros((64, 128), BF16)

    sub = iota((8, 1024), 0)

    def columns(i):
        lows, highs = [], []
        for j in range(2):
            low, high = jnp.zeros((8, 1024), F32), jnp.zeros((8, 1024), F32)
            for n in range(4):
                z = 8 * i + 4 * j + n
                low = jnp.where(sub // 2 == n, shifted(uptake[z, 0:8, :], 2 * n, 0), low)
                high = jnp.where(sub // 2 == n, shifted(uptake[z, 24:32, :], 2 * n + 2, 0), high)
            lows.append(low)
            highs.append(high)
        rows = pl.ds(pl.multiple_of(16 * i, 16), 16)
        xl[rows, :] = jnp.concatenate(lows, axis=0).astype(BF16)
        xh[rows, :] = jnp.concatenate(highs, axis=0).astype(BF16)

    loop(0, 4, columns)


def far_along_z(nz, iz, to_low, to_high):
    if nz != 4:
        return to_low, to_high
    one = jnp.where(iz < 2, to_high, to_low)
    return one, one


def halves(sub, first, second):
    return jnp.where(sub < 4, first, shifted(second, 4, 1))


def uppers(sub, first, second):
    return jnp.where(sub < 4, shifted(first, 4, 1), second)


def far_messages(window):
    planes, _, width = window.shape
    pairs = window.reshape(planes // 2, 2, 8, width)
    sub = iota((planes // 2, 8, width), 1)
    size = (planes * 4, width)
    return halves(sub, pairs[:, 0], pairs[:, 1]).reshape(size), uppers(sub, pairs[:, 0], pairs[:, 1]).reshape(size)


def far_tile(from_low, from_high):
    width = from_low.shape[-1]
    low, high = from_low.reshape(-1, 8, width), from_high.reshape(-1, 8, width)
    sub = iota(low.shape, 1)
    even = jnp.where(sub < 4, high, shifted(low, 4, 1))
    odd = jnp.where(sub < 4, shifted(high, 4, 1), low)
    return jnp.stack([even, odd], axis=1).reshape(-1, 8, width)


def first_x_kernel(own, r1, r2, uxl, uxh, zl, zh, q1, xl, xh):
    q1[4:20] = r1[...]
    for ref, planes in ((zl, slice(0, 4)), (zh, slice(20, 24))):
        for t in range(4):
            q1[planes, :, lanes(t)] = ref[uptake_part(8 + t)].astype(F32).reshape(4, 16, 128)
    for ref, d in ((xl, 0), (xh, 2)):
        for n, src in enumerate((own, zl, zh)):
            ref[0:BLOCK, lanes(n)] = src[0:BLOCK, lanes(d)]
        for t in range(2):
            ref[rates2_part(0, t)] = zl[uptake_part(12 + t)]
            ref[rates2_part(1, t)] = r2[:, lanes(t)].astype(BF16)
            ref[rates2_part(2, t)] = zh[uptake_part(12 + t)]
    sub = iota((8, 128), 0)
    lows, highs = [], []
    for t in range(8):
        xl[uptake_part(t)] = uxl[:, lanes(t)]
        xh[uptake_part(t)] = uxh[:, lanes(t)]
        both = [ref[uptake_part(t)].astype(F32) for ref in (zl, zh)]
        planes = [both[0][0:32], both[0][32:64], both[1][0:32], both[1][32:64]]
        to_low, to_high = jnp.zeros((8, 128), F32), jnp.zeros((8, 128), F32)
        for n, p in enumerate(planes):
            here = sub // 2 == n
            to_low = jnp.where(here, shifted(p[0:8], 2 * n, 0), to_low)
            to_high = jnp.where(here, shifted(p[24:32], 2 * n + 2, 0), to_high)
        lows.append(to_low)
        highs.append(to_high)
    xl[uptake_part(8)] = jnp.concatenate(lows, axis=0).astype(BF16)
    xh[uptake_part(8)] = jnp.concatenate(highs, axis=0).astype(BF16)


FAR = 80


def source_window_kernel(nz, own, zl, zh, z2l, z2h, r2, firstl, firsth, f2, q2, nl, nh, fl, fh):
    iz = lax.axis_index("gz")
    zeros = jnp.zeros((10, 8, 256), F32)
    f2[0:10] = zeros
    f2[22:32] = zeros
    f2[10:22] = own[...].reshape(12, 8, 256)
    for ref, planes in ((zl, slice(2, 14)), (zh, slice(18, 30))):
        part = jnp.concatenate([ref[240:288, 0:256], ref[240:288, 256:512]], axis=0).astype(F32)
        f2[planes] = f2[planes] + part.reshape(12, 8, 256)
    for ref, planes, exists in ((z2l, slice(0, 6), iz >= 2), (z2h, slice(26, 32), iz < nz - 2)):
        part = jnp.where(exists, ref[0:48, :].astype(F32), 0.0)
        f2[planes] = f2[planes] + part.reshape(6, 8, 256)
    q2[0:4] = z2l[48:80, :].astype(F32).reshape(4, 8, 256)
    q2[28:32] = z2h[48:80, :].astype(F32).reshape(4, 8, 256)
    q2[12:20] = r2[...].reshape(8, 8, 256)
    for ref, planes in ((firstl, slice(4, 12)), (firsth, slice(20, 28))):
        for t in range(2):
            q2[planes, :, lanes(t)] = ref[uptake_part(12 + t)].astype(F32).reshape(8, 8, 128)
    for i, near in enumerate((nl, nh)):
        near[0:256, :] = f2[...].reshape(256, 256).astype(BF16)
        near[256:288, :] = z2l[48:80, :]
        near[288:320, :] = z2h[48:80, :]
        for n in range(4):
            rows = slice(288 + 32 * (n // 2) + 16 * i, 304 + 32 * (n // 2) + 16 * i)
            cols = slice(256 * (n % 2), 256 * (n % 2) + 256)
            near[320 + 32 * n : 336 + 32 * n, :] = zl[rows, cols]
            near[336 + 32 * n : 352 + 32 * n, :] = zh[rows, cols]
    for i, ref in enumerate((f2, q2)):
        to_low, to_high = far_messages(ref[...])
        fl[128 * i : 128 * i + 128, :] = to_low.astype(BF16)
        fh[128 * i : 128 * i + 128, :] = to_high.astype(BF16)


O = 5
Q = 2
BASE = 1.0 + 6.0 * KAPPA


def scatter(blocks, hot, left):
    lane = iota((128, 128), 1)
    for i, (ref, part) in enumerate(blocks):
        name = ref[256:272, part].astype(F32).astype(jnp.int32)[0:1]
        tiles = lax.shift_right_logical(name, 6)
        at_y = (name & 63) * 16 + (lane[0:1] & 15)
        at_y = jnp.broadcast_to(at_y.astype(F32), (128, 128)).T.astype(jnp.int32)
        for t in range(NT):
            hot[128 * i : 128 * i + 128, lanes(t)] = jnp.where(at_y == lane + 128 * t, 1.0, 0.0).astype(BF16)
        values = ref[0:256, part].astype(F32)
        for tile in range(4):
            left[256 * tile : 256 * tile + 256, lanes(i)] = jnp.where(tiles == tile, values, 0.0).astype(BF16)
    for n in range(4):
        cols = slice(n * 256, (n + 1) * 256)
        sums = jnp.dot(left[...], hot[:, cols], preferred_element_type=F32)
        for tile in range(4):
            bz, bx = tile // 2, tile % 2
            yield 16 * bz, slice(16 * bx, 16 * bx + 16), cols, sums[256 * tile : 256 * tile + 256].reshape(16, 16, 256)


def sweep(src, dst, source, gg, z, sourced):
    for t, here, sums in plane(src, z + O):
        inner = KAPPA * sums
        g = gg[z + Q, :, lanes(t)]
        if sourced:
            body = inner[0:32] + source[z, :, lanes(t)]
            dst[z + O, 0:32, lanes(t)] = KEEP * here[0:32] + g[0:32] * body
            dst[z + O, 32:40, lanes(t)] = KEEP * here[32:40] + g[32:40] * inner[32:40]
        else:
            dst[z + O, :, lanes(t)] = KEEP * here + g * inner


def own_kernel(
    nz, own, zl, zh, density, uptake, s_out, g_out, v_out, edge_out,
    dens, upt, s0, g0, v1, edge, va, hot, left, sems,
):
    iz = lax.axis_index("gz")
    loads = [pltpu.make_async_copy(density, dens, sems.at[0]), pltpu.make_async_copy(uptake, upt, sems.at[1])]
    stores = [
        pltpu.make_async_copy(src, dst, sems.at[2 + i])
        for i, (src, dst) in enumerate(((s0, s_out), (g0, g_out), (v1, v_out), (edge, edge_out)))
    ]
    for copy in loads:
        copy.start()
    for p in (3, 4, 37, 38):
        va[p] = jnp.zeros((40, 1024), F32)
    for n in range(4):
        ref, valid = (zl, iz > 0) if n < 2 else (zh, iz < nz - 1)
        q = n if n < 2 else 32 + n
        rows = slice(32 * (n % 2), 32 * (n % 2) + 32)
        for t in range(NT):
            g0[q, :, lanes(t)] = jnp.where(valid, OMEGA, 0.0) / (ref[uptake_part(t)].astype(F32)[rows] + BASE)

    blocks = [(ref, lanes(1)) for ref in (own, zl, zh)]
    waiting = list(loads[0:1])
    for z, rows, cols, sums in scatter(blocks, hot, left):
        while waiting:
            waiting.pop().wait()
        planes = slice(z, z + 16)
        s0[planes, rows, cols] = dens[planes, rows, cols] + sums
    stores[0].start()
    loads[1].wait()

    def own_plane(z):
        va[z + O, 0:32, :] = dens[z]
        va[z + O, 32:40, :] = jnp.zeros((8, 1024), F32)
        g0[z + Q] = OMEGA / (upt[z] + BASE)

    loop(0, C, own_plane)
    stores[1].start()

    def first(z):
        for t, here, sums in plane(va, z + O):
            inner = KAPPA * sums
            body = inner[0:32] + s0[z, :, lanes(t)]
            v1[z + 1, :, lanes(t)] = KEEP * here[0:32] + g0[z + Q, :, lanes(t)] * body
            edge[z, :, lanes(t)] = inner[32:40]

    loop(0, C, first, 2)
    for z in (-1, C):
        for t in range(NT):
            near = va[z + O + (1 if z < 0 else -1), 0:32, lanes(t)]
            v1[z + 1, :, lanes(t)] = g0[z + Q, :, lanes(t)] * (KAPPA * near)
    for copy in stores[2:]:
        copy.start()
    for copy in stores:
        copy.wait()


def pre_kernel(
    nz, nx, xl, xh, zl, zh, q1, s0, g0, v1, edge_in, uptake,
    c1, mxl, mxh, v_out, g_out, s_out,
    va, vb, supply, upt, dh, gg, edge, hot, left, rs, xp, usl, ush, sems,
):
    iz, ix = lax.axis_index("gz"), lax.axis_index("xy")
    k = KAPPA
    loads = [
        pltpu.make_async_copy(src, dst, sems.at[i])
        for i, (src, dst) in enumerate(
            (
                (s0, supply),
                (v1, vb.at[4:38, 0:32, :]),
                (g0, gg.at[:, 0:32, :]),
                (edge_in, edge),
                (uptake, upt),
            )
        )
    ]
    for copy in loads:
        copy.start()

    for p in (1, 2, 39, 40):
        va[p] = jnp.zeros((40, 1024), F32)
    for p in (2, 3, 38, 39):
        vb[p] = jnp.zeros((40, 1024), F32)
    for p in (4, 37):
        vb[p, 32:40, :] = jnp.zeros((8, 1024), F32)

    sub8 = iota((8, 1024), 0)
    for t in range(NT):
        usl[0:64, lanes(t)] = xl[uptake_part(t)].astype(F32)
        ush[0:64, lanes(t)] = xh[uptake_part(t)].astype(F32)
        usl[64:72, lanes(t)] = xl[uptake_part(8)].astype(F32)[8 * t : 8 * t + 8]
        ush[64:72, lanes(t)] = xh[uptake_part(8)].astype(F32)[8 * t : 8 * t + 8]

    def set_halo(q, low, high, valid_z):
        gz = jnp.where(valid_z, OMEGA, 0.0)
        d = jnp.where(sub8 < 2, high, jnp.where(sub8 >= 6, low, 0.0)) + BASE
        dh[q] = d
        omega = jnp.where(sub8 < 2, jnp.where(ix < nx - 1, gz, 0.0), jnp.where(sub8 >= 6, jnp.where(ix > 0, gz, 0.0), 0.0))
        gg[q, 32:40, :] = omega / d

    def halos(i):
        rows = pl.ds(pl.multiple_of(8 * i, 8), 8)
        low, high = usl[rows, :], ush[rows, :]
        for n in range(4):
            set_halo(4 * i + n + Q, shifted(low, 6 - 2 * n, 0), shifted(high, -2 * n, 0), True)

    loop(0, C // 4, halos)
    low, high = usl[64:72, :], ush[64:72, :]
    for n in range(4):
        exists = iz > 0 if n < 2 else iz < nz - 1
        set_halo(n if n < 2 else 32 + n, shifted(low, 6 - 2 * n, 0), shifted(high, -2 * n, 0), exists)

    blocks = [(ref, lanes(n)) for ref in (xl, xh) for n in range(3)]
    waiting = list(loads[0:3])
    for z, rows, cols, sums in scatter(blocks, hot, left):
        while waiting:
            waiting.pop().wait()
        supply[z : z + 16, rows, cols] = supply[z : z + 16, rows, cols] + sums
        g = gg[z + Q : z + Q + 16, rows, cols]
        vb[z + O : z + O + 16, rows, cols] = vb[z + O : z + O + 16, rows, cols] + g * sums
    loads[3].wait()

    s_copy = pltpu.make_async_copy(supply, s_out, sems.at[7])
    s_copy.start()

    def edges(z):
        vb[z + O, 32:40, :] = gg[z + Q, 32:40, :] * edge[z]

    loop(0, C, edges)

    loop(0, C, lambda z: sweep(vb, va, supply, gg, z, True), 2)
    loop(0, 4, lambda i: sweep(vb, va, supply, gg, jnp.where(i < 2, i - 2, i + C - 2), False))
    loads[4].wait()
    v_copy = pltpu.make_async_copy(va.at[3:39], v_out, sems.at[5])
    g_copy = pltpu.make_async_copy(gg, g_out, sems.at[6])
    v_copy.start()
    g_copy.start()

    def residual(z, rates, sourced):
        for t, here, sums in plane(va, z + O):
            r = k * sums
            if rates is not None:
                inner = r[0:32] - (rates(t) + BASE) * here[0:32]
                if sourced:
                    inner = inner + supply[z, :, lanes(t)]
                r = jnp.concatenate([inner, r[32:40] - dh[z + Q, :, lanes(t)] * here[32:40]], axis=0)
            yield t, r

    def coarse(m, zs, rates, sourced):
        parts = [residual(zs[i], rates[i], sourced) for i in range(2)]
        for (t, first), (_, second) in zip(*parts):
            xp[t, m, 0:20, :] = halve_rows(first + second, rs, t)

    def from_message(ref, n):
        return lambda t: ref[uptake_part(t)].astype(F32)[32 * n : 32 * n + 32]

    def inner(m):
        zs = (2 * m - 4, 2 * m - 3)
        coarse(m, zs, [lambda t, z=z: upt[z, :, lanes(t)] for z in zs], True)

    loop(2, 18, inner)
    for m, ref, z in ((1, zl, -2), (18, zh, C)):
        coarse(m, (z, z + 1), [from_message(ref, 0), from_message(ref, 1)], False)

    def outer(i):
        for t, r in residual(jnp.where(i == 0, -3, 34), None, False):
            xp[t, 19 * i, 0:20, :] = halve_rows(r, rs, t)

    loop(0, 2, outer)

    sub = iota((20, 8, 128), 1)
    for t, tile in enumerate(halve_lanes(xp, 20, 24)):
        last = tile[:, 16:24]
        last = jnp.where(sub < 2, last, jnp.where(sub >= 6, shifted(last, 4, 1), 0.0))
        c1[:, 0:16, lanes(t)] = tile[:, 0:16]
        c1[:, 16:24, lanes(t)] = last

    sub1 = iota((5, 8, 512), 1)
    first, last, halo = [c1[:, 8 * n : 8 * n + 8].reshape(5, 4, 8, 512) for n in range(3)]
    sub4 = iota((5, 4, 8, 512), 2)
    to_high = in_three(sub1, jnp.where(sub4 >= 4, last, halo), *HIGH_PACK)
    to_low = in_three(sub1, jnp.where(sub4 >= 4, halo, first), *LOW_PACK)
    sub1 = iota((12, 8, 512), 1)
    first = q1[:, 0:8, :].reshape(12, 2, 8, 512)
    last = q1[:, 8:16, :].reshape(12, 2, 8, 512)
    low_rates = halves(sub1, first[:, 0], first[:, 1]).reshape(96, 512)
    high_rates = uppers(sub1, last[:, 0], last[:, 1]).reshape(96, 512)
    filler = jnp.zeros((8, 512), F32)
    for ref, sources, rates in ((mxl, to_low, low_rates), (mxh, to_high, high_rates)):
        ref[0:128, :] = jnp.concatenate([sources.reshape(120, 512), filler], axis=0).astype(BF16)
        ref[128:224, :] = rates.astype(BF16)

    v_copy.wait()
    g_copy.wait()
    s_copy.wait()


def edges_kernel(v_in, s_in, vzl, vzh, pxl, pxh, cnl, cnh, vx, vz, sx, sz, sems):
    copies = [
        (v_in.at[:, 0:8, :], vx.at[:, 0:8, :]),
        (v_in.at[:, 24:40, :], vx.at[:, 8:24, :]),
        (v_in.at[0:4], vz.at[0]),
        (v_in.at[32:36], vz.at[1]),
        (s_in.at[:, 0:8, :], sx.at[:, 0:8, :]),
        (s_in.at[:, 24:32, :], sx.at[:, 8:16, :]),
        (s_in.at[0], sz.at[0]),
        (s_in.at[31], sz.at[1]),
    ]
    copies = [pltpu.make_async_copy(src, dst, sems.at[i]) for i, (src, dst) in enumerate(copies)]
    for copy in copies:
        copy.start()
    sub8 = iota((8, 1024), 0)
    for copy in copies:
        copy.wait()

    for i, (level0, corners) in enumerate(((vzl, cnl), (vzh, cnh))):
        level0[0:160, :] = vz[i].reshape(160, 1024).astype(BF16)
        last = jnp.concatenate([sz[i], jnp.zeros((16, 1024), F32)], axis=0)
        level0[160:208, :] = last.astype(BF16)
        planes = [vz[i, n] for n in range(4)]
        low = [pack_low((v[0:8], v[32:40]), (w[0:8], w[32:40])) for v, w in (planes[0:2], planes[2:4])]
        high = [pack_high((v[24:32], v[32:40]), (w[24:32], w[32:40])) for v, w in (planes[0:2], planes[2:4])]
        corners[...] = jnp.concatenate(low + high, axis=0).astype(BF16)

    def sides(i):
        lows, highs = [], []
        for j in range(2):
            p = 4 * i + 2 * j
            v, w = vx[p], vx[p + 1]
            lows.append(pack_low((v[0:8], v[16:24]), (w[0:8], w[16:24])))
            highs.append(pack_high((v[8:16], v[16:24]), (w[8:16], w[16:24])))
        rows = pl.ds(pl.multiple_of(16 * i, 16), 16)
        pxl[rows, :] = jnp.concatenate(lows, axis=0).astype(BF16)
        pxh[rows, :] = jnp.concatenate(highs, axis=0).astype(BF16)

    loop(0, 9, sides)

    def sources(i):
        lows, highs = [], []
        for j in range(2):
            low, high = jnp.zeros((8, 1024), F32), jnp.zeros((8, 1024), F32)
            for n in range(8):
                z = 16 * i + 8 * j + n
                low = jnp.where(sub8 == n, shifted(sx[z, 0:8, :], n, 0), low)
                high = jnp.where(sub8 == n, shifted(sx[z, 8:16, :], n + 1, 0), high)
            lows.append(low)
            highs.append(high)
        rows = pl.ds(pl.multiple_of(16 * i + 144, 16), 16)
        pxl[rows, :] = jnp.concatenate(lows, axis=0).astype(BF16)
        pxh[rows, :] = jnp.concatenate(highs, axis=0).astype(BF16)

    loop(0, 2, sources)


def outer_rows(sub):
    return (sub < 2) | (sub >= 6)


def pack_pair(sub, a, b):
    return jnp.where(outer_rows(sub), a, shifted(b, 4, 0))


def pack_low(first, second):
    sub = iota((8, 1024), 0)
    a, b = [jnp.where(sub < 4, near, halo) for near, halo in (first, second)]
    return pack_pair(sub, a, b)


def pack_high(first, second):
    sub = iota((8, 1024), 0)
    a, b = [jnp.where(sub >= 4, near, halo) for near, halo in (first, second)]
    return pack_pair(sub, a, b)


def in_three(sub, tiles, free, turns):
    spare = (sub == free) | (sub == free + 1)
    last = tiles[:, 3]
    parts = [jnp.where(spare, shifted(last, turn, 1), tiles[:, i]) for i, turn in enumerate(turns)]
    return jnp.stack(parts, axis=1)


def out_of_three(sub, parts, free, turns):
    last = None
    for i, turn in enumerate(turns):
        back = shifted(parts[:, i], -turn, 1)
        home = (free - turn) % 8
        here = (sub == home) | (sub == home + 1)
        last = jnp.where(here, back, 0.0 if last is None else last)
    return jnp.stack([parts[:, 0], parts[:, 1], parts[:, 2], last], axis=1)


HIGH_PACK = (2, (-2, 4, 2))
LOW_PACK = (4, (-2, 4, 2))


def middle_kernel(nz, nx, c1, q_in, r2, cnl, cnh, vzl, vzh, mxl, mxh, f1, g1, v1, g2, z1l, z1h, z2l, z2h, q0, va, vv, rs, xp):
    iz, ix = lax.axis_index("gz"), lax.axis_index("xy")
    k = spread(1)
    base = 1.0 + 6.0 * k
    sub5 = iota((5, 8, 512), 1)
    low = out_of_three(sub5, mxl[0:128, :].astype(F32)[0:120].reshape(5, 3, 8, 512), *HIGH_PACK).reshape(20, 8, 512)
    high = out_of_three(sub5, mxh[0:128, :].astype(F32)[0:120].reshape(5, 3, 8, 512), *LOW_PACK).reshape(20, 8, 512)
    sub = iota((20, 8, 512), 1)
    for p in (0, 1, 22, 23):
        f1[p] = jnp.zeros((24, 512), F32)
    f1[2:22, 0:8] = c1[:, 0:8] + jnp.where(sub < 2, low, 0.0)
    f1[2:22, 8:16] = c1[:, 8:16] + jnp.where(sub >= 6, high, 0.0)
    f1[2:22, 16:24] = c1[:, 16:24] + jnp.where(sub >= 4, low, high)
    low, high = [ref[128:224, :].astype(F32).reshape(12, 8, 512) for ref in (mxl, mxh)]
    sub12 = iota((12, 8, 512), 1)
    even = jnp.where(sub12 >= 4, shifted(low, 4, 1), high)
    odd = jnp.where(sub12 >= 4, low, shifted(high, 4, 1))
    q0[:, 0:16] = q_in[...]
    q0[:, 16:24] = jnp.stack([even, odd], axis=1).reshape(24, 8, 512)
    shape = (24, 24, 128)
    valid = inside(shape, 0, -4, None, iz, 16, nz) & inside(shape, 1, 0, 20, ix, 16, nx)
    for t in range(4):
        g = jnp.where(valid, OMEGA, 0.0) / (q0[:, :, lanes(t)] + base)
        g1[:, :, lanes(t)] = g
        va[:, :, lanes(t)] = g * f1[:, :, lanes(t)]
    for p in (0, 1, 24, 25):
        vv[p] = jnp.zeros((24, 512), F32)

    def sweep(p):
        for t, here, sums in plane(va, p):
            vv[p + 1, :, lanes(t)] = KEEP * here + g1[p, :, lanes(t)] * (f1[p, :, lanes(t)] + k * sums)

    loop(1, 23, sweep, 2)
    v1[...] = vv[1:25]

    def residual(p):
        for t, here, sums in plane(vv, p + 1):
            yield t, f1[p, :, lanes(t)] + k * sums - (q0[p, :, lanes(t)] + base) * here

    def coarse(m):
        for (t, first), (_, second) in zip(residual(2 * m), residual(2 * m + 1)):
            xp[t, m] = halve_rows((first + second)[0:16], rs, t)

    loop(0, 12, coarse)
    for t, tile in enumerate(halve_lanes(xp, 12, 8)):
        g2[:, lanes(t)] = tile.reshape(96, 128)
        for ref in (z1l, z1h):
            ref[240:288, lanes(t)] = tile[0:6].reshape(48, 128).astype(BF16)
            ref[240:288, lanes(2 + t)] = tile[6:12].reshape(48, 128).astype(BF16)
    for ref, corners, level0 in ((z1l, cnl, vzl), (z1h, cnh, vzh)):
        ref[288:320, :] = corners[:, 0:512]
        ref[320:352, :] = corners[:, 512:1024]
        ref[352:560, :] = level0[:, 0:512]
        ref[560:768, :] = level0[:, 512:1024]
    for ref, p in ((z1l, 2), (z1h, 18)):
        ref[0:144, :] = vv[p : p + 6].reshape(144, 512).astype(BF16)
        ref[144:240, :] = f1[p : p + 4].reshape(96, 512).astype(BF16)
    low, high = far_along_z(nz, iz, g2[0:48, :], g2[48:96, :])
    z2l[0:48, :] = low.astype(BF16)
    z2h[0:48, :] = high.astype(BF16)
    low, high = far_along_z(nz, iz, r2[0:32, :], r2[32:64, :])
    z2l[48:80, :] = low.astype(BF16)
    z2h[48:80, :] = high.astype(BF16)


def back_kernel(
    nz, nx, f_in, g1, v1, z1l, z1h, xl, xh, vxl_in, vxh_in, own2, n2l, n2h, m2l, m2h, q_own, v_in, g_in, s_in,
    out_hbm,
    f2, q2, h2, a2, b2, rs, xp, xpr, wa, w1, zsl, zsh, vb, ws,
    v2, gg, supply, fsl, fsh, out, f1, vxl, vxh, sems,
):
    iz, ix = lax.axis_index("gz"), lax.axis_index("xy")
    matrix = doubling()
    level0 = [
        pltpu.make_async_copy(src, dst, sems.at[i])
        for i, (src, dst) in enumerate(((v_in, v2), (g_in, gg), (s_in, supply)))
    ]
    for copy in level0:
        copy.start()

    f1[...] = f_in[...]
    wa[...] = v1[...]
    for ref, p in ((z1l, 1), (z1h, 17)):
        wa[p : p + 6] = wa[p : p + 6] + ref[0:144, :].astype(F32).reshape(6, 24, 512)
        f1[p + 1 : p + 5] = f1[p + 1 : p + 5] + ref[144:240, :].astype(F32).reshape(4, 24, 512)

    f2[:, 0:8, :] = own2[...]
    f2[:, 8:16, :] = n2h[0:256, :].astype(F32).reshape(32, 8, 256)
    f2[:, 16:24, :] = far_tile(m2l[0:128, :].astype(F32), m2h[0:128, :].astype(F32))
    f2[:, 24:32, :] = n2l[0:256, :].astype(F32).reshape(32, 8, 256)
    q2[:, 0:8, :] = q_own[...]
    q2[:, 16:24, :] = far_tile(m2l[128:256, :].astype(F32), m2h[128:256, :].astype(F32))
    for ref, rows in ((xh, slice(8, 16)), (xl, slice(24, 32))):
        for n in range(3):
            for t in range(2):
                part = ref[rates2_part(n, t)].astype(F32).reshape(8, 8, 128)
                q2[8 * n + 4 : 8 * n + 12, rows, lanes(t)] = part
    for ref, rows in ((n2h, slice(8, 16)), (n2l, slice(24, 32))):
        outer = ref[256:320, :].astype(F32).reshape(8, 8, 256)
        q2[0:4, rows, :] = outer[0:4]
        q2[28:32, rows, :] = outer[4:8]

    k = spread(2)
    base = 1.0 + 6.0 * k
    shape = (32, 32, 128)
    valid = inside(shape, 0, -12, None, iz, 8, nz) & inside(shape, 1, 0, 20, ix, 8, nx)
    for t in range(2):
        g = jnp.where(valid, OMEGA, 0.0) / (q2[:, :, lanes(t)] + base)
        h2[:, :, lanes(t)] = g
        a2[:, :, lanes(t)] = g * f2[:, :, lanes(t)]
    b2[0] = a2[0]
    b2[31] = a2[31]

    def sweep2(src, dst):
        def body(p):
            for t, here, sums in plane(src, p):
                dst[p, :, lanes(t)] = KEEP * here + h2[p, :, lanes(t)] * (f2[p, :, lanes(t)] + k * sums)

        return body

    loop(1, 31, sweep2(a2, b2), 2)

    def coarse(m):
        total, rates = [0.0, 0.0], [0.0, 0.0]
        for j in range(2):
            p = 2 * m + j
            for t, here, sums in plane(b2, p):
                r = f2[p, :, lanes(t)] + k * sums - (q2[p, :, lanes(t)] + base) * here
                total[t] = total[t] + r
                rates[t] = rates[t] + q2[p, :, lanes(t)]
        for t in range(2):
            xp[t, m] = halve_rows(total[t], rs, t)
            xpr[t, m] = halve_rows(rates[t], rs, t + 2)

    for t in range(2):
        for m in (0, 15):
            xp[t, m] = jnp.zeros((16, 128), F32)
            xpr[t, m] = jnp.zeros((16, 128), F32)
    loop(1, 15, coarse)

    shape = (16, 16, 128)
    valid = inside(shape, 0, -6, None, iz, 4, nz) & inside(shape, 1, 0, 10, ix, 4, nx)
    k3 = spread(3)
    (source,) = halve_lanes(xp, 16, 16)
    (rates,) = halve_lanes(xpr, 16, 16)
    g = jnp.where(valid, OMEGA, 0.0) / (rates + (1.0 + 6.0 * k3))
    v = g * source
    lane = iota(shape, 2)
    for repeat in range(3):
        edge = jnp.zeros((1, 16, 128), F32)
        sums = jnp.concatenate([v[1:], edge], axis=0) + jnp.concatenate([edge, v[:-1]], axis=0)
        sums = sums + shifted(v, 1, 1) + shifted(v, -1, 1)
        sums = sums + jnp.where(lane == 0, 0.0, shifted(v, 1, 2)) + jnp.where(lane == 127, 0.0, shifted(v, -1, 2))
        v = KEEP * v + g * (source + k3 * sums)

    wide = split_dot(v[4:12].reshape(128, 128), matrix).reshape(8, 16, 256)
    for m in range(8):
        for t in range(2):
            part = wide[m, :, lanes(t)]
            rs[t, pl.ds(0, 16, stride=2), :] = part
            rs[t, pl.ds(1, 16, stride=2), :] = part
            for j in range(2):
                p = 8 + 2 * m + j
                b2[p, :, lanes(t)] = b2[p, :, lanes(t)] + rs[t, 0:32, :]
    loop(9, 23, sweep2(b2, a2), 2)
    loop(10, 22, sweep2(a2, b2), 2)

    w = b2[10:22]
    near, far = w[:, 8:16], w[:, 24:32]
    near = jnp.where(iota((12, 8, 256), 1) < 2, near, shifted(far, 4, 1))
    w = jnp.concatenate([w[:, 0:8], near], axis=1).reshape(192, 256)
    wide = [split_dot(w[:, lanes(t)], matrix) for t in range(2)]
    wide = jnp.concatenate(wide, axis=1).reshape(12, 16, 512)
    for m in range(12):
        for t in range(4):
            part = wide[m, :, lanes(t)]
            rs[t, pl.ds(0, 16, stride=2), :] = part
            rs[t, pl.ds(1, 16, stride=2), :] = part
            for j in range(2):
                p = 2 * m + j
                wa[p, :, lanes(t)] = wa[p, :, lanes(t)] + rs[t, 0:24, :]
    k1 = spread(1)

    def sweep1(src, dst):
        def body(p):
            for t, here, sums in plane(src, p):
                dst[p, :, lanes(t)] = KEEP * here + g1[p, :, lanes(t)] * (f1[p, :, lanes(t)] + k1 * sums)

        return body

    loop(2, 22, sweep1(wa, w1), 2)
    loop(3, 21, sweep1(w1, wa), 2)

    sub = iota((18, 8, 128), 1)
    for t in range(4):
        halo = wa[3:21, 16:24, lanes(t)]
        halo = jnp.where(sub < 2, halo, shifted(halo, 4, 1))
        w = jnp.concatenate([wa[3:21, 0:16, lanes(t)], halo], axis=1)
        ws[:, :, t * 256 : t * 256 + 256] = split_dot(w.reshape(432, 128), matrix).reshape(18, 24, 256)

    for copy in level0:
        copy.wait()
    for ref, message in ((zsl, z1l), (zsh, z1h)):
        ref[:, 0:512] = message[352:560, :].astype(F32)
        ref[:, 512:1024] = message[560:768, :].astype(F32)
    for ref, src, near in ((vxl, vxl_in, n2l), (vxh, vxh_in, n2h)):
        ref[...] = src[...]
        for n in range(4):
            cols = slice(256 * n, 256 * n + 256)
            for i, rows in enumerate((slice(0, 16), slice(128, 144))):
                corner = near[320 + 32 * n + 16 * i : 336 + 32 * n + 16 * i, :].astype(F32)
                ref[rows, cols] = (src[rows, cols].astype(F32) + corner).astype(BF16)
    for i in range(4):
        v2[i] = v2[i] + zsl[40 * i : 40 * i + 40, :]
        v2[32 + i] = v2[32 + i] + zsh[40 * i : 40 * i + 40, :]

    s8 = iota((8, 128), 0)

    outer = outer_rows(s8)

    def correct(i):
        rows = pl.ds(pl.multiple_of(16 * i, 16), 16)
        for t in range(NT):
            low = vxl[rows, lanes(t)].astype(F32)
            high = vxh[rows, lanes(t)].astype(F32)
            for n in range(2):
                part = ws[2 * i + n, :, lanes(t)]
                rs[t, pl.ds(0, 24, stride=2), :] = part
                rs[t, pl.ds(1, 24, stride=2), :] = part
                for j in range(2):
                    p = 4 * i + 2 * n + j
                    lo, hi = low[8 * n : 8 * n + 8], high[8 * n : 8 * n + 8]
                    if j:
                        lo, hi = shifted(lo, 4, 0), shifted(hi, 4, 0)
                    v2[p, 0:8, lanes(t)] = v2[p, 0:8, lanes(t)] + rs[t, 0:8, :] + jnp.where(s8 < 2, lo, 0.0)
                    v2[p, 8:24, lanes(t)] = v2[p, 8:24, lanes(t)] + rs[t, 8:24, :]
                    v2[p, 24:32, lanes(t)] = v2[p, 24:32, lanes(t)] + rs[t, 24:32, :] + jnp.where(s8 >= 6, hi, 0.0)
                    extra = jnp.where(outer, jnp.where(s8 >= 4, lo, hi), 0.0)
                    v2[p, 32:40, lanes(t)] = v2[p, 32:40, lanes(t)] + rs[t, 32:40, :] + extra

    loop(0, 9, correct)
    k0 = spread(0)

    def first(i):
        rows = pl.ds(pl.multiple_of(16 * i + 144, 16), 16)
        for t in range(NT):
            fsl[:, lanes(t)] = vxl[rows, lanes(t)].astype(F32)
            fsh[:, lanes(t)] = vxh[rows, lanes(t)].astype(F32)

        def step(j):
            z = 16 * i + j
            start = pl.multiple_of((j // 8) * 8, 8)
            turn = lax.rem(j, 8)
            for t, here, sums in plane(v2, z + 2):
                lo = pltpu.roll(fsl[pl.ds(start, 8), lanes(t)], 7 - turn, 0)
                hi = pltpu.roll(fsh[pl.ds(start, 8), lanes(t)], lax.rem(8 - turn, 8), 0)
                f = jnp.where(s8 == 7, lo, jnp.where(s8 == 0, hi, 0.0))
                g = gg[z + 2, :, lanes(t)]
                inner = k0 * sums
                vb[z + 1, 0:32, lanes(t)] = KEEP * here[0:32] + g[0:32] * (supply[z, :, lanes(t)] + inner[0:32])
                vb[z + 1, 32:40, lanes(t)] = KEEP * here[32:40] + g[32:40] * (f + inner[32:40])

        loop(0, 16, step, 2)

    loop(0, 2, first)
    for p, ref in ((1, zsl), (34, zsh)):
        for t, here, sums in plane(v2, p):
            g = gg[p, :, lanes(t)]
            vb[p - 1, :, lanes(t)] = KEEP * here + g * (ref[160:200, lanes(t)] + k0 * sums)

    def second(z):
        for t, here, sums in plane(vb, z + 1):
            g = gg[z + 2, 0:32, lanes(t)]
            out[z, :, lanes(t)] = KEEP * here[0:32] + g * (supply[z, :, lanes(t)] + k0 * sums[0:32])

    stores = []
    for i in range(4):
        part = pl.ds(8 * i, 8)
        loop(8 * i, 8 * i + 8, second, 2)
        stores.append(pltpu.make_async_copy(out.at[part], out_hbm.at[part], sems.at[3 + i]))
        stores[i].start()
    for copy in stores:
        copy.wait()


VMEM = pl.BlockSpec(memory_space=pltpu.VMEM)
SMEM = pl.BlockSpec(memory_space=pltpu.SMEM)
ANY = pl.BlockSpec(memory_space=pl.ANY)


def call(kernel, outs, scratch, smem, args, out_specs=None, in_hbm=0):
    moved = sum(a.size * a.dtype.itemsize for a in list(args) + list(outs))
    return pl.pallas_call(
        kernel,
        out_shape=tuple(outs),
        in_specs=[SMEM] * smem + [VMEM] * (len(args) - smem - in_hbm) + [ANY] * in_hbm,
        out_specs=tuple(out_specs or [VMEM] * len(outs)),
        scratch_shapes=scratch,
        compiler_params=pltpu.CompilerParams(vmem_limit_bytes=58 * 2**20),
        cost_estimate=pl.CostEstimate(flops=20 * moved, bytes_accessed=moved, transcendentals=0),
    )(*args)


def shaped(shape, dtype=F32):
    return jax.ShapeDtypeStruct(shape, dtype)


def both_ways(to_low, to_high, axis, distance=1):
    count = lax.axis_size(axis)
    up = [(i, i + distance) for i in range(count - distance)]
    down = [(j, i) for i, j in up]
    return lax.ppermute(to_high, axis, up), lax.ppermute(to_low, axis, down)


def two_away(to_low, to_high):
    count = lax.axis_size("gz")
    if count != 4:
        return both_ways(to_low, to_high, "gz", 2)
    came = lax.ppermute(to_low, "gz", [(i, (i + 2) % 4) for i in range(4)])
    return came, came


def shards(density, uptake, brick_values, brick_ids, slot_counts):
    nz, nx = lax.axis_size("gz"), lax.axis_size("xy")
    scratch = pltpu.VMEM
    half = lambda *shape: shaped(shape, BF16)
    full = lambda *shape: shaped(shape, F32)

    own, r1, r2, zl, zh, uxl, uxh = call(
        lambda *refs: first_kernel(2 * nx, *refs),
        [
            half(BLOCK, 384), full(16, 16, 512), full(64, 256), half(Z_ROWS, 384), half(Z_ROWS, 384),
            half(64, 1024), half(64, 1024),
        ],
        [
            scratch((8, 32, 128), F32), scratch((8, 16, 16, 128), F32), scratch((4, 16, 128), F32),
            scratch((4, 8, 8, 128), F32), scratch((SLOTS, BRICK), F32), scratch((C, C, 1024), F32),
            pltpu.SemaphoreType.DMA((1,)),
        ],
        2,
        (brick_ids, slot_counts, brick_values, uptake),
        in_hbm=1,
    )
    zl, zh = both_ways(zl, zh, "gz")
    q1, xl, xh = call(
        first_x_kernel,
        [full(24, 16, 512), half(X_ROWS, 384), half(X_ROWS, 384)],
        [],
        0,
        (own, r1, r2, uxl, uxh, zl, zh),
    )
    s0, g0, v1, edge = call(
        lambda *refs: own_kernel(nz, *refs),
        [full(C, C, 1024), full(36, C, 1024), full(34, C, 1024), full(C, 8, 1024)],
        [
            scratch((C, C, 1024), F32),
            scratch((C, C, 1024), F32),
            scratch((C, C, 1024), F32),
            scratch((36, C, 1024), F32),
            scratch((34, C, 1024), F32),
            scratch((C, 8, 1024), F32),
            scratch((42, 40, 1024), F32),
            scratch((384, 1024), BF16),
            scratch((1024, 384), BF16),
            pltpu.SemaphoreType.DMA((6,)),
        ],
        0,
        (own, zl, zh, density, uptake),
        [ANY] * 4,
        in_hbm=2,
    )
    xl, xh = both_ways(xl, xh, "xy")

    c1, mxl, mxh, v2, gg, supply = call(
        lambda *refs: pre_kernel(nz, nx, *refs),
        [
            full(20, 24, 512),
            half(224, 512),
            half(224, 512),
            full(36, 40, 1024),
            full(36, 40, 1024),
            full(C, C, 1024),
        ],
        [
            scratch((42, 40, 1024), F32),
            scratch((42, 40, 1024), F32),
            scratch((C, C, 1024), F32),
            scratch((C, C, 1024), F32),
            scratch((36, 8, 1024), F32),
            scratch((36, 40, 1024), F32),
            scratch((C, 8, 1024), F32),
            scratch((768, 1024), BF16),
            scratch((1024, 768), BF16),
            scratch((8, 40, 128), F32),
            scratch((8, 20, 24, 128), F32),
            scratch((72, 1024), F32),
            scratch((72, 1024), F32),
            pltpu.SemaphoreType.DMA((8,)),
        ],
        0,
        (xl, xh, zl, zh, q1, s0, g0, v1, edge, uptake),
        [VMEM] * 3 + [ANY] * 3,
        in_hbm=5,
    )
    mxl, mxh = both_ways(mxl, mxh, "xy")
    vzl, vzh, pxl, pxh, cnl, cnh = call(
        edges_kernel,
        [
            half(208, 1024), half(208, 1024), half(176, 1024), half(176, 1024), half(32, 1024), half(32, 1024),
        ],
        [
            scratch((36, 24, 1024), F32), scratch((2, 4, 40, 1024), F32), scratch((C, 16, 1024), F32),
            scratch((2, C, 1024), F32), pltpu.SemaphoreType.DMA((8,)),
        ],
        0,
        (v2, supply),
        in_hbm=2,
    )
    pxl, pxh, mxl, mxh = lax.optimization_barrier((pxl, pxh, mxl, mxh))
    vxl, vxh = both_ways(pxl, pxh, "xy")
    f1, g1, v1, g2, z1l, z1h, z2l, z2h = call(
        lambda *refs: middle_kernel(nz, nx, *refs),
        [
            full(24, 24, 512), full(24, 24, 512), full(24, 24, 512), full(96, 256),
            half(768, 512), half(768, 512), half(FAR, 256), half(FAR, 256),
        ],
        [
            scratch((24, 24, 512), F32), scratch((24, 24, 512), F32), scratch((26, 24, 512), F32),
            scratch((4, 16, 128), F32), scratch((4, 12, 8, 128), F32),
        ],
        0,
        (c1, q1, r2, cnl, cnh, vzl, vzh, mxl, mxh),
    )
    z1l, z1h = both_ways(z1l, z1h, "gz")
    z2l, z2h = two_away(z2l, z2h)
    own2, q2, nl, nh, fl, fh = call(
        lambda *refs: source_window_kernel(nz, *refs),
        [full(32, 8, 256), full(32, 8, 256), half(448, 256), half(448, 256), half(256, 256), half(256, 256)],
        [],
        0,
        (g2, z1l, z1h, z2l, z2h, r2, zl, zh),
    )
    nl, nh = both_ways(nl, nh, "xy")
    fl, fh = both_ways(fl, fh, "xy", 2)
    window2 = scratch((32, 32, 256), F32)
    window1 = scratch((24, 24, 512), F32)
    (concentration,) = call(
        lambda *refs: back_kernel(nz, nx, *refs),
        [full(C, C, 1024)],
        [
            window2, window2, window2, window2, window2,
            scratch((8, 48, 128), F32),
            scratch((2, 16, 16, 128), F32),
            scratch((2, 16, 16, 128), F32),
            window1, window1,
            scratch((208, 1024), F32),
            scratch((208, 1024), F32),
            scratch((34, 40, 1024), F32),
            scratch((18, 24, 1024), F32),
            scratch((36, 40, 1024), F32),
            scratch((36, 40, 1024), F32),
            scratch((C, C, 1024), F32),
            scratch((16, 1024), F32),
            scratch((16, 1024), F32),
            scratch((C, C, 1024), F32),
            window1,
            scratch((176, 1024), BF16),
            scratch((176, 1024), BF16),
            pltpu.SemaphoreType.DMA((7,)),
        ],
        0,
        (f1, g1, v1, z1l, z1h, xl, xh, vxl, vxh, own2, nl, nh, fl, fh, q2, v2, gg, supply),
        [ANY],
        in_hbm=3,
    )
    return supply, concentration


def solution(mesh):
    return jax.shard_map(
        shards,
        mesh=mesh,
        in_specs=(
            P("gz", "xy", None),
            P("gz", "xy", None),
            P(("gz", "xy"), None),
            P(("gz", "xy")),
            P(("gz", "xy"), None),
        ),
        out_specs=(P("gz", "xy", None), P("gz", "xy", None)),
        check_vma=False,
    )
```

```python
import jax
import jax.numpy as jnp
from jax import lax
from jax.experimental import pallas as pl
from jax.experimental.pallas import tpu as pltpu
from jax.sharding import PartitionSpec as P

EDGE = 16
CAP = 8
BRICK = 4096
SLOTS = 72
KAPPA = 32.0
OMEGA = 0.8
KEEP = 1.0 - OMEGA

C = 32
NT = 8
F32 = jnp.float32
BF16 = jnp.bfloat16


def spread(level):
    return KAPPA / 4.0**level


def shifted(values, distance, axis):
    return pltpu.roll(values, distance % values.shape[axis], axis)


def iota(shape, dim):
    return lax.broadcasted_iota(jnp.int32, shape, dim)


def lanes(t):
    return slice(t * 128, (t + 1) * 128)


def plane(ref, p):
    count = ref.shape[2] // 128
    rows = ref.shape[1]
    lane = iota((rows, 128), 1)
    before, here = None, ref[p, :, lanes(0)]
    for t in range(count):
        after = ref[p, :, lanes(t + 1)] if t + 1 < count else None
        low = jnp.where(lane == 127, 0.0 if before is None else before, here)
        high = jnp.where(lane == 0, 0.0 if after is None else after, here)
        sums = shifted(low, 1, 1) + shifted(high, -1, 1)
        sums = sums + (shifted(here, 1, 0) + shifted(here, -1, 0))
        sums = sums + (ref[p - 1, :, lanes(t)] + ref[p + 1, :, lanes(t)])
        yield t, here, sums
        before, here = here, after


def loop(start, stop, body, unroll=1):
    def step(i, carry):
        body(i)
        return carry

    lax.fori_loop(start, stop, step, 0, unroll=unroll)


def split_dot(a, b):
    high = a.astype(BF16)
    low = (a - high.astype(F32)).astype(BF16)
    return jnp.dot(high, b, preferred_element_type=F32) + jnp.dot(low, b, preferred_element_type=F32)


def pooling():
    return jnp.where(iota((256, 128), 0) // 2 == iota((256, 128), 1), 0.125, 0.0).astype(BF16)


def doubling():
    return jnp.where(iota((128, 256), 1) // 2 == iota((128, 256), 0), 1.0, 0.0).astype(BF16)


def halve_rows(values, rs, t):
    rows = values.shape[0]
    rs[t, 0:rows, :] = values
    return rs[t, pl.ds(0, rows // 2, stride=2), :] + rs[t, pl.ds(1, rows // 2, stride=2), :]


def halve_lanes(xp, planes, rows):
    matrix = pooling()
    tiles = []
    for t in range(0, xp.shape[0], 2):
        pair = jnp.concatenate([xp[t].reshape(planes * rows, 128), xp[t + 1].reshape(planes * rows, 128)], axis=1)
        tiles.append(split_dot(pair, matrix).reshape(planes, rows, 128))
    return tiles


def inside(shape, dim, first, wrap, index, size, count):
    place = iota(shape, dim) + first
    if wrap is not None:
        place = jnp.where(place < wrap, place, place - shape[dim])
    place = place + index * size
    return (place >= 0) & (place < count * size)


BLOCK = 272
X_ROWS = BLOCK + 3 * 64 + 2 * 64
Z_ROWS = BLOCK + 5 * 64


def uptake_part(t):
    return slice(BLOCK + 64 * (t // 3), BLOCK + 64 * (t // 3) + 64), lanes(t % 3)


def rates2_part(n, t):
    k = 3 * t + n
    first = BLOCK + 3 * 64 + 64 * (k % 2)
    return slice(first, first + 64), lanes(k // 2)


def transposed_bricks(bricks_x, ids, counts, bricks, xs, targets):
    xs[...] = bricks[...].astype(F32)
    row = iota((1, 8, 128), 1)
    group = iota((1, 8, 128), 2) // 16
    group16 = iota((16, 128), 1) // 16
    per_y = 64

    def block(j, out, part):
        start = pl.multiple_of(j * 8, 8)
        x = jnp.stack([xs[pl.ds(start, 8), lanes(k)] for k in range(32)])
        for s in (4, 2, 1):
            up = shifted(shifted(x, -s, 1), 16 * s, 2)
            down = shifted(shifted(x, s, 1), -16 * s, 2)
            row_bit = (row // s) % 2
            group_bit = (group // s) % 2
            x = jnp.where(row_bit == group_bit, x, jnp.where(row_bit == 0, up, down))
        x = jnp.where(group < counts[0, j], x, 0.0)
        out[0:256, part] = x.reshape(256, 128).astype(BF16)
        names = jnp.zeros((16, 128), jnp.int32)
        for e in range(CAP):
            number = ids[j * 8 + e]
            by = lax.rem(number, per_y)
            rest = lax.div(number, per_y)
            bx = lax.rem(rest, 2)
            bz = lax.rem(lax.div(rest, bricks_x), 2)
            names = jnp.where(group16 == e, (bz * 2 + bx) * per_y + by, names)
        out[256:272, part] = names.astype(F32).astype(BF16)

    for i, out in enumerate(targets):
        for d in range(3):
            block(3 * i + d, out, lanes(d))


def first_kernel(bricks_x, ids, counts, bricks, uptake_in, own, r1, r2, zl, zh, xl, xh, rs, xp, rs1, xp1, xs, uptake, sems):
    load = pltpu.make_async_copy(uptake_in, uptake, sems.at[0])
    load.start()
    transposed_bricks(bricks_x, ids, counts, bricks, xs, (zl, own, zh))
    load.wait()

    def pair(m):
        for t in range(NT):
            both = uptake[2 * m, :, lanes(t)] + uptake[2 * m + 1, :, lanes(t)]
            xp[t, m] = halve_rows(both, rs, t)

    loop(0, 16, pair)
    for t, tile in enumerate(halve_lanes(xp, 16, 16)):
        r1[:, :, lanes(t)] = tile

    def pair1(m):
        for t in range(4):
            both = r1[2 * m, :, lanes(t)] + r1[2 * m + 1, :, lanes(t)]
            xp1[t, m] = halve_rows(both, rs1, t)

    loop(0, 8, pair1)
    for t, tile in enumerate(halve_lanes(xp1, 8, 8)):
        r2[:, lanes(t)] = tile.reshape(64, 128)
    for ref, u, r in ((zl, slice(0, 2), slice(0, 4)), (zh, slice(30, 32), slice(12, 16))):
        for t in range(8):
            ref[uptake_part(t)] = uptake[u, :, lanes(t)].reshape(64, 128).astype(BF16)
        for t in range(4):
            ref[uptake_part(8 + t)] = r1[r, :, lanes(t)].reshape(64, 128).astype(BF16)
        for t in range(2):
            ref[uptake_part(12 + t)] = r2[:, lanes(t)].astype(BF16)
        ref[uptake_part(14)] = jnp.zeros((64, 128), BF16)

    sub = iota((8, 1024), 0)

    def columns(i):
        lows, highs = [], []
        for j in range(2):
            low, high = jnp.zeros((8, 1024), F32), jnp.zeros((8, 1024), F32)
            for n in range(4):
                z = 8 * i + 4 * j + n
                low = jnp.where(sub // 2 == n, shifted(uptake[z, 0:8, :], 2 * n, 0), low)
                high = jnp.where(sub // 2 == n, shifted(uptake[z, 24:32, :], 2 * n + 2, 0), high)
            lows.append(low)
            highs.append(high)
        rows = pl.ds(pl.multiple_of(16 * i, 16), 16)
        xl[rows, :] = jnp.concatenate(lows, axis=0).astype(BF16)
        xh[rows, :] = jnp.concatenate(highs, axis=0).astype(BF16)

    loop(0, 4, columns)


def far_along_z(nz, iz, to_low, to_high):
    if nz != 4:
        return to_low, to_high
    one = jnp.where(iz < 2, to_high, to_low)
    return one, one


def halves(sub, first, second):
    return jnp.where(sub < 4, first, shifted(second, 4, 1))


def uppers(sub, first, second):
    return jnp.where(sub < 4, shifted(first, 4, 1), second)


def far_messages(window):
    planes, _, width = window.shape
    pairs = window.reshape(planes // 2, 2, 8, width)
    sub = iota((planes // 2, 8, width), 1)
    size = (planes * 4, width)
    return halves(sub, pairs[:, 0], pairs[:, 1]).reshape(size), uppers(sub, pairs[:, 0], pairs[:, 1]).reshape(size)


def far_tile(from_low, from_high):
    width = from_low.shape[-1]
    low, high = from_low.reshape(-1, 8, width), from_high.reshape(-1, 8, width)
    sub = iota(low.shape, 1)
    even = jnp.where(sub < 4, high, shifted(low, 4, 1))
    odd = jnp.where(sub < 4, shifted(high, 4, 1), low)
    return jnp.stack([even, odd], axis=1).reshape(-1, 8, width)


def first_x_kernel(own, r1, r2, uxl, uxh, zl, zh, q1, xl, xh):
    q1[4:20] = r1[...]
    for ref, planes in ((zl, slice(0, 4)), (zh, slice(20, 24))):
        for t in range(4):
            q1[planes, :, lanes(t)] = ref[uptake_part(8 + t)].astype(F32).reshape(4, 16, 128)
    for ref, d in ((xl, 0), (xh, 2)):
        for n, src in enumerate((own, zl, zh)):
            ref[0:BLOCK, lanes(n)] = src[0:BLOCK, lanes(d)]
        for t in range(2):
            ref[rates2_part(0, t)] = zl[uptake_part(12 + t)]
            ref[rates2_part(1, t)] = r2[:, lanes(t)].astype(BF16)
            ref[rates2_part(2, t)] = zh[uptake_part(12 + t)]
    sub = iota((8, 128), 0)
    lows, highs = [], []
    for t in range(8):
        xl[uptake_part(t)] = uxl[:, lanes(t)]
        xh[uptake_part(t)] = uxh[:, lanes(t)]
        both = [ref[uptake_part(t)].astype(F32) for ref in (zl, zh)]
        planes = [both[0][0:32], both[0][32:64], both[1][0:32], both[1][32:64]]
        to_low, to_high = jnp.zeros((8, 128), F32), jnp.zeros((8, 128), F32)
        for n, p in enumerate(planes):
            here = sub // 2 == n
            to_low = jnp.where(here, shifted(p[0:8], 2 * n, 0), to_low)
            to_high = jnp.where(here, shifted(p[24:32], 2 * n + 2, 0), to_high)
        lows.append(to_low)
        highs.append(to_high)
    xl[uptake_part(8)] = jnp.concatenate(lows, axis=0).astype(BF16)
    xh[uptake_part(8)] = jnp.concatenate(highs, axis=0).astype(BF16)


FAR = 80


def source_window_kernel(nz, own, zl, zh, z2l, z2h, r2, firstl, firsth, f2, q2, nl, nh, fl, fh):
    iz = lax.axis_index("gz")
    zeros = jnp.zeros((10, 8, 256), F32)
    f2[0:10] = zeros
    f2[22:32] = zeros
    f2[10:22] = own[...].reshape(12, 8, 256)
    for ref, planes in ((zl, slice(2, 14)), (zh, slice(18, 30))):
        part = jnp.concatenate([ref[240:288, 0:256], ref[240:288, 256:512]], axis=0).astype(F32)
        f2[planes] = f2[planes] + part.reshape(12, 8, 256)
    for ref, planes, exists in ((z2l, slice(0, 6), iz >= 2), (z2h, slice(26, 32), iz < nz - 2)):
        part = jnp.where(exists, ref[0:48, :].astype(F32), 0.0)
        f2[planes] = f2[planes] + part.reshape(6, 8, 256)
    q2[0:4] = z2l[48:80, :].astype(F32).reshape(4, 8, 256)
    q2[28:32] = z2h[48:80, :].astype(F32).reshape(4, 8, 256)
    q2[12:20] = r2[...].reshape(8, 8, 256)
    for ref, planes in ((firstl, slice(4, 12)), (firsth, slice(20, 28))):
        for t in range(2):
            q2[planes, :, lanes(t)] = ref[uptake_part(12 + t)].astype(F32).reshape(8, 8, 128)
    for i, near in enumerate((nl, nh)):
        near[0:256, :] = f2[...].reshape(256, 256).astype(BF16)
        near[256:288, :] = z2l[48:80, :]
        near[288:320, :] = z2h[48:80, :]
        for n in range(4):
            rows = slice(288 + 32 * (n // 2) + 16 * i, 304 + 32 * (n // 2) + 16 * i)
            cols = slice(256 * (n % 2), 256 * (n % 2) + 256)
            near[320 + 32 * n : 336 + 32 * n, :] = zl[rows, cols]
            near[336 + 32 * n : 352 + 32 * n, :] = zh[rows, cols]
    for i, ref in enumerate((f2, q2)):
        to_low, to_high = far_messages(ref[...])
        fl[128 * i : 128 * i + 128, :] = to_low.astype(BF16)
        fh[128 * i : 128 * i + 128, :] = to_high.astype(BF16)


O = 5
Q = 2
BASE = 1.0 + 6.0 * KAPPA


def scatter(blocks, hot, left):
    lane = iota((128, 128), 1)
    for i, (ref, part) in enumerate(blocks):
        name = ref[256:272, part].astype(F32).astype(jnp.int32)[0:1]
        tiles = lax.shift_right_logical(name, 6)
        at_y = (name & 63) * 16 + (lane[0:1] & 15)
        at_y = jnp.broadcast_to(at_y.astype(F32), (128, 128)).T.astype(jnp.int32)
        for t in range(NT):
            hot[128 * i : 128 * i + 128, lanes(t)] = jnp.where(at_y == lane + 128 * t, 1.0, 0.0).astype(BF16)
        values = ref[0:256, part].astype(F32)
        for tile in range(4):
            left[256 * tile : 256 * tile + 256, lanes(i)] = jnp.where(tiles == tile, values, 0.0).astype(BF16)
    for n in range(4):
        cols = slice(n * 256, (n + 1) * 256)
        sums = jnp.dot(left[...], hot[:, cols], preferred_element_type=F32)
        for tile in range(4):
            bz, bx = tile // 2, tile % 2
            yield 16 * bz, slice(16 * bx, 16 * bx + 16), cols, sums[256 * tile : 256 * tile + 256].reshape(16, 16, 256)


def sweep(src, dst, source, gg, z, sourced):
    for t, here, sums in plane(src, z + O):
        inner = KAPPA * sums
        g = gg[z + Q, :, lanes(t)]
        if sourced:
            body = inner[0:32] + source[z, :, lanes(t)]
            dst[z + O, 0:32, lanes(t)] = KEEP * here[0:32] + g[0:32] * body
            dst[z + O, 32:40, lanes(t)] = KEEP * here[32:40] + g[32:40] * inner[32:40]
        else:
            dst[z + O, :, lanes(t)] = KEEP * here + g * inner


def own_kernel(
    nz, own, zl, zh, density, uptake, s_out, g_out, v_out, edge_out,
    dens, upt, s0, g0, v1, edge, va, hot, left, sems,
):
    iz = lax.axis_index("gz")
    loads = [pltpu.make_async_copy(density, dens, sems.at[0]), pltpu.make_async_copy(uptake, upt, sems.at[1])]
    stores = [
        pltpu.make_async_copy(src, dst, sems.at[2 + i])
        for i, (src, dst) in enumerate(((s0, s_out), (g0, g_out), (v1, v_out), (edge, edge_out)))
    ]
    for copy in loads:
        copy.start()
    for p in (3, 4, 37, 38):
        va[p] = jnp.zeros((40, 1024), F32)
    for n in range(4):
        ref, valid = (zl, iz > 0) if n < 2 else (zh, iz < nz - 1)
        q = n if n < 2 else 32 + n
        rows = slice(32 * (n % 2), 32 * (n % 2) + 32)
        for t in range(NT):
            g0[q, :, lanes(t)] = jnp.where(valid, OMEGA, 0.0) / (ref[uptake_part(t)].astype(F32)[rows] + BASE)

    blocks = [(ref, lanes(1)) for ref in (own, zl, zh)]
    waiting = list(loads[0:1])
    for z, rows, cols, sums in scatter(blocks, hot, left):
        while waiting:
            waiting.pop().wait()
        planes = slice(z, z + 16)
        s0[planes, rows, cols] = dens[planes, rows, cols] + sums
    stores[0].start()
    loads[1].wait()

    def own_plane(z):
        va[z + O, 0:32, :] = dens[z]
        va[z + O, 32:40, :] = jnp.zeros((8, 1024), F32)
        g0[z + Q] = OMEGA / (upt[z] + BASE)

    loop(0, C, own_plane)
    stores[1].start()

    def first(z):
        for t, here, sums in plane(va, z + O):
            inner = KAPPA * sums
            body = inner[0:32] + s0[z, :, lanes(t)]
            v1[z + 1, :, lanes(t)] = KEEP * here[0:32] + g0[z + Q, :, lanes(t)] * body
            edge[z, :, lanes(t)] = inner[32:40]

    loop(0, C, first, 4)
    for z in (-1, C):
        for t in range(NT):
            near = va[z + O + (1 if z < 0 else -1), 0:32, lanes(t)]
            v1[z + 1, :, lanes(t)] = g0[z + Q, :, lanes(t)] * (KAPPA * near)
    for copy in stores[2:]:
        copy.start()
    for copy in stores:
        copy.wait()


def pre_kernel(
    nz, nx, xl, xh, zl, zh, q1, s0, g0, v1, edge_in, uptake,
    c1, mxl, mxh, v_out, g_out, s_out,
    va, vb, supply, upt, dh, gg, edge, hot, left, rs, xp, usl, ush, sems,
):
    iz, ix = lax.axis_index("gz"), lax.axis_index("xy")
    k = KAPPA
    loads = [
        pltpu.make_async_copy(src, dst, sems.at[i])
        for i, (src, dst) in enumerate(
            (
                (s0, supply),
                (v1, vb.at[4:38, 0:32, :]),
                (g0, gg.at[:, 0:32, :]),
                (edge_in, edge),
                (uptake, upt),
            )
        )
    ]
    for copy in loads:
        copy.start()

    for p in (1, 2, 39, 40):
        va[p] = jnp.zeros((40, 1024), F32)
    for p in (2, 3, 38, 39):
        vb[p] = jnp.zeros((40, 1024), F32)
    for p in (4, 37):
        vb[p, 32:40, :] = jnp.zeros((8, 1024), F32)

    sub8 = iota((8, 1024), 0)
    for t in range(NT):
        usl[0:64, lanes(t)] = xl[uptake_part(t)].astype(F32)
        ush[0:64, lanes(t)] = xh[uptake_part(t)].astype(F32)
        usl[64:72, lanes(t)] = xl[uptake_part(8)].astype(F32)[8 * t : 8 * t + 8]
        ush[64:72, lanes(t)] = xh[uptake_part(8)].astype(F32)[8 * t : 8 * t + 8]

    def set_halo(q, low, high, valid_z):
        gz = jnp.where(valid_z, OMEGA, 0.0)
        d = jnp.where(sub8 < 2, high, jnp.where(sub8 >= 6, low, 0.0)) + BASE
        dh[q] = d
        omega = jnp.where(sub8 < 2, jnp.where(ix < nx - 1, gz, 0.0), jnp.where(sub8 >= 6, jnp.where(ix > 0, gz, 0.0), 0.0))
        gg[q, 32:40, :] = omega / d

    def halos(i):
        rows = pl.ds(pl.multiple_of(8 * i, 8), 8)
        low, high = usl[rows, :], ush[rows, :]
        for n in range(4):
            set_halo(4 * i + n + Q, shifted(low, 6 - 2 * n, 0), shifted(high, -2 * n, 0), True)

    loop(0, C // 4, halos)
    low, high = usl[64:72, :], ush[64:72, :]
    for n in range(4):
        exists = iz > 0 if n < 2 else iz < nz - 1
        set_halo(n if n < 2 else 32 + n, shifted(low, 6 - 2 * n, 0), shifted(high, -2 * n, 0), exists)

    blocks = [(ref, lanes(n)) for ref in (xl, xh) for n in range(3)]
    waiting = list(loads[0:3])
    for z, rows, cols, sums in scatter(blocks, hot, left):
        while waiting:
            waiting.pop().wait()
        supply[z : z + 16, rows, cols] = supply[z : z + 16, rows, cols] + sums
        g = gg[z + Q : z + Q + 16, rows, cols]
        vb[z + O : z + O + 16, rows, cols] = vb[z + O : z + O + 16, rows, cols] + g * sums
    loads[3].wait()

    s_copy = pltpu.make_async_copy(supply, s_out, sems.at[7])
    s_copy.start()

    def edges(z):
        vb[z + O, 32:40, :] = gg[z + Q, 32:40, :] * edge[z]

    loop(0, C, edges)

    loop(0, C, lambda z: sweep(vb, va, supply, gg, z, True), 4)
    loop(0, 4, lambda i: sweep(vb, va, supply, gg, jnp.where(i < 2, i - 2, i + C - 2), False))
    loads[4].wait()
    v_copy = pltpu.make_async_copy(va.at[3:39], v_out, sems.at[5])
    g_copy = pltpu.make_async_copy(gg, g_out, sems.at[6])
    v_copy.start()
    g_copy.start()

    def residual(z, rates, sourced):
        for t, here, sums in plane(va, z + O):
            r = k * sums
            if rates is not None:
                inner = r[0:32] - (rates(t) + BASE) * here[0:32]
                if sourced:
                    inner = inner + supply[z, :, lanes(t)]
                r = jnp.concatenate([inner, r[32:40] - dh[z + Q, :, lanes(t)] * here[32:40]], axis=0)
            yield t, r

    def coarse(m, zs, rates, sourced):
        parts = [residual(zs[i], rates[i], sourced) for i in range(2)]
        for (t, first), (_, second) in zip(*parts):
            xp[t, m, 0:20, :] = halve_rows(first + second, rs, t)

    def from_message(ref, n):
        return lambda t: ref[uptake_part(t)].astype(F32)[32 * n : 32 * n + 32]

    def inner(m):
        zs = (2 * m - 4, 2 * m - 3)
        coarse(m, zs, [lambda t, z=z: upt[z, :, lanes(t)] for z in zs], True)

    loop(2, 18, inner, 2)
    for m, ref, z in ((1, zl, -2), (18, zh, C)):
        coarse(m, (z, z + 1), [from_message(ref, 0), from_message(ref, 1)], False)

    def outer(i):
        for t, r in residual(jnp.where(i == 0, -3, 34), None, False):
            xp[t, 19 * i, 0:20, :] = halve_rows(r, rs, t)

    loop(0, 2, outer)

    sub = iota((20, 8, 128), 1)
    for t, tile in enumerate(halve_lanes(xp, 20, 24)):
        last = tile[:, 16:24]
        last = jnp.where(sub < 2, last, jnp.where(sub >= 6, shifted(last, 4, 1), 0.0))
        c1[:, 0:16, lanes(t)] = tile[:, 0:16]
        c1[:, 16:24, lanes(t)] = last

    sub1 = iota((5, 8, 512), 1)
    first, last, halo = [c1[:, 8 * n : 8 * n + 8].reshape(5, 4, 8, 512) for n in range(3)]
    sub4 = iota((5, 4, 8, 512), 2)
    to_high = in_three(sub1, jnp.where(sub4 >= 4, last, halo), *HIGH_PACK)
    to_low = in_three(sub1, jnp.where(sub4 >= 4, halo, first), *LOW_PACK)
    sub1 = iota((12, 8, 512), 1)
    first = q1[:, 0:8, :].reshape(12, 2, 8, 512)
    last = q1[:, 8:16, :].reshape(12, 2, 8, 512)
    low_rates = halves(sub1, first[:, 0], first[:, 1]).reshape(96, 512)
    high_rates = uppers(sub1, last[:, 0], last[:, 1]).reshape(96, 512)
    filler = jnp.zeros((8, 512), F32)
    for ref, sources, rates in ((mxl, to_low, low_rates), (mxh, to_high, high_rates)):
        ref[0:128, :] = jnp.concatenate([sources.reshape(120, 512), filler], axis=0).astype(BF16)
        ref[128:224, :] = rates.astype(BF16)

    v_copy.wait()
    g_copy.wait()
    s_copy.wait()


def edges_kernel(v_in, s_in, vzl, vzh, pxl, pxh, cnl, cnh, vx, vz, sx, sz, sems):
    copies = [
        (v_in.at[:, 0:8, :], vx.at[:, 0:8, :]),
        (v_in.at[:, 24:40, :], vx.at[:, 8:24, :]),
        (v_in.at[0:4], vz.at[0]),
        (v_in.at[32:36], vz.at[1]),
        (s_in.at[:, 0:8, :], sx.at[:, 0:8, :]),
        (s_in.at[:, 24:32, :], sx.at[:, 8:16, :]),
        (s_in.at[0], sz.at[0]),
        (s_in.at[31], sz.at[1]),
    ]
    copies = [pltpu.make_async_copy(src, dst, sems.at[i]) for i, (src, dst) in enumerate(copies)]
    for copy in copies:
        copy.start()
    sub8 = iota((8, 1024), 0)
    for copy in copies:
        copy.wait()

    for i, (level0, corners) in enumerate(((vzl, cnl), (vzh, cnh))):
        level0[0:160, :] = vz[i].reshape(160, 1024).astype(BF16)
        last = jnp.concatenate([sz[i], jnp.zeros((16, 1024), F32)], axis=0)
        level0[160:208, :] = last.astype(BF16)
        planes = [vz[i, n] for n in range(4)]
        low = [pack_low((v[0:8], v[32:40]), (w[0:8], w[32:40])) for v, w in (planes[0:2], planes[2:4])]
        high = [pack_high((v[24:32], v[32:40]), (w[24:32], w[32:40])) for v, w in (planes[0:2], planes[2:4])]
        corners[...] = jnp.concatenate(low + high, axis=0).astype(BF16)

    def sides(i):
        lows, highs = [], []
        for j in range(2):
            p = 4 * i + 2 * j
            v, w = vx[p], vx[p + 1]
            lows.append(pack_low((v[0:8], v[16:24]), (w[0:8], w[16:24])))
            highs.append(pack_high((v[8:16], v[16:24]), (w[8:16], w[16:24])))
        rows = pl.ds(pl.multiple_of(16 * i, 16), 16)
        pxl[rows, :] = jnp.concatenate(lows, axis=0).astype(BF16)
        pxh[rows, :] = jnp.concatenate(highs, axis=0).astype(BF16)

    loop(0, 9, sides)

    def sources(i):
        lows, highs = [], []
        for j in range(2):
            low, high = jnp.zeros((8, 1024), F32), jnp.zeros((8, 1024), F32)
            for n in range(8):
                z = 16 * i + 8 * j + n
                low = jnp.where(sub8 == n, shifted(sx[z, 0:8, :], n, 0), low)
                high = jnp.where(sub8 == n, shifted(sx[z, 8:16, :], n + 1, 0), high)
            lows.append(low)
            highs.append(high)
        rows = pl.ds(pl.multiple_of(16 * i + 144, 16), 16)
        pxl[rows, :] = jnp.concatenate(lows, axis=0).astype(BF16)
        pxh[rows, :] = jnp.concatenate(highs, axis=0).astype(BF16)

    loop(0, 2, sources)


def outer_rows(sub):
    return (sub < 2) | (sub >= 6)


def pack_pair(sub, a, b):
    return jnp.where(outer_rows(sub), a, shifted(b, 4, 0))


def pack_low(first, second):
    sub = iota((8, 1024), 0)
    a, b = [jnp.where(sub < 4, near, halo) for near, halo in (first, second)]
    return pack_pair(sub, a, b)


def pack_high(first, second):
    sub = iota((8, 1024), 0)
    a, b = [jnp.where(sub >= 4, near, halo) for near, halo in (first, second)]
    return pack_pair(sub, a, b)


def in_three(sub, tiles, free, turns):
    spare = (sub == free) | (sub == free + 1)
    last = tiles[:, 3]
    parts = [jnp.where(spare, shifted(last, turn, 1), tiles[:, i]) for i, turn in enumerate(turns)]
    return jnp.stack(parts, axis=1)


def out_of_three(sub, parts, free, turns):
    last = None
    for i, turn in enumerate(turns):
        back = shifted(parts[:, i], -turn, 1)
        home = (free - turn) % 8
        here = (sub == home) | (sub == home + 1)
        last = jnp.where(here, back, 0.0 if last is None else last)
    return jnp.stack([parts[:, 0], parts[:, 1], parts[:, 2], last], axis=1)


HIGH_PACK = (2, (-2, 4, 2))
LOW_PACK = (4, (-2, 4, 2))


def middle_kernel(nz, nx, c1, q_in, r2, cnl, cnh, vzl, vzh, mxl, mxh, f1, g1, v1, g2, z1l, z1h, z2l, z2h, q0, va, vv, rs, xp):
    iz, ix = lax.axis_index("gz"), lax.axis_index("xy")
    k = spread(1)
    base = 1.0 + 6.0 * k
    sub5 = iota((5, 8, 512), 1)
    low = out_of_three(sub5, mxl[0:128, :].astype(F32)[0:120].reshape(5, 3, 8, 512), *HIGH_PACK).reshape(20, 8, 512)
    high = out_of_three(sub5, mxh[0:128, :].astype(F32)[0:120].reshape(5, 3, 8, 512), *LOW_PACK).reshape(20, 8, 512)
    sub = iota((20, 8, 512), 1)
    for p in (0, 1, 22, 23):
        f1[p] = jnp.zeros((24, 512), F32)
    f1[2:22, 0:8] = c1[:, 0:8] + jnp.where(sub < 2, low, 0.0)
    f1[2:22, 8:16] = c1[:, 8:16] + jnp.where(sub >= 6, high, 0.0)
    f1[2:22, 16:24] = c1[:, 16:24] + jnp.where(sub >= 4, low, high)
    low, high = [ref[128:224, :].astype(F32).reshape(12, 8, 512) for ref in (mxl, mxh)]
    sub12 = iota((12, 8, 512), 1)
    even = jnp.where(sub12 >= 4, shifted(low, 4, 1), high)
    odd = jnp.where(sub12 >= 4, low, shifted(high, 4, 1))
    q0[:, 0:16] = q_in[...]
    q0[:, 16:24] = jnp.stack([even, odd], axis=1).reshape(24, 8, 512)
    shape = (24, 24, 128)
    valid = inside(shape, 0, -4, None, iz, 16, nz) & inside(shape, 1, 0, 20, ix, 16, nx)
    for t in range(4):
        g = jnp.where(valid, OMEGA, 0.0) / (q0[:, :, lanes(t)] + base)
        g1[:, :, lanes(t)] = g
        va[:, :, lanes(t)] = g * f1[:, :, lanes(t)]
    for p in (0, 1, 24, 25):
        vv[p] = jnp.zeros((24, 512), F32)

    def sweep(p):
        for t, here, sums in plane(va, p):
            vv[p + 1, :, lanes(t)] = KEEP * here + g1[p, :, lanes(t)] * (f1[p, :, lanes(t)] + k * sums)

    loop(1, 23, sweep, 2)
    v1[...] = vv[1:25]

    def residual(p):
        for t, here, sums in plane(vv, p + 1):
            yield t, f1[p, :, lanes(t)] + k * sums - (q0[p, :, lanes(t)] + base) * here

    def coarse(m):
        for (t, first), (_, second) in zip(residual(2 * m), residual(2 * m + 1)):
            xp[t, m] = halve_rows((first + second)[0:16], rs, t)

    loop(0, 12, coarse)
    for t, tile in enumerate(halve_lanes(xp, 12, 8)):
        g2[:, lanes(t)] = tile.reshape(96, 128)
        for ref in (z1l, z1h):
            ref[240:288, lanes(t)] = tile[0:6].reshape(48, 128).astype(BF16)
            ref[240:288, lanes(2 + t)] = tile[6:12].reshape(48, 128).astype(BF16)
    for ref, corners, level0 in ((z1l, cnl, vzl), (z1h, cnh, vzh)):
        ref[288:320, :] = corners[:, 0:512]
        ref[320:352, :] = corners[:, 512:1024]
        ref[352:560, :] = level0[:, 0:512]
        ref[560:768, :] = level0[:, 512:1024]
    for ref, p in ((z1l, 2), (z1h, 18)):
        ref[0:144, :] = vv[p : p + 6].reshape(144, 512).astype(BF16)
        ref[144:240, :] = f1[p : p + 4].reshape(96, 512).astype(BF16)
    low, high = far_along_z(nz, iz, g2[0:48, :], g2[48:96, :])
    z2l[0:48, :] = low.astype(BF16)
    z2h[0:48, :] = high.astype(BF16)
    low, high = far_along_z(nz, iz, r2[0:32, :], r2[32:64, :])
    z2l[48:80, :] = low.astype(BF16)
    z2h[48:80, :] = high.astype(BF16)


def back_kernel(
    nz, nx, f_in, g1, v1, z1l, z1h, xl, xh, vxl_in, vxh_in, own2, n2l, n2h, m2l, m2h, q_own, v_in, g_in, s_in,
    out_hbm,
    f2, q2, h2, a2, b2, rs, xp, xpr, wa, w1, zsl, zsh, vb, ws,
    v2, gg, supply, fsl, fsh, out, f1, vxl, vxh, sems,
):
    iz, ix = lax.axis_index("gz"), lax.axis_index("xy")
    matrix = doubling()
    level0 = [
        pltpu.make_async_copy(src, dst, sems.at[i])
        for i, (src, dst) in enumerate(((v_in, v2), (g_in, gg), (s_in, supply)))
    ]
    for copy in level0:
        copy.start()

    f1[...] = f_in[...]
    wa[...] = v1[...]
    for ref, p in ((z1l, 1), (z1h, 17)):
        wa[p : p + 6] = wa[p : p + 6] + ref[0:144, :].astype(F32).reshape(6, 24, 512)
        f1[p + 1 : p + 5] = f1[p + 1 : p + 5] + ref[144:240, :].astype(F32).reshape(4, 24, 512)

    f2[:, 0:8, :] = own2[...]
    f2[:, 8:16, :] = n2h[0:256, :].astype(F32).reshape(32, 8, 256)
    f2[:, 16:24, :] = far_tile(m2l[0:128, :].astype(F32), m2h[0:128, :].astype(F32))
    f2[:, 24:32, :] = n2l[0:256, :].astype(F32).reshape(32, 8, 256)
    q2[:, 0:8, :] = q_own[...]
    q2[:, 16:24, :] = far_tile(m2l[128:256, :].astype(F32), m2h[128:256, :].astype(F32))
    for ref, rows in ((xh, slice(8, 16)), (xl, slice(24, 32))):
        for n in range(3):
            for t in range(2):
                part = ref[rates2_part(n, t)].astype(F32).reshape(8, 8, 128)
                q2[8 * n + 4 : 8 * n + 12, rows, lanes(t)] = part
    for ref, rows in ((n2h, slice(8, 16)), (n2l, slice(24, 32))):
        outer = ref[256:320, :].astype(F32).reshape(8, 8, 256)
        q2[0:4, rows, :] = outer[0:4]
        q2[28:32, rows, :] = outer[4:8]

    k = spread(2)
    base = 1.0 + 6.0 * k
    shape = (32, 32, 128)
    valid = inside(shape, 0, -12, None, iz, 8, nz) & inside(shape, 1, 0, 20, ix, 8, nx)
    for t in range(2):
        g = jnp.where(valid, OMEGA, 0.0) / (q2[:, :, lanes(t)] + base)
        h2[:, :, lanes(t)] = g
        a2[:, :, lanes(t)] = g * f2[:, :, lanes(t)]
    b2[0] = a2[0]
    b2[31] = a2[31]

    def sweep2(src, dst):
        def body(p):
            for t, here, sums in plane(src, p):
                dst[p, :, lanes(t)] = KEEP * here + h2[p, :, lanes(t)] * (f2[p, :, lanes(t)] + k * sums)

        return body

    loop(1, 31, sweep2(a2, b2), 2)

    def coarse(m):
        total, rates = [0.0, 0.0], [0.0, 0.0]
        for j in range(2):
            p = 2 * m + j
            for t, here, sums in plane(b2, p):
                r = f2[p, :, lanes(t)] + k * sums - (q2[p, :, lanes(t)] + base) * here
                total[t] = total[t] + r
                rates[t] = rates[t] + q2[p, :, lanes(t)]
        for t in range(2):
            xp[t, m] = halve_rows(total[t], rs, t)
            xpr[t, m] = halve_rows(rates[t], rs, t + 2)

    for t in range(2):
        for m in (0, 15):
            xp[t, m] = jnp.zeros((16, 128), F32)
            xpr[t, m] = jnp.zeros((16, 128), F32)
    loop(1, 15, coarse)

    shape = (16, 16, 128)
    valid = inside(shape, 0, -6, None, iz, 4, nz) & inside(shape, 1, 0, 10, ix, 4, nx)
    k3 = spread(3)
    (source,) = halve_lanes(xp, 16, 16)
    (rates,) = halve_lanes(xpr, 16, 16)
    g = jnp.where(valid, OMEGA, 0.0) / (rates + (1.0 + 6.0 * k3))
    v = g * source
    lane = iota(shape, 2)
    for repeat in range(3):
        edge = jnp.zeros((1, 16, 128), F32)
        sums = jnp.concatenate([v[1:], edge], axis=0) + jnp.concatenate([edge, v[:-1]], axis=0)
        sums = sums + shifted(v, 1, 1) + shifted(v, -1, 1)
        sums = sums + jnp.where(lane == 0, 0.0, shifted(v, 1, 2)) + jnp.where(lane == 127, 0.0, shifted(v, -1, 2))
        v = KEEP * v + g * (source + k3 * sums)

    wide = split_dot(v[4:12].reshape(128, 128), matrix).reshape(8, 16, 256)
    for m in range(8):
        for t in range(2):
            part = wide[m, :, lanes(t)]
            rs[t, pl.ds(0, 16, stride=2), :] = part
            rs[t, pl.ds(1, 16, stride=2), :] = part
            for j in range(2):
                p = 8 + 2 * m + j
                b2[p, :, lanes(t)] = b2[p, :, lanes(t)] + rs[t, 0:32, :]
    loop(9, 23, sweep2(b2, a2), 2)
    loop(10, 22, sweep2(a2, b2), 2)

    w = b2[10:22]
    near, far = w[:, 8:16], w[:, 24:32]
    near = jnp.where(iota((12, 8, 256), 1) < 2, near, shifted(far, 4, 1))
    w = jnp.concatenate([w[:, 0:8], near], axis=1).reshape(192, 256)
    wide = [split_dot(w[:, lanes(t)], matrix) for t in range(2)]
    wide = jnp.concatenate(wide, axis=1).reshape(12, 16, 512)
    for m in range(12):
        for t in range(4):
            part = wide[m, :, lanes(t)]
            rs[t, pl.ds(0, 16, stride=2), :] = part
            rs[t, pl.ds(1, 16, stride=2), :] = part
            for j in range(2):
                p = 2 * m + j
                wa[p, :, lanes(t)] = wa[p, :, lanes(t)] + rs[t, 0:24, :]
    k1 = spread(1)

    def sweep1(src, dst):
        def body(p):
            for t, here, sums in plane(src, p):
                dst[p, :, lanes(t)] = KEEP * here + g1[p, :, lanes(t)] * (f1[p, :, lanes(t)] + k1 * sums)

        return body

    loop(2, 22, sweep1(wa, w1), 2)
    loop(3, 21, sweep1(w1, wa), 2)

    sub = iota((18, 8, 128), 1)
    for t in range(4):
        halo = wa[3:21, 16:24, lanes(t)]
        halo = jnp.where(sub < 2, halo, shifted(halo, 4, 1))
        w = jnp.concatenate([wa[3:21, 0:16, lanes(t)], halo], axis=1)
        ws[:, :, t * 256 : t * 256 + 256] = split_dot(w.reshape(432, 128), matrix).reshape(18, 24, 256)

    for copy in level0:
        copy.wait()
    for ref, message in ((zsl, z1l), (zsh, z1h)):
        ref[:, 0:512] = message[352:560, :].astype(F32)
        ref[:, 512:1024] = message[560:768, :].astype(F32)
    for ref, src, near in ((vxl, vxl_in, n2l), (vxh, vxh_in, n2h)):
        ref[...] = src[...]
        for n in range(4):
            cols = slice(256 * n, 256 * n + 256)
            for i, rows in enumerate((slice(0, 16), slice(128, 144))):
                corner = near[320 + 32 * n + 16 * i : 336 + 32 * n + 16 * i, :].astype(F32)
                ref[rows, cols] = (src[rows, cols].astype(F32) + corner).astype(BF16)
    for i in range(4):
        v2[i] = v2[i] + zsl[40 * i : 40 * i + 40, :]
        v2[32 + i] = v2[32 + i] + zsh[40 * i : 40 * i + 40, :]

    s8 = iota((8, 128), 0)

    outer = outer_rows(s8)

    def correct(i):
        rows = pl.ds(pl.multiple_of(16 * i, 16), 16)
        for t in range(NT):
            low = vxl[rows, lanes(t)].astype(F32)
            high = vxh[rows, lanes(t)].astype(F32)
            for n in range(2):
                part = ws[2 * i + n, :, lanes(t)]
                rs[t, pl.ds(0, 24, stride=2), :] = part
                rs[t, pl.ds(1, 24, stride=2), :] = part
                for j in range(2):
                    p = 4 * i + 2 * n + j
                    lo, hi = low[8 * n : 8 * n + 8], high[8 * n : 8 * n + 8]
                    if j:
                        lo, hi = shifted(lo, 4, 0), shifted(hi, 4, 0)
                    v2[p, 0:8, lanes(t)] = v2[p, 0:8, lanes(t)] + rs[t, 0:8, :] + jnp.where(s8 < 2, lo, 0.0)
                    v2[p, 8:24, lanes(t)] = v2[p, 8:24, lanes(t)] + rs[t, 8:24, :]
                    v2[p, 24:32, lanes(t)] = v2[p, 24:32, lanes(t)] + rs[t, 24:32, :] + jnp.where(s8 >= 6, hi, 0.0)
                    extra = jnp.where(outer, jnp.where(s8 >= 4, lo, hi), 0.0)
                    v2[p, 32:40, lanes(t)] = v2[p, 32:40, lanes(t)] + rs[t, 32:40, :] + extra

    loop(0, 9, correct)
    k0 = spread(0)

    def first(i):
        rows = pl.ds(pl.multiple_of(16 * i + 144, 16), 16)
        for t in range(NT):
            fsl[:, lanes(t)] = vxl[rows, lanes(t)].astype(F32)
            fsh[:, lanes(t)] = vxh[rows, lanes(t)].astype(F32)

        def step(j):
            z = 16 * i + j
            start = pl.multiple_of((j // 8) * 8, 8)
            turn = lax.rem(j, 8)
            for t, here, sums in plane(v2, z + 2):
                lo = pltpu.roll(fsl[pl.ds(start, 8), lanes(t)], 7 - turn, 0)
                hi = pltpu.roll(fsh[pl.ds(start, 8), lanes(t)], lax.rem(8 - turn, 8), 0)
                f = jnp.where(s8 == 7, lo, jnp.where(s8 == 0, hi, 0.0))
                g = gg[z + 2, :, lanes(t)]
                inner = k0 * sums
                vb[z + 1, 0:32, lanes(t)] = KEEP * here[0:32] + g[0:32] * (supply[z, :, lanes(t)] + inner[0:32])
                vb[z + 1, 32:40, lanes(t)] = KEEP * here[32:40] + g[32:40] * (f + inner[32:40])

        loop(0, 16, step, 4)

    loop(0, 2, first)
    for p, ref in ((1, zsl), (34, zsh)):
        for t, here, sums in plane(v2, p):
            g = gg[p, :, lanes(t)]
            vb[p - 1, :, lanes(t)] = KEEP * here + g * (ref[160:200, lanes(t)] + k0 * sums)

    def second(z):
        for t, here, sums in plane(vb, z + 1):
            g = gg[z + 2, 0:32, lanes(t)]
            out[z, :, lanes(t)] = KEEP * here[0:32] + g * (supply[z, :, lanes(t)] + k0 * sums[0:32])

    stores = []
    for i in range(4):
        part = pl.ds(8 * i, 8)
        loop(8 * i, 8 * i + 8, second, 4)
        stores.append(pltpu.make_async_copy(out.at[part], out_hbm.at[part], sems.at[3 + i]))
        stores[i].start()
    for copy in stores:
        copy.wait()


VMEM = pl.BlockSpec(memory_space=pltpu.VMEM)
SMEM = pl.BlockSpec(memory_space=pltpu.SMEM)
ANY = pl.BlockSpec(memory_space=pl.ANY)


def call(kernel, outs, scratch, smem, args, out_specs=None, in_hbm=0):
    moved = sum(a.size * a.dtype.itemsize for a in list(args) + list(outs))
    return pl.pallas_call(
        kernel,
        out_shape=tuple(outs),
        in_specs=[SMEM] * smem + [VMEM] * (len(args) - smem - in_hbm) + [ANY] * in_hbm,
        out_specs=tuple(out_specs or [VMEM] * len(outs)),
        scratch_shapes=scratch,
        compiler_params=pltpu.CompilerParams(vmem_limit_bytes=58 * 2**20),
        cost_estimate=pl.CostEstimate(flops=20 * moved, bytes_accessed=moved, transcendentals=0),
    )(*args)


def shaped(shape, dtype=F32):
    return jax.ShapeDtypeStruct(shape, dtype)


def both_ways(to_low, to_high, axis, distance=1):
    count = lax.axis_size(axis)
    up = [(i, i + distance) for i in range(count - distance)]
    down = [(j, i) for i, j in up]
    return lax.ppermute(to_high, axis, up), lax.ppermute(to_low, axis, down)


def two_away(to_low, to_high):
    count = lax.axis_size("gz")
    if count != 4:
        return both_ways(to_low, to_high, "gz", 2)
    came = lax.ppermute(to_low, "gz", [(i, (i + 2) % 4) for i in range(4)])
    return came, came


def shards(density, uptake, brick_values, brick_ids, slot_counts):
    nz, nx = lax.axis_size("gz"), lax.axis_size("xy")
    scratch = pltpu.VMEM
    half = lambda *shape: shaped(shape, BF16)
    full = lambda *shape: shaped(shape, F32)

    own, r1, r2, zl, zh, uxl, uxh = call(
        lambda *refs: first_kernel(2 * nx, *refs),
        [
            half(BLOCK, 384), full(16, 16, 512), full(64, 256), half(Z_ROWS, 384), half(Z_ROWS, 384),
            half(64, 1024), half(64, 1024),
        ],
        [
            scratch((8, 32, 128), F32), scratch((8, 16, 16, 128), F32), scratch((4, 16, 128), F32),
            scratch((4, 8, 8, 128), F32), scratch((SLOTS, BRICK), F32), scratch((C, C, 1024), F32),
            pltpu.SemaphoreType.DMA((1,)),
        ],
        2,
        (brick_ids, slot_counts, brick_values, uptake),
        in_hbm=1,
    )
    zl, zh = both_ways(zl, zh, "gz")
    q1, xl, xh = call(
        first_x_kernel,
        [full(24, 16, 512), half(X_ROWS, 384), half(X_ROWS, 384)],
        [],
        0,
        (own, r1, r2, uxl, uxh, zl, zh),
    )
    s0, g0, v1, edge = call(
        lambda *refs: own_kernel(nz, *refs),
        [full(C, C, 1024), full(36, C, 1024), full(34, C, 1024), full(C, 8, 1024)],
        [
            scratch((C, C, 1024), F32),
            scratch((C, C, 1024), F32),
            scratch((C, C, 1024), F32),
            scratch((36, C, 1024), F32),
            scratch((34, C, 1024), F32),
            scratch((C, 8, 1024), F32),
            scratch((42, 40, 1024), F32),
            scratch((384, 1024), BF16),
            scratch((1024, 384), BF16),
            pltpu.SemaphoreType.DMA((6,)),
        ],
        0,
        (own, zl, zh, density, uptake),
        [ANY] * 4,
        in_hbm=2,
    )
    xl, xh = both_ways(xl, xh, "xy")

    c1, mxl, mxh, v2, gg, supply = call(
        lambda *refs: pre_kernel(nz, nx, *refs),
        [
            full(20, 24, 512),
            half(224, 512),
            half(224, 512),
            full(36, 40, 1024),
            full(36, 40, 1024),
            full(C, C, 1024),
        ],
        [
            scratch((42, 40, 1024), F32),
            scratch((42, 40, 1024), F32),
            scratch((C, C, 1024), F32),
            scratch((C, C, 1024), F32),
            scratch((36, 8, 1024), F32),
            scratch((36, 40, 1024), F32),
            scratch((C, 8, 1024), F32),
            scratch((768, 1024), BF16),
            scratch((1024, 768), BF16),
            scratch((8, 40, 128), F32),
            scratch((8, 20, 24, 128), F32),
            scratch((72, 1024), F32),
            scratch((72, 1024), F32),
            pltpu.SemaphoreType.DMA((8,)),
        ],
        0,
        (xl, xh, zl, zh, q1, s0, g0, v1, edge, uptake),
        [VMEM] * 3 + [ANY] * 3,
        in_hbm=5,
    )
    mxl, mxh = both_ways(mxl, mxh, "xy")
    vzl, vzh, pxl, pxh, cnl, cnh = call(
        edges_kernel,
        [
            half(208, 1024), half(208, 1024), half(176, 1024), half(176, 1024), half(32, 1024), half(32, 1024),
        ],
        [
            scratch((36, 24, 1024), F32), scratch((2, 4, 40, 1024), F32), scratch((C, 16, 1024), F32),
            scratch((2, C, 1024), F32), pltpu.SemaphoreType.DMA((8,)),
        ],
        0,
        (v2, supply),
        in_hbm=2,
    )
    pxl, pxh, mxl, mxh = lax.optimization_barrier((pxl, pxh, mxl, mxh))
    vxl, vxh = both_ways(pxl, pxh, "xy")
    f1, g1, v1, g2, z1l, z1h, z2l, z2h = call(
        lambda *refs: middle_kernel(nz, nx, *refs),
        [
            full(24, 24, 512), full(24, 24, 512), full(24, 24, 512), full(96, 256),
            half(768, 512), half(768, 512), half(FAR, 256), half(FAR, 256),
        ],
        [
            scratch((24, 24, 512), F32), scratch((24, 24, 512), F32), scratch((26, 24, 512), F32),
            scratch((4, 16, 128), F32), scratch((4, 12, 8, 128), F32),
        ],
        0,
        (c1, q1, r2, cnl, cnh, vzl, vzh, mxl, mxh),
    )
    z1l, z1h = both_ways(z1l, z1h, "gz")
    z2l, z2h = two_away(z2l, z2h)
    own2, q2, nl, nh, fl, fh = call(
        lambda *refs: source_window_kernel(nz, *refs),
        [full(32, 8, 256), full(32, 8, 256), half(448, 256), half(448, 256), half(256, 256), half(256, 256)],
        [],
        0,
        (g2, z1l, z1h, z2l, z2h, r2, zl, zh),
    )
    nl, nh = both_ways(nl, nh, "xy")
    fl, fh = both_ways(fl, fh, "xy", 2)
    window2 = scratch((32, 32, 256), F32)
    window1 = scratch((24, 24, 512), F32)
    (concentration,) = call(
        lambda *refs: back_kernel(nz, nx, *refs),
        [full(C, C, 1024)],
        [
            window2, window2, window2, window2, window2,
            scratch((8, 48, 128), F32),
            scratch((2, 16, 16, 128), F32),
            scratch((2, 16, 16, 128), F32),
            window1, window1,
            scratch((208, 1024), F32),
            scratch((208, 1024), F32),
            scratch((34, 40, 1024), F32),
            scratch((18, 24, 1024), F32),
            scratch((36, 40, 1024), F32),
            scratch((36, 40, 1024), F32),
            scratch((C, C, 1024), F32),
            scratch((16, 1024), F32),
            scratch((16, 1024), F32),
            scratch((C, C, 1024), F32),
            window1,
            scratch((176, 1024), BF16),
            scratch((176, 1024), BF16),
            pltpu.SemaphoreType.DMA((7,)),
        ],
        0,
        (f1, g1, v1, z1l, z1h, xl, xh, vxl, vxh, own2, nl, nh, fl, fh, q2, v2, gg, supply),
        [ANY],
        in_hbm=3,
    )
    return supply, concentration


def solution(mesh):
    return jax.shard_map(
        shards,
        mesh=mesh,
        in_specs=(
            P("gz", "xy", None),
            P("gz", "xy", None),
            P(("gz", "xy"), None),
            P(("gz", "xy")),
            P(("gz", "xy"), None),
        ),
        out_specs=(P("gz", "xy", None), P("gz", "xy", None)),
        check_vma=False,
    )
```
